32 devices in a mesh: blk: 8 (over z, y), dp: 4 (over x, core).
Axes of the slice: x: 2, y: 2, z: 4, core: 2. Of those that a mesh axis runs over, the one named last changes fastest.
Arguments:
- tokens: bfloat16 [4, 3072, 640], P('dp', 'blk'), may hold values from -6 to 6
- lengths: int32 [4, 4], P('dp'), may hold values from 0 to 3072, as said below
- cotangent: bfloat16 [4, 3072, 640], P('dp', 'blk'), may hold values from -6 to 6
- norm_in: float32 [640], replicated, may hold values from 0.1 to 1.9
- w_query: bfloat16 [640, 1024], replicated, may hold values from -0.25 to 0.25
- w_key: bfloat16 [640, 256], replicated, may hold values from -0.25 to 0.25
- w_value: bfloat16 [640, 256], replicated, may hold values from -0.25 to 0.25
- query_gain: float32 [256], replicated, may hold values from 0.1 to 1.9
- key_gain: float32 [256], replicated, may hold values from 0.1 to 1.9
- w_out: bfloat16 [1024, 640], replicated, may hold values from -0.1875 to 0.1875
- norm_attn: float32 [640], replicated, may hold values from 0.1 to 1.9
- norm_pre: float32 [640], replicated, may hold values from 0.1 to 1.9
- w_gate: bfloat16 [640, 2048], replicated, may hold values from -0.25 to 0.25
- w_up: bfloat16 [640, 2048], replicated, may hold values from -0.25 to 0.25
- w_down: bfloat16 [2048, 640], replicated, may hold values from -0.125 to 0.125
- norm_post: float32 [640], replicated, may hold values from 0.1 to 1.9
Outputs:
- output: bfloat16 [4, 3072, 640], P('dp', 'blk')
- input_grad: bfloat16 [4, 3072, 640], P('dp', 'blk')
- grad_norm_in: float32 [640], replicated
- grad_query: float32 [640, 1024], replicated
- grad_key: float32 [640, 256], replicated
- grad_value: float32 [640, 256], replicated
- grad_query_gain: float32 [256], replicated
- grad_key_gain: float32 [256], replicated
- grad_out: float32 [1024, 640], replicated
- grad_norm_attn: float32 [640], replicated
- grad_norm_pre: float32 [640], replicated
- grad_gate: float32 [640, 2048], replicated
- grad_up: float32 [640, 2048], replicated
- grad_down: float32 [2048, 640], replicated
- grad_norm_post: float32 [640], replicated
The draws below stay inside these ranges and needn't reach their ends.
Inputs may be any that keep to these rules, and one draw needn't show every extreme that they name: Each row holds the lengths of a group's sequences in order, summing to 3072: one, two or four positive lengths followed by zeros; some group in every draw is a single sequence of 3072 tokens.
All inputs are finite; a program needn't handle non-finite values.
Results may differ from the reference program's by a relative error of at most 0.025.
Values may be sent and summed in bfloat16 or wider, within the bound.
A program may use at most 192 MiB of HBM per device.

```python
import jax
import jax.numpy as jnp
from jax import lax

D = 640
FF = 2048
HEADS = 4
HEAD = 256
TOK_DEV = 384
GROUP = 3072
N_BLK = 8
N_DP = 4


def draw_lengths(key, part):
    key = jax.random.fold_in(key, 7)
    group = TOK_DEV * N_BLK
    quarter = group // 4
    order = jax.random.permutation(jax.random.fold_in(key, 1), N_DP)
    kind = order % 3
    cut_two = jax.random.randint(jax.random.fold_in(key, 2), (N_DP,), quarter, 3 * quarter + 1)
    jitter = jax.random.randint(jax.random.fold_in(key, 3), (N_DP, 3), -(quarter // 4), quarter // 4 + 1)
    bounds = quarter * jnp.arange(1, 4, dtype=jnp.int32)[None, :] + jitter
    zeros_col = jnp.zeros((N_DP, 1), jnp.int32)
    edges = jnp.concatenate([zeros_col, bounds, zeros_col + group], axis=1)
    four = edges[:, 1:] - edges[:, :-1]
    two = jnp.stack([cut_two, group - cut_two, cut_two * 0, cut_two * 0], axis=1)
    one = jnp.stack([cut_two * 0 + group, cut_two * 0, cut_two * 0, cut_two * 0], axis=1)
    picked = jnp.where((kind == 0)[:, None], one, jnp.where((kind == 1)[:, None], two, four))
    return picked.astype(jnp.int32)


def shard_levels(own_key, dims, shards, smallest, largest):
    level = 1.0
    for axis_at, blocks in shards:
        steps = jax.random.uniform(jax.random.fold_in(jax.random.fold_in(own_key, 6), axis_at), (blocks,), jnp.float32, smallest / len(shards), largest / len(shards))
        level = level * jnp.repeat(jnp.exp(steps), dims[axis_at] // blocks).reshape((-1,) + (1,) * (len(dims) - 1 - axis_at))
    return level


def scatter_about(key, dims, deviation, limit, cuts=(), kind=jnp.bfloat16):
    entries = jax.random.normal(key, dims, jnp.float32) * deviation
    if len(cuts) > 0:
        entries = shard_levels(key, dims, cuts, -0.22, 0.18) * entries
    return jnp.clip(entries, min=-limit, max=limit).astype(kind)


def setup_inputs(seed: int = 0) -> dict:
    key_list = jax.random.split(jax.random.key(seed), 17)
    return {
        "tokens": scatter_about(key_list[0], (N_DP, GROUP, D), 1.0, 6.0, ((0, 4), (1, 8))),
        "lengths": draw_lengths(jax.random.fold_in(key_list[16], 71), 0),
        "cotangent": scatter_about(key_list[2], (N_DP, GROUP, D), 1.0, 6.0, ((0, 4), (1, 8))),
        "norm_in": jnp.clip(1.0 + 0.18 * jax.random.normal(key_list[3], (D,), jnp.float32), 0.1, 1.9),
        "w_query": scatter_about(key_list[4], (D, HEADS * HEAD), D ** -0.5, 0.25),
        "w_key": scatter_about(key_list[5], (D, HEAD), D ** -0.5, 0.25),
        "w_value": scatter_about(key_list[6], (D, HEAD), D ** -0.5, 0.25),
        "query_gain": jnp.clip(1.0 + 0.18 * jax.random.normal(key_list[7], (HEAD,), jnp.float32), 0.1, 1.9),
        "key_gain": jnp.clip(1.0 + 0.18 * jax.random.normal(key_list[8], (HEAD,), jnp.float32), 0.1, 1.9),
        "w_out": scatter_about(key_list[9], (HEADS * HEAD, D), (HEADS * HEAD) ** -0.5, 0.1875),
        "norm_attn": jnp.clip(1.0 + 0.18 * jax.random.normal(key_list[10], (D,), jnp.float32), 0.1, 1.9),
        "norm_pre": jnp.clip(1.0 + 0.18 * jax.random.normal(key_list[11], (D,), jnp.float32), 0.1, 1.9),
        "w_gate": scatter_about(key_list[12], (D, FF), D ** -0.5, 0.25),
        "w_up": scatter_about(key_list[13], (D, FF), D ** -0.5, 0.25),
        "w_down": scatter_about(key_list[14], (FF, D), FF ** -0.5, 0.125),
        "norm_post": jnp.clip(1.0 + 0.18 * jax.random.normal(key_list[15], (D,), jnp.float32), 0.1, 1.9),
    }


EPS = 1e-06
BASE = 1000000.0
NEG = -1e+30

@jax.custom_vjp
def low(v):
    return lax.optimization_barrier(v.astype(jnp.bfloat16)).astype(jnp.float32)

@jax.custom_vjp
def low_back(v):
    return v

def low_keep(v):
    return (low(v), None)

def low_pass(kept, grad):
    return (grad,)

def back_keep(v):
    return (v, None)

def back_low(kept, grad):
    return (low(grad),)
low.defvjp(low_keep, low_pass)
low_back.defvjp(back_keep, back_low)

def normed(value, gain):
    return value * lax.rsqrt(lax.optimization_barrier(jnp.mean(value * value, axis=-1, keepdims=True)) + EPS) * gain

def segment_of(index, row):
    ends = jnp.cumsum(row)
    seg = lax.optimization_barrier(jnp.sum((index[:, None] >= ends[None, :]).astype(jnp.int32), axis=1))
    starts = ends - row
    slots = jnp.arange(row.shape[0], dtype=jnp.int32)
    begin = lax.optimization_barrier(jnp.sum(jnp.where(slots[None, :] == seg[:, None], starts[None, :], 0), axis=1))
    return (seg, index - begin)

def rotary_tables(places, head):
    half = head // 2
    freq = jnp.exp(-(2.0 * jnp.arange(half, dtype=jnp.float32) / head) * jnp.log(BASE))
    angle = places.astype(jnp.float32)[:, None] * freq[None, :]
    return (jnp.cos(angle), jnp.sin(angle))

def prepare(proj, gain, cosine, sine):
    value = normed(proj, gain)
    half = value.shape[-1] // 2
    first = value[..., :half]
    second = value[..., half:]
    return jnp.concatenate([first * cosine - second * sine, second * cosine + first * sine], axis=-1)

def matmul(left, right):
    return jnp.dot(left, right, precision=lax.Precision.HIGHEST)

def reference(tokens, lengths, cotangent, norm_in, w_query, w_key, w_value, query_gain, key_gain, w_out, norm_attn, norm_pre, w_gate, w_up, w_down, norm_post):
    parts = tokens.shape[0]
    group = tokens.shape[1]
    width = tokens.shape[2]
    head = query_gain.shape[0]
    heads = w_query.shape[1] // head
    index = jnp.arange(group, dtype=jnp.int32)
    segs, places = jax.vmap(lambda row: segment_of(index, row))(lengths)
    cosine, sine = rotary_tables(places.reshape(-1), head)
    block = min(512, group)
    scale = head ** (-0.5)

    def attend_group(item):
        query, keys, values, seg = item

        def one_block(piece):
            q_blk, s_blk, i_blk = piece
            raw = jnp.einsum('qhd,kd->hqk', q_blk, keys, precision=lax.Precision.HIGHEST)
            scores = scale * low_back(raw)
            allowed = (s_blk[:, None] == seg[None, :]) & (i_blk[:, None] >= index[None, :])
            scores = jnp.where(allowed[None], scores, NEG)
            top = lax.optimization_barrier(jnp.max(scores, axis=-1, keepdims=True))
            expo = jnp.where(allowed[None], jnp.exp(scores - top), 0.0)
            probs = expo / lax.optimization_barrier(jnp.sum(expo, axis=-1, keepdims=True))
            return jnp.einsum('hqk,kd->qhd', low(probs), values, precision=lax.Precision.HIGHEST)
        pieces = (query.reshape(group // block, block, heads, head), seg.reshape(group // block, block), index.reshape(group // block, block))
        return lax.map(jax.checkpoint(one_block), pieces).reshape(group, heads, head)

    def forward(x, norm_in, w_query, w_key, w_value, query_gain, key_gain, w_out, norm_attn, norm_pre, w_gate, w_up, w_down, norm_post):
        normal_a = low(normed(x, norm_in))
        q_proj = low_back(matmul(normal_a, w_query)).reshape(-1, heads, head)
        k_proj = low_back(matmul(normal_a, w_key))
        v_proj = low_back(matmul(normal_a, w_value))
        query = low(prepare(q_proj, query_gain, cosine[:, None, :], sine[:, None, :]))
        keys = low(prepare(k_proj, key_gain, cosine, sine))
        values = low(v_proj)
        attended = lax.map(jax.checkpoint(attend_group), (query.reshape(parts, group, heads, head), keys.reshape(parts, group, head), values.reshape(parts, group, head), segs))
        joined = low(low_back(attended.reshape(-1, heads * head)))
        a_proj = low_back(matmul(joined, w_out))
        x_mid = x + normed(a_proj, norm_attn)
        mixed = low(normed(x_mid, norm_pre))
        gate = low_back(matmul(mixed, w_gate))
        upper = low_back(matmul(mixed, w_up))
        hidden = low(jax.nn.gelu(gate, approximate=True) * upper)
        f_proj = low_back(matmul(hidden, w_down))
        return x_mid + normed(f_proj, norm_post)
    flat = tokens.astype(jnp.float32).reshape(-1, width)
    weights = (norm_in, w_query, w_key, w_value, query_gain, key_gain, w_out, norm_attn, norm_pre, w_gate, w_up, w_down, norm_post)
    weights = tuple((w.astype(jnp.float32) for w in weights))
    result, pull = jax.vjp(forward, flat, *weights)
    grads = pull(cotangent.astype(jnp.float32).reshape(-1, width))
    output = result.reshape(parts, group, width).astype(jnp.bfloat16)
    input_grad = grads[0].reshape(parts, group, width).astype(jnp.bfloat16)
    return (output, input_grad, grads[1], grads[2], grads[3], grads[4], grads[5], grads[6], grads[7], grads[8], grads[9], grads[10], grads[11], grads[12], grads[13])
```

```python
import functools

import jax
import jax.numpy as jnp
from jax import lax
from jax.experimental import pallas as pl
from jax.experimental.pallas import tpu as pltpu
from jax.sharding import PartitionSpec as P

EPS = 1e-06
BASE = 1000000.0
NEG = -1e30


def shifted(array, axis, by):
    peers = lax.axis_size(axis)
    return lax.ppermute(array, axis, [(i, (i + by) % peers) for i in range(peers)])


def from_behind(block, axis, distance):
    devices = range(lax.axis_size(axis))
    route = [(i - distance, i) for i in devices if i - distance in devices]
    return lax.ppermute(block, axis, route)


def normed(value, gain):
    return value * lax.rsqrt(jnp.mean(value * value, axis=-1, keepdims=True) + EPS) * gain


def normed_back(value, gain, grad):
    return jax.vjp(normed, value, gain)[1](grad)


def segment_of(index, row):
    ends = jnp.cumsum(row)
    seg = jnp.sum((index[:, None] >= ends[None, :]).astype(jnp.int32), axis=1)
    starts = ends - row
    slots = jnp.arange(row.shape[0], dtype=jnp.int32)
    begin = jnp.sum(jnp.where(slots[None, :] == seg[:, None], starts[None, :], 0), axis=1)
    return (seg, index - begin)


def rotary_tables(places, head):
    half = head // 2
    freq = jnp.exp(-(2.0 * jnp.arange(half, dtype=jnp.float32) / head) * jnp.log(BASE))
    angle = places.astype(jnp.float32)[:, None] * freq[None, :]
    return (jnp.cos(angle), jnp.sin(angle))


def prepare(proj, gain, cosine, sine):
    value = normed(proj, gain)
    half = value.shape[-1] // 2
    first = value[..., :half]
    second = value[..., half:]
    return jnp.concatenate(
        [first * cosine - second * sine, second * cosine + first * sine], axis=-1
    )


def pass_home(grads):
    return shifted(grads.astype(jnp.bfloat16), "blk", 1).astype(grads.dtype)


MESH = pl.DeviceIdType.MESH


def where_am_i():
    place = lax.axis_index("blk")
    part = lax.axis_index("dp")
    return {
        "z": place // 2,
        "y": lax.rem(place, 2),
        "x": part // 2,
        "core": lax.rem(part, 2),
        "place": place,
        "part": part,
    }


def peers_of(me):
    place, part = me["place"], me["part"]
    return {
        "core": {"blk": place, "dp": part + 1 - 2 * me["core"]},
        "x": {"blk": place, "dp": part + 2 - 4 * me["x"]},
        "y": {"blk": place + 1 - 2 * me["y"], "dp": part},
        "up": {"blk": place + 2, "dp": part},
        "down": {"blk": place - 2, "dp": part},
    }


def greet(me, peers, z_count):
    barrier = pltpu.get_barrier_semaphore()
    for name in ("core", "x", "y"):
        pl.semaphore_signal(barrier, inc=1, device_id=peers[name], device_id_type=MESH)

    @pl.when(me["z"] < z_count - 1)
    def _():
        pl.semaphore_signal(barrier, inc=1, device_id=peers["up"], device_id_type=MESH)

    @pl.when(me["z"] > 0)
    def _():
        pl.semaphore_signal(barrier, inc=1, device_id=peers["down"], device_id_type=MESH)

    ends = (me["z"] == 0).astype(jnp.int32) + (me["z"] == z_count - 1).astype(jnp.int32)
    pl.semaphore_wait(barrier, 5 - ends)


def add_into(target, start, row, extra, count, rows):
    step = 16
    for candidate in (160, 128, 80, 64, 48, 32):
        if rows % candidate == 0:
            step = candidate
            break

    def body(index, carry):
        e = index // (rows // step)
        at = pl.multiple_of(lax.rem(index, rows // step) * step, 16)
        here = pl.ds(pl.multiple_of(row + at, 16), step)
        target[start + e, here, :] = target[start + e, here, :] + extra[e, pl.ds(at, step), :]
        return carry

    lax.fori_loop(0, count * (rows // step), body, 0)


STAGES = 10


class Chunk:
    def __init__(self, number, grad, total, row, rows, first, landing, sems, me, peers, z_count):
        self.grad, self.total, self.row, self.rows = grad, total, row, rows
        self.first, self.second = ("x", "y") if first == "x" else ("y", "x")
        self.land0, self.land1, self.land2 = landing
        self.send, self.recv, self.local = sems
        self.number, self.me, self.peers, self.z_count = number, me, peers, z_count
        self.b1, self.b2, self.core = me[self.first], me[self.second], me["core"]
        self.quad = 4 * self.core
        self.pair = self.quad + 2 * self.b1
        self.own = self.pair + self.b2
        self.half = rows // 2

    def piece(self, start, count, upper=None):
        if upper is None:
            return self.grad.at[pl.ds(start, count), pl.ds(self.row, self.rows), :]
        row = self.row if upper else self.row + self.half
        return self.grad.at[pl.ds(start, count), pl.ds(row, self.half), :]

    def spot(self, start, count, upper=None):
        if upper is None:
            return self.total.at[pl.ds(start, count), pl.ds(self.row, self.rows), :]
        row = self.row if upper else self.row + self.half
        return self.total.at[pl.ds(start, count), pl.ds(row, self.half), :]

    def keep(self, upper):
        return pltpu.make_async_copy(
            self.piece(self.own, 1, upper), self.spot(self.own, 1, upper), self.local.at[self.number]
        )

    def copy(self, stage, peer, source, target):
        return pltpu.make_async_remote_copy(
            src_ref=source,
            dst_ref=target,
            send_sem=self.send.at[self.number, stage],
            recv_sem=self.recv.at[self.number, stage],
            device_id=self.peers[peer],
            device_id_type=MESH,
        )

    def reduce_up(self):
        return self.copy(3, "up", self.piece(self.own, 1, True), self.land2.at[:, pl.ds(self.rows, self.half), :])

    def reduce_down(self):
        return self.copy(4, "down", self.piece(self.own, 1, False), self.land2.at[:, pl.ds(self.rows + self.half, self.half), :])

    def spread_down(self, fresh=False):
        here = self.spot(self.own, 1, True)
        return self.copy(5, "down", self.piece(self.own, 1, True) if fresh else here, here)

    def spread_up(self, fresh=False):
        here = self.spot(self.own, 1, False)
        return self.copy(6, "up", self.piece(self.own, 1, False) if fresh else here, here)

    def step0(self):
        return self.copy(0, "core", self.piece(4 - self.quad, 4), self.land0)

    def step1(self):
        return self.copy(1, self.first, self.piece(self.quad + 2 - 2 * self.b1, 2), self.land1)

    def step2(self):
        return self.copy(2, self.second, self.piece(self.pair + 1 - self.b2, 1), self.land2.at[:, pl.ds(0, self.rows), :])

    def gather(self, stage):
        start, count, peer = ((self.own, 1, self.second), (self.pair, 2, self.first), (self.quad, 4, "core"))[stage - 7]
        here = self.spot(start, count)
        return self.copy(stage, peer, here, here)

    def arrive_upper(self):
        z, last = self.me["z"], self.z_count - 1

        @pl.when(z > 0)
        def _():
            self.reduce_up().wait_recv()
            add_into(self.grad, self.own, self.row, self.land2.at[:, pl.ds(self.rows, self.half), :], 1, self.half)

            @pl.when(z < last)
            def _():
                self.reduce_up().start()

            @pl.when(z == last)
            def _():
                self.spread_down(True).start()
                self.keep(True).start()

    def arrive_lower(self):
        z, last = self.me["z"], self.z_count - 1

        @pl.when(z < last)
        def _():
            self.reduce_down().wait_recv()
            add_into(self.grad, self.own, self.row + self.half, self.land2.at[:, pl.ds(self.rows + self.half, self.half), :], 1, self.half)

            @pl.when(z > 0)
            def _():
                self.reduce_down().start()

            @pl.when(z == 0)
            def _():
                self.spread_up(True).start()
                self.keep(False).start()

    def back_upper(self):
        z, last = self.me["z"], self.z_count - 1

        @pl.when(z < last)
        def _():
            self.spread_down().wait_recv()

            @pl.when(z > 0)
            def _():
                self.spread_down().start()

    def back_lower(self):
        z, last = self.me["z"], self.z_count - 1

        @pl.when(z > 0)
        def _():
            self.spread_up().wait_recv()

            @pl.when(z < last)
            def _():
                self.spread_up().start()

    def tick(self, op):
        z, last = self.me["z"], self.z_count - 1
        if op == 0:
            self.step0().start()
        elif op == 1:
            self.step0().wait_recv()
            add_into(self.grad, self.quad, self.row, self.land0, 4, self.rows)
            self.step1().start()
        elif op == 2:
            self.step1().wait_recv()
            add_into(self.grad, self.pair, self.row, self.land1, 2, self.rows)
            self.step2().start()
        elif op == 3:
            self.step2().wait_recv()
            add_into(self.grad, self.own, self.row, self.land2, 1, self.rows)

            @pl.when(z == 0)
            def _():
                self.reduce_up().start()

            @pl.when(z == last)
            def _():
                self.reduce_down().start()

        elif op == 4:
            pl.when((z > 0) & (2 * z < self.z_count))(self.arrive_upper)
            pl.when((z < last) & (2 * z >= self.z_count))(self.arrive_lower)
        elif op == 5:
            pl.when((z < last) & (2 * z >= self.z_count))(self.arrive_upper)
            pl.when((z > 0) & (2 * z < self.z_count))(self.arrive_lower)
        elif op == 6:
            pl.when(z == last)(self.arrive_upper)
            pl.when(z == 0)(self.arrive_lower)
        elif op == 7:
            pl.when((z < last) & (2 * z >= self.z_count))(self.back_upper)
            pl.when((z > 0) & (2 * z < self.z_count))(self.back_lower)
        elif op == 8:

            @pl.when((z > 0) & (2 * z < self.z_count))
            def _():
                self.back_upper()
                self.gather(7).start()

            @pl.when((z < last) & (2 * z >= self.z_count))
            def _():
                self.back_lower()
                self.gather(7).start()

        elif op == 9:

            @pl.when(z == 0)
            def _():
                self.back_upper()
                self.keep(False).wait()
                self.gather(7).start()

            @pl.when(z == last)
            def _():
                self.back_lower()
                self.keep(True).wait()
                self.gather(7).start()

        elif op == 10:
            self.gather(7).wait_recv()
            self.gather(8).start()
        elif op == 11:
            self.gather(8).wait_recv()
            self.gather(9).start()
        elif op == 12:
            self.gather(9).wait_recv()
            self.drain()

    OPS = 13

    def drain(self):
        z, last = self.me["z"], self.z_count - 1
        self.step0().wait_send()
        self.step1().wait_send()
        self.step2().wait_send()
        for stage in (7, 8, 9):
            self.gather(stage).wait_send()

        @pl.when(z < last)
        def _():
            self.reduce_up().wait_send()
            self.spread_up().wait_send()

        @pl.when(z > 0)
        def _():
            self.reduce_down().wait_send()
            self.spread_down().wait_send()


def sum_kernel(z_count, plan, *refs):
    n = 1 + max(item[0] for item in plan)
    parts = len(plan)
    ins, outs = refs[:n], refs[n : 2 * n]
    rest = refs[2 * n :]
    grads, rest = rest[:n], rest[n:]
    landings = rest[: 3 * parts]
    send, recv, local, load = rest[3 * parts :]
    me = where_am_i()
    peers = peers_of(me)
    loads = [pltpu.make_async_copy(ins[i], grads[i], load.at[i]) for i in range(n)]
    for item in loads:
        item.start()
    greet(me, peers, z_count)
    for item in loads:
        item.wait()
    chunks = []
    for number, (i, row, rows, first) in enumerate(plan):
        landing = landings[3 * number : 3 * number + 3]
        chunks.append(
            Chunk(number, grads[i], outs[i], row, rows, first, landing, (send, recv, local), me, peers, z_count)
        )
    for at in range(parts + Chunk.OPS - 1):
        for number in range(parts):
            if 0 <= at - number < Chunk.OPS:
                chunks[number].tick(at - number)


def sum_call(arrays, plan, z_count):
    landing = []
    for i, row, rows, first in plan:
        columns, kind = arrays[i].shape[2], arrays[i].dtype
        landing += [
            pltpu.VMEM((4, rows, columns), kind),
            pltpu.VMEM((2, rows, columns), kind),
            pltpu.VMEM((1, 2 * rows, columns), kind),
        ]
    n = len(arrays)
    return pl.pallas_call(
        functools.partial(sum_kernel, z_count, plan),
        out_shape=tuple(jax.ShapeDtypeStruct(v.shape, v.dtype) for v in arrays),
        in_specs=[pl.BlockSpec(memory_space=pl.ANY)] * n,
        out_specs=tuple([pl.BlockSpec(memory_space=pl.ANY)] * n),
        scratch_shapes=[pltpu.VMEM(v.shape, v.dtype) for v in arrays]
        + landing
        + [
            pltpu.SemaphoreType.DMA((len(plan), STAGES)),
            pltpu.SemaphoreType.DMA((len(plan), STAGES)),
            pltpu.SemaphoreType.DMA((len(plan),)),
            pltpu.SemaphoreType.DMA((n,)),
        ],
        compiler_params=pltpu.CompilerParams(
            collective_id=0, has_side_effects=True, vmem_limit_bytes=56 * 2**20
        ),
    )(*arrays)


def columns_to_panels(value):
    rows, columns = value.shape
    return jnp.transpose(value.reshape(rows, 8, columns // 8), (1, 0, 2)).astype(jnp.bfloat16)


def panels_to_columns(panels):
    count, rows, width = panels.shape
    return jnp.transpose(panels.astype(jnp.float32), (1, 0, 2)).reshape(rows, count * width)


def sum_gradients(grads):
    (g_in, g_query, g_key, g_value, g_qgain, g_kgain, g_out, g_attn, g_pre, g_gate, g_up, g_down, g_post) = grads
    z_count = lax.axis_size("blk") // 2
    width = g_in.shape[0]
    gains = [g_in, g_attn, g_pre, g_post, g_qgain, g_kgain]
    sizes = [v.shape[0] for v in gains]
    flat = jnp.concatenate(gains)
    gain_rows = 32
    flat = jnp.pad(flat, (0, 8 * gain_rows * 128 - flat.shape[0])).reshape(8, gain_rows, 128)
    down = g_down.astype(jnp.bfloat16).reshape(8, -1, width)
    out = g_out.astype(jnp.bfloat16).reshape(8, -1, width)
    both = jnp.stack([g_key, g_value])
    head = g_key.shape[1]
    both = jnp.transpose(both.reshape(2, 2, width // 2, 2, head // 2), (0, 1, 3, 2, 4)).reshape(8, width // 2, head // 2)
    arrays = [down, columns_to_panels(g_gate), columns_to_panels(g_up), out, columns_to_panels(g_query), both.astype(jnp.bfloat16), flat]
    plan = []
    for i, v in enumerate(arrays[:-1]):
        rows = v.shape[1] // 2
        plan += [(i, 0, rows, "x"), (i, rows, rows, "y")]
    plan.append((6, 0, gain_rows, "x"))
    down, gate, up, out, query, both, flat = sum_call(arrays, plan, z_count)
    both = jnp.transpose(both.astype(jnp.float32).reshape(2, 2, 2, width // 2, head // 2), (0, 1, 3, 2, 4)).reshape(2, width, head)
    flat = flat.reshape(-1)
    cuts, at = [], 0
    for size in sizes:
        cuts.append(flat[at : at + size])
        at += size
    g_in, g_attn, g_pre, g_post, g_qgain, g_kgain = cuts
    return (
        g_in,
        panels_to_columns(query),
        both[0],
        both[1],
        g_qgain,
        g_kgain,
        out.astype(jnp.float32).reshape(g_out.shape),
        g_attn,
        g_pre,
        panels_to_columns(gate),
        panels_to_columns(up),
        down.astype(jnp.float32).reshape(g_down.shape),
        g_post,
    )


def per_device(
    tokens,
    lengths,
    cotangent,
    norm_in,
    w_query,
    w_key,
    w_value,
    query_gain,
    key_gain,
    w_out,
    norm_attn,
    norm_pre,
    w_gate,
    w_up,
    w_down,
    norm_post,
):
    rows = tokens.shape[1]
    head = query_gain.shape[0]
    heads = w_query.shape[1] // head
    scale = head ** (-0.5)
    count = lax.axis_size("blk")
    place = lax.axis_index("blk")
    row = lengths[0]
    local_idx = place * rows + jnp.arange(rows, dtype=jnp.int32)
    seg_q, pos_q = segment_of(local_idx, row)
    cosine, sine = rotary_tables(pos_q, head)

    def block_mask(source):
        key_idx = source * rows + jnp.arange(rows, dtype=jnp.int32)
        seg_k, unused = segment_of(key_idx, row)
        return (seg_q[:, None] == seg_k[None, :]) & (local_idx[:, None] >= key_idx[None, :])

    x_in = tokens[0].astype(jnp.float32)
    normal_a = normed(x_in, norm_in).astype(jnp.bfloat16)
    q_proj = jnp.dot(normal_a, w_query, preferred_element_type=jnp.float32).reshape(
        rows, heads, head
    )
    k_proj = jnp.dot(normal_a, w_key, preferred_element_type=jnp.float32)
    v_proj = jnp.dot(normal_a, w_value, preferred_element_type=jnp.float32)
    query = prepare(q_proj, query_gain, cosine[:, None, :], sine[:, None, :]).astype(jnp.bfloat16)
    keys = prepare(k_proj, key_gain, cosine, sine).astype(jnp.bfloat16)
    values = v_proj.astype(jnp.bfloat16)
    q_heads = jnp.transpose(query, (1, 0, 2))

    def absorb(state, pair, source):
        allowed = block_mask(source)
        big, total, accum = state
        raw = jnp.einsum("hqd,kd->hqk", q_heads, pair[0], preferred_element_type=jnp.float32)
        scores = jnp.where(allowed[None], scale * raw, NEG)
        big_new = jnp.maximum(big, jnp.max(scores, axis=-1, keepdims=True))
        expo = jnp.where(allowed[None], jnp.exp(scores - big_new), 0.0)
        fade = jnp.exp(big - big_new)
        total = total * fade + jnp.sum(expo, axis=-1, keepdims=True)
        accum = accum * fade + jnp.einsum(
            "hqk,kd->hqd", expo.astype(jnp.bfloat16), pair[1], preferred_element_type=jnp.float32
        )
        return (big_new, total, accum)

    pair = jnp.stack([keys, values])
    state = (
        jnp.full((heads, rows, 1), NEG, jnp.float32),
        jnp.zeros((heads, rows, 1), jnp.float32),
        jnp.zeros((heads, rows, head), jnp.float32),
    )
    state = absorb(state, pair, place)

    def cycle_forward(step, carry):
        inner, moving = carry
        moving = from_behind(moving, "blk", 1)
        return (absorb(inner, moving, (place - step) % count), moving)

    state, unused_pair = lax.fori_loop(1, count, cycle_forward, (state, pair))
    big, total, accum = state
    attended = accum / total
    lse = big + jnp.log(total)
    joined = jnp.transpose(attended, (1, 0, 2)).reshape(rows, heads * head).astype(jnp.bfloat16)
    a_proj = jnp.dot(joined, w_out, preferred_element_type=jnp.float32)
    x_mid = x_in + normed(a_proj, norm_attn)
    mixed = normed(x_mid, norm_pre).astype(jnp.bfloat16)
    gate = jnp.dot(mixed, w_gate, preferred_element_type=jnp.float32)
    upper = jnp.dot(mixed, w_up, preferred_element_type=jnp.float32)

    def activate(gate_in, upper_in):
        return jax.nn.gelu(gate_in, approximate=True) * upper_in

    hidden = activate(gate, upper).astype(jnp.bfloat16)
    f_proj = jnp.dot(hidden, w_down, preferred_element_type=jnp.float32)
    output = x_mid + normed(f_proj, norm_post)
    grad_y = cotangent[0].astype(jnp.float32)
    d_fproj, g_post = normed_back(f_proj, norm_post, grad_y)
    d_fproj = d_fproj.astype(jnp.bfloat16)
    g_down = jnp.einsum("tf,td->fd", hidden, d_fproj, preferred_element_type=jnp.float32)
    d_hidden = jnp.einsum("td,fd->tf", d_fproj, w_down, preferred_element_type=jnp.float32)
    d_gate, d_upper = jax.vjp(activate, gate, upper)[1](d_hidden)
    d_gate = d_gate.astype(jnp.bfloat16)
    d_upper = d_upper.astype(jnp.bfloat16)
    g_gate = jnp.einsum("td,tf->df", mixed, d_gate, preferred_element_type=jnp.float32)
    g_up = jnp.einsum("td,tf->df", mixed, d_upper, preferred_element_type=jnp.float32)
    d_mixed = jnp.einsum(
        "tf,df->td", d_gate, w_gate, preferred_element_type=jnp.float32
    ) + jnp.einsum("tf,df->td", d_upper, w_up, preferred_element_type=jnp.float32)
    d_mid, g_pre = normed_back(x_mid, norm_pre, d_mixed)
    d_mid = grad_y + d_mid
    d_aproj, g_attn = normed_back(a_proj, norm_attn, d_mid)
    d_aproj = d_aproj.astype(jnp.bfloat16)
    g_out = jnp.einsum("tn,td->nd", joined, d_aproj, preferred_element_type=jnp.float32)
    d_joined = jnp.einsum("td,nd->tn", d_aproj, w_out, preferred_element_type=jnp.float32).astype(
        jnp.bfloat16
    )
    do_heads = jnp.transpose(d_joined.reshape(rows, heads, head), (1, 0, 2))
    delta = jnp.sum(do_heads.astype(jnp.float32) * attended, axis=-1, keepdims=True)

    def visit(d_query, moving, grads, source):
        allowed = block_mask(source)
        raw = jnp.einsum("hqd,kd->hqk", q_heads, moving[0], preferred_element_type=jnp.float32)
        probs = jnp.where(allowed[None], jnp.exp(scale * raw - lse), 0.0)
        dv_add = jnp.einsum(
            "hqk,hqd->kd", probs.astype(jnp.bfloat16), do_heads, preferred_element_type=jnp.float32
        )
        d_probs = jnp.einsum("hqd,kd->hqk", do_heads, moving[1], preferred_element_type=jnp.float32)
        d_scores = (scale * probs * (d_probs - delta)).astype(jnp.bfloat16)
        dq_add = jnp.einsum("hqk,kd->hqd", d_scores, moving[0], preferred_element_type=jnp.float32)
        dk_add = jnp.einsum("hqk,hqd->kd", d_scores, q_heads, preferred_element_type=jnp.float32)
        return (d_query + dq_add, grads + jnp.stack([dk_add, dv_add]))

    d_query = jnp.zeros((heads, rows, head), jnp.float32)
    grads = jnp.zeros((2, rows, head), jnp.float32)
    d_query, grads = visit(d_query, pair, grads, place)

    def cycle_backward(step, carry):
        dq_in, moving, grads_in = carry
        moving = from_behind(moving, "blk", 1)
        grads_in = pass_home(grads_in)
        dq_in, grads_in = visit(dq_in, moving, grads_in, (place - step) % count)
        return (dq_in, moving, grads_in)

    d_query, unused_pair, grads = lax.fori_loop(1, count, cycle_backward, (d_query, pair, grads))
    grads = pass_home(grads)

    def query_piece(proj, gain):
        return prepare(proj, gain, cosine[:, None, :], sine[:, None, :])

    def key_piece(proj, gain):
        return prepare(proj, gain, cosine, sine)

    d_qproj, g_qgain = jax.vjp(query_piece, q_proj, query_gain)[1](
        jnp.transpose(d_query, (1, 0, 2))
    )
    d_kproj, g_kgain = jax.vjp(key_piece, k_proj, key_gain)[1](grads[0])
    d_qproj = d_qproj.reshape(rows, heads * head).astype(jnp.bfloat16)
    d_kproj = d_kproj.astype(jnp.bfloat16)
    d_vproj = grads[1].astype(jnp.bfloat16)
    g_query = jnp.einsum("td,tn->dn", normal_a, d_qproj, preferred_element_type=jnp.float32)
    g_key = jnp.einsum("td,tn->dn", normal_a, d_kproj, preferred_element_type=jnp.float32)
    g_value = jnp.einsum("td,tn->dn", normal_a, d_vproj, preferred_element_type=jnp.float32)
    d_normal = jnp.einsum("tn,dn->td", d_qproj, w_query, preferred_element_type=jnp.float32)
    d_normal = d_normal + jnp.einsum(
        "tn,dn->td", d_kproj, w_key, preferred_element_type=jnp.float32
    )
    d_normal = d_normal + jnp.einsum(
        "tn,dn->td", d_vproj, w_value, preferred_element_type=jnp.float32
    )
    d_input, g_in = normed_back(x_in, norm_in, d_normal)
    input_grad = (d_mid + d_input).astype(jnp.bfloat16)
    (
        g_in,
        g_query,
        g_key,
        g_value,
        g_qgain,
        g_kgain,
        g_out,
        g_attn,
        g_pre,
        g_gate,
        g_up,
        g_down,
        g_post,
    ) = sum_gradients(
        (
            g_in,
            g_query,
            g_key,
            g_value,
            g_qgain,
            g_kgain,
            g_out,
            g_attn,
            g_pre,
            g_gate,
            g_up,
            g_down,
            g_post,
        )
    )
    return (
        output.astype(jnp.bfloat16)[None],
        input_grad[None],
        g_in,
        g_query,
        g_key,
        g_value,
        g_qgain,
        g_kgain,
        g_out,
        g_attn,
        g_pre,
        g_gate,
        g_up,
        g_down,
        g_post,
    )


def solution(mesh):
    in_specs = (
        P("dp", "blk", None),
        P("dp", None),
        P("dp", "blk", None),
        P(),
        P(),
        P(),
        P(),
        P(),
        P(),
        P(),
        P(),
        P(),
        P(),
        P(),
        P(),
        P(),
    )
    out_specs = (
        P("dp", "blk", None),
        P("dp", "blk", None),
        P(),
        P(),
        P(),
        P(),
        P(),
        P(),
        P(),
        P(),
        P(),
        P(),
        P(),
        P(),
        P(),
    )
    return jax.shard_map(
        per_device, mesh=mesh, in_specs=in_specs, out_specs=out_specs, check_vma=False
    )
```

```python
import functools

import jax
import jax.numpy as jnp
from jax import lax
from jax.experimental import pallas as pl
from jax.experimental.pallas import tpu as pltpu
from jax.sharding import PartitionSpec as P

EPS = 1e-06
BASE = 1000000.0
NEG = -1e30


def shifted(array, axis, by):
    peers = lax.axis_size(axis)
    return lax.ppermute(array, axis, [(i, (i + by) % peers) for i in range(peers)])


def from_behind(block, axis, distance):
    devices = range(lax.axis_size(axis))
    route = [(i - distance, i) for i in devices if i - distance in devices]
    return lax.ppermute(block, axis, route)


def normed(value, gain):
    return value * lax.rsqrt(jnp.mean(value * value, axis=-1, keepdims=True) + EPS) * gain


def normed_back(value, gain, grad):
    return jax.vjp(normed, value, gain)[1](grad)


def segment_of(index, row):
    ends = jnp.cumsum(row)
    seg = jnp.sum((index[:, None] >= ends[None, :]).astype(jnp.int32), axis=1)
    starts = ends - row
    slots = jnp.arange(row.shape[0], dtype=jnp.int32)
    begin = jnp.sum(jnp.where(slots[None, :] == seg[:, None], starts[None, :], 0), axis=1)
    return (seg, index - begin)


def rotary_tables(places, head):
    half = head // 2
    freq = jnp.exp(-(2.0 * jnp.arange(half, dtype=jnp.float32) / head) * jnp.log(BASE))
    angle = places.astype(jnp.float32)[:, None] * freq[None, :]
    return (jnp.cos(angle), jnp.sin(angle))


def prepare(proj, gain, cosine, sine):
    value = normed(proj, gain)
    half = value.shape[-1] // 2
    first = value[..., :half]
    second = value[..., half:]
    return jnp.concatenate(
        [first * cosine - second * sine, second * cosine + first * sine], axis=-1
    )


def pass_home(grads):
    return shifted(grads.astype(jnp.bfloat16), "blk", 1).astype(grads.dtype)


MESH = pl.DeviceIdType.MESH


def where_am_i():
    place = lax.axis_index("blk")
    part = lax.axis_index("dp")
    return {
        "z": place // 2,
        "y": lax.rem(place, 2),
        "x": part // 2,
        "core": lax.rem(part, 2),
        "place": place,
        "part": part,
    }


def peers_of(me):
    place, part = me["place"], me["part"]
    return {
        "core": {"blk": place, "dp": part + 1 - 2 * me["core"]},
        "x": {"blk": place, "dp": part + 2 - 4 * me["x"]},
        "y": {"blk": place + 1 - 2 * me["y"], "dp": part},
        "up": {"blk": place + 2, "dp": part},
        "down": {"blk": place - 2, "dp": part},
    }


def greet(me, peers, z_count):
    barrier = pltpu.get_barrier_semaphore()
    for name in ("core", "x", "y"):
        pl.semaphore_signal(barrier, inc=1, device_id=peers[name], device_id_type=MESH)

    @pl.when(me["z"] < z_count - 1)
    def _():
        pl.semaphore_signal(barrier, inc=1, device_id=peers["up"], device_id_type=MESH)

    @pl.when(me["z"] > 0)
    def _():
        pl.semaphore_signal(barrier, inc=1, device_id=peers["down"], device_id_type=MESH)

    ends = (me["z"] == 0).astype(jnp.int32) + (me["z"] == z_count - 1).astype(jnp.int32)
    pl.semaphore_wait(barrier, 5 - ends)


def add_into(target, start, row, extra, count, rows):
    step = rows if rows < 32 else 16
    for candidate in (160, 128, 80, 64, 48, 32):
        if rows % candidate == 0:
            step = candidate
            break

    def body(index, carry):
        e = index // (rows // step)
        at = pl.multiple_of(lax.rem(index, rows // step) * step, 8)
        here = pl.ds(pl.multiple_of(row + at, 8), step)
        target[start + e, here, :] = target[start + e, here, :] + extra[e, pl.ds(at, step), :]
        return carry

    lax.fori_loop(0, count * (rows // step), body, 0)


STAGES = 10


class Chunk:
    def __init__(self, number, grad, total, row, rows, first, landing, sems, me, peers, z_count):
        self.grad, self.total, self.row, self.rows = grad, total, row, rows
        self.first, self.second = ("x", "y") if first == "x" else ("y", "x")
        self.land0, self.land1, self.land2 = landing
        self.send, self.recv, self.local = sems
        self.number, self.me, self.peers, self.z_count = number, me, peers, z_count
        self.b1, self.b2, self.core = me[self.first], me[self.second], me["core"]
        self.quad = 4 * self.core
        self.pair = self.quad + 2 * self.b1
        self.own = self.pair + self.b2
        self.half = rows // 2

    def piece(self, start, count, upper=None):
        if upper is None:
            return self.grad.at[pl.ds(start, count), pl.ds(self.row, self.rows), :]
        row = self.row if upper else self.row + self.half
        return self.grad.at[pl.ds(start, count), pl.ds(row, self.half), :]

    def spot(self, count, upper=None):
        row, rows = self.row, self.rows
        if upper is not None:
            row, rows = (row if upper else row + self.half), self.half
        here, columns = pl.ds(row, rows), self.grad.shape[2]
        start = {1: self.own, 2: self.pair, 4: self.quad}[count]
        if len(self.total.shape) == 2:
            return self.total.at[here, pl.ds(pl.multiple_of(start * columns, 128), count * columns)]
        if len(self.total.shape) == 4:
            if count == 4:
                return self.total.at[self.core, :, here, :]
            if count == 2:
                return self.total.at[self.core, self.b1, here, :]
            return self.total.at[self.core, self.b1, here, pl.ds(pl.multiple_of(self.b2 * columns, 128), columns)]
        if count == 1:
            return self.total.at[start, here, :]
        return self.total.at[pl.ds(start, count), here, :]

    def mine(self, upper):
        return self.grad.at[self.own, pl.ds(self.row if upper else self.row + self.half, self.half), :]

    def keep(self, upper):
        return pltpu.make_async_copy(
            self.mine(upper), self.spot(1, upper), self.local.at[self.number]
        )

    def copy(self, stage, peer, source, target):
        return pltpu.make_async_remote_copy(
            src_ref=source,
            dst_ref=target,
            send_sem=self.send.at[self.number, stage],
            recv_sem=self.recv.at[self.number, stage],
            device_id=self.peers[peer],
            device_id_type=MESH,
        )

    def reduce_up(self):
        return self.copy(3, "up", self.piece(self.own, 1, True), self.land2.at[:, pl.ds(self.rows, self.half), :])

    def reduce_down(self):
        return self.copy(4, "down", self.piece(self.own, 1, False), self.land2.at[:, pl.ds(self.rows + self.half, self.half), :])

    def spread_down(self, fresh=False):
        here = self.spot(1, True)
        return self.copy(5, "down", self.mine(True) if fresh else here, here)

    def spread_up(self, fresh=False):
        here = self.spot(1, False)
        return self.copy(6, "up", self.mine(False) if fresh else here, here)

    def step0(self):
        return self.copy(0, "core", self.piece(4 - self.quad, 4), self.land0)

    def step1(self):
        return self.copy(1, self.first, self.piece(self.quad + 2 - 2 * self.b1, 2), self.land1)

    def step2(self):
        return self.copy(2, self.second, self.piece(self.pair + 1 - self.b2, 1), self.land2.at[:, pl.ds(0, self.rows), :])

    def gather(self, stage):
        count, peer = ((1, self.second), (2, self.first), (4, "core"))[stage - 7]
        here = self.spot(count)
        return self.copy(stage, peer, here, here)

    def arrive_upper(self):
        z, last = self.me["z"], self.z_count - 1

        @pl.when(z > 0)
        def _():
            self.reduce_up().wait_recv()
            add_into(self.grad, self.own, self.row, self.land2.at[:, pl.ds(self.rows, self.half), :], 1, self.half)

            @pl.when(z < last)
            def _():
                self.reduce_up().start()

            @pl.when(z == last)
            def _():
                self.spread_down(True).start()
                self.keep(True).start()

    def arrive_lower(self):
        z, last = self.me["z"], self.z_count - 1

        @pl.when(z < last)
        def _():
            self.reduce_down().wait_recv()
            add_into(self.grad, self.own, self.row + self.half, self.land2.at[:, pl.ds(self.rows + self.half, self.half), :], 1, self.half)

            @pl.when(z > 0)
            def _():
                self.reduce_down().start()

            @pl.when(z == 0)
            def _():
                self.spread_up(True).start()
                self.keep(False).start()

    def back_upper(self):
        z, last = self.me["z"], self.z_count - 1

        @pl.when(z < last)
        def _():
            self.spread_down().wait_recv()

            @pl.when(z > 0)
            def _():
                self.spread_down().start()

    def back_lower(self):
        z, last = self.me["z"], self.z_count - 1

        @pl.when(z > 0)
        def _():
            self.spread_up().wait_recv()

            @pl.when(z < last)
            def _():
                self.spread_up().start()

    def tick(self, op):
        z, last = self.me["z"], self.z_count - 1
        if op == 0:
            self.step0().start()
        elif op == 1:
            self.step0().wait_recv()
            add_into(self.grad, self.quad, self.row, self.land0, 4, self.rows)
            self.step1().start()
        elif op == 2:
            self.step1().wait_recv()
            add_into(self.grad, self.pair, self.row, self.land1, 2, self.rows)
            self.step2().start()
        elif op == 3:
            self.step2().wait_recv()
            add_into(self.grad, self.own, self.row, self.land2, 1, self.rows)

            @pl.when(z == 0)
            def _():
                self.reduce_up().start()

            @pl.when(z == last)
            def _():
                self.reduce_down().start()

        elif op == 4:
            pl.when((z > 0) & (2 * z < self.z_count))(self.arrive_upper)
            pl.when((z < last) & (2 * z >= self.z_count))(self.arrive_lower)
        elif op == 5:
            pl.when((z < last) & (2 * z >= self.z_count))(self.arrive_upper)
            pl.when((z > 0) & (2 * z < self.z_count))(self.arrive_lower)
        elif op == 6:
            pl.when(z == last)(self.arrive_upper)
            pl.when(z == 0)(self.arrive_lower)
        elif op == 7:
            pl.when((z < last) & (2 * z >= self.z_count))(self.back_upper)
            pl.when((z > 0) & (2 * z < self.z_count))(self.back_lower)
        elif op == 8:

            @pl.when((z > 0) & (2 * z < self.z_count))
            def _():
                self.back_upper()
                self.gather(7).start()

            @pl.when((z < last) & (2 * z >= self.z_count))
            def _():
                self.back_lower()
                self.gather(7).start()

        elif op == 9:

            @pl.when(z == 0)
            def _():
                self.back_upper()
                self.keep(False).wait()
                self.gather(7).start()

            @pl.when(z == last)
            def _():
                self.back_lower()
                self.keep(True).wait()
                self.gather(7).start()

        elif op == 10:
            self.gather(7).wait_recv()
            self.gather(8).start()
        elif op == 11:
            self.gather(8).wait_recv()
            self.gather(9).start()
        elif op == 12:
            self.gather(9).wait_recv()
            self.drain()

    OPS = 13

    def drain(self):
        z, last = self.me["z"], self.z_count - 1
        self.step0().wait_send()
        self.step1().wait_send()
        self.step2().wait_send()
        for stage in (7, 8, 9):
            self.gather(stage).wait_send()

        @pl.when(z < last)
        def _():
            self.reduce_up().wait_send()
            self.spread_up().wait_send()

        @pl.when(z > 0)
        def _():
            self.reduce_down().wait_send()
            self.spread_down().wait_send()


def sum_kernel(z_count, plan, *refs):
    n = 1 + max(item[0] for item in plan)
    parts = len(plan)
    ins, outs = refs[:n], refs[n : 2 * n]
    rest = refs[2 * n :]
    grads, rest = rest[:n], rest[n:]
    landings = rest[: 3 * parts]
    send, recv, local, load = rest[3 * parts :]
    me = where_am_i()
    peers = peers_of(me)
    loads = [pltpu.make_async_copy(ins[i], grads[i], load.at[i]) for i in range(n)]
    for item in loads:
        item.start()
    greet(me, peers, z_count)
    for item in loads:
        item.wait()
    chunks = []
    for number, (i, row, rows, first) in enumerate(plan):
        landing = landings[3 * number : 3 * number + 3]
        chunks.append(
            Chunk(number, grads[i], outs[i], row, rows, first, landing, (send, recv, local), me, peers, z_count)
        )
    for at in range(parts + Chunk.OPS - 1):
        for number in range(parts):
            if 0 <= at - number < Chunk.OPS:
                chunks[number].tick(at - number)


def sum_call(arrays, plan, z_count):
    landing = []
    for i, row, rows, first in plan:
        columns, kind = arrays[i].shape[2], arrays[i].dtype
        landing += [
            pltpu.VMEM((4, rows, columns), kind),
            pltpu.VMEM((2, rows, columns), kind),
            pltpu.VMEM((1, 2 * rows, columns), kind),
        ]
    n = len(arrays)
    return pl.pallas_call(
        functools.partial(sum_kernel, z_count, plan),
        out_shape=tuple(jax.ShapeDtypeStruct(v.shape, v.dtype) for v in arrays),
        in_specs=[pl.BlockSpec(memory_space=pl.ANY)] * n,
        out_specs=tuple([pl.BlockSpec(memory_space=pl.ANY)] * n),
        scratch_shapes=[pltpu.VMEM(v.shape, v.dtype) for v in arrays]
        + landing
        + [
            pltpu.SemaphoreType.DMA((len(plan), STAGES)),
            pltpu.SemaphoreType.DMA((len(plan), STAGES)),
            pltpu.SemaphoreType.DMA((len(plan),)),
            pltpu.SemaphoreType.DMA((n,)),
        ],
        compiler_params=pltpu.CompilerParams(
            collective_id=0, has_side_effects=True, vmem_limit_bytes=56 * 2**20
        ),
    )(*arrays)


def columns_to_panels(value):
    rows, columns = value.shape
    return jnp.transpose(value.reshape(rows, 8, columns // 8), (1, 0, 2)).astype(jnp.bfloat16)


def panels_to_columns(panels):
    count, rows, width = panels.shape
    return jnp.transpose(panels.astype(jnp.float32), (1, 0, 2)).reshape(rows, count * width)


def sum_gradients(grads):
    (g_in, g_query, g_key, g_value, g_qgain, g_kgain, g_out, g_attn, g_pre, g_gate, g_up, g_down, g_post) = grads
    z_count = lax.axis_size("blk") // 2
    width = g_in.shape[0]
    gains = [g_in, g_attn, g_pre, g_post, g_qgain, g_kgain]
    sizes = [v.shape[0] for v in gains]
    flat = jnp.concatenate(gains)
    gain_rows = 32
    flat = jnp.pad(flat, (0, 8 * gain_rows * 128 - flat.shape[0])).reshape(8, gain_rows, 128)
    down = g_down.astype(jnp.bfloat16).reshape(8, -1, width)
    out = g_out.astype(jnp.bfloat16).reshape(8, -1, width)
    both = jnp.stack([g_key, g_value])
    head = g_key.shape[1]
    both = jnp.transpose(both.reshape(2, 2, width // 2, 2, head // 2), (0, 1, 3, 2, 4)).reshape(8, width // 2, head // 2)
    arrays = [down, columns_to_panels(g_gate), columns_to_panels(g_up), out, columns_to_panels(g_query), both.astype(jnp.bfloat16), flat]
    plan = []
    for i, v in enumerate(arrays[:-1]):
        rows = v.shape[1] // 2
        plan += [(i, 0, rows, "x"), (i, rows, rows, "y")]
    plan.append((6, 0, gain_rows, "x"))
    down, gate, up, out, query, both, flat = sum_call(arrays, plan, z_count)
    both = jnp.transpose(both.astype(jnp.float32).reshape(2, 2, 2, width // 2, head // 2), (0, 1, 3, 2, 4)).reshape(2, width, head)
    flat = flat.reshape(-1)
    cuts, at = [], 0
    for size in sizes:
        cuts.append(flat[at : at + size])
        at += size
    g_in, g_attn, g_pre, g_post, g_qgain, g_kgain = cuts
    return (
        g_in,
        panels_to_columns(query),
        both[0],
        both[1],
        g_qgain,
        g_kgain,
        out.astype(jnp.float32).reshape(g_out.shape),
        g_attn,
        g_pre,
        panels_to_columns(gate),
        panels_to_columns(up),
        down.astype(jnp.float32).reshape(g_down.shape),
        g_post,
    )


LOG2E = 1.4426950408889634
LN2 = 0.6931471805599453


def dot(left, right):
    return jnp.dot(left, right, preferred_element_type=jnp.float32)


def dot_nt(left, right):
    return lax.dot_general(left, right, (((1,), (1,)), ((), ())), preferred_element_type=jnp.float32)


def inverse_rms(value):
    return lax.rsqrt(jnp.mean(value * value, axis=-1, keepdims=True) + EPS)


def rms_back(value, inverse, gain, grad):
    scaled = grad * gain
    normal = value * inverse
    mean = jnp.mean(scaled * normal, axis=-1, keepdims=True)
    terms = grad * normal
    return inverse * (scaled - normal * mean), jnp.sum(terms.reshape(-1, 8, terms.shape[-1]), axis=0)


def turn(value, cosine, sine):
    half = value.shape[-1] // 2
    first, second = value[:, :half], value[:, half:]
    return jnp.concatenate([first * cosine - second * sine, second * cosine + first * sine], axis=-1)


def turn_back(grad, cosine, sine):
    half = grad.shape[-1] // 2
    first, second = grad[:, :half], grad[:, half:]
    return jnp.concatenate([first * cosine + second * sine, second * cosine - first * sine], axis=-1)


def bf16(value):
    return value.astype(jnp.bfloat16)


def f32(value):
    return value.astype(jnp.float32)


class Reducer:
    def __init__(self):
        self.waiting, self.active = [], []

    def add(self, *chunks):
        self.waiting += chunks

    def tick(self):
        self.active = [item for item in self.active if item[1] < Chunk.OPS]
        if self.waiting:
            self.active.append([self.waiting.pop(0), 0])
        for item in self.active:
            item[0].tick(item[1])
            item[1] += 1
        return bool(self.active)

    def finish(self):
        while self.tick():
            pass


class Names(dict):
    __getattr__ = dict.__getitem__


def layer_kernel(sizes, names, *refs):
    r = Names(zip(names, refs, strict=True))
    rows, width, hidden, heads, head, z_count = sizes
    scale = head**-0.5
    tile = 128
    tiles = [slice(at, at + tile) for at in range(0, rows, tile)]
    half = head // 2
    me = where_am_i()
    peers = peers_of(me)
    z, y, place = me["z"], me["y"], me["place"]
    last = z_count - 1

    weights = ["x", "w_key", "w_value", "w_query", "w_out", "w_gate", "w_up", "w_down", "dy"]
    joined = heads * head
    wide_k, wide_v = slice(joined, joined + head), slice(joined + head, joined + 2 * head)
    spots = {"w_query": slice(0, joined), "w_key": wide_k, "w_value": wide_v}
    loads = {}
    for i, name in enumerate(weights):
        spot = r.w_first.at[:, spots[name]] if name in spots else r[name]
        loads[name] = pltpu.make_async_copy(r[name + "_in"], spot, r.load_sem.at[i])
    for name in weights:
        loads[name].start()
    greet(me, peers, z_count)

    token = place * rows + lax.broadcasted_iota(jnp.int32, (1, rows), 1)
    begin = jnp.zeros((1, rows), jnp.int32)
    end = jnp.int32(0)
    for j in range(r.lengths.shape[1]):
        end = end + r.lengths[0, j]
        begin = jnp.where(token >= end, end, begin)

    def allowed(source, at, count):
        key = source * rows + at + lax.broadcasted_iota(jnp.int32, (count, rows), 0)
        return (key >= begin) & (key <= token)

    loads["x"].wait()
    loads["w_key"].wait()
    loads["w_value"].wait()
    for t in tiles:
        x = f32(r.x[t, :])
        a = bf16(x * inverse_rms(x) * r.norm_in[...])
        r.a[t, :] = a
        kp = dot(a, r.w_first[:, wide_k])
        r.kp[t, :] = kp
        k = turn(kp * inverse_rms(kp) * r.key_gain[...], r.cosine[t, :], r.sine[t, :])
        r.kv[place, t, 0:head] = bf16(k)
        r.kv[place, t, head : 2 * head] = bf16(dot(a, r.w_first[:, wide_v]))

    def send_kv(source, route):
        peer = peers["up"] if route == 0 else peers["y"]
        return pltpu.make_async_remote_copy(
            src_ref=r.kv.at[source],
            dst_ref=r.kv.at[source],
            send_sem=r.kv_send.at[route, source],
            recv_sem=r.kv_recv.at[source],
            device_id=peer,
            device_id_type=MESH,
        )

    pl.when(z < last)(lambda: send_kv(place, 0).start())
    pl.when(y == 0)(lambda: send_kv(place, 1).start())

    loads["w_query"].wait()
    for h in range(heads):
        for t in tiles:
            qp = dot(r.a[t, :], r.w_first[:, h * head : (h + 1) * head])
            r.qp[t, h * head : (h + 1) * head] = qp
            q = turn(qp * inverse_rms(qp) * r.query_gain[...], r.cosine[t, :], r.sine[t, :])
            q = bf16(q * (scale * LOG2E))
            r.q[h * rows + t.start : h * rows + t.stop, :] = q
            r.qt[:, h * rows + t.start : h * rows + t.stop] = q.T

    def visit(source, first):
        vt = r.kv[source, :, head : 2 * head].T

        def one_head(h, carry):
            here = pl.ds(pl.multiple_of(h * rows, 128), rows)
            for t in tiles:
                s = dot(r.kv[source, t, 0:head], r.qt[:, here])
                p = jnp.where(allowed(source, t.start, tile), jnp.exp2(s), 0.0)
                total = jnp.sum(p, axis=0, keepdims=True)
                if first and t.start == 0:
                    r.total[:, here] = total
                else:
                    r.total[:, here] = r.total[:, here] + total
                r.pt[t, :] = bf16(p)
            o = dot(vt, r.pt[...])
            r.ot[:, here] = o if first else r.ot[:, here] + o
            return carry

        lax.fori_loop(0, heads, one_head, 0)

    visit(place, True)

    @pl.when(y == 1)
    def _():
        send_kv(place - 1, 1).wait_recv()
        visit(place - 1, False)

    for back in range(1, z_count):

        @pl.when(back <= z)
        def _():
            mine = place - 2 * back
            other = mine + 1 - 2 * y
            send_kv(mine, 0).wait_recv()
            pl.when(z < last)(lambda: send_kv(mine, 0).start())
            send_kv(mine, 1).start()
            visit(mine, False)
            send_kv(other, 1).wait_recv()
            visit(other, False)

    for h in range(heads):
        here = slice(h * rows, (h + 1) * rows)
        total = r.total[:, here]
        o = r.ot[:, here] * (1.0 / total)
        r.lse[:, here] = jnp.log2(total)
        r.ot[:, here] = o
        r.ob[:, h * head : (h + 1) * head] = bf16(o).T

    loads["w_out"].wait()
    for t in tiles:
        ap = dot(r.ob[t, 0:joined], r.w_out[...])
        r.ap[t, :] = ap
        x1 = f32(r.x[t, :]) + ap * inverse_rms(ap) * r.norm_attn[...]
        r.x1[t, :] = x1
        m = bf16(x1 * inverse_rms(x1) * r.norm_pre[...])
        r.m[t, :] = m
        r.mt[:, t] = m.T
    loads["w_gate"].wait()
    loads["w_up"].wait()
    block = hidden // 8

    def feed(j, carry):
        cols = pl.ds(pl.multiple_of(j * block, 128), block)
        for t in tiles:
            gate = dot(r.m[t, :], r.w_gate[:, cols])
            up = dot(r.m[t, :], r.w_up[:, cols])
            inner = 0.7978845608028654 * (gate + 0.044715 * gate * gate * gate)
            th = jnp.tanh(inner)
            cdf = 0.5 * (1.0 + th)
            act = gate * cdf
            slope = cdf + 0.5 * gate * (1.0 - th * th) * 0.7978845608028654 * (1.0 + 3 * 0.044715 * gate * gate)
            r.hid[t, cols] = bf16(act * up)
            r.side_gate[t, cols] = bf16(slope * up)
            r.side_up[t, cols] = bf16(act)
        return carry

    lax.fori_loop(0, 8, feed, 0)
    loads["w_down"].wait()
    loads["dy"].wait()
    r.gains[...] = jnp.zeros_like(r.gains)

    def gain(k, terms):
        r.gains[k, :, 0 : terms.shape[1]] = r.gains[k, :, 0 : terms.shape[1]] + terms

    for t in tiles:
        f = dot(r.hid[t, :], r.w_down[...])
        inverse = inverse_rms(f)
        dy = f32(r.dy[t, :])
        r.out[t, :] = bf16(r.x1[t, :] + f * inverse * r.norm_post[...])
        df, g = rms_back(f, inverse, r.norm_post[...], dy)
        r.df[t, :] = bf16(df)
        gain(3, g)

    def down_grad(j, carry):
        cols = pl.ds(pl.multiple_of(j * block, 128), block)
        r.g_down[j] = bf16(dot(r.hid[:, cols].T, r.df[...]))
        return carry

    lax.fori_loop(0, 8, down_grad, 0)

    chunks, number = {}, 0
    sems = (r.red_send, r.red_recv, r.red_local)
    for name, count in r_plan(sizes):
        grad, total = r["g_" + name], r["t_" + name]
        step = grad.shape[1] // count
        chunks[name] = []
        for i in range(count):
            landing = tuple(r[f"land{k}_{name}"].at[i] for k in range(3))
            first = "x" if i % 2 == 0 else "y"
            chunks[name].append(Chunk(number, grad, total, i * step, step, first, landing, sems, me, peers, z_count))
            number += 1
    reducer = Reducer()
    reducer.add(*chunks["down"])
    reducer.tick()

    def feed_back(j, carry):
        cols = pl.ds(pl.multiple_of(j * block, 128), block)
        for t in tiles:
            dh = dot_nt(r.df[t, :], r.w_down[cols, :])
            r.side_gate[t, cols] = bf16(dh * f32(r.side_gate[t, cols]))
            r.side_up[t, cols] = bf16(dh * f32(r.side_up[t, cols]))
        r.g_gate[j] = bf16(dot(r.mt[...], r.side_gate[:, cols]))
        r.g_up[j] = bf16(dot(r.mt[...], r.side_up[:, cols]))
        return carry

    lax.fori_loop(0, 8, feed_back, 0)
    reducer.add(*chunks["gate"], *chunks["up"])
    reducer.tick()
    for t in tiles:
        dm = dot_nt(r.side_gate[t, :], r.w_gate[...]) + dot_nt(r.side_up[t, :], r.w_up[...])
        x1 = r.x1[t, :]
        dx1, g = rms_back(x1, inverse_rms(x1), r.norm_pre[...], dm)
        gain(2, g)
        dx1 = dx1 + f32(r.dy[t, :])
        r.x1[t, :] = dx1
        ap = r.ap[t, :]
        dap, g = rms_back(ap, inverse_rms(ap), r.norm_attn[...], dx1)
        gain(1, g)
        r.dap[t, :] = bf16(dap)
    reducer.tick()
    for h in range(heads):
        here = slice(h * rows, (h + 1) * rows)
        wide = slice(h * head, (h + 1) * head)
        ot = r.ot[:, here]
        g = bf16(dot(bf16(ot), r.dap[...]))
        r.g_out[2 * h] = g[0:half]
        r.g_out[2 * h + 1] = g[half:head]
        do = bf16(dot_nt(r.dap[...], r.w_out[wide, :]))
        r.do[here, :] = do
        dot_rows = do.T
        r.dot[:, here] = dot_rows
        r.delta[:, here] = jnp.sum(f32(dot_rows) * ot, axis=0, keepdims=True)
    reducer.add(*chunks["out"])

    r.ot[...] = jnp.zeros_like(r.ot)

    def visit_back(source, target):
        r.dkv[...] = jnp.zeros_like(r.dkv)
        kt = r.kv[source, :, 0:head].T

        def one_head(h, carry):
            here = pl.ds(pl.multiple_of(h * rows, 128), rows)
            for t in tiles:
                s = dot(r.kv[source, t, 0:head], r.qt[:, here])
                p = jnp.where(allowed(source, t.start, tile), jnp.exp2(s - r.lse[:, here]), 0.0)
                dp = dot(r.kv[source, t, head : 2 * head], r.dot[:, here])
                ds = bf16(p * (dp - r.delta[:, here]))
                r.pt[t, :] = ds
                r.dkv[t, 0:head] = r.dkv[t, 0:head] + dot(ds, r.q[here, :])
                r.dkv[t, head : 2 * head] = r.dkv[t, head : 2 * head] + dot(bf16(p), r.do[here, :])
            r.ot[:, here] = r.ot[:, here] + dot(kt, r.pt[...])
            return carry

        lax.fori_loop(0, heads, one_head, 0)
        target[...] = bf16(r.dkv[...])

    def stage_y(row):
        return r.w_gate.at[0:rows, row * 2 * head : (row + 1) * 2 * head]

    def stage_z(row):
        return r.w_up.at[0:rows, row * 2 * head : (row + 1) * 2 * head]

    def to_partner(row):
        return pltpu.make_async_remote_copy(
            src_ref=stage_y(row),
            dst_ref=r.from_partner.at[row],
            send_sem=r.dkv_send.at[0, row],
            recv_sem=r.dkv_recv.at[0, row],
            device_id=peers["y"],
            device_id_type=MESH,
        )

    def to_below(row):
        return pltpu.make_async_remote_copy(
            src_ref=stage_z(row),
            dst_ref=r.from_above.at[row],
            send_sem=r.dkv_send.at[1, row],
            recv_sem=r.dkv_recv.at[1, row],
            device_id=peers["down"],
            device_id_type=MESH,
        )

    def pass_down(row):
        @pl.when(row < z)
        def _():
            to_partner(row).wait_recv()
            pl.when(z < last)(lambda: to_below(row).wait_recv())
            for t in tiles:
                value = f32(stage_z(row)[t, :]) + f32(r.from_partner[row, t, :])
                above = jnp.where(z < last, f32(r.from_above[row, t, :]), 0.0)
                stage_z(row)[t, :] = bf16(value + above)
            to_below(row).start()

    for row in range(z_count):

        @pl.when((row < z) | ((row == z) & (y == 1)))
        def _():
            visit_back(2 * row + 1 - y, stage_y(row))
            to_partner(row).start()

        reducer.tick()

        @pl.when(row <= z)
        def _():
            visit_back(2 * row + y, stage_z(row))

        if row > 0:
            pass_down(row - 1)
        reducer.tick()

    for h in range(heads):
        wide = slice(h * head, (h + 1) * head)
        for t in tiles:
            dq = (r.ot[:, h * rows + t.start : h * rows + t.stop] * scale).T
            qp = r.qp[t, wide]
            inverse = inverse_rms(qp)
            dqp, g = rms_back(qp, inverse, r.query_gain[...], turn_back(dq, r.cosine[t, :], r.sine[t, :]))
            gain(4, g)
            r.ob[t, wide] = bf16(dqp)
    for t in tiles:
        r.at[:, t] = r.a[t, :].T
    for p in range(4):
        g = bf16(dot(r.at[...], r.ob[:, p * head : (p + 1) * head]))
        r.g_query[2 * p] = g[:, 0:half]
        r.g_query[2 * p + 1] = g[:, half:head]
    reducer.add(*chunks["query"])
    reducer.tick()

    row_total = r.dkv

    for row in range(z_count):

        @pl.when(row == z)
        def _():
            pl.when(y == 0)(lambda: to_partner(row).wait_recv())
            pl.when(z < last)(lambda: to_below(row).wait_recv())
            for t in tiles:
                beside = jnp.where(y == 0, f32(r.from_partner[row, t, :]), 0.0)
                above = jnp.where(z < last, f32(r.from_above[row, t, :]), 0.0)
                row_total[t, :] = f32(stage_z(row)[t, :]) + beside + above

    for t in tiles:
        dk = r.dkv[t, 0:head] * LN2
        kp = r.kp[t, :]
        dkp, g = rms_back(kp, inverse_rms(kp), r.key_gain[...], turn_back(dk, r.cosine[t, :], r.sine[t, :]))
        gain(5, g)
        r.ob[t, wide_k] = bf16(dkp)
        r.ob[t, wide_v] = bf16(r.dkv[t, head : 2 * head])
        da = dot_nt(r.ob[t, :], r.w_first[...])
        x = f32(r.x[t, :])
        dx, g = rms_back(x, inverse_rms(x), r.norm_in[...], da)
        gain(0, g)
        r.dx[t, :] = bf16(r.x1[t, :] + dx)
    low = width // 2
    for upper in range(2):
        g = bf16(dot(r.at[upper * low : (upper + 1) * low, :], r.ob[:, joined : joined + 2 * head]))
        for p in range(4):
            which, side = p // 2, p % 2
            r.g_kv[4 * which + 2 * upper + side] = g[:, p * half : (p + 1) * half]
    r.g_gain[...] = jnp.zeros_like(r.g_gain)
    at = 0
    for k, size in enumerate((width, width, width, width, head, head)):
        g = jnp.sum(r.gains[k], axis=0, keepdims=True)
        for part in range(size // 128):
            r.g_gain[at // 16, at % 16 : at % 16 + 1, :] = g[:, part * 128 : (part + 1) * 128]
            at += 1
    reducer.add(*chunks["kv"], *chunks["gain"])
    reducer.finish()

    pl.when(z < last)(lambda: send_kv(place, 0).wait_send())
    pl.when(y == 0)(lambda: send_kv(place, 1).wait_send())
    for back in range(1, z_count):

        @pl.when(back <= z)
        def _():
            mine = place - 2 * back
            pl.when(z < last)(lambda: send_kv(mine, 0).wait_send())
            send_kv(mine, 1).wait_send()

    for row in range(z_count):
        pl.when((row < z) | ((row == z) & (y == 1)))(lambda: to_partner(row).wait_send())
        pl.when(row < z)(lambda: to_below(row).wait_send())


def r_plan(sizes):
    return [("down", 2), ("gate", 2), ("up", 2), ("out", 2), ("query", 2), ("kv", 2), ("gain", 1)]


def gradient_shapes(sizes):
    rows, width, hidden, heads, head, z_count = sizes
    joined, half = heads * head, head // 2
    return {
        "down": ((8, hidden // 8, width), (8, hidden // 8, width)),
        "gate": ((8, width, hidden // 8), (width, hidden)),
        "up": ((8, width, hidden // 8), (width, hidden)),
        "out": ((8, joined // 8, width), (8, joined // 8, width)),
        "query": ((8, width, joined // 8), (width, joined)),
        "kv": ((8, width // 2, half), (2, 2, width // 2, head)),
        "gain": ((8, 16, 128), (8, 16, 128)),
    }


def layer_scratch(sizes):
    rows, width, hidden, heads, head, z_count = sizes
    joined = heads * head
    low, wide = jnp.bfloat16, jnp.float32
    arrays = {
        "x": ((rows, width), low),
        "w_first": ((width, joined + 2 * head), low),
        "w_out": ((joined, width), low),
        "w_gate": ((width, hidden), low),
        "w_up": ((width, hidden), low),
        "w_down": ((hidden, width), low),
        "dy": ((rows, width), low),
        "a": ((rows, width), low),
        "at": ((width, rows), low),
        "gains": ((6, 8, width), wide),
        "kp": ((rows, head), wide),
        "kv": ((2 * z_count, rows, 2 * head), low),
        "qp": ((rows, joined), wide),
        "q": ((heads * rows, head), low),
        "qt": ((head, heads * rows), low),
        "pt": ((rows, rows), low),
        "ot": ((head, heads * rows), wide),
        "total": ((1, heads * rows), wide),
        "lse": ((1, heads * rows), wide),
        "delta": ((1, heads * rows), wide),
        "ob": ((rows, joined + 2 * head), low),
        "ap": ((rows, width), wide),
        "x1": ((rows, width), wide),
        "m": ((rows, width), low),
        "mt": ((width, rows), low),
        "hid": ((rows, hidden), low),
        "side_gate": ((rows, hidden), low),
        "side_up": ((rows, hidden), low),
        "df": ((rows, width), low),
        "dap": ((rows, width), low),
        "do": ((heads * rows, head), low),
        "dot": ((head, heads * rows), low),
        "dkv": ((rows, 2 * head), wide),
        "from_partner": ((z_count, rows, 2 * head), low),
        "from_above": ((z_count, rows, 2 * head), low),
    }
    shapes = gradient_shapes(sizes)
    pieces = 0
    for name, count in r_plan(sizes):
        (eight, high, columns), kind = shapes[name][0], wide if name == "gain" else low
        step = high // count
        pieces += count
        arrays["g_" + name] = (shapes[name][0], kind)
        arrays["land0_" + name] = ((count, 4, step, columns), kind)
        arrays["land1_" + name] = ((count, 2, step, columns), kind)
        arrays["land2_" + name] = ((count, 1, 2 * step, columns), kind)
    sems = {
        "load_sem": (9,),
        "kv_send": (2, 2 * z_count),
        "kv_recv": (2 * z_count,),
        "dkv_send": (2, z_count),
        "dkv_recv": (2, z_count),
        "red_send": (pieces, STAGES),
        "red_recv": (pieces, STAGES),
        "red_local": (pieces,),
    }
    return arrays, sems


def layer_bytes(sizes):
    total = 0
    for shape, kind in layer_scratch(sizes)[0].values():
        size = jnp.dtype(kind).itemsize
        for n in shape[:-2]:
            size *= n
        total += size * max(shape[-2], 8) * max(shape[-1], 128)
    return total


VMEM_BYTES = 64 * 2**20


def whole_layer(sizes, tokens, lengths, cotangent, norm_in, w_query, w_key, w_value, query_gain, key_gain, w_out, norm_attn, norm_pre, w_gate, w_up, w_down, norm_post):
    rows, width, hidden, heads, head, z_count = sizes
    place = lax.axis_index("blk")
    seg, pos = segment_of(place * rows + jnp.arange(rows, dtype=jnp.int32), lengths[0])
    cosine, sine = rotary_tables(pos, head)
    inputs = {
        "lengths": lengths,
        "cosine": cosine,
        "sine": sine,
        "norm_in": norm_in[None],
        "query_gain": query_gain[None],
        "key_gain": key_gain[None],
        "norm_attn": norm_attn[None],
        "norm_pre": norm_pre[None],
        "norm_post": norm_post[None],
        "x_in": tokens[0],
        "w_key_in": w_key,
        "w_value_in": w_value,
        "w_query_in": w_query,
        "w_out_in": w_out,
        "w_gate_in": w_gate,
        "w_up_in": w_up,
        "w_down_in": w_down,
        "dy_in": cotangent[0],
    }
    spaces = {name: pltpu.SMEM if name == "lengths" else pl.ANY if name.endswith("_in") and name != "norm_in" else pltpu.VMEM for name in inputs}
    shapes = gradient_shapes(sizes)
    outputs = {"out": (rows, width), "dx": (rows, width)}
    outputs.update({"t_" + name: shapes[name][1] for name in shapes})
    arrays, sems = layer_scratch(sizes)
    names = list(inputs) + list(outputs) + list(arrays) + list(sems)
    results = pl.pallas_call(
        functools.partial(layer_kernel, sizes, names),
        out_shape=tuple(
            jax.ShapeDtypeStruct(shape, jnp.float32 if name == "t_gain" else jnp.bfloat16) for name, shape in outputs.items()
        ),
        in_specs=[pl.BlockSpec(memory_space=spaces[name]) for name in inputs],
        out_specs=tuple(
            pl.BlockSpec(memory_space=pl.ANY if name.startswith("t_") else pltpu.VMEM) for name in outputs
        ),
        scratch_shapes=[pltpu.VMEM(*item) for item in arrays.values()]
        + [pltpu.SemaphoreType.DMA(item) for item in sems.values()],
        compiler_params=pltpu.CompilerParams(
            collective_id=1, has_side_effects=True, vmem_limit_bytes=VMEM_BYTES
        ),
    )(*inputs.values())
    r = Names(zip(outputs, results, strict=True))
    flat = r.t_gain.reshape(-1)
    cuts, at = [], 0
    for size in (width, width, width, width, head, head):
        cuts.append(flat[at : at + size])
        at += size
    g_in, g_attn, g_pre, g_post, g_qgain, g_kgain = cuts
    both = r.t_kv.reshape(2, width, head)
    return (
        r.out[None],
        r.dx[None],
        g_in,
        f32(r.t_query),
        f32(both[0]),
        f32(both[1]),
        g_qgain,
        g_kgain,
        f32(r.t_out.reshape(heads * head, width)),
        g_attn,
        g_pre,
        f32(r.t_gate),
        f32(r.t_up),
        f32(r.t_down.reshape(hidden, width)),
        g_post,
    )


def per_device(
    tokens,
    lengths,
    cotangent,
    norm_in,
    w_query,
    w_key,
    w_value,
    query_gain,
    key_gain,
    w_out,
    norm_attn,
    norm_pre,
    w_gate,
    w_up,
    w_down,
    norm_post,
):
    rows = tokens.shape[1]
    head = query_gain.shape[0]
    heads = w_query.shape[1] // head
    sizes = (rows, tokens.shape[2], w_gate.shape[1], heads, head, lax.axis_size("blk") // 2)
    if layer_bytes(sizes) <= VMEM_BYTES:
        return whole_layer(
            sizes,
            tokens,
            lengths,
            cotangent,
            norm_in,
            w_query,
            w_key,
            w_value,
            query_gain,
            key_gain,
            w_out,
            norm_attn,
            norm_pre,
            w_gate,
            w_up,
            w_down,
            norm_post,
        )
    scale = head ** (-0.5)
    count = lax.axis_size("blk")
    place = lax.axis_index("blk")
    row = lengths[0]
    local_idx = place * rows + jnp.arange(rows, dtype=jnp.int32)
    seg_q, pos_q = segment_of(local_idx, row)
    cosine, sine = rotary_tables(pos_q, head)

    def block_mask(source):
        key_idx = source * rows + jnp.arange(rows, dtype=jnp.int32)
        seg_k, unused = segment_of(key_idx, row)
        return (seg_q[:, None] == seg_k[None, :]) & (local_idx[:, None] >= key_idx[None, :])

    x_in = tokens[0].astype(jnp.float32)
    normal_a = normed(x_in, norm_in).astype(jnp.bfloat16)
    q_proj = jnp.dot(normal_a, w_query, preferred_element_type=jnp.float32).reshape(
        rows, heads, head
    )
    k_proj = jnp.dot(normal_a, w_key, preferred_element_type=jnp.float32)
    v_proj = jnp.dot(normal_a, w_value, preferred_element_type=jnp.float32)
    query = prepare(q_proj, query_gain, cosine[:, None, :], sine[:, None, :]).astype(jnp.bfloat16)
    keys = prepare(k_proj, key_gain, cosine, sine).astype(jnp.bfloat16)
    values = v_proj.astype(jnp.bfloat16)
    q_heads = jnp.transpose(query, (1, 0, 2))

    def absorb(state, pair, source):
        allowed = block_mask(source)
        big, total, accum = state
        raw = jnp.einsum("hqd,kd->hqk", q_heads, pair[0], preferred_element_type=jnp.float32)
        scores = jnp.where(allowed[None], scale * raw, NEG)
        big_new = jnp.maximum(big, jnp.max(scores, axis=-1, keepdims=True))
        expo = jnp.where(allowed[None], jnp.exp(scores - big_new), 0.0)
        fade = jnp.exp(big - big_new)
        total = total * fade + jnp.sum(expo, axis=-1, keepdims=True)
        accum = accum * fade + jnp.einsum(
            "hqk,kd->hqd", expo.astype(jnp.bfloat16), pair[1], preferred_element_type=jnp.float32
        )
        return (big_new, total, accum)

    pair = jnp.stack([keys, values])
    state = (
        jnp.full((heads, rows, 1), NEG, jnp.float32),
        jnp.zeros((heads, rows, 1), jnp.float32),
        jnp.zeros((heads, rows, head), jnp.float32),
    )
    state = absorb(state, pair, place)

    def cycle_forward(step, carry):
        inner, moving = carry
        moving = from_behind(moving, "blk", 1)
        return (absorb(inner, moving, (place - step) % count), moving)

    state, unused_pair = lax.fori_loop(1, count, cycle_forward, (state, pair))
    big, total, accum = state
    attended = accum / total
    lse = big + jnp.log(total)
    joined = jnp.transpose(attended, (1, 0, 2)).reshape(rows, heads * head).astype(jnp.bfloat16)
    a_proj = jnp.dot(joined, w_out, preferred_element_type=jnp.float32)
    x_mid = x_in + normed(a_proj, norm_attn)
    mixed = normed(x_mid, norm_pre).astype(jnp.bfloat16)
    gate = jnp.dot(mixed, w_gate, preferred_element_type=jnp.float32)
    upper = jnp.dot(mixed, w_up, preferred_element_type=jnp.float32)

    def activate(gate_in, upper_in):
        return jax.nn.gelu(gate_in, approximate=True) * upper_in

    hidden = activate(gate, upper).astype(jnp.bfloat16)
    f_proj = jnp.dot(hidden, w_down, preferred_element_type=jnp.float32)
    output = x_mid + normed(f_proj, norm_post)
    grad_y = cotangent[0].astype(jnp.float32)
    d_fproj, g_post = normed_back(f_proj, norm_post, grad_y)
    d_fproj = d_fproj.astype(jnp.bfloat16)
    g_down = jnp.einsum("tf,td->fd", hidden, d_fproj, preferred_element_type=jnp.float32)
    d_hidden = jnp.einsum("td,fd->tf", d_fproj, w_down, preferred_element_type=jnp.float32)
    d_gate, d_upper = jax.vjp(activate, gate, upper)[1](d_hidden)
    d_gate = d_gate.astype(jnp.bfloat16)
    d_upper = d_upper.astype(jnp.bfloat16)
    g_gate = jnp.einsum("td,tf->df", mixed, d_gate, preferred_element_type=jnp.float32)
    g_up = jnp.einsum("td,tf->df", mixed, d_upper, preferred_element_type=jnp.float32)
    d_mixed = jnp.einsum(
        "tf,df->td", d_gate, w_gate, preferred_element_type=jnp.float32
    ) + jnp.einsum("tf,df->td", d_upper, w_up, preferred_element_type=jnp.float32)
    d_mid, g_pre = normed_back(x_mid, norm_pre, d_mixed)
    d_mid = grad_y + d_mid
    d_aproj, g_attn = normed_back(a_proj, norm_attn, d_mid)
    d_aproj = d_aproj.astype(jnp.bfloat16)
    g_out = jnp.einsum("tn,td->nd", joined, d_aproj, preferred_element_type=jnp.float32)
    d_joined = jnp.einsum("td,nd->tn", d_aproj, w_out, preferred_element_type=jnp.float32).astype(
        jnp.bfloat16
    )
    do_heads = jnp.transpose(d_joined.reshape(rows, heads, head), (1, 0, 2))
    delta = jnp.sum(do_heads.astype(jnp.float32) * attended, axis=-1, keepdims=True)

    def visit(d_query, moving, grads, source):
        allowed = block_mask(source)
        raw = jnp.einsum("hqd,kd->hqk", q_heads, moving[0], preferred_element_type=jnp.float32)
        probs = jnp.where(allowed[None], jnp.exp(scale * raw - lse), 0.0)
        dv_add = jnp.einsum(
            "hqk,hqd->kd", probs.astype(jnp.bfloat16), do_heads, preferred_element_type=jnp.float32
        )
        d_probs = jnp.einsum("hqd,kd->hqk", do_heads, moving[1], preferred_element_type=jnp.float32)
        d_scores = (scale * probs * (d_probs - delta)).astype(jnp.bfloat16)
        dq_add = jnp.einsum("hqk,kd->hqd", d_scores, moving[0], preferred_element_type=jnp.float32)
        dk_add = jnp.einsum("hqk,hqd->kd", d_scores, q_heads, preferred_element_type=jnp.float32)
        return (d_query + dq_add, grads + jnp.stack([dk_add, dv_add]))

    d_query = jnp.zeros((heads, rows, head), jnp.float32)
    grads = jnp.zeros((2, rows, head), jnp.float32)
    d_query, grads = visit(d_query, pair, grads, place)

    def cycle_backward(step, carry):
        dq_in, moving, grads_in = carry
        moving = from_behind(moving, "blk", 1)
        grads_in = pass_home(grads_in)
        dq_in, grads_in = visit(dq_in, moving, grads_in, (place - step) % count)
        return (dq_in, moving, grads_in)

    d_query, unused_pair, grads = lax.fori_loop(1, count, cycle_backward, (d_query, pair, grads))
    grads = pass_home(grads)

    def query_piece(proj, gain):
        return prepare(proj, gain, cosine[:, None, :], sine[:, None, :])

    def key_piece(proj, gain):
        return prepare(proj, gain, cosine, sine)

    d_qproj, g_qgain = jax.vjp(query_piece, q_proj, query_gain)[1](
        jnp.transpose(d_query, (1, 0, 2))
    )
    d_kproj, g_kgain = jax.vjp(key_piece, k_proj, key_gain)[1](grads[0])
    d_qproj = d_qproj.reshape(rows, heads * head).astype(jnp.bfloat16)
    d_kproj = d_kproj.astype(jnp.bfloat16)
    d_vproj = grads[1].astype(jnp.bfloat16)
    g_query = jnp.einsum("td,tn->dn", normal_a, d_qproj, preferred_element_type=jnp.float32)
    g_key = jnp.einsum("td,tn->dn", normal_a, d_kproj, preferred_element_type=jnp.float32)
    g_value = jnp.einsum("td,tn->dn", normal_a, d_vproj, preferred_element_type=jnp.float32)
    d_normal = jnp.einsum("tn,dn->td", d_qproj, w_query, preferred_element_type=jnp.float32)
    d_normal = d_normal + jnp.einsum(
        "tn,dn->td", d_kproj, w_key, preferred_element_type=jnp.float32
    )
    d_normal = d_normal + jnp.einsum(
        "tn,dn->td", d_vproj, w_value, preferred_element_type=jnp.float32
    )
    d_input, g_in = normed_back(x_in, norm_in, d_normal)
    input_grad = (d_mid + d_input).astype(jnp.bfloat16)
    (
        g_in,
        g_query,
        g_key,
        g_value,
        g_qgain,
        g_kgain,
        g_out,
        g_attn,
        g_pre,
        g_gate,
        g_up,
        g_down,
        g_post,
    ) = sum_gradients(
        (
            g_in,
            g_query,
            g_key,
            g_value,
            g_qgain,
            g_kgain,
            g_out,
            g_attn,
            g_pre,
            g_gate,
            g_up,
            g_down,
            g_post,
        )
    )
    return (
        output.astype(jnp.bfloat16)[None],
        input_grad[None],
        g_in,
        g_query,
        g_key,
        g_value,
        g_qgain,
        g_kgain,
        g_out,
        g_attn,
        g_pre,
        g_gate,
        g_up,
        g_down,
        g_post,
    )


def solution(mesh):
    in_specs = (
        P("dp", "blk", None),
        P("dp", None),
        P("dp", "blk", None),
        P(),
        P(),
        P(),
        P(),
        P(),
        P(),
        P(),
        P(),
        P(),
        P(),
        P(),
        P(),
        P(),
    )
    out_specs = (
        P("dp", "blk", None),
        P("dp", "blk", None),
        P(),
        P(),
        P(),
        P(),
        P(),
        P(),
        P(),
        P(),
        P(),
        P(),
        P(),
        P(),
        P(),
    )
    return jax.shard_map(
        per_device, mesh=mesh, in_specs=in_specs, out_specs=out_specs, check_vma=False
    )
```

```python
import functools

import jax
import jax.numpy as jnp
from jax import lax
from jax.experimental import pallas as pl
from jax.experimental.pallas import tpu as pltpu
from jax.sharding import PartitionSpec as P

EPS = 1e-06
BASE = 1000000.0
NEG = -1e30


def shifted(array, axis, by):
    peers = lax.axis_size(axis)
    return lax.ppermute(array, axis, [(i, (i + by) % peers) for i in range(peers)])


def from_behind(block, axis, distance):
    devices = range(lax.axis_size(axis))
    route = [(i - distance, i) for i in devices if i - distance in devices]
    return lax.ppermute(block, axis, route)


def normed(value, gain):
    return value * lax.rsqrt(jnp.mean(value * value, axis=-1, keepdims=True) + EPS) * gain


def normed_back(value, gain, grad):
    return jax.vjp(normed, value, gain)[1](grad)


def segment_of(index, row):
    ends = jnp.cumsum(row)
    seg = jnp.sum((index[:, None] >= ends[None, :]).astype(jnp.int32), axis=1)
    starts = ends - row
    slots = jnp.arange(row.shape[0], dtype=jnp.int32)
    begin = jnp.sum(jnp.where(slots[None, :] == seg[:, None], starts[None, :], 0), axis=1)
    return (seg, index - begin)


def rotary_tables(places, head):
    half = head // 2
    freq = jnp.exp(-(2.0 * jnp.arange(half, dtype=jnp.float32) / head) * jnp.log(BASE))
    angle = places.astype(jnp.float32)[:, None] * freq[None, :]
    return (jnp.cos(angle), jnp.sin(angle))


def prepare(proj, gain, cosine, sine):
    value = normed(proj, gain)
    half = value.shape[-1] // 2
    first = value[..., :half]
    second = value[..., half:]
    return jnp.concatenate(
        [first * cosine - second * sine, second * cosine + first * sine], axis=-1
    )


def pass_home(grads):
    return shifted(grads.astype(jnp.bfloat16), "blk", 1).astype(grads.dtype)


MESH = pl.DeviceIdType.MESH


def where_am_i():
    place = lax.axis_index("blk")
    part = lax.axis_index("dp")
    return {
        "z": place // 2,
        "y": lax.rem(place, 2),
        "x": part // 2,
        "core": lax.rem(part, 2),
        "place": place,
        "part": part,
    }


def peers_of(me):
    place, part = me["place"], me["part"]
    return {
        "core": {"blk": place, "dp": part + 1 - 2 * me["core"]},
        "x": {"blk": place, "dp": part + 2 - 4 * me["x"]},
        "y": {"blk": place + 1 - 2 * me["y"], "dp": part},
        "up": {"blk": place + 2, "dp": part},
        "down": {"blk": place - 2, "dp": part},
    }


def greet(me, peers, z_count):
    barrier = pltpu.get_barrier_semaphore()
    for name in ("core", "x", "y"):
        pl.semaphore_signal(barrier, inc=1, device_id=peers[name], device_id_type=MESH)

    @pl.when(me["z"] < z_count - 1)
    def _():
        pl.semaphore_signal(barrier, inc=1, device_id=peers["up"], device_id_type=MESH)

    @pl.when(me["z"] > 0)
    def _():
        pl.semaphore_signal(barrier, inc=1, device_id=peers["down"], device_id_type=MESH)

    ends = (me["z"] == 0).astype(jnp.int32) + (me["z"] == z_count - 1).astype(jnp.int32)
    pl.semaphore_wait(barrier, 5 - ends)


def add_into(target, start, row, extra, count, rows):
    step = rows if rows < 32 else 16
    for candidate in (160, 128, 80, 64, 48, 32):
        if rows % candidate == 0:
            step = candidate
            break

    def body(index, carry):
        e = index // (rows // step)
        at = pl.multiple_of(lax.rem(index, rows // step) * step, 8)
        here = pl.ds(pl.multiple_of(row + at, 8), step)
        target[start + e, here, :] = target[start + e, here, :] + extra[e, pl.ds(at, step), :]
        return carry

    lax.fori_loop(0, count * (rows // step), body, 0)


STAGES = 10


class Chunk:
    def __init__(self, number, grad, total, row, rows, first, landing, sems, me, peers, z_count):
        self.grad, self.total, self.row, self.rows = grad, total, row, rows
        self.first, self.second = ("x", "y") if first == "x" else ("y", "x")
        self.land0, self.land1, self.land2 = landing
        self.send, self.recv, self.local = sems
        self.number, self.me, self.peers, self.z_count = number, me, peers, z_count
        self.b1, self.b2, self.core = me[self.first], me[self.second], me["core"]
        self.quad = 4 * self.core
        self.pair = self.quad + 2 * self.b1
        self.own = self.pair + self.b2
        self.half = rows // 2

    def piece(self, start, count, upper=None):
        if upper is None:
            return self.grad.at[pl.ds(start, count), pl.ds(self.row, self.rows), :]
        row = self.row if upper else self.row + self.half
        return self.grad.at[pl.ds(start, count), pl.ds(row, self.half), :]

    def spot(self, count, upper=None):
        row, rows = self.row, self.rows
        if upper is not None:
            row, rows = (row if upper else row + self.half), self.half
        here, columns = pl.ds(row, rows), self.grad.shape[2]
        start = {1: self.own, 2: self.pair, 4: self.quad}[count]
        if len(self.total.shape) == 2:
            return self.total.at[here, pl.ds(pl.multiple_of(start * columns, 128), count * columns)]
        if len(self.total.shape) == 4:
            if count == 4:
                return self.total.at[self.core, :, here, :]
            if count == 2:
                return self.total.at[self.core, self.b1, here, :]
            return self.total.at[self.core, self.b1, here, pl.ds(pl.multiple_of(self.b2 * columns, 128), columns)]
        if count == 1:
            return self.total.at[start, here, :]
        return self.total.at[pl.ds(start, count), here, :]

    def mine(self, upper):
        return self.grad.at[self.own, pl.ds(self.row if upper else self.row + self.half, self.half), :]

    def keep(self, upper):
        return pltpu.make_async_copy(
            self.mine(upper), self.spot(1, upper), self.local.at[self.number]
        )

    def copy(self, stage, peer, source, target):
        return pltpu.make_async_remote_copy(
            src_ref=source,
            dst_ref=target,
            send_sem=self.send.at[self.number, stage],
            recv_sem=self.recv.at[self.number, stage],
            device_id=self.peers[peer],
            device_id_type=MESH,
        )

    def reduce_up(self):
        return self.copy(3, "up", self.piece(self.own, 1, True), self.land2.at[:, pl.ds(self.rows, self.half), :])

    def reduce_down(self):
        return self.copy(4, "down", self.piece(self.own, 1, False), self.land2.at[:, pl.ds(self.rows + self.half, self.half), :])

    def spread_down(self, fresh=False):
        here = self.spot(1, True)
        return self.copy(5, "down", self.mine(True) if fresh else here, here)

    def spread_up(self, fresh=False):
        here = self.spot(1, False)
        return self.copy(6, "up", self.mine(False) if fresh else here, here)

    def step0(self):
        return self.copy(0, "core", self.piece(4 - self.quad, 4), self.land0)

    def step1(self):
        return self.copy(1, self.first, self.piece(self.quad + 2 - 2 * self.b1, 2), self.land1)

    def step2(self):
        return self.copy(2, self.second, self.piece(self.pair + 1 - self.b2, 1), self.land2.at[:, pl.ds(0, self.rows), :])

    def gather(self, stage):
        count, peer = ((1, self.second), (2, self.first), (4, "core"))[stage - 7]
        here = self.spot(count)
        return self.copy(stage, peer, here, here)

    def arrive_upper(self):
        z, last = self.me["z"], self.z_count - 1

        @pl.when(z > 0)
        def _():
            self.reduce_up().wait_recv()
            add_into(self.grad, self.own, self.row, self.land2.at[:, pl.ds(self.rows, self.half), :], 1, self.half)

            @pl.when(z < last)
            def _():
                self.reduce_up().start()

            @pl.when(z == last)
            def _():
                self.spread_down(True).start()
                self.keep(True).start()

    def arrive_lower(self):
        z, last = self.me["z"], self.z_count - 1

        @pl.when(z < last)
        def _():
            self.reduce_down().wait_recv()
            add_into(self.grad, self.own, self.row + self.half, self.land2.at[:, pl.ds(self.rows + self.half, self.half), :], 1, self.half)

            @pl.when(z > 0)
            def _():
                self.reduce_down().start()

            @pl.when(z == 0)
            def _():
                self.spread_up(True).start()
                self.keep(False).start()

    def back_upper(self):
        z, last = self.me["z"], self.z_count - 1

        @pl.when(z < last)
        def _():
            self.spread_down().wait_recv()

            @pl.when(z > 0)
            def _():
                self.spread_down().start()

    def back_lower(self):
        z, last = self.me["z"], self.z_count - 1

        @pl.when(z > 0)
        def _():
            self.spread_up().wait_recv()

            @pl.when(z < last)
            def _():
                self.spread_up().start()

    def tick(self, op):
        z, last = self.me["z"], self.z_count - 1
        if op == 0:
            self.step0().start()
        elif op == 1:
            self.step0().wait_recv()
            add_into(self.grad, self.quad, self.row, self.land0, 4, self.rows)
            self.step1().start()
        elif op == 2:
            self.step1().wait_recv()
            add_into(self.grad, self.pair, self.row, self.land1, 2, self.rows)
            self.step2().start()
        elif op == 3:
            self.step2().wait_recv()
            add_into(self.grad, self.own, self.row, self.land2, 1, self.rows)

            @pl.when(z == 0)
            def _():
                self.reduce_up().start()

            @pl.when(z == last)
            def _():
                self.reduce_down().start()

        elif op == 4:
            pl.when((z > 0) & (2 * z < self.z_count))(self.arrive_upper)
            pl.when((z < last) & (2 * z >= self.z_count))(self.arrive_lower)
        elif op == 5:
            pl.when((z < last) & (2 * z >= self.z_count))(self.arrive_upper)
            pl.when((z > 0) & (2 * z < self.z_count))(self.arrive_lower)
        elif op == 6:
            pl.when(z == last)(self.arrive_upper)
            pl.when(z == 0)(self.arrive_lower)
        elif op == 7:
            pl.when((z < last) & (2 * z >= self.z_count))(self.back_upper)
            pl.when((z > 0) & (2 * z < self.z_count))(self.back_lower)
        elif op == 8:

            @pl.when((z > 0) & (2 * z < self.z_count))
            def _():
                self.back_upper()
                self.gather(7).start()

            @pl.when((z < last) & (2 * z >= self.z_count))
            def _():
                self.back_lower()
                self.gather(7).start()

        elif op == 9:

            @pl.when(z == 0)
            def _():
                self.back_upper()
                self.keep(False).wait()
                self.gather(7).start()

            @pl.when(z == last)
            def _():
                self.back_lower()
                self.keep(True).wait()
                self.gather(7).start()

        elif op == 10:
            self.gather(7).wait_recv()
            self.gather(8).start()
        elif op == 11:
            self.gather(8).wait_recv()
            self.gather(9).start()
        elif op == 12:
            self.gather(9).wait_recv()
            self.drain()

    OPS = 13

    def drain(self):
        z, last = self.me["z"], self.z_count - 1
        self.step0().wait_send()
        self.step1().wait_send()
        self.step2().wait_send()
        for stage in (7, 8, 9):
            self.gather(stage).wait_send()

        @pl.when(z < last)
        def _():
            self.reduce_up().wait_send()
            self.spread_up().wait_send()

        @pl.when(z > 0)
        def _():
            self.reduce_down().wait_send()
            self.spread_down().wait_send()


def sum_kernel(z_count, plan, *refs):
    n = 1 + max(item[0] for item in plan)
    parts = len(plan)
    ins, outs = refs[:n], refs[n : 2 * n]
    rest = refs[2 * n :]
    grads, rest = rest[:n], rest[n:]
    landings = rest[: 3 * parts]
    send, recv, local, load = rest[3 * parts :]
    me = where_am_i()
    peers = peers_of(me)
    loads = [pltpu.make_async_copy(ins[i], grads[i], load.at[i]) for i in range(n)]
    for item in loads:
        item.start()
    greet(me, peers, z_count)
    for item in loads:
        item.wait()
    chunks = []
    for number, (i, row, rows, first) in enumerate(plan):
        landing = landings[3 * number : 3 * number + 3]
        chunks.append(
            Chunk(number, grads[i], outs[i], row, rows, first, landing, (send, recv, local), me, peers, z_count)
        )
    for at in range(parts + Chunk.OPS - 1):
        for number in range(parts):
            if 0 <= at - number < Chunk.OPS:
                chunks[number].tick(at - number)


def sum_call(arrays, plan, z_count):
    landing = []
    for i, row, rows, first in plan:
        columns, kind = arrays[i].shape[2], arrays[i].dtype
        landing += [
            pltpu.VMEM((4, rows, columns), kind),
            pltpu.VMEM((2, rows, columns), kind),
            pltpu.VMEM((1, 2 * rows, columns), kind),
        ]
    n = len(arrays)
    return pl.pallas_call(
        functools.partial(sum_kernel, z_count, plan),
        out_shape=tuple(jax.ShapeDtypeStruct(v.shape, v.dtype) for v in arrays),
        in_specs=[pl.BlockSpec(memory_space=pl.ANY)] * n,
        out_specs=tuple([pl.BlockSpec(memory_space=pl.ANY)] * n),
        scratch_shapes=[pltpu.VMEM(v.shape, v.dtype) for v in arrays]
        + landing
        + [
            pltpu.SemaphoreType.DMA((len(plan), STAGES)),
            pltpu.SemaphoreType.DMA((len(plan), STAGES)),
            pltpu.SemaphoreType.DMA((len(plan),)),
            pltpu.SemaphoreType.DMA((n,)),
        ],
        compiler_params=pltpu.CompilerParams(
            collective_id=0, has_side_effects=True, vmem_limit_bytes=56 * 2**20
        ),
    )(*arrays)


def columns_to_panels(value):
    rows, columns = value.shape
    return jnp.transpose(value.reshape(rows, 8, columns // 8), (1, 0, 2)).astype(jnp.bfloat16)


def panels_to_columns(panels):
    count, rows, width = panels.shape
    return jnp.transpose(panels.astype(jnp.float32), (1, 0, 2)).reshape(rows, count * width)


def sum_gradients(grads):
    (g_in, g_query, g_key, g_value, g_qgain, g_kgain, g_out, g_attn, g_pre, g_gate, g_up, g_down, g_post) = grads
    z_count = lax.axis_size("blk") // 2
    width = g_in.shape[0]
    gains = [g_in, g_attn, g_pre, g_post, g_qgain, g_kgain]
    sizes = [v.shape[0] for v in gains]
    flat = jnp.concatenate(gains)
    gain_rows = 32
    flat = jnp.pad(flat, (0, 8 * gain_rows * 128 - flat.shape[0])).reshape(8, gain_rows, 128)
    down = g_down.astype(jnp.bfloat16).reshape(8, -1, width)
    out = g_out.astype(jnp.bfloat16).reshape(8, -1, width)
    both = jnp.stack([g_key, g_value])
    head = g_key.shape[1]
    both = jnp.transpose(both.reshape(2, 2, width // 2, 2, head // 2), (0, 1, 3, 2, 4)).reshape(8, width // 2, head // 2)
    arrays = [down, columns_to_panels(g_gate), columns_to_panels(g_up), out, columns_to_panels(g_query), both.astype(jnp.bfloat16), flat]
    plan = []
    for i, v in enumerate(arrays[:-1]):
        rows = v.shape[1] // 2
        plan += [(i, 0, rows, "x"), (i, rows, rows, "y")]
    plan.append((6, 0, gain_rows, "x"))
    down, gate, up, out, query, both, flat = sum_call(arrays, plan, z_count)
    both = jnp.transpose(both.astype(jnp.float32).reshape(2, 2, 2, width // 2, head // 2), (0, 1, 3, 2, 4)).reshape(2, width, head)
    flat = flat.reshape(-1)
    cuts, at = [], 0
    for size in sizes:
        cuts.append(flat[at : at + size])
        at += size
    g_in, g_attn, g_pre, g_post, g_qgain, g_kgain = cuts
    return (
        g_in,
        panels_to_columns(query),
        both[0],
        both[1],
        g_qgain,
        g_kgain,
        out.astype(jnp.float32).reshape(g_out.shape),
        g_attn,
        g_pre,
        panels_to_columns(gate),
        panels_to_columns(up),
        down.astype(jnp.float32).reshape(g_down.shape),
        g_post,
    )


LOG2E = 1.4426950408889634
LN2 = 0.6931471805599453
PIECES = (2, 2, 2, 2, 2, 2, 1)
FIRST = ['x', 'y', 'x', 'y', 'x', 'y', 'x', 'y', 'x', 'y', 'x', 'y', 'x']
SCHEDULES = {
    4: (
        (0, 0), ("S", 0), (1, 0), (0, 1), ("F", 0), (1, 1), ("F", 1), ("M", 0), (2, 0), (0, 2), ("O", 0), ("X", 0), (3, 0), ("W", 0), (1, 2),
        ("X", 1), (0, 3), (0, 4), (5, 0), (2, 1), (6, 0), (1, 3), ("W", 1), (1, 4), (0, 5), (4, 0), (6, 1), (1, 5), (3, 1), ("P", 0), (6, 2),
        ("X", 2), ("P", 1), (3, 2), (7, 0), ("W", 2), (2, 2), ("X", 3), ("P", 2), ("W", 3), ("Q", 0), (6, 3), (4, 1), (1, 6), ("Q", 1), (3, 3),
        (7, 1), (5, 1), ("Q", 2), (6, 4), (2, 3), (1, 7), ("Q", 3), (3, 4), ("G", 0), (8, 0), (2, 4), (6, 5), (9, 0), (0, 6), (3, 5), (7, 2),
        ("T", 0), (1, 8), (8, 1), (4, 2), (6, 6), ("K", 0), (1, 9), (0, 7), (6, 7), (9, 1), (2, 5), (7, 3), (3, 6), (11, 0), (10, 0), (12, 0), (5, 2),
        (0, 8), (6, 8), (8, 2), (4, 3), (3, 7), (11, 1), (12, 1), (2, 6), (0, 9), (10, 1), (5, 3), (2, 7), (3, 8), (9, 2), (2, 8), (6, 9), (4, 4),
        (11, 2), (7, 4), (3, 9), (1, 10), (8, 3), (0, 10), (10, 2), (5, 4), (2, 9), (8, 4), (9, 3), (7, 5), (6, 10), (4, 5), (12, 2), (11, 3), (5, 5),
        (7, 6), (10, 3), (12, 3), (11, 4), (4, 6), (8, 5), (5, 6), (3, 10), (7, 7), (11, 5), (9, 4), (10, 4), (4, 7), (11, 6), (8, 6), (7, 8),
        (2, 10), (9, 5), (5, 7), (12, 4), (11, 7), (4, 8), (0, 11), (7, 9), (4, 9), (11, 8), (10, 5), (8, 7), (6, 11), (12, 5), (5, 8), (10, 6),
        (7, 10), (11, 9), (12, 6), (3, 11), (8, 8), (10, 7), (5, 9), (9, 6), (4, 10), (12, 7), (9, 7), (10, 8), (12, 8), (11, 10), (12, 9), (10, 9),
        (1, 11), (8, 9), (12, 10), (5, 10), (7, 11), (9, 8), (9, 9), (11, 11), (2, 11), (11, 12), (8, 10), (2, 12), (9, 10), (4, 11), (12, 11),
        (10, 10), (6, 12), (5, 11), (8, 11), (3, 12), (12, 12), (0, 12), (4, 12), (1, 12), (10, 11), (9, 11), (10, 12), (9, 12), (5, 12), (7, 12),
        (8, 12),
    )
}


def dot(left, right):
    return jnp.dot(left, right, preferred_element_type=jnp.float32)


def dot_nt(left, right):
    return lax.dot_general(left, right, (((1,), (1,)), ((), ())), preferred_element_type=jnp.float32)


def inverse_rms(value):
    return lax.rsqrt(jnp.mean(value * value, axis=-1, keepdims=True) + EPS)


def rms_back(value, inverse, gain, grad):
    scaled = grad * gain
    normal = value * inverse
    mean = jnp.mean(scaled * normal, axis=-1, keepdims=True)
    terms = grad * normal
    return inverse * (scaled - normal * mean), jnp.sum(terms.reshape(-1, 8, terms.shape[-1]), axis=0)


def turn(value, cosine, sine):
    half = value.shape[-1] // 2
    first, second = value[:, :half], value[:, half:]
    return jnp.concatenate([first * cosine - second * sine, second * cosine + first * sine], axis=-1)


def turn_back(grad, cosine, sine):
    half = grad.shape[-1] // 2
    first, second = grad[:, :half], grad[:, half:]
    return jnp.concatenate([first * cosine + second * sine, second * cosine - first * sine], axis=-1)


def dot_tn(left, right):
    return lax.dot_general(left, right, (((0,), (0,)), ((), ())), preferred_element_type=jnp.float32)


def bf16(value):
    return value.astype(jnp.bfloat16)


def f32(value):
    return value.astype(jnp.float32)


class Names(dict):
    __getattr__ = dict.__getitem__


def layer_kernel(sizes, schedule, names, *refs):
    r = Names(zip(names, refs, strict=True))
    rows, width, hidden, heads, head, z_count = sizes
    scale = head**-0.5
    tile = 128
    tiles = [slice(at, at + tile) for at in range(0, rows, tile)]
    half = head // 2
    me = where_am_i()
    peers = peers_of(me)
    z, y, place = me["z"], me["y"], me["place"]
    last = z_count - 1

    weights = ["x", "w_key", "w_value", "w_query", "w_out", "w_gate", "w_up", "w_down", "dy"]
    joined = heads * head
    wide_k, wide_v = slice(joined, joined + head), slice(joined + head, joined + 2 * head)
    spots = {"w_query": slice(0, joined), "w_key": wide_k, "w_value": wide_v}
    loads = {}
    for i, name in enumerate(weights):
        spot = r.w_first.at[:, spots[name]] if name in spots else r[name]
        loads[name] = pltpu.make_async_copy(r[name + "_in"], spot, r.load_sem.at[i])
    for name in weights:
        loads[name].start()
    greet(me, peers, z_count)

    def begins(token):
        begin, end = jnp.zeros_like(token), jnp.int32(0)
        for j in range(r.lengths.shape[1]):
            end = end + r.lengths[0, j]
            begin = jnp.where(token >= end, end, begin)
        return begin

    token = place * rows + lax.broadcasted_iota(jnp.int32, (1, rows), 1)
    begin = begins(token)
    entry = f32(lax.broadcasted_iota(jnp.int32, (1, half), 1))
    speed = jnp.exp(-(2.0 * entry / head) * jnp.log(BASE))
    for t in tiles:
        column = place * rows + t.start + lax.broadcasted_iota(jnp.int32, (tile, 1), 0)
        angle = f32(column - begins(column)) * speed
        r.cosine[t, :] = jnp.cos(angle)
        r.sine[t, :] = jnp.sin(angle)
    gain_in = r.norm_in[...].reshape(1, width)
    gain_q = r.query_gain[...].reshape(1, head)
    gain_k = r.key_gain[...].reshape(1, head)
    gain_attn = r.norm_attn[...].reshape(1, width)
    gain_pre = r.norm_pre[...].reshape(1, width)
    gain_post = r.norm_post[...].reshape(1, width)

    def allowed(source):
        key = source * rows + lax.broadcasted_iota(jnp.int32, (rows, rows), 0)
        return (key >= begin) & (key <= token)

    loads["x"].wait()
    loads["w_key"].wait()
    loads["w_value"].wait()
    for t in tiles:
        x = f32(r.x[t, :])
        r.a[t, :] = bf16(x * inverse_rms(x) * gain_in)
    r.kp[...] = dot(r.a[...], r.w_first[:, wide_k])
    r.kv[place, :, head : 2 * head] = bf16(dot(r.a[...], r.w_first[:, wide_v]))
    for t in tiles:
        kp = r.kp[t, :]
        r.kv[place, t, 0:head] = bf16(turn(kp * inverse_rms(kp) * gain_k, r.cosine[t, :], r.sine[t, :]))

    def send_kv(source, route):
        peer = peers["up"] if route == 0 else peers["y"]
        return pltpu.make_async_remote_copy(
            src_ref=r.kv.at[source],
            dst_ref=r.kv.at[source],
            send_sem=r.kv_send.at[route, source],
            recv_sem=r.kv_recv.at[source],
            device_id=peer,
            device_id_type=MESH,
        )

    pl.when(z < last)(lambda: send_kv(place, 0).start())
    pl.when(y == 0)(lambda: send_kv(place, 1).start())

    loads["w_query"].wait()
    for h in range(heads):
        wide = slice(h * head, (h + 1) * head)
        r.qp[:, wide] = dot(r.a[...], r.w_first[:, wide])
        for t in tiles:
            qp = r.qp[t, wide]
            q = turn(qp * inverse_rms(qp) * gain_q, r.cosine[t, :], r.sine[t, :])
            q = bf16(q * (scale * LOG2E))
            r.q[h * rows + t.start : h * rows + t.stop, :] = q
            r.qt[:, h * rows + t.start : h * rows + t.stop] = q.T

    columns = [slice(h * rows, (h + 1) * rows) for h in range(heads)]

    def visit(source, first):
        vt = r.kv[source, :, head : 2 * head].T
        mask = allowed(source)
        for here in columns:
            p = jnp.where(mask, jnp.exp2(dot(r.kv[source, :, 0:head], r.qt[:, here])), 0.0)
            total = jnp.sum(p, axis=0, keepdims=True)
            o = dot(vt, bf16(p))
            r.total[:, here] = total if first else r.total[:, here] + total
            r.ot[:, here] = o if first else r.ot[:, here] + o

    visit(place, True)

    @pl.when(y == 1)
    def _():
        send_kv(place - 1, 1).wait_recv()
        visit(place - 1, False)

    for back in range(1, z_count + 1):
        mine = place - 2 * back

        @pl.when(back <= z)
        def _():
            send_kv(mine, 0).wait_recv()
            pl.when(z < last)(lambda: send_kv(mine, 0).start())
            send_kv(mine, 1).start()

        if back > 1:

            @pl.when(back - 1 <= z)
            def _():
                other = mine + 3 - 2 * y
                send_kv(other, 1).wait_recv()
                visit(other, False)

        pl.when(back <= z)(lambda: visit(mine, False))

    for h, here in enumerate(columns):
        total = r.total[:, here]
        o = r.ot[:, here] * (1.0 / total)
        r.lse[:, here] = jnp.log2(total)
        r.ot[:, here] = o
        r.ob[:, h * head : (h + 1) * head] = bf16(o).T

    loads["w_out"].wait()
    r.ap[...] = dot(r.ob[:, 0:joined], r.w_out[...])
    for t in tiles:
        ap = r.ap[t, :]
        x1 = f32(r.x[t, :]) + ap * inverse_rms(ap) * gain_attn
        r.x1[t, :] = x1
        r.m[t, :] = bf16(x1 * inverse_rms(x1) * gain_pre)
    loads["w_gate"].wait()
    loads["w_up"].wait()
    block = hidden // 8
    quarters = [slice(j * 2 * block, (j + 1) * 2 * block) for j in range(4)]
    for cols in quarters:
        gate = dot(r.m[...], r.w_gate[:, cols])
        up = dot(r.m[...], r.w_up[:, cols])
        inner = 0.7978845608028654 * (gate + 0.044715 * gate * gate * gate)
        th = jnp.tanh(inner)
        cdf = 0.5 * (1.0 + th)
        act = gate * cdf
        slope = cdf + 0.5 * gate * (1.0 - th * th) * 0.7978845608028654 * (1.0 + 3 * 0.044715 * gate * gate)
        r.hid[:, cols] = bf16(act * up)
        r.side_gate[:, cols] = bf16(slope * up)
        r.side_up[:, cols] = bf16(act)
    loads["w_down"].wait()
    loads["dy"].wait()
    r.wide[...] = dot(r.hid[...], r.w_down[...])
    r.gains[...] = jnp.zeros_like(r.gains)

    def gain(k, terms):
        r.gains[k, :, 0 : terms.shape[1]] = r.gains[k, :, 0 : terms.shape[1]] + terms

    for t in tiles:
        f = r.wide[t, :]
        inverse = inverse_rms(f)
        r.out[t, :] = bf16(r.x1[t, :] + f * inverse * gain_post)
        df, g = rms_back(f, inverse, gain_post, f32(r.dy[t, :]))
        r.df[t, :] = bf16(df)
        gain(3, g)
    for j in range(8):
        r.g_down[j] = bf16(dot_tn(r.hid[:, j * block : (j + 1) * block], r.df[...]))

    chunks, number = {}, 0
    sems = (r.red_send, r.red_recv, r.red_local)
    for name, count in r_plan(sizes):
        grad, total = r["g_" + name], r["t_" + name]
        step = grad.shape[1] // count
        chunks[name] = []
        for i in range(count):
            landing = tuple(r[f"land{k}_{name}"].at[i] for k in range(3))
            chunks[name].append(Chunk(number, grad, total, i * step, step, FIRST[number], landing, sems, me, peers, z_count))
            number += 1
    chunks = [chunk for name, count in r_plan(sizes) for chunk in chunks[name]]

    def side_grads(part):
        for cols in quarters:
            dh = dot_nt(r.df[...], r.w_down[cols, :])
            r.side_gate[:, cols] = bf16(dh * f32(r.side_gate[:, cols]))
            r.side_up[:, cols] = bf16(dh * f32(r.side_up[:, cols]))

    def feed_grads(part):
        grad, side = ((r.g_gate, r.side_gate), (r.g_up, r.side_up))[part]
        for j in range(8):
            grad[j] = bf16(dot_tn(r.m[...], side[:, j * block : (j + 1) * block]))

    def middle_back(part):
        r.wide[...] = dot_nt(r.side_gate[...], r.w_gate[...]) + dot_nt(r.side_up[...], r.w_up[...])
        for t in tiles:
            x1 = r.x1[t, :]
            dx1, g = rms_back(x1, inverse_rms(x1), gain_pre, r.wide[t, :])
            gain(2, g)
            dx1 = dx1 + f32(r.dy[t, :])
            r.x1[t, :] = dx1
            ap = r.ap[t, :]
            dap, g = rms_back(ap, inverse_rms(ap), gain_attn, dx1)
            gain(1, g)
            r.dap[t, :] = bf16(dap)

    def out_back(part):
        for h, here in enumerate(columns):
            wide = slice(h * head, (h + 1) * head)
            g = bf16(dot_tn(r.ob[:, wide], r.dap[...]))
            r.g_out[2 * h] = g[0:half]
            r.g_out[2 * h + 1] = g[half:head]
            do = bf16(dot_nt(r.dap[...], r.w_out[wide, :]))
            r.do[here, :] = do
            turned = do.T
            r.dot[:, here] = turned
            r.delta[:, here] = jnp.sum(f32(turned) * r.ot[:, here], axis=0, keepdims=True)
        r.ot[...] = jnp.zeros_like(r.ot)

    def visit_back(source, target):
        kt = r.kv[source, :, 0:head].T
        mask = allowed(source)
        for here in columns:
            s = dot(r.kv[source, :, 0:head], r.qt[:, here])
            p = jnp.where(mask, jnp.exp2(s - r.lse[:, here]), 0.0)
            dp = dot(r.kv[source, :, head : 2 * head], r.dot[:, here])
            r.probs[:, here] = bf16(p)
            r.dscores[:, here] = bf16(p * (dp - r.delta[:, here]))
        target[:, 0:head] = bf16(dot(r.dscores[...], r.q[...]))
        target[:, head : 2 * head] = bf16(dot(r.probs[...], r.do[...]))
        for here in columns:
            r.ot[:, here] = r.ot[:, here] + dot(kt, r.dscores[:, here])

    def stage_y(row):
        return r.w_gate.at[0:rows, row * 2 * head : (row + 1) * 2 * head]

    def stage_z(row):
        return r.w_up.at[0:rows, row * 2 * head : (row + 1) * 2 * head]

    def to_partner(row):
        return pltpu.make_async_remote_copy(
            src_ref=stage_y(row),
            dst_ref=r.from_partner.at[row],
            send_sem=r.dkv_send.at[0, row],
            recv_sem=r.dkv_recv.at[0, row],
            device_id=peers["y"],
            device_id_type=MESH,
        )

    def to_below(row):
        return pltpu.make_async_remote_copy(
            src_ref=stage_z(row),
            dst_ref=r.from_above.at[row],
            send_sem=r.dkv_send.at[1, row],
            recv_sem=r.dkv_recv.at[1, row],
            device_id=peers["down"],
            device_id_type=MESH,
        )

    def visit_other(row):
        @pl.when((row < z) | ((row == z) & (y == 1)))
        def _():
            visit_back(2 * row + 1 - y, stage_y(row))
            to_partner(row).start()

    def visit_own(row):
        pl.when(row <= z)(lambda: visit_back(2 * row + y, stage_z(row)))

    def pass_down(row):
        @pl.when(row < z)
        def _():
            to_partner(row).wait_recv()
            pl.when(z < last)(lambda: to_below(row).wait_recv())
            for t in tiles:
                value = f32(stage_z(row)[t, :]) + f32(r.from_partner[row, t, :])
                above = jnp.where(z < last, f32(r.from_above[row, t, :]), 0.0)
                stage_z(row)[t, :] = bf16(value + above)
            to_below(row).start()

    def queries_back(h):
        wide = slice(h * head, (h + 1) * head)
        for t in tiles:
            dq = (r.ot[:, h * rows + t.start : h * rows + t.stop] * scale).T
            qp = r.qp[t, wide]
            dqp, g = rms_back(qp, inverse_rms(qp), gain_q, turn_back(dq, r.cosine[t, :], r.sine[t, :]))
            gain(4, g)
            r.ob[t, wide] = bf16(dqp)

    def query_grad(part):
        for h in range(heads):
            g = bf16(dot_tn(r.a[...], r.ob[:, h * head : (h + 1) * head]))
            r.g_query[2 * h] = g[:, 0:half]
            r.g_query[2 * h + 1] = g[:, half:head]

    def own_total(part):
        for row in range(z_count):

            @pl.when(row == z)
            def _():
                pl.when(y == 0)(lambda: to_partner(row).wait_recv())
                pl.when(z < last)(lambda: to_below(row).wait_recv())
                for t in tiles:
                    beside = jnp.where(y == 0, f32(r.from_partner[row, t, :]), 0.0)
                    above = jnp.where(z < last, f32(r.from_above[row, t, :]), 0.0)
                    r.dkv[t, :] = f32(stage_z(row)[t, :]) + beside + above

    def keys_back(part):
        for t in tiles:
            dk = r.dkv[t, 0:head] * LN2
            kp = r.kp[t, :]
            dkp, g = rms_back(kp, inverse_rms(kp), gain_k, turn_back(dk, r.cosine[t, :], r.sine[t, :]))
            gain(5, g)
            r.ob[t, wide_k] = bf16(dkp)
            r.ob[t, wide_v] = bf16(r.dkv[t, head : 2 * head])
        low = width // 2
        g = bf16(dot_tn(r.a[...], r.ob[:, joined : joined + 2 * head]))
        for p in range(8):
            which, upper, side = p // 4, (p // 2) % 2, p % 2
            left = which * head + side * half
            r.g_kv[p] = g[upper * low : (upper + 1) * low, left : left + half]
        r.wide[...] = dot_nt(r.ob[...], r.w_first[...])
        for t in tiles:
            x = f32(r.x[t, :])
            dx, g = rms_back(x, inverse_rms(x), gain_in, r.wide[t, :])
            gain(0, g)
            r.dx[t, :] = bf16(r.x1[t, :] + dx)
        r.g_gain[...] = jnp.zeros_like(r.g_gain)
        at = 0
        for k, size in enumerate((width, width, width, width, head, head)):
            g = jnp.sum(r.gains[k], axis=0, keepdims=True)
            for part in range(size // 128):
                r.g_gain[at // 16, at % 16 : at % 16 + 1, :] = g[:, part * 128 : (part + 1) * 128]
                at += 1

    work = {
        "S": side_grads,
        "F": feed_grads,
        "M": middle_back,
        "O": out_back,
        "X": visit_other,
        "W": visit_own,
        "P": pass_down,
        "Q": queries_back,
        "G": query_grad,
        "T": own_total,
        "K": keys_back,
    }
    for what, step in schedule:
        if what in work:
            work[what](step)
        else:
            chunks[what].tick(step)

    pl.when(z < last)(lambda: send_kv(place, 0).wait_send())
    pl.when(y == 0)(lambda: send_kv(place, 1).wait_send())
    for back in range(1, z_count):

        @pl.when(back <= z)
        def _():
            mine = place - 2 * back
            pl.when(z < last)(lambda: send_kv(mine, 0).wait_send())
            send_kv(mine, 1).wait_send()

    for row in range(z_count):
        pl.when((row < z) | ((row == z) & (y == 1)))(lambda: to_partner(row).wait_send())
        pl.when(row < z)(lambda: to_below(row).wait_send())


def r_plan(sizes):
    return list(zip(("down", "gate", "up", "out", "query", "kv", "gain"), PIECES, strict=True))


def gradient_shapes(sizes):
    rows, width, hidden, heads, head, z_count = sizes
    joined, half = heads * head, head // 2
    return {
        "down": ((8, hidden // 8, width), (8, hidden // 8, width)),
        "gate": ((8, width, hidden // 8), (width, hidden)),
        "up": ((8, width, hidden // 8), (width, hidden)),
        "out": ((8, joined // 8, width), (8, joined // 8, width)),
        "query": ((8, width, joined // 8), (width, joined)),
        "kv": ((8, width // 2, half), (2, 2, width // 2, head)),
        "gain": ((8, 16, 128), (8, 16, 128)),
    }


def layer_scratch(sizes):
    rows, width, hidden, heads, head, z_count = sizes
    joined = heads * head
    low, wide = jnp.bfloat16, jnp.float32
    arrays = {
        "x": ((rows, width), low),
        "w_first": ((width, joined + 2 * head), low),
        "w_out": ((joined, width), low),
        "w_gate": ((width, hidden), low),
        "w_up": ((width, hidden), low),
        "w_down": ((hidden, width), low),
        "dy": ((rows, width), low),
        "a": ((rows, width), low),
        "gains": ((6, 8, width), wide),
        "kp": ((rows, head), wide),
        "kv": ((2 * z_count, rows, 2 * head), low),
        "qp": ((rows, joined), wide),
        "q": ((heads * rows, head), low),
        "qt": ((head, heads * rows), low),
        "cosine": ((rows, head // 2), wide),
        "sine": ((rows, head // 2), wide),
        "wide": ((rows, width), wide),
        "probs": ((rows, heads * rows), low),
        "dscores": ((rows, heads * rows), low),
        "ot": ((head, heads * rows), wide),
        "total": ((1, heads * rows), wide),
        "lse": ((1, heads * rows), wide),
        "delta": ((1, heads * rows), wide),
        "ob": ((rows, joined + 2 * head), low),
        "ap": ((rows, width), wide),
        "x1": ((rows, width), wide),
        "m": ((rows, width), low),
        "hid": ((rows, hidden), low),
        "side_gate": ((rows, hidden), low),
        "side_up": ((rows, hidden), low),
        "df": ((rows, width), low),
        "dap": ((rows, width), low),
        "do": ((heads * rows, head), low),
        "dot": ((head, heads * rows), low),
        "dkv": ((rows, 2 * head), wide),
        "from_partner": ((z_count, rows, 2 * head), low),
        "from_above": ((z_count, rows, 2 * head), low),
    }
    shapes = gradient_shapes(sizes)
    pieces = 0
    for name, count in r_plan(sizes):
        (eight, high, columns), kind = shapes[name][0], wide if name == "gain" else low
        step = high // count
        pieces += count
        arrays["g_" + name] = (shapes[name][0], kind)
        arrays["land0_" + name] = ((count, 4, step, columns), kind)
        arrays["land1_" + name] = ((count, 2, step, columns), kind)
        arrays["land2_" + name] = ((count, 1, 2 * step, columns), kind)
    sems = {
        "load_sem": (9,),
        "kv_send": (2, 2 * z_count),
        "kv_recv": (2 * z_count,),
        "dkv_send": (2, z_count),
        "dkv_recv": (2, z_count),
        "red_send": (pieces, STAGES),
        "red_recv": (pieces, STAGES),
        "red_local": (pieces,),
    }
    return arrays, sems


def layer_bytes(sizes):
    total = 0
    for shape, kind in layer_scratch(sizes)[0].values():
        size = jnp.dtype(kind).itemsize
        for n in shape[:-2]:
            size *= n
        total += size * max(shape[-2], 8) * max(shape[-1], 128)
    return total


VMEM_BYTES = 64 * 2**20


def widen_kernel(count, *refs):
    ins, table = refs[:count], refs[count]
    outs, gains = refs[count + 1 : 2 * count + 1], refs[2 * count + 1 : 2 * count + 7]
    narrow, broad, (came, gone) = refs[2 * count + 7 : 3 * count + 7], refs[3 * count + 7 : 4 * count + 7], refs[4 * count + 7 :]
    loads = [pltpu.make_async_copy(ins[i], narrow[i], came.at[i]) for i in range(count)]
    stores = [pltpu.make_async_copy(broad[i], outs[i], gone.at[i]) for i in range(count)]
    for item in loads:
        item.start()
    at = 0
    for gain in gains:
        for part in range(gain.shape[0] // 128):
            gain[part * 128 : (part + 1) * 128] = table[at // 16, at % 16, :]
            at += 1
    for i in range(count):
        loads[i].wait()

        def body(j, carry):
            here = pl.ds(pl.multiple_of(j * 32, 32), 32)
            broad[i][here, :] = f32(narrow[i][here, :])
            return carry

        lax.fori_loop(0, narrow[i].shape[0] // 32, body, 0)
        stores[i].start()
    for item in stores:
        item.wait()


def widen(matrices, table, gain_sizes):
    count = len(matrices)
    anywhere, vmem = pl.BlockSpec(memory_space=pl.ANY), pl.BlockSpec(memory_space=pltpu.VMEM)
    return pl.pallas_call(
        functools.partial(widen_kernel, count),
        out_shape=tuple(jax.ShapeDtypeStruct(v.shape, jnp.float32) for v in matrices)
        + tuple(jax.ShapeDtypeStruct((n,), jnp.float32) for n in gain_sizes),
        in_specs=[anywhere] * count + [vmem],
        out_specs=tuple([anywhere] * count + [vmem] * len(gain_sizes)),
        scratch_shapes=[pltpu.VMEM(v.shape, v.dtype) for v in matrices]
        + [pltpu.VMEM(v.shape, jnp.float32) for v in matrices]
        + [pltpu.SemaphoreType.DMA((count,))] * 2,
        compiler_params=pltpu.CompilerParams(vmem_limit_bytes=VMEM_BYTES),
    )(*matrices, table)


def whole_layer(sizes, tokens, lengths, cotangent, norm_in, w_query, w_key, w_value, query_gain, key_gain, w_out, norm_attn, norm_pre, w_gate, w_up, w_down, norm_post):
    rows, width, hidden, heads, head, z_count = sizes
    joined = heads * head
    inputs = {
        "lengths": lengths,
        "norm_in": norm_in,
        "query_gain": query_gain,
        "key_gain": key_gain,
        "norm_attn": norm_attn,
        "norm_pre": norm_pre,
        "norm_post": norm_post,
        "x_in": tokens[0],
        "w_key_in": w_key,
        "w_value_in": w_value,
        "w_query_in": w_query,
        "w_out_in": w_out,
        "w_gate_in": w_gate,
        "w_up_in": w_up,
        "w_down_in": w_down,
        "dy_in": cotangent[0],
    }
    spaces = {name: pltpu.SMEM if name == "lengths" else pl.ANY if name.endswith("_in") and name != "norm_in" else pltpu.VMEM for name in inputs}
    shapes = gradient_shapes(sizes)
    outputs = {"out": (rows, width), "dx": (rows, width)}
    outputs.update({"t_" + name: shapes[name][1] for name in shapes})
    arrays, sems = layer_scratch(sizes)
    names = list(inputs) + list(outputs) + list(arrays) + list(sems)
    results = pl.pallas_call(
        functools.partial(layer_kernel, sizes, SCHEDULES[z_count], names),
        out_shape=tuple(
            jax.ShapeDtypeStruct(shape, jnp.float32 if name == "t_gain" else jnp.bfloat16) for name, shape in outputs.items()
        ),
        in_specs=[pl.BlockSpec(memory_space=spaces[name]) for name in inputs],
        out_specs=tuple(
            pl.BlockSpec(memory_space=pl.ANY if name.startswith("t_") else pltpu.VMEM) for name in outputs
        ),
        scratch_shapes=[pltpu.VMEM(*item) for item in arrays.values()]
        + [pltpu.SemaphoreType.DMA(item) for item in sems.values()],
        compiler_params=pltpu.CompilerParams(
            collective_id=1, has_side_effects=True, vmem_limit_bytes=VMEM_BYTES
        ),
    )(*inputs.values())
    r = Names(zip(outputs, results, strict=True))
    both = r.t_kv.reshape(2, width, head)
    matrices = [
        r.t_query,
        both[0],
        both[1],
        r.t_out.reshape(joined, width),
        r.t_gate,
        r.t_up,
        r.t_down.reshape(hidden, width),
    ]
    sums = widen(matrices, r.t_gain, (width, width, width, width, head, head))
    g_query, g_key, g_value, g_out, g_gate, g_up, g_down, g_in, g_attn, g_pre, g_post, g_qgain, g_kgain = sums
    return (
        r.out[None],
        r.dx[None],
        g_in,
        g_query,
        g_key,
        g_value,
        g_qgain,
        g_kgain,
        g_out,
        g_attn,
        g_pre,
        g_gate,
        g_up,
        g_down,
        g_post,
    )


def per_device(
    tokens,
    lengths,
    cotangent,
    norm_in,
    w_query,
    w_key,
    w_value,
    query_gain,
    key_gain,
    w_out,
    norm_attn,
    norm_pre,
    w_gate,
    w_up,
    w_down,
    norm_post,
):
    rows = tokens.shape[1]
    head = query_gain.shape[0]
    heads = w_query.shape[1] // head
    sizes = (rows, tokens.shape[2], w_gate.shape[1], heads, head, lax.axis_size("blk") // 2)
    if sizes[-1] in SCHEDULES and layer_bytes(sizes) <= VMEM_BYTES:
        return whole_layer(
            sizes,
            tokens,
            lengths,
            cotangent,
            norm_in,
            w_query,
            w_key,
            w_value,
            query_gain,
            key_gain,
            w_out,
            norm_attn,
            norm_pre,
            w_gate,
            w_up,
            w_down,
            norm_post,
        )
    scale = head ** (-0.5)
    count = lax.axis_size("blk")
    place = lax.axis_index("blk")
    row = lengths[0]
    local_idx = place * rows + jnp.arange(rows, dtype=jnp.int32)
    seg_q, pos_q = segment_of(local_idx, row)
    cosine, sine = rotary_tables(pos_q, head)

    def block_mask(source):
        key_idx = source * rows + jnp.arange(rows, dtype=jnp.int32)
        seg_k, unused = segment_of(key_idx, row)
        return (seg_q[:, None] == seg_k[None, :]) & (local_idx[:, None] >= key_idx[None, :])

    x_in = tokens[0].astype(jnp.float32)
    normal_a = normed(x_in, norm_in).astype(jnp.bfloat16)
    q_proj = jnp.dot(normal_a, w_query, preferred_element_type=jnp.float32).reshape(
        rows, heads, head
    )
    k_proj = jnp.dot(normal_a, w_key, preferred_element_type=jnp.float32)
    v_proj = jnp.dot(normal_a, w_value, preferred_element_type=jnp.float32)
    query = prepare(q_proj, query_gain, cosine[:, None, :], sine[:, None, :]).astype(jnp.bfloat16)
    keys = prepare(k_proj, key_gain, cosine, sine).astype(jnp.bfloat16)
    values = v_proj.astype(jnp.bfloat16)
    q_heads = jnp.transpose(query, (1, 0, 2))

    def absorb(state, pair, source):
        allowed = block_mask(source)
        big, total, accum = state
        raw = jnp.einsum("hqd,kd->hqk", q_heads, pair[0], preferred_element_type=jnp.float32)
        scores = jnp.where(allowed[None], scale * raw, NEG)
        big_new = jnp.maximum(big, jnp.max(scores, axis=-1, keepdims=True))
        expo = jnp.where(allowed[None], jnp.exp(scores - big_new), 0.0)
        fade = jnp.exp(big - big_new)
        total = total * fade + jnp.sum(expo, axis=-1, keepdims=True)
        accum = accum * fade + jnp.einsum(
            "hqk,kd->hqd", expo.astype(jnp.bfloat16), pair[1], preferred_element_type=jnp.float32
        )
        return (big_new, total, accum)

    pair = jnp.stack([keys, values])
    state = (
        jnp.full((heads, rows, 1), NEG, jnp.float32),
        jnp.zeros((heads, rows, 1), jnp.float32),
        jnp.zeros((heads, rows, head), jnp.float32),
    )
    state = absorb(state, pair, place)

    def cycle_forward(step, carry):
        inner, moving = carry
        moving = from_behind(moving, "blk", 1)
        return (absorb(inner, moving, (place - step) % count), moving)

    state, unused_pair = lax.fori_loop(1, count, cycle_forward, (state, pair))
    big, total, accum = state
    attended = accum / total
    lse = big + jnp.log(total)
    joined = jnp.transpose(attended, (1, 0, 2)).reshape(rows, heads * head).astype(jnp.bfloat16)
    a_proj = jnp.dot(joined, w_out, preferred_element_type=jnp.float32)
    x_mid = x_in + normed(a_proj, norm_attn)
    mixed = normed(x_mid, norm_pre).astype(jnp.bfloat16)
    gate = jnp.dot(mixed, w_gate, preferred_element_type=jnp.float32)
    upper = jnp.dot(mixed, w_up, preferred_element_type=jnp.float32)

    def activate(gate_in, upper_in):
        return jax.nn.gelu(gate_in, approximate=True) * upper_in

    hidden = activate(gate, upper).astype(jnp.bfloat16)
    f_proj = jnp.dot(hidden, w_down, preferred_element_type=jnp.float32)
    output = x_mid + normed(f_proj, norm_post)
    grad_y = cotangent[0].astype(jnp.float32)
    d_fproj, g_post = normed_back(f_proj, norm_post, grad_y)
    d_fproj = d_fproj.astype(jnp.bfloat16)
    g_down = jnp.einsum("tf,td->fd", hidden, d_fproj, preferred_element_type=jnp.float32)
    d_hidden = jnp.einsum("td,fd->tf", d_fproj, w_down, preferred_element_type=jnp.float32)
    d_gate, d_upper = jax.vjp(activate, gate, upper)[1](d_hidden)
    d_gate = d_gate.astype(jnp.bfloat16)
    d_upper = d_upper.astype(jnp.bfloat16)
    g_gate = jnp.einsum("td,tf->df", mixed, d_gate, preferred_element_type=jnp.float32)
    g_up = jnp.einsum("td,tf->df", mixed, d_upper, preferred_element_type=jnp.float32)
    d_mixed = jnp.einsum(
        "tf,df->td", d_gate, w_gate, preferred_element_type=jnp.float32
    ) + jnp.einsum("tf,df->td", d_upper, w_up, preferred_element_type=jnp.float32)
    d_mid, g_pre = normed_back(x_mid, norm_pre, d_mixed)
    d_mid = grad_y + d_mid
    d_aproj, g_attn = normed_back(a_proj, norm_attn, d_mid)
    d_aproj = d_aproj.astype(jnp.bfloat16)
    g_out = jnp.einsum("tn,td->nd", joined, d_aproj, preferred_element_type=jnp.float32)
    d_joined = jnp.einsum("td,nd->tn", d_aproj, w_out, preferred_element_type=jnp.float32).astype(
        jnp.bfloat16
    )
    do_heads = jnp.transpose(d_joined.reshape(rows, heads, head), (1, 0, 2))
    delta = jnp.sum(do_heads.astype(jnp.float32) * attended, axis=-1, keepdims=True)

    def visit(d_query, moving, grads, source):
        allowed = block_mask(source)
        raw = jnp.einsum("hqd,kd->hqk", q_heads, moving[0], preferred_element_type=jnp.float32)
        probs = jnp.where(allowed[None], jnp.exp(scale * raw - lse), 0.0)
        dv_add = jnp.einsum(
            "hqk,hqd->kd", probs.astype(jnp.bfloat16), do_heads, preferred_element_type=jnp.float32
        )
        d_probs = jnp.einsum("hqd,kd->hqk", do_heads, moving[1], preferred_element_type=jnp.float32)
        d_scores = (scale * probs * (d_probs - delta)).astype(jnp.bfloat16)
        dq_add = jnp.einsum("hqk,kd->hqd", d_scores, moving[0], preferred_element_type=jnp.float32)
        dk_add = jnp.einsum("hqk,hqd->kd", d_scores, q_heads, preferred_element_type=jnp.float32)
        return (d_query + dq_add, grads + jnp.stack([dk_add, dv_add]))

    d_query = jnp.zeros((heads, rows, head), jnp.float32)
    grads = jnp.zeros((2, rows, head), jnp.float32)
    d_query, grads = visit(d_query, pair, grads, place)

    def cycle_backward(step, carry):
        dq_in, moving, grads_in = carry
        moving = from_behind(moving, "blk", 1)
        grads_in = pass_home(grads_in)
        dq_in, grads_in = visit(dq_in, moving, grads_in, (place - step) % count)
        return (dq_in, moving, grads_in)

    d_query, unused_pair, grads = lax.fori_loop(1, count, cycle_backward, (d_query, pair, grads))
    grads = pass_home(grads)

    def query_piece(proj, gain):
        return prepare(proj, gain, cosine[:, None, :], sine[:, None, :])

    def key_piece(proj, gain):
        return prepare(proj, gain, cosine, sine)

    d_qproj, g_qgain = jax.vjp(query_piece, q_proj, query_gain)[1](
        jnp.transpose(d_query, (1, 0, 2))
    )
    d_kproj, g_kgain = jax.vjp(key_piece, k_proj, key_gain)[1](grads[0])
    d_qproj = d_qproj.reshape(rows, heads * head).astype(jnp.bfloat16)
    d_kproj = d_kproj.astype(jnp.bfloat16)
    d_vproj = grads[1].astype(jnp.bfloat16)
    g_query = jnp.einsum("td,tn->dn", normal_a, d_qproj, preferred_element_type=jnp.float32)
    g_key = jnp.einsum("td,tn->dn", normal_a, d_kproj, preferred_element_type=jnp.float32)
    g_value = jnp.einsum("td,tn->dn", normal_a, d_vproj, preferred_element_type=jnp.float32)
    d_normal = jnp.einsum("tn,dn->td", d_qproj, w_query, preferred_element_type=jnp.float32)
    d_normal = d_normal + jnp.einsum(
        "tn,dn->td", d_kproj, w_key, preferred_element_type=jnp.float32
    )
    d_normal = d_normal + jnp.einsum(
        "tn,dn->td", d_vproj, w_value, preferred_element_type=jnp.float32
    )
    d_input, g_in = normed_back(x_in, norm_in, d_normal)
    input_grad = (d_mid + d_input).astype(jnp.bfloat16)
    (
        g_in,
        g_query,
        g_key,
        g_value,
        g_qgain,
        g_kgain,
        g_out,
        g_attn,
        g_pre,
        g_gate,
        g_up,
        g_down,
        g_post,
    ) = sum_gradients(
        (
            g_in,
            g_query,
            g_key,
            g_value,
            g_qgain,
            g_kgain,
            g_out,
            g_attn,
            g_pre,
            g_gate,
            g_up,
            g_down,
            g_post,
        )
    )
    return (
        output.astype(jnp.bfloat16)[None],
        input_grad[None],
        g_in,
        g_query,
        g_key,
        g_value,
        g_qgain,
        g_kgain,
        g_out,
        g_attn,
        g_pre,
        g_gate,
        g_up,
        g_down,
        g_post,
    )


def solution(mesh):
    in_specs = (
        P("dp", "blk", None),
        P("dp", None),
        P("dp", "blk", None),
        P(),
        P(),
        P(),
        P(),
        P(),
        P(),
        P(),
        P(),
        P(),
        P(),
        P(),
        P(),
        P(),
    )
    out_specs = (
        P("dp", "blk", None),
        P("dp", "blk", None),
        P(),
        P(),
        P(),
        P(),
        P(),
        P(),
        P(),
        P(),
        P(),
        P(),
        P(),
        P(),
        P(),
    )
    return jax.shard_map(
        per_device, mesh=mesh, in_specs=in_specs, out_specs=out_specs, check_vma=False
    )
```

```python
import functools

import jax
import jax.numpy as jnp
from jax import lax
from jax.experimental import pallas as pl
from jax.experimental.pallas import tpu as pltpu
from jax.sharding import PartitionSpec as P

BLOCKS, PARTS = "blk", "dp"
EPS = 1e-06
BASE = 1000000.0
NEG = -1e30


def shifted(array, axis, by):
    peers = lax.axis_size(axis)
    return lax.ppermute(array, axis, [(i, (i + by) % peers) for i in range(peers)])


def from_behind(block, axis, distance):
    devices = range(lax.axis_size(axis))
    route = [(i - distance, i) for i in devices if i - distance in devices]
    return lax.ppermute(block, axis, route)


def normed(value, gain):
    return value * lax.rsqrt(jnp.mean(value * value, axis=-1, keepdims=True) + EPS) * gain


def normed_back(value, gain, grad):
    return jax.vjp(normed, value, gain)[1](grad)


def segment_of(index, row):
    ends = jnp.cumsum(row)
    seg = jnp.sum((index[:, None] >= ends[None, :]).astype(jnp.int32), axis=1)
    starts = ends - row
    slots = jnp.arange(row.shape[0], dtype=jnp.int32)
    begin = jnp.sum(jnp.where(slots[None, :] == seg[:, None], starts[None, :], 0), axis=1)
    return (seg, index - begin)


def rotary_tables(places, head):
    half = head // 2
    freq = jnp.exp(-(2.0 * jnp.arange(half, dtype=jnp.float32) / head) * jnp.log(BASE))
    angle = places.astype(jnp.float32)[:, None] * freq[None, :]
    return (jnp.cos(angle), jnp.sin(angle))


def prepare(proj, gain, cosine, sine):
    value = normed(proj, gain)
    half = value.shape[-1] // 2
    first = value[..., :half]
    second = value[..., half:]
    return jnp.concatenate(
        [first * cosine - second * sine, second * cosine + first * sine], axis=-1
    )


def pass_home(grads):
    return shifted(grads.astype(jnp.bfloat16), BLOCKS, 1).astype(grads.dtype)


MESH = pl.DeviceIdType.MESH


def where_am_i():
    place = lax.axis_index(BLOCKS)
    part = lax.axis_index(PARTS)
    return {
        "z": place // 2,
        "y": lax.rem(place, 2),
        "x": part // 2,
        "core": lax.rem(part, 2),
        "place": place,
        "part": part,
    }


def peers_of(me):
    place, part = me["place"], me["part"]
    return {
        "core": {BLOCKS: place, PARTS: part + 1 - 2 * me["core"]},
        "x": {BLOCKS: place, PARTS: part + 2 - 4 * me["x"]},
        "y": {BLOCKS: place + 1 - 2 * me["y"], PARTS: part},
        "up": {BLOCKS: place + 2, PARTS: part},
        "down": {BLOCKS: place - 2, PARTS: part},
    }


def greet(me, peers, z_count):
    barrier = pltpu.get_barrier_semaphore()
    for name in ("core", "x", "y"):
        pl.semaphore_signal(barrier, inc=1, device_id=peers[name], device_id_type=MESH)

    @pl.when(me["z"] < z_count - 1)
    def _():
        pl.semaphore_signal(barrier, inc=1, device_id=peers["up"], device_id_type=MESH)

    @pl.when(me["z"] > 0)
    def _():
        pl.semaphore_signal(barrier, inc=1, device_id=peers["down"], device_id_type=MESH)

    ends = (me["z"] == 0).astype(jnp.int32) + (me["z"] == z_count - 1).astype(jnp.int32)
    pl.semaphore_wait(barrier, 5 - ends)


def add_into(target, start, row, extra, count, rows):
    step = rows if rows < 32 else 16
    for candidate in (160, 128, 80, 64, 48, 32):
        if rows % candidate == 0:
            step = candidate
            break

    def body(index, carry):
        e = index // (rows // step)
        at = pl.multiple_of(lax.rem(index, rows // step) * step, 8)
        here = pl.ds(pl.multiple_of(row + at, 8), step)
        target[start + e, here, :] = target[start + e, here, :] + extra[e, pl.ds(at, step), :]
        return carry

    lax.fori_loop(0, count * (rows // step), body, 0)


STAGES = 10


class Chunk:
    def __init__(self, number, grad, total, row, rows, first, landing, sems, me, peers, z_count):
        self.grad, self.total, self.row, self.rows = grad, total, row, rows
        self.first, self.second = ("x", "y") if first == "x" else ("y", "x")
        self.land0, self.land1, self.land2 = landing
        self.send, self.recv, self.local = sems
        self.number, self.me, self.peers, self.z_count = number, me, peers, z_count
        self.b1, self.b2, self.core = me[self.first], me[self.second], me["core"]
        self.quad = 4 * self.core
        self.pair = self.quad + 2 * self.b1
        self.own = self.pair + self.b2
        self.half = rows // 2

    @staticmethod
    def landing(rows):
        return ((4, rows), (2, rows), (1, 2 * rows))

    def piece(self, start, count, upper=None):
        if upper is None:
            return self.grad.at[pl.ds(start, count), pl.ds(self.row, self.rows), :]
        row = self.row if upper else self.row + self.half
        return self.grad.at[pl.ds(start, count), pl.ds(row, self.half), :]

    def spot(self, count, upper=None):
        row, rows = self.row, self.rows
        if upper is not None:
            row, rows = (row if upper else row + self.half), self.half
        here, columns = pl.ds(row, rows), self.grad.shape[2]
        start = {1: self.own, 2: self.pair, 4: self.quad}[count]
        if len(self.total.shape) == 2:
            return self.total.at[here, pl.ds(pl.multiple_of(start * columns, 128), count * columns)]
        if len(self.total.shape) == 4:
            if count == 4:
                return self.total.at[self.core, :, here, :]
            if count == 2:
                return self.total.at[self.core, self.b1, here, :]
            return self.total.at[self.core, self.b1, here, pl.ds(pl.multiple_of(self.b2 * columns, 128), columns)]
        if count == 1:
            return self.total.at[start, here, :]
        return self.total.at[pl.ds(start, count), here, :]

    def mine(self, upper):
        return self.grad.at[self.own, pl.ds(self.row if upper else self.row + self.half, self.half), :]

    def keep(self, upper):
        return pltpu.make_async_copy(
            self.mine(upper), self.spot(1, upper), self.local.at[self.number]
        )

    def copy(self, stage, peer, source, target):
        return pltpu.make_async_remote_copy(
            src_ref=source,
            dst_ref=target,
            send_sem=self.send.at[self.number, stage],
            recv_sem=self.recv.at[self.number, stage],
            device_id=self.peers[peer],
            device_id_type=MESH,
        )

    def reduce_up(self):
        return self.copy(3, "up", self.piece(self.own, 1, True), self.land2.at[:, pl.ds(self.rows, self.half), :])

    def reduce_down(self):
        return self.copy(4, "down", self.piece(self.own, 1, False), self.land2.at[:, pl.ds(self.rows + self.half, self.half), :])

    def spread_down(self, fresh=False):
        here = self.spot(1, True)
        return self.copy(5, "down", self.mine(True) if fresh else here, here)

    def spread_up(self, fresh=False):
        here = self.spot(1, False)
        return self.copy(6, "up", self.mine(False) if fresh else here, here)

    def step0(self):
        return self.copy(0, "core", self.piece(4 - self.quad, 4), self.land0)

    def step1(self):
        return self.copy(1, self.first, self.piece(self.quad + 2 - 2 * self.b1, 2), self.land1)

    def step2(self):
        return self.copy(2, self.second, self.piece(self.pair + 1 - self.b2, 1), self.land2.at[:, pl.ds(0, self.rows), :])

    def gather(self, stage):
        count, peer = ((1, self.second), (2, self.first), (4, "core"))[stage - 7]
        here = self.spot(count)
        return self.copy(stage, peer, here, here)

    def arrive_upper(self):
        z, last = self.me["z"], self.z_count - 1

        @pl.when(z > 0)
        def _():
            self.reduce_up().wait_recv()
            add_into(self.grad, self.own, self.row, self.land2.at[:, pl.ds(self.rows, self.half), :], 1, self.half)

            @pl.when(z < last)
            def _():
                self.reduce_up().start()

            @pl.when(z == last)
            def _():
                self.spread_down(True).start()
                self.keep(True).start()

    def arrive_lower(self):
        z, last = self.me["z"], self.z_count - 1

        @pl.when(z < last)
        def _():
            self.reduce_down().wait_recv()
            add_into(self.grad, self.own, self.row + self.half, self.land2.at[:, pl.ds(self.rows + self.half, self.half), :], 1, self.half)

            @pl.when(z > 0)
            def _():
                self.reduce_down().start()

            @pl.when(z == 0)
            def _():
                self.spread_up(True).start()
                self.keep(False).start()

    def back_upper(self):
        z, last = self.me["z"], self.z_count - 1

        @pl.when(z < last)
        def _():
            self.spread_down().wait_recv()

            @pl.when(z > 0)
            def _():
                self.spread_down().start()

    def back_lower(self):
        z, last = self.me["z"], self.z_count - 1

        @pl.when(z > 0)
        def _():
            self.spread_up().wait_recv()

            @pl.when(z < last)
            def _():
                self.spread_up().start()

    def tick(self, op):
        z, last = self.me["z"], self.z_count - 1
        if op == 0:
            self.step0().start()
        elif op == 1:
            self.step0().wait_recv()
            add_into(self.grad, self.quad, self.row, self.land0, 4, self.rows)
            self.step1().start()
        elif op == 2:
            self.step1().wait_recv()
            add_into(self.grad, self.pair, self.row, self.land1, 2, self.rows)
            self.step2().start()
        elif op == 3:
            self.step2().wait_recv()
            add_into(self.grad, self.own, self.row, self.land2, 1, self.rows)

            @pl.when(z == 0)
            def _():
                self.reduce_up().start()

            @pl.when(z == last)
            def _():
                self.reduce_down().start()

        elif op == 4:
            pl.when((z > 0) & (2 * z < self.z_count))(self.arrive_upper)
            pl.when((z < last) & (2 * z >= self.z_count))(self.arrive_lower)
        elif op == 5:
            pl.when((z < last) & (2 * z >= self.z_count))(self.arrive_upper)
            pl.when((z > 0) & (2 * z < self.z_count))(self.arrive_lower)
        elif op == 6:
            pl.when(z == last)(self.arrive_upper)
            pl.when(z == 0)(self.arrive_lower)
        elif op == 7:
            pl.when((z < last) & (2 * z >= self.z_count))(self.back_upper)
            pl.when((z > 0) & (2 * z < self.z_count))(self.back_lower)
        elif op == 8:

            @pl.when((z > 0) & (2 * z < self.z_count))
            def _():
                self.back_upper()
                self.gather(7).start()

            @pl.when((z < last) & (2 * z >= self.z_count))
            def _():
                self.back_lower()
                self.gather(7).start()

        elif op == 9:

            @pl.when(z == 0)
            def _():
                self.back_upper()
                self.keep(False).wait()
                self.gather(7).start()

            @pl.when(z == last)
            def _():
                self.back_lower()
                self.keep(True).wait()
                self.gather(7).start()

        elif op == 10:
            self.gather(7).wait_recv()
            self.gather(8).start()
        elif op == 11:
            self.gather(8).wait_recv()
            self.gather(9).start()
        elif op == 12:
            self.gather(9).wait_recv()
            self.drain()

    OPS = 13

    def drain(self):
        z, last = self.me["z"], self.z_count - 1
        self.step0().wait_send()
        self.step1().wait_send()
        self.step2().wait_send()
        for stage in (7, 8, 9):
            self.gather(stage).wait_send()

        @pl.when(z < last)
        def _():
            self.reduce_up().wait_send()
            self.spread_up().wait_send()

        @pl.when(z > 0)
        def _():
            self.reduce_down().wait_send()
            self.spread_down().wait_send()


class LineChunk(Chunk):
    def __init__(self, *args):
        super().__init__(*args[:6], (args[6][0], None, None), *args[7:])
        self.ups, self.downs, self.small = args[6][1:]
        self.entry = self.quad + self.me["z"]
        self.half, self.quarter = self.rows // 2, self.rows // 4
        self.mine_half = pl.multiple_of(self.row + self.b1 * self.half, 16)
        self.mine_quarter = pl.multiple_of(self.mine_half + self.b2 * self.quarter, 16)

    @staticmethod
    def landing(rows):
        return ((4, rows), (3, rows), (3, rows), (1, rows))

    def across(self, stage, name, first, count):
        landing = self.ups if name == "up" else self.downs
        return self.copy(stage, name, self.piece(self.quad + first, count), landing.at[pl.ds(0, count)])

    def back(self, stage, name, first, count):
        here = self.place(self.quad + first, count, self.row, self.rows)
        return self.copy(stage, name, here, here)

    def place(self, start, count, row, rows):
        here, columns = pl.ds(row, rows), self.grad.shape[2]
        if len(self.total.shape) == 2:
            return self.total.at[here, pl.ds(pl.multiple_of(start * columns, 128), count * columns)]
        if count == 1:
            return self.total.at[start, here, :]
        return self.total.at[pl.ds(start, count), here, :]

    def part(self, row, rows):
        return self.grad.at[pl.ds(self.entry, 1), pl.ds(row, rows), :]

    def step1(self):
        other = pl.multiple_of(self.row + (1 - self.b1) * self.half, 16)
        return self.copy(1, self.first, self.part(other, self.half), self.small.at[:, pl.ds(0, self.half), :])

    def step2(self):
        other = pl.multiple_of(self.mine_half + (1 - self.b2) * self.quarter, 16)
        landing = self.small.at[:, pl.ds(self.half, self.quarter), :]
        return self.copy(2, self.second, self.part(other, self.quarter), landing)

    def finished(self):
        return self.grad.at[self.entry, pl.ds(self.mine_quarter, self.quarter), :]

    def keep(self):
        spot = self.place(self.entry, 1, self.mine_quarter, self.quarter)
        return pltpu.make_async_copy(self.finished(), spot, self.local.at[self.number])

    def gather2(self):
        spot = self.place(self.entry, 1, self.mine_quarter, self.quarter)
        return self.copy(7, self.second, self.finished(), spot)

    def gather1(self):
        here = self.place(self.entry, 1, self.mine_half, self.half)
        return self.copy(8, self.first, here, here)

    def gather0(self):
        here = self.place(self.quad, 4, self.row, self.rows)
        return self.copy(9, "core", here, here)

    def at_row(self, k, body):
        pl.when(self.me["z"] == k)(body)

    def from_below(self, k):
        return (k, self.z_count - k)

    def from_above(self, k):
        return (0, k + 1)

    def take_up(self, k):
        first, count = self.from_below(k)
        self.across(3, "up", first, count).wait_recv()
        add_into(self.grad, self.quad + first, self.row, self.ups, count, self.rows)
        if k < self.z_count - 1:
            self.across(3, "up", first + 1, count - 1).start()

    def take_down(self, k):
        first, count = self.from_above(k)
        self.across(4, "down", first, count).wait_recv()
        add_into(self.grad, self.quad + first, self.row, self.downs, count, self.rows)
        if k > 0:
            self.across(4, "down", first, count - 1).start()

    def back_up(self, k):
        self.back(6, "up", 0, k).wait_recv()
        if k < self.z_count - 1:
            self.back(6, "up", 0, k + 1).start()

    def back_down(self, k):
        last = self.z_count - 1
        self.back(5, "down", k + 1, last - k).wait_recv()
        if k > 0:
            self.back(5, "down", k, last - k + 1).start()

    def tick(self, op):
        last, middle = self.z_count - 1, self.z_count // 2
        if op == 0:
            self.step0().start()
        elif op == 1:
            self.step0().wait_recv()
            add_into(self.grad, self.quad, self.row, self.land0, 4, self.rows)
            self.at_row(0, lambda: self.across(3, "up", 1, last).start())
            self.at_row(last, lambda: self.across(4, "down", 0, last).start())
        elif op == 2:
            for k in range(1, last):
                self.at_row(k, functools.partial(self.take_up if k < middle else self.take_down, k))
        elif op == 3:
            for k in range(1, last):

                def arrive(k=k):
                    (self.take_down if k < middle else self.take_up)(k)
                    self.step1().start()

                self.at_row(k, arrive)
        elif op == 4:

            def bottom():
                self.take_down(0)
                self.step1().start()

            def top():
                self.take_up(last)
                self.step1().start()

            self.at_row(0, bottom)
            self.at_row(last, top)
        elif op == 5:
            self.step1().wait_recv()
            add_into(self.grad, self.entry, self.mine_half, self.small, 1, self.half)
            self.step2().start()
        elif op == 6:
            self.step2().wait_recv()
            landing = self.small.at[:, pl.ds(self.half, self.quarter), :]
            add_into(self.grad, self.entry, self.mine_quarter, landing, 1, self.quarter)
            self.keep().start()
            self.gather2().start()
        elif op == 7:
            self.gather2().wait_recv()
            self.keep().wait()
            self.gather1().start()
        elif op == 8:
            self.gather1().wait_recv()
            self.at_row(0, lambda: self.back(6, "up", 0, 1).start())
            self.at_row(last, lambda: self.back(5, "down", last, 1).start())
        elif op == 9:
            for k in range(1, last):
                self.at_row(k, functools.partial(self.back_up if k < middle else self.back_down, k))
        elif op == 10:
            for k in range(1, last):

                def complete(k=k):
                    (self.back_down if k < middle else self.back_up)(k)
                    self.gather0().start()

                self.at_row(k, complete)
        elif op == 11:

            def bottom():
                self.back_down(0)
                self.gather0().start()

            def top():
                self.back_up(last)
                self.gather0().start()

            self.at_row(0, bottom)
            self.at_row(last, top)
        elif op == 12:
            self.gather0().wait_recv()
            self.drain()

    def drain(self):
        last = self.z_count - 1
        for item in (self.step0(), self.step1(), self.step2(), self.gather2(), self.gather1(), self.gather0()):
            item.wait_send()
        for k in range(self.z_count):

            def sent(k=k):
                if k < last:
                    self.across(3, "up", k + 1, last - k).wait_send()
                    self.back(6, "up", 0, k + 1).wait_send()
                if k > 0:
                    self.across(4, "down", 0, k).wait_send()
                    self.back(5, "down", k, last - k + 1).wait_send()

            self.at_row(k, sent)


def sum_kernel(z_count, plan, *refs):
    n = 1 + max(item[0] for item in plan)
    parts = len(plan)
    ins, outs = refs[:n], refs[n : 2 * n]
    rest = refs[2 * n :]
    grads, rest = rest[:n], rest[n:]
    landings = rest[: 3 * parts]
    send, recv, local, load = rest[3 * parts :]
    me = where_am_i()
    peers = peers_of(me)
    loads = [pltpu.make_async_copy(ins[i], grads[i], load.at[i]) for i in range(n)]
    for item in loads:
        item.start()
    greet(me, peers, z_count)
    for item in loads:
        item.wait()
    chunks = []
    for number, (i, row, rows, first) in enumerate(plan):
        landing = landings[3 * number : 3 * number + 3]
        chunks.append(
            Chunk(number, grads[i], outs[i], row, rows, first, landing, (send, recv, local), me, peers, z_count)
        )
    for at in range(parts + Chunk.OPS - 1):
        for number in range(parts):
            if 0 <= at - number < Chunk.OPS:
                chunks[number].tick(at - number)


def sum_call(arrays, plan, z_count):
    landing = []
    for i, row, rows, first in plan:
        columns, kind = arrays[i].shape[2], arrays[i].dtype
        landing += [
            pltpu.VMEM((4, rows, columns), kind),
            pltpu.VMEM((2, rows, columns), kind),
            pltpu.VMEM((1, 2 * rows, columns), kind),
        ]
    n = len(arrays)
    return pl.pallas_call(
        functools.partial(sum_kernel, z_count, plan),
        out_shape=tuple(jax.ShapeDtypeStruct(v.shape, v.dtype) for v in arrays),
        in_specs=[pl.BlockSpec(memory_space=pl.ANY)] * n,
        out_specs=tuple([pl.BlockSpec(memory_space=pl.ANY)] * n),
        scratch_shapes=[pltpu.VMEM(v.shape, v.dtype) for v in arrays]
        + landing
        + [
            pltpu.SemaphoreType.DMA((len(plan), STAGES)),
            pltpu.SemaphoreType.DMA((len(plan), STAGES)),
            pltpu.SemaphoreType.DMA((len(plan),)),
            pltpu.SemaphoreType.DMA((n,)),
        ],
        compiler_params=pltpu.CompilerParams(
            collective_id=0, has_side_effects=True, vmem_limit_bytes=56 * 2**20
        ),
    )(*arrays)


def columns_to_panels(value):
    rows, columns = value.shape
    return jnp.transpose(value.reshape(rows, 8, columns // 8), (1, 0, 2)).astype(jnp.bfloat16)


def panels_to_columns(panels):
    count, rows, width = panels.shape
    return jnp.transpose(panels.astype(jnp.float32), (1, 0, 2)).reshape(rows, count * width)


def sum_gradients(grads):
    (g_in, g_query, g_key, g_value, g_qgain, g_kgain, g_out, g_attn, g_pre, g_gate, g_up, g_down, g_post) = grads
    z_count = lax.axis_size(BLOCKS) // 2
    width = g_in.shape[0]
    gains = [g_in, g_attn, g_pre, g_post, g_qgain, g_kgain]
    sizes = [v.shape[0] for v in gains]
    flat = jnp.concatenate(gains)
    gain_rows = 32
    flat = jnp.pad(flat, (0, 8 * gain_rows * 128 - flat.shape[0])).reshape(8, gain_rows, 128)
    down = g_down.astype(jnp.bfloat16).reshape(8, -1, width)
    out = g_out.astype(jnp.bfloat16).reshape(8, -1, width)
    both = jnp.stack([g_key, g_value])
    head = g_key.shape[1]
    both = jnp.transpose(both.reshape(2, 2, width // 2, 2, head // 2), (0, 1, 3, 2, 4)).reshape(8, width // 2, head // 2)
    arrays = [down, columns_to_panels(g_gate), columns_to_panels(g_up), out, columns_to_panels(g_query), both.astype(jnp.bfloat16), flat]
    plan = []
    for i, v in enumerate(arrays[:-1]):
        rows = v.shape[1] // 2
        plan += [(i, 0, rows, "x"), (i, rows, rows, "y")]
    plan.append((6, 0, gain_rows, "x"))
    down, gate, up, out, query, both, flat = sum_call(arrays, plan, z_count)
    both = jnp.transpose(both.astype(jnp.float32).reshape(2, 2, 2, width // 2, head // 2), (0, 1, 3, 2, 4)).reshape(2, width, head)
    flat = flat.reshape(-1)
    cuts, at = [], 0
    for size in sizes:
        cuts.append(flat[at : at + size])
        at += size
    g_in, g_attn, g_pre, g_post, g_qgain, g_kgain = cuts
    return (
        g_in,
        panels_to_columns(query),
        both[0],
        both[1],
        g_qgain,
        g_kgain,
        out.astype(jnp.float32).reshape(g_out.shape),
        g_attn,
        g_pre,
        panels_to_columns(gate),
        panels_to_columns(up),
        down.astype(jnp.float32).reshape(g_down.shape),
        g_post,
    )


LOG2E = 1.4426950408889634
LN2 = 0.6931471805599453
PIECES = (2, 2, 2, 2, 2, 2, 1)
FIRST = ['y', 'x', 'x', 'u', 'x', 'y', 'y', 'x', 'x', 'x', 'x', 'y', 'x']
SCHEDULES = {
    4: (
        (1, 0), ("S", 0), (0, 0), ("F", 0), (3, 0), (1, 1), ("F", 1), (0, 1), ("M", 0), ("O", 0), (1, 2), (3, 1), (2, 0), (6, 0), ("X", 0), (0, 2),
        (4, 0), ("W", 0), (7, 0), (3, 2), (1, 3), ("X", 1), (0, 3), (7, 1), (4, 1), (1, 4), (6, 1), ("W", 1), (0, 4), (1, 5), (5, 0), (3, 3),
        ("P", 0), ("X", 2), (2, 1), ("W", 2), ("P", 1), (4, 2), ("X", 3), (5, 1), ("W", 3), (1, 6), ("Q", 0), ("P", 2), (6, 2), ("Q", 1), ("Q", 2),
        ("Q", 3), (4, 3), (1, 7), ("G", 0), (8, 0), (4, 4), (9, 0), (7, 2), (3, 4), ("T", 0), (0, 5), (2, 2), (8, 1), (9, 1), (4, 5), (1, 8),
        ("K", 0), (0, 6), (11, 0), (12, 0), (7, 3), (5, 2), (10, 0), (4, 6), (0, 7), (11, 1), (8, 2), (7, 4), (6, 3), (10, 1), (2, 3), (4, 7),
        (12, 1), (9, 2), (11, 2), (1, 9), (0, 8), (5, 3), (7, 5), (2, 4), (3, 5), (10, 2), (8, 3), (11, 3), (0, 9), (12, 2), (9, 3), (4, 8), (5, 4),
        (7, 6), (1, 10), (3, 6), (11, 4), (2, 5), (9, 4), (10, 3), (11, 5), (4, 9), (5, 5), (7, 7), (12, 3), (10, 4), (2, 6), (8, 4), (3, 7), (11, 6),
        (6, 4), (0, 10), (9, 5), (7, 8), (12, 4), (10, 5), (2, 7), (5, 6), (8, 5), (4, 10), (11, 7), (9, 6), (10, 6), (8, 6), (3, 8), (6, 5), (2, 8),
        (5, 7), (7, 9), (10, 7), (9, 7), (6, 6), (1, 11), (11, 8), (0, 11), (2, 9), (8, 7), (11, 9), (5, 8), (7, 10), (12, 5), (10, 8), (8, 8),
        (4, 11), (10, 9), (8, 9), (6, 7), (9, 8), (5, 9), (3, 9), (11, 10), (9, 9), (12, 6), (6, 8), (12, 7), (10, 10), (7, 11), (6, 9), (5, 10),
        (8, 10), (12, 8), (3, 10), (2, 10), (10, 11), (6, 10), (8, 11), (11, 11), (8, 12), (5, 11), (9, 10), (11, 12), (12, 9), (6, 11), (0, 12),
        (2, 11), (3, 11), (12, 10), (9, 11), (12, 11), (7, 12), (1, 12), (9, 12), (5, 12), (4, 12), (2, 12), (12, 12), (3, 12), (10, 12), (6, 12),
    )
}


def dot(left, right):
    return jnp.dot(left, right, preferred_element_type=jnp.float32)


def dot_nt(left, right):
    return lax.dot_general(left, right, (((1,), (1,)), ((), ())), preferred_element_type=jnp.float32)


def inverse_rms(value):
    return lax.rsqrt(jnp.mean(value * value, axis=-1, keepdims=True) + EPS)


def rms_back(value, inverse, gain, grad):
    scaled = grad * gain
    normal = value * inverse
    mean = jnp.mean(scaled * normal, axis=-1, keepdims=True)
    terms = grad * normal
    return inverse * (scaled - normal * mean), jnp.sum(terms.reshape(-1, 8, terms.shape[-1]), axis=0)


def turn(value, cosine, sine):
    half = value.shape[-1] // 2
    first, second = value[:, :half], value[:, half:]
    return jnp.concatenate([first * cosine - second * sine, second * cosine + first * sine], axis=-1)


def turn_back(grad, cosine, sine):
    half = grad.shape[-1] // 2
    first, second = grad[:, :half], grad[:, half:]
    return jnp.concatenate([first * cosine + second * sine, second * cosine - first * sine], axis=-1)


def dot_tn(left, right):
    return lax.dot_general(left, right, (((0,), (0,)), ((), ())), preferred_element_type=jnp.float32)


def bf16(value):
    return value.astype(jnp.bfloat16)


def f32(value):
    return value.astype(jnp.float32)


class Names(dict):
    __getattr__ = dict.__getitem__


def layer_kernel(sizes, schedule, names, *refs):
    r = Names(zip(names, refs, strict=True))
    rows, width, hidden, heads, head, z_count = sizes
    scale = head**-0.5
    tile = 128
    tiles = [slice(at, at + tile) for at in range(0, rows, tile)]
    half = head // 2
    me = where_am_i()
    peers = peers_of(me)
    z, y, place = me["z"], me["y"], me["place"]
    last = z_count - 1

    weights = ["x", "w_key", "w_value", "w_query", "w_out", "w_gate", "w_up", "w_down", "dy"]
    joined = heads * head
    wide_k, wide_v = slice(joined, joined + head), slice(joined + head, joined + 2 * head)
    spots = {"w_query": slice(0, joined), "w_key": wide_k, "w_value": wide_v}
    loads = {}
    for i, name in enumerate(weights):
        spot = r.w_first.at[:, spots[name]] if name in spots else r[name]
        loads[name] = pltpu.make_async_copy(r[name + "_in"], spot, r.load_sem.at[i])
    early = ("x", "w_key", "w_value")
    for name in early:
        loads[name].start()
    greet(me, peers, z_count)

    def begins(token):
        begin, end = jnp.zeros_like(token), jnp.int32(0)
        for j in range(r.lengths.shape[1]):
            end = end + r.lengths[0, j]
            begin = jnp.where(token >= end, end, begin)
        return begin

    token = place * rows + lax.broadcasted_iota(jnp.int32, (1, rows), 1)
    begin = begins(token)
    entry = f32(lax.broadcasted_iota(jnp.int32, (1, half), 1))
    speed = jnp.exp(-(2.0 * entry / head) * jnp.log(BASE))
    for t in tiles:
        column = place * rows + t.start + lax.broadcasted_iota(jnp.int32, (tile, 1), 0)
        angle = f32(column - begins(column)) * speed
        r.cosine[t, :] = jnp.cos(angle)
        r.sine[t, :] = jnp.sin(angle)
    gain_in = r.norm_in[...].reshape(1, width)
    gain_q = r.query_gain[...].reshape(1, head)
    gain_k = r.key_gain[...].reshape(1, head)
    gain_attn = r.norm_attn[...].reshape(1, width)
    gain_pre = r.norm_pre[...].reshape(1, width)
    gain_post = r.norm_post[...].reshape(1, width)

    def allowed(source):
        key = source * rows + lax.broadcasted_iota(jnp.int32, (rows, rows), 0)
        return (key >= begin) & (key <= token)

    loads["x"].wait()
    loads["w_key"].wait()
    loads["w_value"].wait()
    for name in weights:
        if name not in early:
            loads[name].start()
    for t in tiles:
        x = f32(r.x[t, :])
        r.a[t, :] = bf16(x * inverse_rms(x) * gain_in)
    r.kp[...] = dot(r.a[...], r.w_first[:, wide_k])
    r.kv[place, :, head : 2 * head] = bf16(dot(r.a[...], r.w_first[:, wide_v]))
    for t in tiles:
        kp = r.kp[t, :]
        r.kv[place, t, 0:head] = bf16(turn(kp * inverse_rms(kp) * gain_k, r.cosine[t, :], r.sine[t, :]))

    def send_kv(source, route):
        return pltpu.make_async_remote_copy(
            src_ref=r.kv.at[source],
            dst_ref=r.kv.at[source],
            send_sem=r.kv_send.at[route, source],
            recv_sem=r.kv_recv.at[source],
            device_id=peers["y"] if route else peers["up"],
            device_id_type=MESH,
        )

    def send_half(values):
        half_block = r.kv.at[0, :, head * values : head * (values + 1)]
        return pltpu.make_async_remote_copy(
            src_ref=half_block,
            dst_ref=half_block,
            send_sem=r.half_send.at[values],
            recv_sem=r.half_recv.at[values],
            device_id=peers["up"] if values else peers["y"],
            device_id_type=MESH,
        )

    pl.when(z < last)(lambda: send_kv(place, 0).start())
    pl.when(y == 0)(lambda: send_kv(place, 1).start())

    loads["w_query"].wait()
    for h in range(heads):
        wide = slice(h * head, (h + 1) * head)
        r.qp[:, wide] = dot(r.a[...], r.w_first[:, wide])
        for t in tiles:
            qp = r.qp[t, wide]
            q = turn(qp * inverse_rms(qp) * gain_q, r.cosine[t, :], r.sine[t, :])
            q = bf16(q * (scale * LOG2E))
            r.q[h * rows + t.start : h * rows + t.stop, :] = q
            r.qt[:, h * rows + t.start : h * rows + t.stop] = q.T

    columns = [slice(h * rows, (h + 1) * rows) for h in range(heads)]

    def visit(source, first):
        vt = r.kv[source, :, head : 2 * head].T
        mask = allowed(source)
        for here in columns:
            p = jnp.where(mask, jnp.exp2(dot(r.kv[source, :, 0:head], r.qt[:, here])), 0.0)
            total = jnp.sum(p, axis=0, keepdims=True)
            o = dot(vt, bf16(p))
            r.total[:, here] = total if first else r.total[:, here] + total
            r.ot[:, here] = o if first else r.ot[:, here] + o

    visit(place, True)

    @pl.when(y == 1)
    def _():
        send_kv(place - 1, 1).wait_recv()
        pl.when((z == 0) & (z < last))(lambda: send_half(1).start())
        visit(place - 1, False)

    for back in range(1, z_count + 1):
        mine = place - 2 * back

        @pl.when(back <= z)
        def _():
            send_kv(mine, 0).wait_recv()
            pl.when(z < last)(lambda: send_kv(mine, 0).start())
            pl.when(mine > 0)(lambda: send_kv(mine, 1).start())
            pl.when(mine == 0)(lambda: send_half(0).start())

        if back > 1:
            other = mine + 3 - 2 * y

            @pl.when(back - 1 <= z)
            def _():
                pl.when(other > 0)(lambda: send_kv(other, 1).wait_recv())

                @pl.when(other == 0)
                def _():
                    send_half(1).wait_recv()
                    pl.when(z < last)(lambda: send_half(1).start())
                    send_half(0).wait_recv()

                visit(other, False)

        pl.when(back <= z)(lambda: visit(mine, False))

    for h, here in enumerate(columns):
        total = r.total[:, here]
        o = r.ot[:, here] * (1.0 / total)
        r.lse[:, here] = jnp.log2(total)
        r.ot[:, here] = o
        r.ob[:, h * head : (h + 1) * head] = bf16(o).T

    loads["w_out"].wait()
    r.ap[...] = dot(r.ob[:, 0:joined], r.w_out[...])
    for t in tiles:
        ap = r.ap[t, :]
        x1 = f32(r.x[t, :]) + ap * inverse_rms(ap) * gain_attn
        r.x1[t, :] = x1
        r.m[t, :] = bf16(x1 * inverse_rms(x1) * gain_pre)
    loads["w_gate"].wait()
    loads["w_up"].wait()
    block = hidden // 8
    quarters = [slice(j * 2 * block, (j + 1) * 2 * block) for j in range(4)]
    for cols in quarters:
        gate = dot(r.m[...], r.w_gate[:, cols])
        up = dot(r.m[...], r.w_up[:, cols])
        inner = 0.7978845608028654 * (gate + 0.044715 * gate * gate * gate)
        th = jnp.tanh(inner)
        cdf = 0.5 * (1.0 + th)
        act = gate * cdf
        slope = cdf + 0.5 * gate * (1.0 - th * th) * 0.7978845608028654 * (1.0 + 3 * 0.044715 * gate * gate)
        r.hid[:, cols] = bf16(act * up)
        r.side_gate[:, cols] = bf16(slope * up)
        r.side_up[:, cols] = bf16(act)
    loads["w_down"].wait()
    loads["dy"].wait()
    r.wide[...] = dot(r.hid[...], r.w_down[...])
    r.gains[...] = jnp.zeros_like(r.gains)

    def gain(k, terms):
        r.gains[k, :, 0 : terms.shape[1]] = r.gains[k, :, 0 : terms.shape[1]] + terms

    for t in tiles:
        f = r.wide[t, :]
        inverse = inverse_rms(f)
        r.out[t, :] = bf16(r.x1[t, :] + f * inverse * gain_post)
        df, g = rms_back(f, inverse, gain_post, f32(r.dy[t, :]))
        r.df[t, :] = bf16(df)
        gain(3, g)
    for j in range(8):
        r.g_down[j] = bf16(dot_tn(r.hid[:, j * block : (j + 1) * block], r.df[...]))

    chunks = []
    sems = (r.red_send, r.red_recv, r.red_local)
    for name, count in r_plan(sizes):
        grad, total = r["g_" + name], r["t_" + name]
        step = grad.shape[1] // count
        for i in range(count):
            number, kind = len(chunks), FIRST[len(chunks)]
            make, first = (LineChunk, {"u": "x", "v": "y"}[kind]) if kind in "uv" else (Chunk, kind)
            landing = tuple(r[f"land{k}_{number}"] for k in range(len(make.landing(step))))
            chunks.append(make(number, grad, total, i * step, step, first, landing, sems, me, peers, z_count))

    def side_grads(part):
        for cols in quarters:
            dh = dot_nt(r.df[...], r.w_down[cols, :])
            r.side_gate[:, cols] = bf16(dh * f32(r.side_gate[:, cols]))
            r.side_up[:, cols] = bf16(dh * f32(r.side_up[:, cols]))

    def feed_grads(part):
        grad, side = ((r.g_gate, r.side_gate), (r.g_up, r.side_up))[part]
        for j in range(8):
            grad[j] = bf16(dot_tn(r.m[...], side[:, j * block : (j + 1) * block]))

    def middle_back(part):
        r.wide[...] = dot_nt(r.side_gate[...], r.w_gate[...]) + dot_nt(r.side_up[...], r.w_up[...])
        for t in tiles:
            x1 = r.x1[t, :]
            dx1, g = rms_back(x1, inverse_rms(x1), gain_pre, r.wide[t, :])
            gain(2, g)
            dx1 = dx1 + f32(r.dy[t, :])
            r.x1[t, :] = dx1
            ap = r.ap[t, :]
            dap, g = rms_back(ap, inverse_rms(ap), gain_attn, dx1)
            gain(1, g)
            r.dap[t, :] = bf16(dap)

    def out_back(part):
        for h, here in enumerate(columns):
            wide = slice(h * head, (h + 1) * head)
            g = bf16(dot_tn(r.ob[:, wide], r.dap[...]))
            r.g_out[2 * h] = g[0:half]
            r.g_out[2 * h + 1] = g[half:head]
            do = bf16(dot_nt(r.dap[...], r.w_out[wide, :]))
            r.do[here, :] = do
            turned = do.T
            r.dot[:, here] = turned
            r.delta[:, here] = jnp.sum(f32(turned) * r.ot[:, here], axis=0, keepdims=True)
        r.ot[...] = jnp.zeros_like(r.ot)

    probs, dscores = r.hid.at[:, 0 : heads * rows], r.side_gate.at[:, 0 : heads * rows]

    def visit_back(source, target):
        kt = r.kv[source, :, 0:head].T
        mask = allowed(source)
        for here in columns:
            s = dot(r.kv[source, :, 0:head], r.qt[:, here])
            p = jnp.where(mask, jnp.exp2(s - r.lse[:, here]), 0.0)
            dp = dot(r.kv[source, :, head : 2 * head], r.dot[:, here])
            probs[:, here] = bf16(p)
            dscores[:, here] = bf16(p * (dp - r.delta[:, here]))
        target[:, 0:head] = bf16(dot(dscores[...], r.q[...]))
        target[:, head : 2 * head] = bf16(dot(probs[...], r.do[...]))
        for here in columns:
            r.ot[:, here] = r.ot[:, here] + dot(kt, dscores[:, here])

    def stage_y(row):
        return r.w_gate.at[0:rows, row * 2 * head : (row + 1) * 2 * head]

    def stage_z(row):
        return r.w_up.at[0:rows, row * 2 * head : (row + 1) * 2 * head]

    def to_partner(row):
        return pltpu.make_async_remote_copy(
            src_ref=stage_y(row),
            dst_ref=r.from_partner.at[row],
            send_sem=r.dkv_send.at[0, row],
            recv_sem=r.dkv_recv.at[0, row],
            device_id=peers["y"],
            device_id_type=MESH,
        )

    def to_below(row):
        return pltpu.make_async_remote_copy(
            src_ref=stage_z(row),
            dst_ref=r.from_above.at[row],
            send_sem=r.dkv_send.at[1, row],
            recv_sem=r.dkv_recv.at[1, row],
            device_id=peers["down"],
            device_id_type=MESH,
        )

    def visit_other(row):
        @pl.when((row < z) | ((row == z) & (y == 1)))
        def _():
            visit_back(2 * row + 1 - y, stage_y(row))
            to_partner(row).start()

    def visit_own(row):
        pl.when(row <= z)(lambda: visit_back(2 * row + y, stage_z(row)))

    def pass_down(row):
        @pl.when(row < z)
        def _():
            to_partner(row).wait_recv()
            pl.when(z < last)(lambda: to_below(row).wait_recv())
            for t in tiles:
                value = f32(stage_z(row)[t, :]) + f32(r.from_partner[row, t, :])
                above = jnp.where(z < last, f32(r.from_above[row, t, :]), 0.0)
                stage_z(row)[t, :] = bf16(value + above)
            to_below(row).start()

    def queries_back(h):
        wide = slice(h * head, (h + 1) * head)
        for t in tiles:
            dq = (r.ot[:, h * rows + t.start : h * rows + t.stop] * scale).T
            qp = r.qp[t, wide]
            dqp, g = rms_back(qp, inverse_rms(qp), gain_q, turn_back(dq, r.cosine[t, :], r.sine[t, :]))
            gain(4, g)
            r.ob[t, wide] = bf16(dqp)

    def query_grad(part):
        for h in range(heads):
            g = bf16(dot_tn(r.a[...], r.ob[:, h * head : (h + 1) * head]))
            r.g_query[2 * h] = g[:, 0:half]
            r.g_query[2 * h + 1] = g[:, half:head]

    def own_total(part):
        for row in range(z_count):

            @pl.when(row == z)
            def _():
                pl.when(y == 0)(lambda: to_partner(row).wait_recv())
                pl.when(z < last)(lambda: to_below(row).wait_recv())
                for t in tiles:
                    beside = jnp.where(y == 0, f32(r.from_partner[row, t, :]), 0.0)
                    above = jnp.where(z < last, f32(r.from_above[row, t, :]), 0.0)
                    r.dkv[t, :] = f32(stage_z(row)[t, :]) + beside + above

    def keys_back(part):
        for t in tiles:
            dk = r.dkv[t, 0:head] * LN2
            kp = r.kp[t, :]
            dkp, g = rms_back(kp, inverse_rms(kp), gain_k, turn_back(dk, r.cosine[t, :], r.sine[t, :]))
            gain(5, g)
            r.ob[t, wide_k] = bf16(dkp)
            r.ob[t, wide_v] = bf16(r.dkv[t, head : 2 * head])
        low = width // 2
        g = bf16(dot_tn(r.a[...], r.ob[:, joined : joined + 2 * head]))
        for p in range(8):
            which, upper, side = p // 4, (p // 2) % 2, p % 2
            left = which * head + side * half
            r.g_kv[p] = g[upper * low : (upper + 1) * low, left : left + half]
        r.wide[...] = dot_nt(r.ob[...], r.w_first[...])
        for t in tiles:
            x = f32(r.x[t, :])
            dx, g = rms_back(x, inverse_rms(x), gain_in, r.wide[t, :])
            gain(0, g)
            r.dx[t, :] = bf16(r.x1[t, :] + dx)
        r.g_gain[...] = jnp.zeros_like(r.g_gain)
        at = 0
        for k, size in enumerate((width, width, width, width, head, head)):
            g = jnp.sum(r.gains[k], axis=0, keepdims=True)
            for part in range(size // 128):
                r.g_gain[at // 16, at % 16 : at % 16 + 1, :] = g[:, part * 128 : (part + 1) * 128]
                at += 1

    work = {
        "S": side_grads,
        "F": feed_grads,
        "M": middle_back,
        "O": out_back,
        "X": visit_other,
        "W": visit_own,
        "P": pass_down,
        "Q": queries_back,
        "G": query_grad,
        "T": own_total,
        "K": keys_back,
    }
    for what, step in schedule:
        if what in work:
            work[what](step)
        else:
            chunks[what].tick(step)

    pl.when(z < last)(lambda: send_kv(place, 0).wait_send())
    pl.when(y == 0)(lambda: send_kv(place, 1).wait_send())
    pl.when((y == 1) & (z < last))(lambda: send_half(1).wait_send())
    pl.when((y == 0) & (z > 0))(lambda: send_half(0).wait_send())
    for back in range(1, z_count):

        @pl.when(back <= z)
        def _():
            mine = place - 2 * back
            pl.when(z < last)(lambda: send_kv(mine, 0).wait_send())
            pl.when(mine > 0)(lambda: send_kv(mine, 1).wait_send())

    for row in range(z_count):
        pl.when((row < z) | ((row == z) & (y == 1)))(lambda: to_partner(row).wait_send())
        pl.when(row < z)(lambda: to_below(row).wait_send())


def r_plan(sizes):
    return list(zip(("down", "gate", "up", "out", "query", "kv", "gain"), PIECES, strict=True))


def gradient_shapes(sizes):
    rows, width, hidden, heads, head, z_count = sizes
    joined, half = heads * head, head // 2
    return {
        "down": ((8, hidden // 8, width), (8, hidden // 8, width)),
        "gate": ((8, width, hidden // 8), (width, hidden)),
        "up": ((8, width, hidden // 8), (width, hidden)),
        "out": ((8, joined // 8, width), (8, joined // 8, width)),
        "query": ((8, width, joined // 8), (width, joined)),
        "kv": ((8, width // 2, half), (2, 2, width // 2, head)),
        "gain": ((8, 16, 128), (8, 16, 128)),
    }


def layer_scratch(sizes):
    rows, width, hidden, heads, head, z_count = sizes
    joined = heads * head
    low, wide = jnp.bfloat16, jnp.float32
    arrays = {
        "x": ((rows, width), low),
        "w_first": ((width, joined + 2 * head), low),
        "w_out": ((joined, width), low),
        "w_gate": ((width, hidden), low),
        "w_up": ((width, hidden), low),
        "w_down": ((hidden, width), low),
        "dy": ((rows, width), low),
        "a": ((rows, width), low),
        "gains": ((6, 8, width), wide),
        "kp": ((rows, head), wide),
        "kv": ((2 * z_count, rows, 2 * head), low),
        "qp": ((rows, joined), wide),
        "q": ((heads * rows, head), low),
        "qt": ((head, heads * rows), low),
        "cosine": ((rows, head // 2), wide),
        "sine": ((rows, head // 2), wide),
        "wide": ((rows, width), wide),
        "ot": ((head, heads * rows), wide),
        "total": ((1, heads * rows), wide),
        "lse": ((1, heads * rows), wide),
        "delta": ((1, heads * rows), wide),
        "ob": ((rows, joined + 2 * head), low),
        "ap": ((rows, width), wide),
        "x1": ((rows, width), wide),
        "m": ((rows, width), low),
        "hid": ((rows, hidden), low),
        "side_gate": ((rows, hidden), low),
        "side_up": ((rows, hidden), low),
        "df": ((rows, width), low),
        "dap": ((rows, width), low),
        "do": ((heads * rows, head), low),
        "dot": ((head, heads * rows), low),
        "dkv": ((rows, 2 * head), wide),
        "from_partner": ((z_count, rows, 2 * head), low),
        "from_above": ((z_count, rows, 2 * head), low),
    }
    shapes = gradient_shapes(sizes)
    pieces = 0
    for name, count in r_plan(sizes):
        (eight, high, columns), kind = shapes[name][0], wide if name == "gain" else low
        step = high // count
        pieces += count
        arrays["g_" + name] = (shapes[name][0], kind)
        for number in range(pieces - count, pieces):
            for k, shape in enumerate(LineChunk.landing(step) if FIRST[number] in "uv" else Chunk.landing(step)):
                arrays[f"land{k}_{number}"] = (shape + (columns,), kind)
    sems = {
        "load_sem": (9,),
        "kv_send": (2, 2 * z_count),
        "kv_recv": (2 * z_count,),
        "half_send": (2,),
        "half_recv": (2,),
        "dkv_send": (2, z_count),
        "dkv_recv": (2, z_count),
        "red_send": (pieces, STAGES),
        "red_recv": (pieces, STAGES),
        "red_local": (pieces,),
    }
    return arrays, sems


def layer_bytes(sizes):
    total = 0
    for shape, kind in layer_scratch(sizes)[0].values():
        size = jnp.dtype(kind).itemsize
        for n in shape[:-2]:
            size *= n
        total += size * max(shape[-2], 8) * max(shape[-1], 128)
    return total


VMEM_BYTES = 64 * 2**20


def widen_kernel(count, *refs):
    ins, table, both, tokens = refs[: count - 2], refs[count - 2], refs[count - 1], refs[count : count + 2]
    refs = refs[count + 2 :]
    outs, gains, tokens_out = refs[:count], refs[count : count + 6], refs[count + 6 : count + 8]
    refs = refs[count + 8 :]
    narrow, broad, (came, gone) = refs[: count + 2], refs[count + 2 : 2 * count + 2], refs[2 * count + 2 :]
    ins = (both.at[0], both.at[1]) + ins + tokens
    outs = outs + tokens_out
    loads = [pltpu.make_async_copy(ins[i], narrow[i], came.at[i]) for i in range(count + 2)]
    stores = [pltpu.make_async_copy((broad + narrow[count:])[i], outs[i], gone.at[i]) for i in range(count + 2)]
    for item in loads:
        item.start()
    at = 0
    for gain in gains:
        for part in range(gain.shape[0] // 128):
            gain[part * 128 : (part + 1) * 128] = table[at // 16, at % 16, :]
            at += 1
    for i in range(count):
        loads[i].wait()

        def body(j, carry):
            here = pl.ds(pl.multiple_of(j * 32, 32), 32)
            broad[i][here, :] = f32(narrow[i][here, :])
            return carry

        lax.fori_loop(0, narrow[i].shape[0] // 32, body, 0)
        stores[i].start()
    for i in (count, count + 1):
        loads[i].wait()
        stores[i].start()
    for item in stores:
        item.wait()


def widen(both, matrices, table, tokens, gain_sizes):
    count = len(matrices) + 2
    shapes = [both.shape[1:]] * 2 + [v.shape for v in matrices]
    anywhere, vmem = pl.BlockSpec(memory_space=pl.ANY), pl.BlockSpec(memory_space=pltpu.VMEM)
    return pl.pallas_call(
        functools.partial(widen_kernel, count),
        out_shape=tuple(jax.ShapeDtypeStruct(shape, jnp.float32) for shape in shapes)
        + tuple(jax.ShapeDtypeStruct((n,), jnp.float32) for n in gain_sizes)
        + tuple(jax.ShapeDtypeStruct(v.shape, v.dtype) for v in tokens),
        in_specs=[anywhere] * len(matrices) + [vmem] + [anywhere] * 3,
        out_specs=tuple([anywhere] * count + [vmem] * len(gain_sizes) + [anywhere] * 2),
        scratch_shapes=[pltpu.VMEM(shape, jnp.bfloat16) for shape in shapes + [v.shape for v in tokens]]
        + [pltpu.VMEM(shape, jnp.float32) for shape in shapes]
        + [pltpu.SemaphoreType.DMA((count + 2,))] * 2,
        compiler_params=pltpu.CompilerParams(vmem_limit_bytes=VMEM_BYTES),
    )(*matrices, table, both, *tokens)


def whole_layer(sizes, tokens, lengths, cotangent, norm_in, w_query, w_key, w_value, query_gain, key_gain, w_out, norm_attn, norm_pre, w_gate, w_up, w_down, norm_post):
    rows, width, hidden, heads, head, z_count = sizes
    joined = heads * head
    inputs = {
        "lengths": lengths,
        "norm_in": norm_in,
        "query_gain": query_gain,
        "key_gain": key_gain,
        "norm_attn": norm_attn,
        "norm_pre": norm_pre,
        "norm_post": norm_post,
        "x_in": tokens[0],
        "w_key_in": w_key,
        "w_value_in": w_value,
        "w_query_in": w_query,
        "w_out_in": w_out,
        "w_gate_in": w_gate,
        "w_up_in": w_up,
        "w_down_in": w_down,
        "dy_in": cotangent[0],
    }
    spaces = {name: pltpu.SMEM if name == "lengths" else pl.ANY if name.endswith("_in") and name != "norm_in" else pltpu.VMEM for name in inputs}
    shapes = gradient_shapes(sizes)
    outputs = {"out": (rows, width), "dx": (rows, width)}
    outputs.update({"t_" + name: shapes[name][1] for name in shapes})
    arrays, sems = layer_scratch(sizes)
    names = list(inputs) + list(outputs) + list(arrays) + list(sems)
    results = pl.pallas_call(
        functools.partial(layer_kernel, sizes, SCHEDULES[z_count], names),
        out_shape=tuple(
            jax.ShapeDtypeStruct(shape, jnp.float32 if name == "t_gain" else jnp.bfloat16) for name, shape in outputs.items()
        ),
        in_specs=[pl.BlockSpec(memory_space=spaces[name]) for name in inputs],
        out_specs=tuple(
            pl.BlockSpec(memory_space=pl.ANY if name.startswith("t_") else pltpu.VMEM) for name in outputs
        ),
        scratch_shapes=[pltpu.VMEM(*item) for item in arrays.values()]
        + [pltpu.SemaphoreType.DMA(item) for item in sems.values()],
        compiler_params=pltpu.CompilerParams(
            collective_id=1, has_side_effects=True, vmem_limit_bytes=VMEM_BYTES
        ),
    )(*inputs.values())
    r = Names(zip(outputs, results, strict=True))
    matrices = [
        r.t_query,
        r.t_out.reshape(joined, width),
        r.t_gate,
        r.t_up,
        r.t_down.reshape(hidden, width),
    ]
    both = r.t_kv.reshape(2, width, head)
    sums = widen(both, matrices, r.t_gain, (r.out, r.dx), (width, width, width, width, head, head))
    g_key, g_value, g_query, g_out, g_gate, g_up, g_down = sums[:7]
    g_in, g_attn, g_pre, g_post, g_qgain, g_kgain, output, input_grad = sums[7:]
    return (
        output[None],
        input_grad[None],
        g_in,
        g_query,
        g_key,
        g_value,
        g_qgain,
        g_kgain,
        g_out,
        g_attn,
        g_pre,
        g_gate,
        g_up,
        g_down,
        g_post,
    )


def per_device(
    tokens,
    lengths,
    cotangent,
    norm_in,
    w_query,
    w_key,
    w_value,
    query_gain,
    key_gain,
    w_out,
    norm_attn,
    norm_pre,
    w_gate,
    w_up,
    w_down,
    norm_post,
):
    rows = tokens.shape[1]
    head = query_gain.shape[0]
    heads = w_query.shape[1] // head
    sizes = (rows, tokens.shape[2], w_gate.shape[1], heads, head, lax.axis_size(BLOCKS) // 2)
    if sizes[-1] in SCHEDULES and layer_bytes(sizes) <= VMEM_BYTES:
        return whole_layer(
            sizes,
            tokens,
            lengths,
            cotangent,
            norm_in,
            w_query,
            w_key,
            w_value,
            query_gain,
            key_gain,
            w_out,
            norm_attn,
            norm_pre,
            w_gate,
            w_up,
            w_down,
            norm_post,
        )
    scale = head ** (-0.5)
    count = lax.axis_size(BLOCKS)
    place = lax.axis_index(BLOCKS)
    row = lengths[0]
    local_idx = place * rows + jnp.arange(rows, dtype=jnp.int32)
    seg_q, pos_q = segment_of(local_idx, row)
    cosine, sine = rotary_tables(pos_q, head)

    def block_mask(source):
        key_idx = source * rows + jnp.arange(rows, dtype=jnp.int32)
        seg_k, unused = segment_of(key_idx, row)
        return (seg_q[:, None] == seg_k[None, :]) & (local_idx[:, None] >= key_idx[None, :])

    x_in = tokens[0].astype(jnp.float32)
    normal_a = normed(x_in, norm_in).astype(jnp.bfloat16)
    q_proj = jnp.dot(normal_a, w_query, preferred_element_type=jnp.float32).reshape(
        rows, heads, head
    )
    k_proj = jnp.dot(normal_a, w_key, preferred_element_type=jnp.float32)
    v_proj = jnp.dot(normal_a, w_value, preferred_element_type=jnp.float32)
    query = prepare(q_proj, query_gain, cosine[:, None, :], sine[:, None, :]).astype(jnp.bfloat16)
    keys = prepare(k_proj, key_gain, cosine, sine).astype(jnp.bfloat16)
    values = v_proj.astype(jnp.bfloat16)
    q_heads = jnp.transpose(query, (1, 0, 2))

    def absorb(state, pair, source):
        allowed = block_mask(source)
        big, total, accum = state
        raw = jnp.einsum("hqd,kd->hqk", q_heads, pair[0], preferred_element_type=jnp.float32)
        scores = jnp.where(allowed[None], scale * raw, NEG)
        big_new = jnp.maximum(big, jnp.max(scores, axis=-1, keepdims=True))
        expo = jnp.where(allowed[None], jnp.exp(scores - big_new), 0.0)
        fade = jnp.exp(big - big_new)
        total = total * fade + jnp.sum(expo, axis=-1, keepdims=True)
        accum = accum * fade + jnp.einsum(
            "hqk,kd->hqd", expo.astype(jnp.bfloat16), pair[1], preferred_element_type=jnp.float32
        )
        return (big_new, total, accum)

    pair = jnp.stack([keys, values])
    state = (
        jnp.full((heads, rows, 1), NEG, jnp.float32),
        jnp.zeros((heads, rows, 1), jnp.float32),
        jnp.zeros((heads, rows, head), jnp.float32),
    )
    state = absorb(state, pair, place)

    def cycle_forward(step, carry):
        inner, moving = carry
        moving = from_behind(moving, BLOCKS, 1)
        return (absorb(inner, moving, (place - step) % count), moving)

    state, unused_pair = lax.fori_loop(1, count, cycle_forward, (state, pair))
    big, total, accum = state
    attended = accum / total
    lse = big + jnp.log(total)
    joined = jnp.transpose(attended, (1, 0, 2)).reshape(rows, heads * head).astype(jnp.bfloat16)
    a_proj = jnp.dot(joined, w_out, preferred_element_type=jnp.float32)
    x_mid = x_in + normed(a_proj, norm_attn)
    mixed = normed(x_mid, norm_pre).astype(jnp.bfloat16)
    gate = jnp.dot(mixed, w_gate, preferred_element_type=jnp.float32)
    upper = jnp.dot(mixed, w_up, preferred_element_type=jnp.float32)

    def activate(gate_in, upper_in):
        return jax.nn.gelu(gate_in, approximate=True) * upper_in

    hidden = activate(gate, upper).astype(jnp.bfloat16)
    f_proj = jnp.dot(hidden, w_down, preferred_element_type=jnp.float32)
    output = x_mid + normed(f_proj, norm_post)
    grad_y = cotangent[0].astype(jnp.float32)
    d_fproj, g_post = normed_back(f_proj, norm_post, grad_y)
    d_fproj = d_fproj.astype(jnp.bfloat16)
    g_down = dot_tn(hidden, d_fproj)
    d_hidden = dot_nt(d_fproj, w_down)
    d_gate, d_upper = jax.vjp(activate, gate, upper)[1](d_hidden)
    d_gate = d_gate.astype(jnp.bfloat16)
    d_upper = d_upper.astype(jnp.bfloat16)
    g_gate = dot_tn(mixed, d_gate)
    g_up = dot_tn(mixed, d_upper)
    d_mixed = dot_nt(d_gate, w_gate) + dot_nt(d_upper, w_up)
    d_mid, g_pre = normed_back(x_mid, norm_pre, d_mixed)
    d_mid = grad_y + d_mid
    d_aproj, g_attn = normed_back(a_proj, norm_attn, d_mid)
    d_aproj = d_aproj.astype(jnp.bfloat16)
    g_out = dot_tn(joined, d_aproj)
    d_joined = dot_nt(d_aproj, w_out).astype(
        jnp.bfloat16
    )
    do_heads = jnp.transpose(d_joined.reshape(rows, heads, head), (1, 0, 2))
    delta = jnp.sum(do_heads.astype(jnp.float32) * attended, axis=-1, keepdims=True)

    def visit(d_query, moving, grads, source):
        allowed = block_mask(source)
        raw = jnp.einsum("hqd,kd->hqk", q_heads, moving[0], preferred_element_type=jnp.float32)
        probs = jnp.where(allowed[None], jnp.exp(scale * raw - lse), 0.0)
        dv_add = jnp.einsum(
            "hqk,hqd->kd", probs.astype(jnp.bfloat16), do_heads, preferred_element_type=jnp.float32
        )
        d_probs = jnp.einsum("hqd,kd->hqk", do_heads, moving[1], preferred_element_type=jnp.float32)
        d_scores = (scale * probs * (d_probs - delta)).astype(jnp.bfloat16)
        dq_add = jnp.einsum("hqk,kd->hqd", d_scores, moving[0], preferred_element_type=jnp.float32)
        dk_add = jnp.einsum("hqk,hqd->kd", d_scores, q_heads, preferred_element_type=jnp.float32)
        return (d_query + dq_add, grads + jnp.stack([dk_add, dv_add]))

    d_query = jnp.zeros((heads, rows, head), jnp.float32)
    grads = jnp.zeros((2, rows, head), jnp.float32)
    d_query, grads = visit(d_query, pair, grads, place)

    def cycle_backward(step, carry):
        dq_in, moving, grads_in = carry
        moving = from_behind(moving, BLOCKS, 1)
        grads_in = pass_home(grads_in)
        dq_in, grads_in = visit(dq_in, moving, grads_in, (place - step) % count)
        return (dq_in, moving, grads_in)

    d_query, unused_pair, grads = lax.fori_loop(1, count, cycle_backward, (d_query, pair, grads))
    grads = pass_home(grads)

    def query_piece(proj, gain):
        return prepare(proj, gain, cosine[:, None, :], sine[:, None, :])

    def key_piece(proj, gain):
        return prepare(proj, gain, cosine, sine)

    d_qproj, g_qgain = jax.vjp(query_piece, q_proj, query_gain)[1](
        jnp.transpose(d_query, (1, 0, 2))
    )
    d_kproj, g_kgain = jax.vjp(key_piece, k_proj, key_gain)[1](grads[0])
    d_qproj = d_qproj.reshape(rows, heads * head).astype(jnp.bfloat16)
    d_kproj = d_kproj.astype(jnp.bfloat16)
    d_vproj = grads[1].astype(jnp.bfloat16)
    g_query = dot_tn(normal_a, d_qproj)
    g_key = dot_tn(normal_a, d_kproj)
    g_value = dot_tn(normal_a, d_vproj)
    d_normal = dot_nt(d_qproj, w_query)
    d_normal = d_normal + dot_nt(d_kproj, w_key)
    d_normal = d_normal + dot_nt(d_vproj, w_value)
    d_input, g_in = normed_back(x_in, norm_in, d_normal)
    input_grad = (d_mid + d_input).astype(jnp.bfloat16)
    (
        g_in,
        g_query,
        g_key,
        g_value,
        g_qgain,
        g_kgain,
        g_out,
        g_attn,
        g_pre,
        g_gate,
        g_up,
        g_down,
        g_post,
    ) = sum_gradients(
        (
            g_in,
            g_query,
            g_key,
            g_value,
            g_qgain,
            g_kgain,
            g_out,
            g_attn,
            g_pre,
            g_gate,
            g_up,
            g_down,
            g_post,
        )
    )
    return (
        output.astype(jnp.bfloat16)[None],
        input_grad[None],
        g_in,
        g_query,
        g_key,
        g_value,
        g_qgain,
        g_kgain,
        g_out,
        g_attn,
        g_pre,
        g_gate,
        g_up,
        g_down,
        g_post,
    )


def solution(mesh):
    in_specs = (
        P(PARTS, BLOCKS, None),
        P(PARTS, None),
        P(PARTS, BLOCKS, None),
        P(),
        P(),
        P(),
        P(),
        P(),
        P(),
        P(),
        P(),
        P(),
        P(),
        P(),
        P(),
        P(),
    )
    out_specs = (
        P(PARTS, BLOCKS, None),
        P(PARTS, BLOCKS, None),
        P(),
        P(),
        P(),
        P(),
        P(),
        P(),
        P(),
        P(),
        P(),
        P(),
        P(),
        P(),
        P(),
    )
    return jax.shard_map(
        per_device, mesh=mesh, in_specs=in_specs, out_specs=out_specs, check_vma=False
    )
```

```python
import functools

import jax
import jax.numpy as jnp
from jax import lax
from jax.experimental import pallas as pl
from jax.experimental.pallas import tpu as pltpu
from jax.sharding import PartitionSpec as P

BLOCKS, PARTS = "blk", "dp"
EPS = 1e-06
BASE = 1000000.0
NEG = -1e30


def shifted(array, axis, by):
    peers = lax.axis_size(axis)
    return lax.ppermute(array, axis, [(i, (i + by) % peers) for i in range(peers)])


def from_behind(block, axis, distance):
    devices = range(lax.axis_size(axis))
    route = [(i - distance, i) for i in devices if i - distance in devices]
    return lax.ppermute(block, axis, route)


def normed(value, gain):
    return value * lax.rsqrt(jnp.mean(value * value, axis=-1, keepdims=True) + EPS) * gain


def normed_back(value, gain, grad):
    return jax.vjp(normed, value, gain)[1](grad)


def segment_of(index, row):
    ends = jnp.cumsum(row)
    seg = jnp.sum((index[:, None] >= ends[None, :]).astype(jnp.int32), axis=1)
    starts = ends - row
    slots = jnp.arange(row.shape[0], dtype=jnp.int32)
    begin = jnp.sum(jnp.where(slots[None, :] == seg[:, None], starts[None, :], 0), axis=1)
    return (seg, index - begin)


def rotary_tables(places, head):
    half = head // 2
    freq = jnp.exp(-(2.0 * jnp.arange(half, dtype=jnp.float32) / head) * jnp.log(BASE))
    angle = places.astype(jnp.float32)[:, None] * freq[None, :]
    return (jnp.cos(angle), jnp.sin(angle))


def prepare(proj, gain, cosine, sine):
    value = normed(proj, gain)
    half = value.shape[-1] // 2
    first = value[..., :half]
    second = value[..., half:]
    return jnp.concatenate(
        [first * cosine - second * sine, second * cosine + first * sine], axis=-1
    )


def pass_home(grads):
    return shifted(grads.astype(jnp.bfloat16), BLOCKS, 1).astype(grads.dtype)


MESH = pl.DeviceIdType.MESH


def where_am_i():
    place = lax.axis_index(BLOCKS)
    part = lax.axis_index(PARTS)
    return {
        "z": place // 2,
        "y": lax.rem(place, 2),
        "x": part // 2,
        "core": lax.rem(part, 2),
        "place": place,
        "part": part,
    }


def peers_of(me):
    place, part = me["place"], me["part"]
    return {
        "core": {BLOCKS: place, PARTS: part + 1 - 2 * me["core"]},
        "x": {BLOCKS: place, PARTS: part + 2 - 4 * me["x"]},
        "y": {BLOCKS: place + 1 - 2 * me["y"], PARTS: part},
        "up": {BLOCKS: place + 2, PARTS: part},
        "down": {BLOCKS: place - 2, PARTS: part},
    }


def greet(me, peers, z_count):
    barrier = pltpu.get_barrier_semaphore()
    for name in ("core", "x", "y"):
        pl.semaphore_signal(barrier, inc=1, device_id=peers[name], device_id_type=MESH)

    @pl.when(me["z"] < z_count - 1)
    def _():
        pl.semaphore_signal(barrier, inc=1, device_id=peers["up"], device_id_type=MESH)

    @pl.when(me["z"] > 0)
    def _():
        pl.semaphore_signal(barrier, inc=1, device_id=peers["down"], device_id_type=MESH)

    ends = (me["z"] == 0).astype(jnp.int32) + (me["z"] == z_count - 1).astype(jnp.int32)
    pl.semaphore_wait(barrier, 5 - ends)


def add_into(target, start, row, extra, count, rows):
    step = rows if rows < 32 else 16
    for candidate in (160, 128, 80, 64, 48, 32):
        if rows % candidate == 0:
            step = candidate
            break

    def body(index, carry):
        e = index // (rows // step)
        at = pl.multiple_of(lax.rem(index, rows // step) * step, 8)
        here = pl.ds(pl.multiple_of(row + at, 8), step)
        target[start + e, here, :] = target[start + e, here, :] + extra[e, pl.ds(at, step), :]
        return carry

    lax.fori_loop(0, count * (rows // step), body, 0)


STAGES = 10


class Chunk:
    def __init__(self, number, grad, total, row, rows, first, landing, sems, me, peers, z_count):
        self.grad, self.total, self.row, self.rows = grad, total, row, rows
        self.first, self.second = ("x", "y") if first == "x" else ("y", "x")
        self.land0, self.land1, self.land2 = landing
        self.send, self.recv, self.local = sems
        self.number, self.me, self.peers, self.z_count = number, me, peers, z_count
        self.b1, self.b2, self.core = me[self.first], me[self.second], me["core"]
        self.quad = 4 * self.core
        self.pair = self.quad + 2 * self.b1
        self.own = self.pair + self.b2
        self.half = rows // 2

    @staticmethod
    def landing(rows):
        return ((4, rows), (2, rows), (1, 2 * rows))

    def piece(self, start, count, upper=None):
        if upper is None:
            return self.grad.at[pl.ds(start, count), pl.ds(self.row, self.rows), :]
        row = self.row if upper else self.row + self.half
        return self.grad.at[pl.ds(start, count), pl.ds(row, self.half), :]

    def spot(self, count, upper=None):
        row, rows = self.row, self.rows
        if upper is not None:
            row, rows = (row if upper else row + self.half), self.half
        here, columns = pl.ds(row, rows), self.grad.shape[2]
        start = {1: self.own, 2: self.pair, 4: self.quad}[count]
        if len(self.total.shape) == 2:
            return self.total.at[here, pl.ds(pl.multiple_of(start * columns, 128), count * columns)]
        if len(self.total.shape) == 4:
            if count == 4:
                return self.total.at[self.core, :, here, :]
            if count == 2:
                return self.total.at[self.core, self.b1, here, :]
            return self.total.at[self.core, self.b1, here, pl.ds(pl.multiple_of(self.b2 * columns, 128), columns)]
        if count == 1:
            return self.total.at[start, here, :]
        return self.total.at[pl.ds(start, count), here, :]

    def mine(self, upper):
        return self.grad.at[self.own, pl.ds(self.row if upper else self.row + self.half, self.half), :]

    def keep(self, upper):
        return pltpu.make_async_copy(
            self.mine(upper), self.spot(1, upper), self.local.at[self.number]
        )

    def copy(self, stage, peer, source, target):
        return pltpu.make_async_remote_copy(
            src_ref=source,
            dst_ref=target,
            send_sem=self.send.at[self.number, stage],
            recv_sem=self.recv.at[self.number, stage],
            device_id=self.peers[peer],
            device_id_type=MESH,
        )

    def reduce_up(self):
        return self.copy(3, "up", self.piece(self.own, 1, True), self.land2.at[:, pl.ds(self.rows, self.half), :])

    def reduce_down(self):
        return self.copy(4, "down", self.piece(self.own, 1, False), self.land2.at[:, pl.ds(self.rows + self.half, self.half), :])

    def spread_down(self, fresh=False):
        here = self.spot(1, True)
        return self.copy(5, "down", self.mine(True) if fresh else here, here)

    def spread_up(self, fresh=False):
        here = self.spot(1, False)
        return self.copy(6, "up", self.mine(False) if fresh else here, here)

    def step0(self):
        return self.copy(0, "core", self.piece(4 - self.quad, 4), self.land0)

    def step1(self):
        return self.copy(1, self.first, self.piece(self.quad + 2 - 2 * self.b1, 2), self.land1)

    def step2(self):
        return self.copy(2, self.second, self.piece(self.pair + 1 - self.b2, 1), self.land2.at[:, pl.ds(0, self.rows), :])

    def gather(self, stage):
        count, peer = ((1, self.second), (2, self.first), (4, "core"))[stage - 7]
        here = self.spot(count)
        return self.copy(stage, peer, here, here)

    def arrive_upper(self):
        z, last = self.me["z"], self.z_count - 1

        @pl.when(z > 0)
        def _():
            self.reduce_up().wait_recv()
            add_into(self.grad, self.own, self.row, self.land2.at[:, pl.ds(self.rows, self.half), :], 1, self.half)

            @pl.when(z < last)
            def _():
                self.reduce_up().start()

            @pl.when(z == last)
            def _():
                self.spread_down(True).start()
                self.keep(True).start()

    def arrive_lower(self):
        z, last = self.me["z"], self.z_count - 1

        @pl.when(z < last)
        def _():
            self.reduce_down().wait_recv()
            add_into(self.grad, self.own, self.row + self.half, self.land2.at[:, pl.ds(self.rows + self.half, self.half), :], 1, self.half)

            @pl.when(z > 0)
            def _():
                self.reduce_down().start()

            @pl.when(z == 0)
            def _():
                self.spread_up(True).start()
                self.keep(False).start()

    def back_upper(self):
        z, last = self.me["z"], self.z_count - 1

        @pl.when(z < last)
        def _():
            self.spread_down().wait_recv()

            @pl.when(z > 0)
            def _():
                self.spread_down().start()

    def back_lower(self):
        z, last = self.me["z"], self.z_count - 1

        @pl.when(z > 0)
        def _():
            self.spread_up().wait_recv()

            @pl.when(z < last)
            def _():
                self.spread_up().start()

    def tick(self, op):
        z, last = self.me["z"], self.z_count - 1
        if op == 0:
            self.step0().start()
        elif op == 1:
            self.step0().wait_recv()
            add_into(self.grad, self.quad, self.row, self.land0, 4, self.rows)
            self.step1().start()
        elif op == 2:
            self.step1().wait_recv()
            add_into(self.grad, self.pair, self.row, self.land1, 2, self.rows)
            self.step2().start()
        elif op == 3:
            self.step2().wait_recv()
            add_into(self.grad, self.own, self.row, self.land2, 1, self.rows)

            @pl.when(z == 0)
            def _():
                self.reduce_up().start()

            @pl.when(z == last)
            def _():
                self.reduce_down().start()

        elif op == 4:
            pl.when((z > 0) & (2 * z < self.z_count))(self.arrive_upper)
            pl.when((z < last) & (2 * z >= self.z_count))(self.arrive_lower)
        elif op == 5:
            pl.when((z < last) & (2 * z >= self.z_count))(self.arrive_upper)
            pl.when((z > 0) & (2 * z < self.z_count))(self.arrive_lower)
        elif op == 6:
            pl.when(z == last)(self.arrive_upper)
            pl.when(z == 0)(self.arrive_lower)
        elif op == 7:
            pl.when((z < last) & (2 * z >= self.z_count))(self.back_upper)
            pl.when((z > 0) & (2 * z < self.z_count))(self.back_lower)
        elif op == 8:

            @pl.when((z > 0) & (2 * z < self.z_count))
            def _():
                self.back_upper()
                self.gather(7).start()

            @pl.when((z < last) & (2 * z >= self.z_count))
            def _():
                self.back_lower()
                self.gather(7).start()

        elif op == 9:

            @pl.when(z == 0)
            def _():
                self.back_upper()
                self.keep(False).wait()
                self.gather(7).start()

            @pl.when(z == last)
            def _():
                self.back_lower()
                self.keep(True).wait()
                self.gather(7).start()

        elif op == 10:
            self.gather(7).wait_recv()
            self.gather(8).start()
        elif op == 11:
            self.gather(8).wait_recv()
            self.gather(9).start()
        elif op == 12:
            self.gather(9).wait_recv()
            self.drain()

    OPS = 13

    def drain(self):
        z, last = self.me["z"], self.z_count - 1
        self.step0().wait_send()
        self.step1().wait_send()
        self.step2().wait_send()
        for stage in (7, 8, 9):
            self.gather(stage).wait_send()

        @pl.when(z < last)
        def _():
            self.reduce_up().wait_send()
            self.spread_up().wait_send()

        @pl.when(z > 0)
        def _():
            self.reduce_down().wait_send()
            self.spread_down().wait_send()


class LineChunk(Chunk):
    def __init__(self, *args):
        super().__init__(*args[:6], (args[6][0], None, None), *args[7:])
        self.ups, self.downs, self.small = args[6][1:]
        self.entry = self.quad + self.me["z"]
        self.half, self.quarter = self.rows // 2, self.rows // 4
        self.mine_half = pl.multiple_of(self.row + self.b1 * self.half, 16)
        self.mine_quarter = pl.multiple_of(self.mine_half + self.b2 * self.quarter, 16)

    @staticmethod
    def landing(rows):
        return ((4, rows), (3, rows), (3, rows), (1, rows))

    def across(self, stage, name, first, count):
        landing = self.ups if name == "up" else self.downs
        return self.copy(stage, name, self.piece(self.quad + first, count), landing.at[pl.ds(0, count)])

    def back(self, stage, name, first, count):
        here = self.place(self.quad + first, count, self.row, self.rows)
        return self.copy(stage, name, here, here)

    def place(self, start, count, row, rows):
        here, columns = pl.ds(row, rows), self.grad.shape[2]
        if len(self.total.shape) == 2:
            return self.total.at[here, pl.ds(pl.multiple_of(start * columns, 128), count * columns)]
        if count == 1:
            return self.total.at[start, here, :]
        return self.total.at[pl.ds(start, count), here, :]

    def part(self, row, rows):
        return self.grad.at[pl.ds(self.entry, 1), pl.ds(row, rows), :]

    def step1(self):
        other = pl.multiple_of(self.row + (1 - self.b1) * self.half, 16)
        return self.copy(1, self.first, self.part(other, self.half), self.small.at[:, pl.ds(0, self.half), :])

    def step2(self):
        other = pl.multiple_of(self.mine_half + (1 - self.b2) * self.quarter, 16)
        landing = self.small.at[:, pl.ds(self.half, self.quarter), :]
        return self.copy(2, self.second, self.part(other, self.quarter), landing)

    def finished(self):
        return self.grad.at[self.entry, pl.ds(self.mine_quarter, self.quarter), :]

    def keep(self):
        spot = self.place(self.entry, 1, self.mine_quarter, self.quarter)
        return pltpu.make_async_copy(self.finished(), spot, self.local.at[self.number])

    def gather2(self):
        spot = self.place(self.entry, 1, self.mine_quarter, self.quarter)
        return self.copy(7, self.second, self.finished(), spot)

    def gather1(self):
        here = self.place(self.entry, 1, self.mine_half, self.half)
        return self.copy(8, self.first, here, here)

    def gather0(self):
        here = self.place(self.quad, 4, self.row, self.rows)
        return self.copy(9, "core", here, here)

    def at_row(self, k, body):
        pl.when(self.me["z"] == k)(body)

    def from_below(self, k):
        return (k, self.z_count - k)

    def from_above(self, k):
        return (0, k + 1)

    def take_up(self, k):
        first, count = self.from_below(k)
        self.across(3, "up", first, count).wait_recv()
        add_into(self.grad, self.quad + first, self.row, self.ups, count, self.rows)
        if k < self.z_count - 1:
            self.across(3, "up", first + 1, count - 1).start()

    def take_down(self, k):
        first, count = self.from_above(k)
        self.across(4, "down", first, count).wait_recv()
        add_into(self.grad, self.quad + first, self.row, self.downs, count, self.rows)
        if k > 0:
            self.across(4, "down", first, count - 1).start()

    def back_up(self, k):
        self.back(6, "up", 0, k).wait_recv()
        if k < self.z_count - 1:
            self.back(6, "up", 0, k + 1).start()

    def back_down(self, k):
        last = self.z_count - 1
        self.back(5, "down", k + 1, last - k).wait_recv()
        if k > 0:
            self.back(5, "down", k, last - k + 1).start()

    def tick(self, op):
        last, middle = self.z_count - 1, self.z_count // 2
        if op == 0:
            self.step0().start()
        elif op == 1:
            self.step0().wait_recv()
            add_into(self.grad, self.quad, self.row, self.land0, 4, self.rows)
            self.at_row(0, lambda: self.across(3, "up", 1, last).start())
            self.at_row(last, lambda: self.across(4, "down", 0, last).start())
        elif op == 2:
            for k in range(1, last):
                self.at_row(k, functools.partial(self.take_up if k < middle else self.take_down, k))
        elif op == 3:
            for k in range(1, last):

                def arrive(k=k):
                    (self.take_down if k < middle else self.take_up)(k)
                    self.step1().start()

                self.at_row(k, arrive)
        elif op == 4:

            def bottom():
                self.take_down(0)
                self.step1().start()

            def top():
                self.take_up(last)
                self.step1().start()

            self.at_row(0, bottom)
            self.at_row(last, top)
        elif op == 5:
            self.step1().wait_recv()
            add_into(self.grad, self.entry, self.mine_half, self.small, 1, self.half)
            self.step2().start()
        elif op == 6:
            self.step2().wait_recv()
            landing = self.small.at[:, pl.ds(self.half, self.quarter), :]
            add_into(self.grad, self.entry, self.mine_quarter, landing, 1, self.quarter)
            self.keep().start()
            self.gather2().start()
        elif op == 7:
            self.gather2().wait_recv()
            self.keep().wait()
            self.gather1().start()
        elif op == 8:
            self.gather1().wait_recv()
            self.at_row(0, lambda: self.back(6, "up", 0, 1).start())
            self.at_row(last, lambda: self.back(5, "down", last, 1).start())
        elif op == 9:
            for k in range(1, last):
                self.at_row(k, functools.partial(self.back_up if k < middle else self.back_down, k))
        elif op == 10:
            for k in range(1, last):

                def complete(k=k):
                    (self.back_down if k < middle else self.back_up)(k)
                    self.gather0().start()

                self.at_row(k, complete)
        elif op == 11:

            def bottom():
                self.back_down(0)
                self.gather0().start()

            def top():
                self.back_up(last)
                self.gather0().start()

            self.at_row(0, bottom)
            self.at_row(last, top)
        elif op == 12:
            self.gather0().wait_recv()
            self.drain()

    def drain(self):
        last = self.z_count - 1
        for item in (self.step0(), self.step1(), self.step2(), self.gather2(), self.gather1(), self.gather0()):
            item.wait_send()
        for k in range(self.z_count):

            def sent(k=k):
                if k < last:
                    self.across(3, "up", k + 1, last - k).wait_send()
                    self.back(6, "up", 0, k + 1).wait_send()
                if k > 0:
                    self.across(4, "down", 0, k).wait_send()
                    self.back(5, "down", k, last - k + 1).wait_send()

            self.at_row(k, sent)


def sum_kernel(z_count, plan, *refs):
    n = 1 + max(item[0] for item in plan)
    parts = len(plan)
    ins, outs = refs[:n], refs[n : 2 * n]
    rest = refs[2 * n :]
    grads, rest = rest[:n], rest[n:]
    landings = rest[: 3 * parts]
    send, recv, local, load = rest[3 * parts :]
    me = where_am_i()
    peers = peers_of(me)
    loads = [pltpu.make_async_copy(ins[i], grads[i], load.at[i]) for i in range(n)]
    for item in loads:
        item.start()
    greet(me, peers, z_count)
    for item in loads:
        item.wait()
    chunks = []
    for number, (i, row, rows, first) in enumerate(plan):
        landing = landings[3 * number : 3 * number + 3]
        chunks.append(
            Chunk(number, grads[i], outs[i], row, rows, first, landing, (send, recv, local), me, peers, z_count)
        )
    for at in range(parts + Chunk.OPS - 1):
        for number in range(parts):
            if 0 <= at - number < Chunk.OPS:
                chunks[number].tick(at - number)


def sum_call(arrays, plan, z_count):
    landing = []
    for i, row, rows, first in plan:
        columns, kind = arrays[i].shape[2], arrays[i].dtype
        landing += [
            pltpu.VMEM((4, rows, columns), kind),
            pltpu.VMEM((2, rows, columns), kind),
            pltpu.VMEM((1, 2 * rows, columns), kind),
        ]
    n = len(arrays)
    return pl.pallas_call(
        functools.partial(sum_kernel, z_count, plan),
        out_shape=tuple(jax.ShapeDtypeStruct(v.shape, v.dtype) for v in arrays),
        in_specs=[pl.BlockSpec(memory_space=pl.ANY)] * n,
        out_specs=tuple([pl.BlockSpec(memory_space=pl.ANY)] * n),
        scratch_shapes=[pltpu.VMEM(v.shape, v.dtype) for v in arrays]
        + landing
        + [
            pltpu.SemaphoreType.DMA((len(plan), STAGES)),
            pltpu.SemaphoreType.DMA((len(plan), STAGES)),
            pltpu.SemaphoreType.DMA((len(plan),)),
            pltpu.SemaphoreType.DMA((n,)),
        ],
        compiler_params=pltpu.CompilerParams(
            collective_id=0, has_side_effects=True, vmem_limit_bytes=56 * 2**20
        ),
    )(*arrays)


def columns_to_panels(value):
    rows, columns = value.shape
    return jnp.transpose(value.reshape(rows, 8, columns // 8), (1, 0, 2)).astype(jnp.bfloat16)


def panels_to_columns(panels):
    count, rows, width = panels.shape
    return jnp.transpose(panels.astype(jnp.float32), (1, 0, 2)).reshape(rows, count * width)


def sum_gradients(grads):
    (g_in, g_query, g_key, g_value, g_qgain, g_kgain, g_out, g_attn, g_pre, g_gate, g_up, g_down, g_post) = grads
    z_count = lax.axis_size(BLOCKS) // 2
    width = g_in.shape[0]
    gains = [g_in, g_attn, g_pre, g_post, g_qgain, g_kgain]
    sizes = [v.shape[0] for v in gains]
    flat = jnp.concatenate(gains)
    gain_rows = 32
    flat = jnp.pad(flat, (0, 8 * gain_rows * 128 - flat.shape[0])).reshape(8, gain_rows, 128)
    down = g_down.astype(jnp.bfloat16).reshape(8, -1, width)
    out = g_out.astype(jnp.bfloat16).reshape(8, -1, width)
    both = jnp.stack([g_key, g_value])
    head = g_key.shape[1]
    both = jnp.transpose(both.reshape(2, 2, width // 2, 2, head // 2), (0, 1, 3, 2, 4)).reshape(8, width // 2, head // 2)
    arrays = [down, columns_to_panels(g_gate), columns_to_panels(g_up), out, columns_to_panels(g_query), both.astype(jnp.bfloat16), flat]
    plan = []
    for i, v in enumerate(arrays[:-1]):
        rows = v.shape[1] // 2
        plan += [(i, 0, rows, "x"), (i, rows, rows, "y")]
    plan.append((6, 0, gain_rows, "x"))
    down, gate, up, out, query, both, flat = sum_call(arrays, plan, z_count)
    both = jnp.transpose(both.astype(jnp.float32).reshape(2, 2, 2, width // 2, head // 2), (0, 1, 3, 2, 4)).reshape(2, width, head)
    flat = flat.reshape(-1)
    cuts, at = [], 0
    for size in sizes:
        cuts.append(flat[at : at + size])
        at += size
    g_in, g_attn, g_pre, g_post, g_qgain, g_kgain = cuts
    return (
        g_in,
        panels_to_columns(query),
        both[0],
        both[1],
        g_qgain,
        g_kgain,
        out.astype(jnp.float32).reshape(g_out.shape),
        g_attn,
        g_pre,
        panels_to_columns(gate),
        panels_to_columns(up),
        down.astype(jnp.float32).reshape(g_down.shape),
        g_post,
    )


LOG2E = 1.4426950408889634
LN2 = 0.6931471805599453
PIECES = (2, 2, 2, 2, 2, 2, 1)
FIRST = ['y', 'y', 'x', 'v', 'x', 'y', 'x', 'x', 'x', 'y', 'x', 'y', 'y']
SCHEDULES = {
    4: (
        (1, 0), (0, 0), ("S", 0), ("F", 0), (1, 1), ("F", 1), (4, 0), ("M", 0), (4, 1), (3, 0), (0, 1), ("O", 0), (1, 2), (3, 1), ("V", 0), (0, 2),
        (4, 2), (2, 0), (7, 0), (5, 0), ("V", 1), (3, 2), (1, 3), (6, 0), (0, 3), ("V", 2), (2, 1), (5, 1), (0, 4), (1, 4), (4, 3), (4, 4), (7, 1),
        (1, 5), (0, 5), (4, 5), (6, 1), (3, 3), ("P", 0), ("P", 1), ("V", 3), (0, 6), (1, 6), ("P", 2), ("Q", 0), ("Q", 1), (7, 2), (4, 6), (5, 2),
        ("Q", 2), (1, 7), ("Q", 3), (6, 2), (3, 4), ("G", 0), (0, 7), (8, 0), (1, 8), (2, 2), (9, 0), (5, 3), ("T", 0), (8, 1), (4, 7), (7, 3),
        ("K", 0), (4, 8), (1, 9), (0, 8), (5, 4), (10, 0), (6, 3), (7, 4), (9, 1), (12, 0), (3, 5), (8, 2), (6, 4), (5, 5), (7, 5), (2, 3), (10, 1),
        (11, 0), (6, 5), (12, 1), (2, 4), (3, 6), (11, 1), (9, 2), (10, 2), (5, 6), (12, 2), (7, 6), (4, 9), (6, 6), (5, 7), (3, 7), (2, 5), (1, 10),
        (11, 2), (6, 7), (12, 3), (8, 3), (0, 9), (7, 7), (12, 4), (8, 4), (10, 3), (9, 3), (5, 8), (10, 4), (9, 4), (11, 3), (4, 10), (2, 6),
        (11, 4), (7, 8), (3, 8), (6, 8), (8, 5), (5, 9), (12, 5), (10, 5), (7, 9), (6, 9), (11, 5), (8, 6), (9, 5), (0, 10), (12, 6), (2, 7), (11, 6),
        (12, 7), (10, 6), (8, 7), (10, 7), (9, 6), (7, 10), (11, 7), (9, 7), (3, 9), (6, 10), (8, 8), (1, 11), (10, 8), (2, 8), (8, 9), (2, 9),
        (12, 8), (12, 9), (10, 9), (9, 8), (11, 8), (9, 9), (5, 10), (7, 11), (11, 9), (4, 11), (12, 10), (8, 10), (3, 10), (0, 11), (11, 10),
        (7, 12), (10, 10), (2, 10), (4, 12), (9, 10), (6, 11), (8, 11), (10, 11), (5, 11), (12, 11), (11, 11), (8, 12), (3, 11), (2, 11), (12, 12),
        (11, 12), (9, 11), (1, 12), (2, 12), (0, 12), (5, 12), (3, 12), (9, 12), (6, 12), (10, 12),
    )
}


def dot(left, right):
    return jnp.dot(left, right, preferred_element_type=jnp.float32)


def dot_nt(left, right):
    return lax.dot_general(left, right, (((1,), (1,)), ((), ())), preferred_element_type=jnp.float32)


def inverse_rms(value):
    return lax.rsqrt(jnp.mean(value * value, axis=-1, keepdims=True) + EPS)


def rms_back(value, inverse, gain, grad):
    scaled = grad * gain
    normal = value * inverse
    mean = jnp.mean(scaled * normal, axis=-1, keepdims=True)
    terms = grad * normal
    return inverse * (scaled - normal * mean), jnp.sum(terms.reshape(-1, 8, terms.shape[-1]), axis=0)


def turn(value, cosine, sine):
    half = value.shape[-1] // 2
    first, second = value[:, :half], value[:, half:]
    return jnp.concatenate([first * cosine - second * sine, second * cosine + first * sine], axis=-1)


def turn_back(grad, cosine, sine):
    half = grad.shape[-1] // 2
    first, second = grad[:, :half], grad[:, half:]
    return jnp.concatenate([first * cosine + second * sine, second * cosine - first * sine], axis=-1)


def dot_tn(left, right):
    return lax.dot_general(left, right, (((0,), (0,)), ((), ())), preferred_element_type=jnp.float32)


def bf16(value):
    return value.astype(jnp.bfloat16)


def f32(value):
    return value.astype(jnp.float32)


class Names(dict):
    __getattr__ = dict.__getitem__


def layer_kernel(sizes, schedule, names, *refs):
    r = Names(zip(names, refs, strict=True))
    rows, width, hidden, heads, head, z_count = sizes
    scale = head**-0.5
    tile = 128
    tiles = [slice(at, at + tile) for at in range(0, rows, tile)]
    half = head // 2
    me = where_am_i()
    peers = peers_of(me)
    z, y, place = me["z"], me["y"], me["place"]
    last = z_count - 1

    weights = ["x", "w_key", "w_value", "w_query", "w_out", "w_gate", "w_up", "w_down", "dy"]
    joined = heads * head
    wide_k, wide_v = slice(joined, joined + head), slice(joined + head, joined + 2 * head)
    spots = {"w_query": slice(0, joined), "w_key": wide_k, "w_value": wide_v}
    pair = ("w_gate", "w_up")
    loads = {}
    for i, name in enumerate(weights):
        if name in spots:
            spot = r.w_first.at[:, spots[name]]
        elif name in pair:
            spot = r.w_pair.at[pair.index(name)]
        else:
            spot = r[name]
        loads[name] = pltpu.make_async_copy(r[name + "_in"], spot, r.load_sem.at[i])
    early = ("x", "w_key", "w_value")
    for name in early:
        loads[name].start()
    greet(me, peers, z_count)

    def begins(token):
        begin, end = jnp.zeros_like(token), jnp.int32(0)
        for j in range(r.lengths.shape[1]):
            end = end + r.lengths[0, j]
            begin = jnp.where(token >= end, end, begin)
        return begin

    token = place * rows + lax.broadcasted_iota(jnp.int32, (1, rows), 1)
    begin = begins(token)
    entry = f32(lax.broadcasted_iota(jnp.int32, (1, half), 1))
    speed = jnp.exp(-(2.0 * entry / head) * jnp.log(BASE))
    for t in tiles:
        column = place * rows + t.start + lax.broadcasted_iota(jnp.int32, (tile, 1), 0)
        angle = f32(column - begins(column)) * speed
        r.cosine[t, :] = jnp.cos(angle)
        r.sine[t, :] = jnp.sin(angle)
    gain_in = r.norm_in[...].reshape(1, width)
    gain_q = r.query_gain[...].reshape(1, head)
    gain_k = r.key_gain[...].reshape(1, head)
    gain_attn = r.norm_attn[...].reshape(1, width)
    gain_pre = r.norm_pre[...].reshape(1, width)
    gain_post = r.norm_post[...].reshape(1, width)

    def allowed(source):
        key = source * rows + lax.broadcasted_iota(jnp.int32, (rows, rows), 0)
        return (key >= begin) & (key <= token)

    loads["x"].wait()
    loads["w_key"].wait()
    loads["w_value"].wait()
    for name in weights:
        if name not in early:
            loads[name].start()
    for t in tiles:
        x = f32(r.x[t, :])
        r.a[t, :] = bf16(x * inverse_rms(x) * gain_in)
    r.kp[...] = dot(r.a[...], r.w_first[:, wide_k])
    r.kv[place, :, head : 2 * head] = bf16(dot(r.a[...], r.w_first[:, wide_v]))
    for t in tiles:
        kp = r.kp[t, :]
        r.kv[place, t, 0:head] = bf16(turn(kp * inverse_rms(kp) * gain_k, r.cosine[t, :], r.sine[t, :]))

    def send_kv(source, route):
        return pltpu.make_async_remote_copy(
            src_ref=r.kv.at[source],
            dst_ref=r.kv.at[source],
            send_sem=r.kv_send.at[route, source],
            recv_sem=r.kv_recv.at[source],
            device_id=peers["y"] if route else peers["up"],
            device_id_type=MESH,
        )

    def send_half(values):
        half_block = r.kv.at[0, :, head * values : head * (values + 1)]
        return pltpu.make_async_remote_copy(
            src_ref=half_block,
            dst_ref=half_block,
            send_sem=r.half_send.at[values],
            recv_sem=r.half_recv.at[values],
            device_id=peers["up"] if values else peers["y"],
            device_id_type=MESH,
        )

    pl.when(z < last)(lambda: send_kv(place, 0).start())
    pl.when(y == 0)(lambda: send_kv(place, 1).start())

    loads["w_query"].wait()
    for h in range(heads):
        wide = slice(h * head, (h + 1) * head)
        r.qp[:, wide] = dot(r.a[...], r.w_first[:, wide])
        for t in tiles:
            qp = r.qp[t, wide]
            q = turn(qp * inverse_rms(qp) * gain_q, r.cosine[t, :], r.sine[t, :])
            q = bf16(q * (scale * LOG2E))
            r.q[h * rows + t.start : h * rows + t.stop, :] = q
            r.qt[:, h * rows + t.start : h * rows + t.stop] = q.T

    columns = [slice(h * rows, (h + 1) * rows) for h in range(heads)]

    def visit(source):
        vt = r.kv[source, :, head : 2 * head].T
        mask = allowed(source)
        for here in columns:
            p = jnp.where(mask, jnp.exp2(dot(r.kv[source, :, 0:head], r.qt[:, here])), 0.0)
            total = jnp.sum(p, axis=0, keepdims=True)
            o = dot(vt, bf16(p))
            r.total[:, here] = r.total[:, here] + total
            r.ot[:, here] = r.ot[:, here] + o

    r.total[...] = jnp.zeros_like(r.total)
    r.ot[...] = jnp.zeros_like(r.ot)

    def take_column(back):
        mine = place - 2 * back

        @pl.when(back <= z)
        def _():
            send_kv(mine, 0).wait_recv()
            pl.when(z < last)(lambda: send_kv(mine, 0).start())
            pl.when(mine > 0)(lambda: send_kv(mine, 1).start())
            pl.when(mine == 0)(lambda: send_half(0).start())

    def attend(step, carry):
        at = step - 1 - y
        back = at // 2 + 1
        other = (at >= 0) & (lax.rem(at + 2, 2) == 1)
        source = jnp.where(at >= 0, place - 2 * back + jnp.where(other, 1 - 2 * y, 0), place - step)

        @pl.when((step == 1) & (y == 1))
        def _():
            send_kv(place - 1, 1).wait_recv()
            pl.when((z == 0) & (z < last))(lambda: send_half(1).start())

        pl.when(at == 0)(lambda: take_column(1))

        @pl.when(other)
        def _():
            take_column(back + 1)
            pl.when(source > 0)(lambda: send_kv(source, 1).wait_recv())

            @pl.when(source == 0)
            def _():
                send_half(1).wait_recv()
                pl.when(z < last)(lambda: send_half(1).start())
                send_half(0).wait_recv()

        visit(source)
        return carry

    lax.fori_loop(0, 1 + y + 2 * z, attend, 0)
    for h, here in enumerate(columns):
        total = r.total[:, here]
        o = r.ot[:, here] * (1.0 / total)
        r.lse[:, here] = jnp.log2(total)
        r.ot[:, here] = o
        r.ob[:, h * head : (h + 1) * head] = bf16(o).T

    loads["w_out"].wait()
    r.ap[...] = dot(r.ob[:, 0:joined], r.w_out[...])
    for t in tiles:
        ap = r.ap[t, :]
        x1 = f32(r.x[t, :]) + ap * inverse_rms(ap) * gain_attn
        r.x1[t, :] = x1
        r.m[t, :] = bf16(x1 * inverse_rms(x1) * gain_pre)
    loads["w_gate"].wait()
    loads["w_up"].wait()
    block = hidden // 8

    def quarters(body):
        def both(pair, carry):
            for quarter in (2 * pair, 2 * pair + 1):
                body(pl.ds(pl.multiple_of(quarter * 2 * block, 128), 2 * block))
            return carry

        lax.fori_loop(0, 2, both, 0)

    def feed(cols):
        gate = dot(r.m[...], r.w_pair[0, :, cols])
        up = dot(r.m[...], r.w_pair[1, :, cols])
        inner = 0.7978845608028654 * (gate + 0.044715 * gate * gate * gate)
        th = jnp.tanh(inner)
        cdf = 0.5 * (1.0 + th)
        act = gate * cdf
        slope = cdf + 0.5 * gate * (1.0 - th * th) * 0.7978845608028654 * (1.0 + 3 * 0.044715 * gate * gate)
        r.hid[:, cols] = bf16(act * up)
        r.side_gate[:, cols] = bf16(slope * up)
        r.side_up[:, cols] = bf16(act)

    quarters(feed)
    loads["w_down"].wait()
    loads["dy"].wait()
    r.wide[...] = dot(r.hid[...], r.w_down[...])
    r.gains[...] = jnp.zeros_like(r.gains)

    def gain(k, terms):
        r.gains[k, :, 0 : terms.shape[1]] = r.gains[k, :, 0 : terms.shape[1]] + terms

    for t in tiles:
        f = r.wide[t, :]
        inverse = inverse_rms(f)
        r.out[t, :] = bf16(r.x1[t, :] + f * inverse * gain_post)
        df, g = rms_back(f, inverse, gain_post, f32(r.dy[t, :]))
        r.df[t, :] = bf16(df)
        gain(3, g)
    def two_blocks(body):
        def both(pair, carry):
            for j in (2 * pair, 2 * pair + 1):
                body(j, pl.ds(pl.multiple_of(j * block, 128), block))
            return carry

        lax.fori_loop(0, 4, both, 0)

    def down_grad(j, cols):
        r.g_down[j] = bf16(dot_tn(r.hid[:, cols], r.df[...]))

    two_blocks(down_grad)

    chunks = []
    sems = (r.red_send, r.red_recv, r.red_local)
    for name, count in r_plan(sizes):
        grad, total = r["g_" + name], r["t_" + name]
        step = grad.shape[1] // count
        for i in range(count):
            number, kind = len(chunks), FIRST[len(chunks)]
            make, first = (LineChunk, {"u": "x", "v": "y"}[kind]) if kind in "uv" else (Chunk, kind)
            landing = tuple(r[f"land{k}_{number}"] for k in range(len(make.landing(step))))
            chunks.append(make(number, grad, total, i * step, step, first, landing, sems, me, peers, z_count))

    def side_grads(part):
        def one(cols):
            dh = dot_nt(r.df[...], r.w_down[cols, :])
            r.side_gate[:, cols] = bf16(dh * f32(r.side_gate[:, cols]))
            r.side_up[:, cols] = bf16(dh * f32(r.side_up[:, cols]))

        quarters(one)

    def feed_grads(part):
        grad, side = ((r.g_gate, r.side_gate), (r.g_up, r.side_up))[part]

        def one(j, cols):
            grad[j] = bf16(dot_tn(r.m[...], side[:, cols]))

        two_blocks(one)

    def middle_back(part):
        r.wide[...] = dot_nt(r.side_gate[...], r.w_pair[0]) + dot_nt(r.side_up[...], r.w_pair[1])
        for t in tiles:
            x1 = r.x1[t, :]
            dx1, g = rms_back(x1, inverse_rms(x1), gain_pre, r.wide[t, :])
            gain(2, g)
            dx1 = dx1 + f32(r.dy[t, :])
            r.x1[t, :] = dx1
            ap = r.ap[t, :]
            dap, g = rms_back(ap, inverse_rms(ap), gain_attn, dx1)
            gain(1, g)
            r.dap[t, :] = bf16(dap)

    def out_back(part):
        for h, here in enumerate(columns):
            wide = slice(h * head, (h + 1) * head)
            g = bf16(dot_tn(r.ob[:, wide], r.dap[...]))
            r.g_out[2 * h] = g[0:half]
            r.g_out[2 * h + 1] = g[half:head]
            do = bf16(dot_nt(r.dap[...], r.w_out[wide, :]))
            r.do[here, :] = do
            turned = do.T
            r.dot[:, here] = turned
            r.delta[:, here] = jnp.sum(f32(turned) * r.ot[:, here], axis=0, keepdims=True)
        r.ot[...] = jnp.zeros_like(r.ot)

    probs, dscores = r.hid.at[:, 0 : heads * rows], r.side_gate.at[:, 0 : heads * rows]

    def visit_back(source, target):
        kt = r.kv[source, :, 0:head].T
        mask = allowed(source)
        for here in columns:
            s = dot(r.kv[source, :, 0:head], r.qt[:, here])
            p = jnp.where(mask, jnp.exp2(s - r.lse[:, here]), 0.0)
            dp = dot(r.kv[source, :, head : 2 * head], r.dot[:, here])
            probs[:, here] = bf16(p)
            dscores[:, here] = bf16(p * (dp - r.delta[:, here]))
        target[:, 0:head] = bf16(dot(dscores[...], r.q[...]))
        target[:, head : 2 * head] = bf16(dot(probs[...], r.do[...]))
        for here in columns:
            r.ot[:, here] = r.ot[:, here] + dot(kt, dscores[:, here])

    def staged(own, row):
        return r.w_pair.at[own, 0:rows, row * 2 * head : (row + 1) * 2 * head]

    def to_partner(row):
        return pltpu.make_async_remote_copy(
            src_ref=staged(0, row),
            dst_ref=r.from_partner.at[row],
            send_sem=r.dkv_send.at[0, row],
            recv_sem=r.dkv_recv.at[0, row],
            device_id=peers["y"],
            device_id_type=MESH,
        )

    def to_below(row):
        return pltpu.make_async_remote_copy(
            src_ref=staged(1, row),
            dst_ref=r.from_above.at[row],
            send_sem=r.dkv_send.at[1, row],
            recv_sem=r.dkv_recv.at[1, row],
            device_id=peers["down"],
            device_id_type=MESH,
        )

    def visit_row(row):
        def one(own, carry):
            column = jnp.where(own == 1, y, 1 - y)

            @pl.when((row < z) | ((row == z) & (column <= y)))
            def _():
                visit_back(2 * row + column, staged(own, row))
                pl.when(own == 0)(lambda: to_partner(row).start())

            return carry

        lax.fori_loop(0, 2, one, 0)

    def pass_down(row):
        @pl.when(row < z)
        def _():
            to_partner(row).wait_recv()
            pl.when(z < last)(lambda: to_below(row).wait_recv())
            for t in tiles:
                value = f32(staged(1, row)[t, :]) + f32(r.from_partner[row, t, :])
                above = jnp.where(z < last, f32(r.from_above[row, t, :]), 0.0)
                staged(1, row)[t, :] = bf16(value + above)
            to_below(row).start()

    def queries_back(h):
        wide = slice(h * head, (h + 1) * head)
        for t in tiles:
            dq = (r.ot[:, h * rows + t.start : h * rows + t.stop] * scale).T
            qp = r.qp[t, wide]
            dqp, g = rms_back(qp, inverse_rms(qp), gain_q, turn_back(dq, r.cosine[t, :], r.sine[t, :]))
            gain(4, g)
            r.ob[t, wide] = bf16(dqp)

    def query_grad(part):
        for h in range(heads):
            g = bf16(dot_tn(r.a[...], r.ob[:, h * head : (h + 1) * head]))
            r.g_query[2 * h] = g[:, 0:half]
            r.g_query[2 * h + 1] = g[:, half:head]

    def own_total(part):
        for row in range(z_count):

            @pl.when(row == z)
            def _():
                pl.when(y == 0)(lambda: to_partner(row).wait_recv())
                pl.when(z < last)(lambda: to_below(row).wait_recv())
                for t in tiles:
                    beside = jnp.where(y == 0, f32(r.from_partner[row, t, :]), 0.0)
                    above = jnp.where(z < last, f32(r.from_above[row, t, :]), 0.0)
                    r.dkv[t, :] = f32(staged(1, row)[t, :]) + beside + above

    def keys_back(part):
        for t in tiles:
            dk = r.dkv[t, 0:head] * LN2
            kp = r.kp[t, :]
            dkp, g = rms_back(kp, inverse_rms(kp), gain_k, turn_back(dk, r.cosine[t, :], r.sine[t, :]))
            gain(5, g)
            r.ob[t, wide_k] = bf16(dkp)
            r.ob[t, wide_v] = bf16(r.dkv[t, head : 2 * head])
        low = width // 2
        g = bf16(dot_tn(r.a[...], r.ob[:, joined : joined + 2 * head]))
        for p in range(8):
            which, upper, side = p // 4, (p // 2) % 2, p % 2
            left = which * head + side * half
            r.g_kv[p] = g[upper * low : (upper + 1) * low, left : left + half]
        r.wide[...] = dot_nt(r.ob[...], r.w_first[...])
        for t in tiles:
            x = f32(r.x[t, :])
            dx, g = rms_back(x, inverse_rms(x), gain_in, r.wide[t, :])
            gain(0, g)
            r.dx[t, :] = bf16(r.x1[t, :] + dx)
        r.g_gain[...] = jnp.zeros_like(r.g_gain)
        at = 0
        for k, size in enumerate((width, width, width, width, head, head)):
            g = jnp.sum(r.gains[k], axis=0, keepdims=True)
            for part in range(size // 128):
                r.g_gain[at // 16, at % 16 : at % 16 + 1, :] = g[:, part * 128 : (part + 1) * 128]
                at += 1

    work = {
        "S": side_grads,
        "F": feed_grads,
        "M": middle_back,
        "O": out_back,
        "V": visit_row,
        "P": pass_down,
        "Q": queries_back,
        "G": query_grad,
        "T": own_total,
        "K": keys_back,
    }
    for what, step in schedule:
        if what in work:
            work[what](step)
        else:
            chunks[what].tick(step)

    pl.when(z < last)(lambda: send_kv(place, 0).wait_send())
    pl.when(y == 0)(lambda: send_kv(place, 1).wait_send())
    pl.when((y == 1) & (z < last))(lambda: send_half(1).wait_send())
    pl.when((y == 0) & (z > 0))(lambda: send_half(0).wait_send())
    for back in range(1, z_count):

        @pl.when(back <= z)
        def _():
            mine = place - 2 * back
            pl.when(z < last)(lambda: send_kv(mine, 0).wait_send())
            pl.when(mine > 0)(lambda: send_kv(mine, 1).wait_send())

    for row in range(z_count):
        pl.when((row < z) | ((row == z) & (y == 1)))(lambda: to_partner(row).wait_send())
        pl.when(row < z)(lambda: to_below(row).wait_send())


def r_plan(sizes):
    return list(zip(("down", "gate", "up", "out", "query", "kv", "gain"), PIECES, strict=True))


def gradient_shapes(sizes):
    rows, width, hidden, heads, head, z_count = sizes
    joined, half = heads * head, head // 2
    return {
        "down": ((8, hidden // 8, width), (8, hidden // 8, width)),
        "gate": ((8, width, hidden // 8), (width, hidden)),
        "up": ((8, width, hidden // 8), (width, hidden)),
        "out": ((8, joined // 8, width), (8, joined // 8, width)),
        "query": ((8, width, joined // 8), (width, joined)),
        "kv": ((8, width // 2, half), (2, 2, width // 2, head)),
        "gain": ((8, 16, 128), (8, 16, 128)),
    }


def layer_scratch(sizes):
    rows, width, hidden, heads, head, z_count = sizes
    joined = heads * head
    low, wide = jnp.bfloat16, jnp.float32
    arrays = {
        "x": ((rows, width), low),
        "w_first": ((width, joined + 2 * head), low),
        "w_out": ((joined, width), low),
        "w_pair": ((2, width, hidden), low),
        "w_down": ((hidden, width), low),
        "dy": ((rows, width), low),
        "a": ((rows, width), low),
        "gains": ((6, 8, width), wide),
        "kp": ((rows, head), wide),
        "kv": ((2 * z_count, rows, 2 * head), low),
        "qp": ((rows, joined), wide),
        "q": ((heads * rows, head), low),
        "qt": ((head, heads * rows), low),
        "cosine": ((rows, head // 2), wide),
        "sine": ((rows, head // 2), wide),
        "wide": ((rows, width), wide),
        "ot": ((head, heads * rows), wide),
        "total": ((1, heads * rows), wide),
        "lse": ((1, heads * rows), wide),
        "delta": ((1, heads * rows), wide),
        "ob": ((rows, joined + 2 * head), low),
        "ap": ((rows, width), wide),
        "x1": ((rows, width), wide),
        "m": ((rows, width), low),
        "hid": ((rows, hidden), low),
        "side_gate": ((rows, hidden), low),
        "side_up": ((rows, hidden), low),
        "df": ((rows, width), low),
        "dap": ((rows, width), low),
        "do": ((heads * rows, head), low),
        "dot": ((head, heads * rows), low),
        "dkv": ((rows, 2 * head), wide),
        "from_partner": ((z_count, rows, 2 * head), low),
        "from_above": ((z_count, rows, 2 * head), low),
    }
    shapes = gradient_shapes(sizes)
    pieces = 0
    for name, count in r_plan(sizes):
        (eight, high, columns), kind = shapes[name][0], wide if name == "gain" else low
        step = high // count
        pieces += count
        arrays["g_" + name] = (shapes[name][0], kind)
        for number in range(pieces - count, pieces):
            for k, shape in enumerate(LineChunk.landing(step) if FIRST[number] in "uv" else Chunk.landing(step)):
                arrays[f"land{k}_{number}"] = (shape + (columns,), kind)
    sems = {
        "load_sem": (9,),
        "kv_send": (2, 2 * z_count),
        "kv_recv": (2 * z_count,),
        "half_send": (2,),
        "half_recv": (2,),
        "dkv_send": (2, z_count),
        "dkv_recv": (2, z_count),
        "red_send": (pieces, STAGES),
        "red_recv": (pieces, STAGES),
        "red_local": (pieces,),
    }
    return arrays, sems


def layer_bytes(sizes):
    total = 0
    for shape, kind in layer_scratch(sizes)[0].values():
        size = jnp.dtype(kind).itemsize
        for n in shape[:-2]:
            size *= n
        total += size * max(shape[-2], 8) * max(shape[-1], 128)
    return total


VMEM_BYTES = 64 * 2**20


def widen_kernel(count, *refs):
    ins, table, both, tokens = refs[: count - 2], refs[count - 2], refs[count - 1], refs[count : count + 2]
    refs = refs[count + 2 :]
    outs, gains, tokens_out = refs[:count], refs[count : count + 6], refs[count + 6 : count + 8]
    refs = refs[count + 8 :]
    narrow, broad, (came, gone) = refs[: count + 2], refs[count + 2 : 2 * count + 2], refs[2 * count + 2 :]
    ins = (both.at[0], both.at[1]) + ins + tokens
    outs = outs + tokens_out
    loads = [pltpu.make_async_copy(ins[i], narrow[i], came.at[i]) for i in range(count + 2)]
    stores = [pltpu.make_async_copy((broad + narrow[count:])[i], outs[i], gone.at[i]) for i in range(count + 2)]
    for item in loads:
        item.start()
    at = 0
    for gain in gains:
        for part in range(gain.shape[0] // 128):
            gain[part * 128 : (part + 1) * 128] = table[at // 16, at % 16, :]
            at += 1
    for i in range(count):
        loads[i].wait()

        def body(j, carry):
            here = pl.ds(pl.multiple_of(j * 32, 32), 32)
            broad[i][here, :] = f32(narrow[i][here, :])
            return carry

        lax.fori_loop(0, narrow[i].shape[0] // 32, body, 0)
        stores[i].start()
    for i in (count, count + 1):
        loads[i].wait()
        stores[i].start()
    for item in stores:
        item.wait()


def widen(both, matrices, table, tokens, gain_sizes):
    count = len(matrices) + 2
    shapes = [both.shape[1:]] * 2 + [v.shape for v in matrices]
    anywhere, vmem = pl.BlockSpec(memory_space=pl.ANY), pl.BlockSpec(memory_space=pltpu.VMEM)
    return pl.pallas_call(
        functools.partial(widen_kernel, count),
        out_shape=tuple(jax.ShapeDtypeStruct(shape, jnp.float32) for shape in shapes)
        + tuple(jax.ShapeDtypeStruct((n,), jnp.float32) for n in gain_sizes)
        + tuple(jax.ShapeDtypeStruct(v.shape, v.dtype) for v in tokens),
        in_specs=[anywhere] * len(matrices) + [vmem] + [anywhere] * 3,
        out_specs=tuple([anywhere] * count + [vmem] * len(gain_sizes) + [anywhere] * 2),
        scratch_shapes=[pltpu.VMEM(shape, jnp.bfloat16) for shape in shapes + [v.shape for v in tokens]]
        + [pltpu.VMEM(shape, jnp.float32) for shape in shapes]
        + [pltpu.SemaphoreType.DMA((count + 2,))] * 2,
        compiler_params=pltpu.CompilerParams(vmem_limit_bytes=VMEM_BYTES),
    )(*matrices, table, both, *tokens)


def whole_layer(sizes, tokens, lengths, cotangent, norm_in, w_query, w_key, w_value, query_gain, key_gain, w_out, norm_attn, norm_pre, w_gate, w_up, w_down, norm_post):
    rows, width, hidden, heads, head, z_count = sizes
    joined = heads * head
    inputs = {
        "lengths": lengths,
        "norm_in": norm_in,
        "query_gain": query_gain,
        "key_gain": key_gain,
        "norm_attn": norm_attn,
        "norm_pre": norm_pre,
        "norm_post": norm_post,
        "x_in": tokens[0],
        "w_key_in": w_key,
        "w_value_in": w_value,
        "w_query_in": w_query,
        "w_out_in": w_out,
        "w_gate_in": w_gate,
        "w_up_in": w_up,
        "w_down_in": w_down,
        "dy_in": cotangent[0],
    }
    spaces = {name: pltpu.SMEM if name == "lengths" else pl.ANY if name.endswith("_in") and name != "norm_in" else pltpu.VMEM for name in inputs}
    shapes = gradient_shapes(sizes)
    outputs = {"out": (rows, width), "dx": (rows, width)}
    outputs.update({"t_" + name: shapes[name][1] for name in shapes})
    arrays, sems = layer_scratch(sizes)
    names = list(inputs) + list(outputs) + list(arrays) + list(sems)
    results = pl.pallas_call(
        functools.partial(layer_kernel, sizes, SCHEDULES[z_count], names),
        out_shape=tuple(
            jax.ShapeDtypeStruct(shape, jnp.float32 if name == "t_gain" else jnp.bfloat16) for name, shape in outputs.items()
        ),
        in_specs=[pl.BlockSpec(memory_space=spaces[name]) for name in inputs],
        out_specs=tuple(
            pl.BlockSpec(memory_space=pl.ANY if name.startswith("t_") else pltpu.VMEM) for name in outputs
        ),
        scratch_shapes=[pltpu.VMEM(*item) for item in arrays.values()]
        + [pltpu.SemaphoreType.DMA(item) for item in sems.values()],
        compiler_params=pltpu.CompilerParams(
            collective_id=1, has_side_effects=True, vmem_limit_bytes=VMEM_BYTES
        ),
    )(*inputs.values())
    r = Names(zip(outputs, results, strict=True))
    matrices = [
        r.t_query,
        r.t_out.reshape(joined, width),
        r.t_gate,
        r.t_up,
        r.t_down.reshape(hidden, width),
    ]
    both = r.t_kv.reshape(2, width, head)
    sums = widen(both, matrices, r.t_gain, (r.out, r.dx), (width, width, width, width, head, head))
    g_key, g_value, g_query, g_out, g_gate, g_up, g_down = sums[:7]
    g_in, g_attn, g_pre, g_post, g_qgain, g_kgain, output, input_grad = sums[7:]
    return (
        output[None],
        input_grad[None],
        g_in,
        g_query,
        g_key,
        g_value,
        g_qgain,
        g_kgain,
        g_out,
        g_attn,
        g_pre,
        g_gate,
        g_up,
        g_down,
        g_post,
    )


def per_device(
    tokens,
    lengths,
    cotangent,
    norm_in,
    w_query,
    w_key,
    w_value,
    query_gain,
    key_gain,
    w_out,
    norm_attn,
    norm_pre,
    w_gate,
    w_up,
    w_down,
    norm_post,
):
    rows = tokens.shape[1]
    head = query_gain.shape[0]
    heads = w_query.shape[1] // head
    sizes = (rows, tokens.shape[2], w_gate.shape[1], heads, head, lax.axis_size(BLOCKS) // 2)
    if sizes[-1] in SCHEDULES and layer_bytes(sizes) <= VMEM_BYTES:
        return whole_layer(
            sizes,
            tokens,
            lengths,
            cotangent,
            norm_in,
            w_query,
            w_key,
            w_value,
            query_gain,
            key_gain,
            w_out,
            norm_attn,
            norm_pre,
            w_gate,
            w_up,
            w_down,
            norm_post,
        )
    scale = head ** (-0.5)
    count = lax.axis_size(BLOCKS)
    place = lax.axis_index(BLOCKS)
    row = lengths[0]
    local_idx = place * rows + jnp.arange(rows, dtype=jnp.int32)
    seg_q, pos_q = segment_of(local_idx, row)
    cosine, sine = rotary_tables(pos_q, head)

    def block_mask(source):
        key_idx = source * rows + jnp.arange(rows, dtype=jnp.int32)
        seg_k, unused = segment_of(key_idx, row)
        return (seg_q[:, None] == seg_k[None, :]) & (local_idx[:, None] >= key_idx[None, :])

    x_in = tokens[0].astype(jnp.float32)
    normal_a = normed(x_in, norm_in).astype(jnp.bfloat16)
    q_proj = jnp.dot(normal_a, w_query, preferred_element_type=jnp.float32).reshape(
        rows, heads, head
    )
    k_proj = jnp.dot(normal_a, w_key, preferred_element_type=jnp.float32)
    v_proj = jnp.dot(normal_a, w_value, preferred_element_type=jnp.float32)
    query = prepare(q_proj, query_gain, cosine[:, None, :], sine[:, None, :]).astype(jnp.bfloat16)
    keys = prepare(k_proj, key_gain, cosine, sine).astype(jnp.bfloat16)
    values = v_proj.astype(jnp.bfloat16)
    q_heads = jnp.transpose(query, (1, 0, 2))

    def absorb(state, pair, source):
        allowed = block_mask(source)
        big, total, accum = state
        raw = jnp.einsum("hqd,kd->hqk", q_heads, pair[0], preferred_element_type=jnp.float32)
        scores = jnp.where(allowed[None], scale * raw, NEG)
        big_new = jnp.maximum(big, jnp.max(scores, axis=-1, keepdims=True))
        expo = jnp.where(allowed[None], jnp.exp(scores - big_new), 0.0)
        fade = jnp.exp(big - big_new)
        total = total * fade + jnp.sum(expo, axis=-1, keepdims=True)
        accum = accum * fade + jnp.einsum(
            "hqk,kd->hqd", expo.astype(jnp.bfloat16), pair[1], preferred_element_type=jnp.float32
        )
        return (big_new, total, accum)

    pair = jnp.stack([keys, values])
    state = (
        jnp.full((heads, rows, 1), NEG, jnp.float32),
        jnp.zeros((heads, rows, 1), jnp.float32),
        jnp.zeros((heads, rows, head), jnp.float32),
    )
    state = absorb(state, pair, place)

    def cycle_forward(step, carry):
        inner, moving = carry
        moving = from_behind(moving, BLOCKS, 1)
        return (absorb(inner, moving, (place - step) % count), moving)

    state, unused_pair = lax.fori_loop(1, count, cycle_forward, (state, pair))
    big, total, accum = state
    attended = accum / total
    lse = big + jnp.log(total)
    joined = jnp.transpose(attended, (1, 0, 2)).reshape(rows, heads * head).astype(jnp.bfloat16)
    a_proj = jnp.dot(joined, w_out, preferred_element_type=jnp.float32)
    x_mid = x_in + normed(a_proj, norm_attn)
    mixed = normed(x_mid, norm_pre).astype(jnp.bfloat16)
    gate = jnp.dot(mixed, w_gate, preferred_element_type=jnp.float32)
    upper = jnp.dot(mixed, w_up, preferred_element_type=jnp.float32)

    def activate(gate_in, upper_in):
        return jax.nn.gelu(gate_in, approximate=True) * upper_in

    hidden = activate(gate, upper).astype(jnp.bfloat16)
    f_proj = jnp.dot(hidden, w_down, preferred_element_type=jnp.float32)
    output = x_mid + normed(f_proj, norm_post)
    grad_y = cotangent[0].astype(jnp.float32)
    d_fproj, g_post = normed_back(f_proj, norm_post, grad_y)
    d_fproj = d_fproj.astype(jnp.bfloat16)
    g_down = dot_tn(hidden, d_fproj)
    d_hidden = dot_nt(d_fproj, w_down)
    d_gate, d_upper = jax.vjp(activate, gate, upper)[1](d_hidden)
    d_gate = d_gate.astype(jnp.bfloat16)
    d_upper = d_upper.astype(jnp.bfloat16)
    g_gate = dot_tn(mixed, d_gate)
    g_up = dot_tn(mixed, d_upper)
    d_mixed = dot_nt(d_gate, w_gate) + dot_nt(d_upper, w_up)
    d_mid, g_pre = normed_back(x_mid, norm_pre, d_mixed)
    d_mid = grad_y + d_mid
    d_aproj, g_attn = normed_back(a_proj, norm_attn, d_mid)
    d_aproj = d_aproj.astype(jnp.bfloat16)
    g_out = dot_tn(joined, d_aproj)
    d_joined = dot_nt(d_aproj, w_out).astype(
        jnp.bfloat16
    )
    do_heads = jnp.transpose(d_joined.reshape(rows, heads, head), (1, 0, 2))
    delta = jnp.sum(do_heads.astype(jnp.float32) * attended, axis=-1, keepdims=True)

    def visit(d_query, moving, grads, source):
        allowed = block_mask(source)
        raw = jnp.einsum("hqd,kd->hqk", q_heads, moving[0], preferred_element_type=jnp.float32)
        probs = jnp.where(allowed[None], jnp.exp(scale * raw - lse), 0.0)
        dv_add = jnp.einsum(
            "hqk,hqd->kd", probs.astype(jnp.bfloat16), do_heads, preferred_element_type=jnp.float32
        )
        d_probs = jnp.einsum("hqd,kd->hqk", do_heads, moving[1], preferred_element_type=jnp.float32)
        d_scores = (scale * probs * (d_probs - delta)).astype(jnp.bfloat16)
        dq_add = jnp.einsum("hqk,kd->hqd", d_scores, moving[0], preferred_element_type=jnp.float32)
        dk_add = jnp.einsum("hqk,hqd->kd", d_scores, q_heads, preferred_element_type=jnp.float32)
        return (d_query + dq_add, grads + jnp.stack([dk_add, dv_add]))

    d_query = jnp.zeros((heads, rows, head), jnp.float32)
    grads = jnp.zeros((2, rows, head), jnp.float32)
    d_query, grads = visit(d_query, pair, grads, place)

    def cycle_backward(step, carry):
        dq_in, moving, grads_in = carry
        moving = from_behind(moving, BLOCKS, 1)
        grads_in = pass_home(grads_in)
        dq_in, grads_in = visit(dq_in, moving, grads_in, (place - step) % count)
        return (dq_in, moving, grads_in)

    d_query, unused_pair, grads = lax.fori_loop(1, count, cycle_backward, (d_query, pair, grads))
    grads = pass_home(grads)

    def query_piece(proj, gain):
        return prepare(proj, gain, cosine[:, None, :], sine[:, None, :])

    def key_piece(proj, gain):
        return prepare(proj, gain, cosine, sine)

    d_qproj, g_qgain = jax.vjp(query_piece, q_proj, query_gain)[1](
        jnp.transpose(d_query, (1, 0, 2))
    )
    d_kproj, g_kgain = jax.vjp(key_piece, k_proj, key_gain)[1](grads[0])
    d_qproj = d_qproj.reshape(rows, heads * head).astype(jnp.bfloat16)
    d_kproj = d_kproj.astype(jnp.bfloat16)
    d_vproj = grads[1].astype(jnp.bfloat16)
    g_query = dot_tn(normal_a, d_qproj)
    g_key = dot_tn(normal_a, d_kproj)
    g_value = dot_tn(normal_a, d_vproj)
    d_normal = dot_nt(d_qproj, w_query)
    d_normal = d_normal + dot_nt(d_kproj, w_key)
    d_normal = d_normal + dot_nt(d_vproj, w_value)
    d_input, g_in = normed_back(x_in, norm_in, d_normal)
    input_grad = (d_mid + d_input).astype(jnp.bfloat16)
    (
        g_in,
        g_query,
        g_key,
        g_value,
        g_qgain,
        g_kgain,
        g_out,
        g_attn,
        g_pre,
        g_gate,
        g_up,
        g_down,
        g_post,
    ) = sum_gradients(
        (
            g_in,
            g_query,
            g_key,
            g_value,
            g_qgain,
            g_kgain,
            g_out,
            g_attn,
            g_pre,
            g_gate,
            g_up,
            g_down,
            g_post,
        )
    )
    return (
        output.astype(jnp.bfloat16)[None],
        input_grad[None],
        g_in,
        g_query,
        g_key,
        g_value,
        g_qgain,
        g_kgain,
        g_out,
        g_attn,
        g_pre,
        g_gate,
        g_up,
        g_down,
        g_post,
    )


def solution(mesh):
    in_specs = (
        P(PARTS, BLOCKS, None),
        P(PARTS, None),
        P(PARTS, BLOCKS, None),
        P(),
        P(),
        P(),
        P(),
        P(),
        P(),
        P(),
        P(),
        P(),
        P(),
        P(),
        P(),
        P(),
    )
    out_specs = (
        P(PARTS, BLOCKS, None),
        P(PARTS, BLOCKS, None),
        P(),
        P(),
        P(),
        P(),
        P(),
        P(),
        P(),
        P(),
        P(),
        P(),
        P(),
        P(),
        P(),
    )
    return jax.shard_map(
        per_device, mesh=mesh, in_specs=in_specs, out_specs=out_specs, check_vma=False
    )
```

```python
import functools

import jax
import jax.numpy as jnp
from jax import lax
from jax.experimental import pallas as pl
from jax.experimental.pallas import tpu as pltpu
from jax.sharding import PartitionSpec as P

BLOCKS, PARTS = "blk", "dp"
EPS = 1e-06
BASE = 1000000.0
NEG = -1e30


def shifted(array, axis, by):
    peers = lax.axis_size(axis)
    return lax.ppermute(array, axis, [(i, (i + by) % peers) for i in range(peers)])


def from_behind(block, axis, distance):
    devices = range(lax.axis_size(axis))
    route = [(i - distance, i) for i in devices if i - distance in devices]
    return lax.ppermute(block, axis, route)


def normed(value, gain):
    return value * lax.rsqrt(jnp.mean(value * value, axis=-1, keepdims=True) + EPS) * gain


def normed_back(value, gain, grad):
    return jax.vjp(normed, value, gain)[1](grad)


def segment_of(index, row):
    ends = jnp.cumsum(row)
    seg = jnp.sum((index[:, None] >= ends[None, :]).astype(jnp.int32), axis=1)
    starts = ends - row
    slots = jnp.arange(row.shape[0], dtype=jnp.int32)
    begin = jnp.sum(jnp.where(slots[None, :] == seg[:, None], starts[None, :], 0), axis=1)
    return (seg, index - begin)


def rotary_tables(places, head):
    half = head // 2
    freq = jnp.exp(-(2.0 * jnp.arange(half, dtype=jnp.float32) / head) * jnp.log(BASE))
    angle = places.astype(jnp.float32)[:, None] * freq[None, :]
    return (jnp.cos(angle), jnp.sin(angle))


def prepare(proj, gain, cosine, sine):
    value = normed(proj, gain)
    half = value.shape[-1] // 2
    first = value[..., :half]
    second = value[..., half:]
    return jnp.concatenate(
        [first * cosine - second * sine, second * cosine + first * sine], axis=-1
    )


def pass_home(grads):
    return shifted(grads.astype(jnp.bfloat16), BLOCKS, 1).astype(grads.dtype)


MESH = pl.DeviceIdType.MESH


def where_am_i():
    place = lax.axis_index(BLOCKS)
    part = lax.axis_index(PARTS)
    return {
        "z": place // 2,
        "y": lax.rem(place, 2),
        "x": part // 2,
        "core": lax.rem(part, 2),
        "place": place,
        "part": part,
    }


def peers_of(me):
    place, part = me["place"], me["part"]
    return {
        "core": {BLOCKS: place, PARTS: part + 1 - 2 * me["core"]},
        "x": {BLOCKS: place, PARTS: part + 2 - 4 * me["x"]},
        "y": {BLOCKS: place + 1 - 2 * me["y"], PARTS: part},
        "up": {BLOCKS: place + 2, PARTS: part},
        "down": {BLOCKS: place - 2, PARTS: part},
    }


def greet(me, peers, z_count):
    barrier = pltpu.get_barrier_semaphore()
    for name in ("core", "x", "y"):
        pl.semaphore_signal(barrier, inc=1, device_id=peers[name], device_id_type=MESH)

    @pl.when(me["z"] < z_count - 1)
    def _():
        pl.semaphore_signal(barrier, inc=1, device_id=peers["up"], device_id_type=MESH)

    @pl.when(me["z"] > 0)
    def _():
        pl.semaphore_signal(barrier, inc=1, device_id=peers["down"], device_id_type=MESH)


def meet(me, z_count):
    ends = (me["z"] == 0).astype(jnp.int32) + (me["z"] == z_count - 1).astype(jnp.int32)
    pl.semaphore_wait(pltpu.get_barrier_semaphore(), 5 - ends)


def add_into(target, start, row, extra, count, rows):
    step = rows if rows < 32 else 16
    for candidate in (160, 128, 80, 64, 48, 32):
        if rows % candidate == 0:
            step = candidate
            break

    def body(index, carry):
        e = index // (rows // step)
        at = pl.multiple_of(lax.rem(index, rows // step) * step, 8)
        here = pl.ds(pl.multiple_of(row + at, 8), step)
        target[start + e, here, :] = target[start + e, here, :] + extra[e, pl.ds(at, step), :]
        return carry

    lax.fori_loop(0, count * (rows // step), body, 0)


STAGES = 10


class Chunk:
    def __init__(self, number, grad, total, row, rows, first, landing, sems, me, peers, z_count):
        self.grad, self.total, self.row, self.rows = grad, total, row, rows
        self.first, self.second = ("x", "y") if first == "x" else ("y", "x")
        self.land0, self.land1, self.land2 = landing
        self.send, self.recv, self.local = sems
        self.number, self.me, self.peers, self.z_count = number, me, peers, z_count
        self.b1, self.b2, self.core = me[self.first], me[self.second], me["core"]
        self.quad = 4 * self.core
        self.pair = self.quad + 2 * self.b1
        self.own = self.pair + self.b2
        self.half = rows // 2

    @staticmethod
    def landing(rows):
        return ((4, rows), (2, rows), (1, 2 * rows))

    def piece(self, start, count, upper=None):
        if upper is None:
            return self.grad.at[pl.ds(start, count), pl.ds(self.row, self.rows), :]
        row = self.row if upper else self.row + self.half
        return self.grad.at[pl.ds(start, count), pl.ds(row, self.half), :]

    def spot(self, count, upper=None):
        row, rows = self.row, self.rows
        if upper is not None:
            row, rows = (row if upper else row + self.half), self.half
        here, columns = pl.ds(row, rows), self.grad.shape[2]
        start = {1: self.own, 2: self.pair, 4: self.quad}[count]
        if len(self.total.shape) == 2:
            return self.total.at[here, pl.ds(pl.multiple_of(start * columns, 128), count * columns)]
        if len(self.total.shape) == 4:
            if count == 4:
                return self.total.at[self.core, :, here, :]
            if count == 2:
                return self.total.at[self.core, self.b1, here, :]
            return self.total.at[self.core, self.b1, here, pl.ds(pl.multiple_of(self.b2 * columns, 128), columns)]
        if count == 1:
            return self.total.at[start, here, :]
        return self.total.at[pl.ds(start, count), here, :]

    def mine(self, upper):
        return self.grad.at[self.own, pl.ds(self.row if upper else self.row + self.half, self.half), :]

    def keep(self, upper):
        return pltpu.make_async_copy(
            self.mine(upper), self.spot(1, upper), self.local.at[self.number]
        )

    def copy(self, stage, peer, source, target):
        return pltpu.make_async_remote_copy(
            src_ref=source,
            dst_ref=target,
            send_sem=self.send.at[self.number, stage],
            recv_sem=self.recv.at[self.number, stage],
            device_id=self.peers[peer],
            device_id_type=MESH,
        )

    def reduce_up(self):
        return self.copy(3, "up", self.piece(self.own, 1, True), self.land2.at[:, pl.ds(self.rows, self.half), :])

    def reduce_down(self):
        return self.copy(4, "down", self.piece(self.own, 1, False), self.land2.at[:, pl.ds(self.rows + self.half, self.half), :])

    def spread_down(self, fresh=False):
        here = self.spot(1, True)
        return self.copy(5, "down", self.mine(True) if fresh else here, here)

    def spread_up(self, fresh=False):
        here = self.spot(1, False)
        return self.copy(6, "up", self.mine(False) if fresh else here, here)

    def step0(self):
        return self.copy(0, "core", self.piece(4 - self.quad, 4), self.land0)

    def step1(self):
        return self.copy(1, self.first, self.piece(self.quad + 2 - 2 * self.b1, 2), self.land1)

    def step2(self):
        return self.copy(2, self.second, self.piece(self.pair + 1 - self.b2, 1), self.land2.at[:, pl.ds(0, self.rows), :])

    def gather(self, stage):
        count, peer = ((1, self.second), (2, self.first), (4, "core"))[stage - 7]
        here = self.spot(count)
        return self.copy(stage, peer, here, here)

    def arrive_upper(self):
        z, last = self.me["z"], self.z_count - 1

        @pl.when(z > 0)
        def _():
            self.reduce_up().wait_recv()
            add_into(self.grad, self.own, self.row, self.land2.at[:, pl.ds(self.rows, self.half), :], 1, self.half)

            @pl.when(z < last)
            def _():
                self.reduce_up().start()

            @pl.when(z == last)
            def _():
                self.spread_down(True).start()
                self.keep(True).start()

    def arrive_lower(self):
        z, last = self.me["z"], self.z_count - 1

        @pl.when(z < last)
        def _():
            self.reduce_down().wait_recv()
            add_into(self.grad, self.own, self.row + self.half, self.land2.at[:, pl.ds(self.rows + self.half, self.half), :], 1, self.half)

            @pl.when(z > 0)
            def _():
                self.reduce_down().start()

            @pl.when(z == 0)
            def _():
                self.spread_up(True).start()
                self.keep(False).start()

    def back_upper(self):
        z, last = self.me["z"], self.z_count - 1

        @pl.when(z < last)
        def _():
            self.spread_down().wait_recv()

            @pl.when(z > 0)
            def _():
                self.spread_down().start()

    def back_lower(self):
        z, last = self.me["z"], self.z_count - 1

        @pl.when(z > 0)
        def _():
            self.spread_up().wait_recv()

            @pl.when(z < last)
            def _():
                self.spread_up().start()

    def tick(self, op):
        z, last = self.me["z"], self.z_count - 1
        if op == 0:
            self.step0().start()
        elif op == 1:
            self.step0().wait_recv()
            add_into(self.grad, self.quad, self.row, self.land0, 4, self.rows)
            self.step1().start()
        elif op == 2:
            self.step1().wait_recv()
            add_into(self.grad, self.pair, self.row, self.land1, 2, self.rows)
            self.step2().start()
        elif op == 3:
            self.step2().wait_recv()
            add_into(self.grad, self.own, self.row, self.land2, 1, self.rows)

            @pl.when(z == 0)
            def _():
                self.reduce_up().start()

            @pl.when(z == last)
            def _():
                self.reduce_down().start()

        elif op == 4:
            pl.when((z > 0) & (2 * z < self.z_count))(self.arrive_upper)
            pl.when((z < last) & (2 * z >= self.z_count))(self.arrive_lower)
        elif op == 5:
            pl.when((z < last) & (2 * z >= self.z_count))(self.arrive_upper)
            pl.when((z > 0) & (2 * z < self.z_count))(self.arrive_lower)
        elif op == 6:
            pl.when(z == last)(self.arrive_upper)
            pl.when(z == 0)(self.arrive_lower)
        elif op == 7:
            pl.when((z < last) & (2 * z >= self.z_count))(self.back_upper)
            pl.when((z > 0) & (2 * z < self.z_count))(self.back_lower)
        elif op == 8:

            @pl.when((z > 0) & (2 * z < self.z_count))
            def _():
                self.back_upper()
                self.gather(7).start()

            @pl.when((z < last) & (2 * z >= self.z_count))
            def _():
                self.back_lower()
                self.gather(7).start()

        elif op == 9:

            @pl.when(z == 0)
            def _():
                self.back_upper()
                self.keep(False).wait()
                self.gather(7).start()

            @pl.when(z == last)
            def _():
                self.back_lower()
                self.keep(True).wait()
                self.gather(7).start()

        elif op == 10:
            self.gather(7).wait_recv()
            self.gather(8).start()
        elif op == 11:
            self.gather(8).wait_recv()
            self.gather(9).start()
        elif op == 12:
            self.gather(9).wait_recv()
            self.drain()

    OPS = 13

    def drain(self):
        z, last = self.me["z"], self.z_count - 1
        self.step0().wait_send()
        self.step1().wait_send()
        self.step2().wait_send()
        for stage in (7, 8, 9):
            self.gather(stage).wait_send()

        @pl.when(z < last)
        def _():
            self.reduce_up().wait_send()
            self.spread_up().wait_send()

        @pl.when(z > 0)
        def _():
            self.reduce_down().wait_send()
            self.spread_down().wait_send()


class LineChunk(Chunk):
    def __init__(self, *args):
        super().__init__(*args[:6], (args[6][0], None, None), *args[7:])
        self.ups, self.downs, self.small = args[6][1:]
        self.entry = self.quad + self.me["z"]
        self.half, self.quarter = self.rows // 2, self.rows // 4
        self.mine_half = pl.multiple_of(self.row + self.b1 * self.half, 16)
        self.mine_quarter = pl.multiple_of(self.mine_half + self.b2 * self.quarter, 16)

    @staticmethod
    def landing(rows):
        return ((4, rows), (3, rows), (3, rows), (1, rows))

    def across(self, stage, name, first, count):
        landing = self.ups if name == "up" else self.downs
        return self.copy(stage, name, self.piece(self.quad + first, count), landing.at[pl.ds(0, count)])

    def back(self, stage, name, first, count):
        here = self.place(self.quad + first, count, self.row, self.rows)
        return self.copy(stage, name, here, here)

    def place(self, start, count, row, rows):
        here, columns = pl.ds(row, rows), self.grad.shape[2]
        if len(self.total.shape) == 2:
            return self.total.at[here, pl.ds(pl.multiple_of(start * columns, 128), count * columns)]
        if count == 1:
            return self.total.at[start, here, :]
        return self.total.at[pl.ds(start, count), here, :]

    def part(self, row, rows):
        return self.grad.at[pl.ds(self.entry, 1), pl.ds(row, rows), :]

    def step1(self):
        other = pl.multiple_of(self.row + (1 - self.b1) * self.half, 16)
        return self.copy(1, self.first, self.part(other, self.half), self.small.at[:, pl.ds(0, self.half), :])

    def step2(self):
        other = pl.multiple_of(self.mine_half + (1 - self.b2) * self.quarter, 16)
        landing = self.small.at[:, pl.ds(self.half, self.quarter), :]
        return self.copy(2, self.second, self.part(other, self.quarter), landing)

    def finished(self):
        return self.grad.at[self.entry, pl.ds(self.mine_quarter, self.quarter), :]

    def keep(self):
        spot = self.place(self.entry, 1, self.mine_quarter, self.quarter)
        return pltpu.make_async_copy(self.finished(), spot, self.local.at[self.number])

    def gather2(self):
        spot = self.place(self.entry, 1, self.mine_quarter, self.quarter)
        return self.copy(7, self.second, self.finished(), spot)

    def gather1(self):
        here = self.place(self.entry, 1, self.mine_half, self.half)
        return self.copy(8, self.first, here, here)

    def gather0(self):
        here = self.place(self.quad, 4, self.row, self.rows)
        return self.copy(9, "core", here, here)

    def at_row(self, k, body):
        pl.when(self.me["z"] == k)(body)

    def from_below(self, k):
        return (k, self.z_count - k)

    def from_above(self, k):
        return (0, k + 1)

    def take_up(self, k):
        first, count = self.from_below(k)
        self.across(3, "up", first, count).wait_recv()
        add_into(self.grad, self.quad + first, self.row, self.ups, count, self.rows)
        if k < self.z_count - 1:
            self.across(3, "up", first + 1, count - 1).start()

    def take_down(self, k):
        first, count = self.from_above(k)
        self.across(4, "down", first, count).wait_recv()
        add_into(self.grad, self.quad + first, self.row, self.downs, count, self.rows)
        if k > 0:
            self.across(4, "down", first, count - 1).start()

    def back_up(self, k):
        self.back(6, "up", 0, k).wait_recv()
        if k < self.z_count - 1:
            self.back(6, "up", 0, k + 1).start()

    def back_down(self, k):
        last = self.z_count - 1
        self.back(5, "down", k + 1, last - k).wait_recv()
        if k > 0:
            self.back(5, "down", k, last - k + 1).start()

    def tick(self, op):
        last, middle = self.z_count - 1, self.z_count // 2
        if op == 0:
            self.step0().start()
        elif op == 1:
            self.step0().wait_recv()
            add_into(self.grad, self.quad, self.row, self.land0, 4, self.rows)
            self.at_row(0, lambda: self.across(3, "up", 1, last).start())
            self.at_row(last, lambda: self.across(4, "down", 0, last).start())
        elif op == 2:
            for k in range(1, last):
                self.at_row(k, functools.partial(self.take_up if k < middle else self.take_down, k))
        elif op == 3:
            for k in range(1, last):

                def arrive(k=k):
                    (self.take_down if k < middle else self.take_up)(k)
                    self.step1().start()

                self.at_row(k, arrive)
        elif op == 4:

            def bottom():
                self.take_down(0)
                self.step1().start()

            def top():
                self.take_up(last)
                self.step1().start()

            self.at_row(0, bottom)
            self.at_row(last, top)
        elif op == 5:
            self.step1().wait_recv()
            add_into(self.grad, self.entry, self.mine_half, self.small, 1, self.half)
            self.step2().start()
        elif op == 6:
            self.step2().wait_recv()
            landing = self.small.at[:, pl.ds(self.half, self.quarter), :]
            add_into(self.grad, self.entry, self.mine_quarter, landing, 1, self.quarter)
            self.keep().start()
            self.gather2().start()
        elif op == 7:
            self.gather2().wait_recv()
            self.keep().wait()
            self.gather1().start()
        elif op == 8:
            self.gather1().wait_recv()
            self.at_row(0, lambda: self.back(6, "up", 0, 1).start())
            self.at_row(last, lambda: self.back(5, "down", last, 1).start())
        elif op == 9:
            for k in range(1, last):
                self.at_row(k, functools.partial(self.back_up if k < middle else self.back_down, k))
        elif op == 10:
            for k in range(1, last):

                def complete(k=k):
                    (self.back_down if k < middle else self.back_up)(k)
                    self.gather0().start()

                self.at_row(k, complete)
        elif op == 11:

            def bottom():
                self.back_down(0)
                self.gather0().start()

            def top():
                self.back_up(last)
                self.gather0().start()

            self.at_row(0, bottom)
            self.at_row(last, top)
        elif op == 12:
            self.gather0().wait_recv()
            self.drain()

    def drain(self):
        last = self.z_count - 1
        for item in (self.step0(), self.step1(), self.step2(), self.gather2(), self.gather1(), self.gather0()):
            item.wait_send()
        for k in range(self.z_count):

            def sent(k=k):
                if k < last:
                    self.across(3, "up", k + 1, last - k).wait_send()
                    self.back(6, "up", 0, k + 1).wait_send()
                if k > 0:
                    self.across(4, "down", 0, k).wait_send()
                    self.back(5, "down", k, last - k + 1).wait_send()

            self.at_row(k, sent)


def sum_kernel(z_count, plan, *refs):
    n = 1 + max(item[0] for item in plan)
    parts = len(plan)
    ins, outs = refs[:n], refs[n : 2 * n]
    rest = refs[2 * n :]
    grads, rest = rest[:n], rest[n:]
    landings = rest[: 3 * parts]
    send, recv, local, load = rest[3 * parts :]
    me = where_am_i()
    peers = peers_of(me)
    loads = [pltpu.make_async_copy(ins[i], grads[i], load.at[i]) for i in range(n)]
    for item in loads:
        item.start()
    greet(me, peers, z_count)
    meet(me, z_count)
    for item in loads:
        item.wait()
    chunks = []
    for number, (i, row, rows, first) in enumerate(plan):
        landing = landings[3 * number : 3 * number + 3]
        chunks.append(
            Chunk(number, grads[i], outs[i], row, rows, first, landing, (send, recv, local), me, peers, z_count)
        )
    for at in range(parts + Chunk.OPS - 1):
        for number in range(parts):
            if 0 <= at - number < Chunk.OPS:
                chunks[number].tick(at - number)


def sum_call(arrays, plan, z_count):
    landing = []
    for i, row, rows, first in plan:
        columns, kind = arrays[i].shape[2], arrays[i].dtype
        landing += [
            pltpu.VMEM((4, rows, columns), kind),
            pltpu.VMEM((2, rows, columns), kind),
            pltpu.VMEM((1, 2 * rows, columns), kind),
        ]
    n = len(arrays)
    return pl.pallas_call(
        functools.partial(sum_kernel, z_count, plan),
        out_shape=tuple(jax.ShapeDtypeStruct(v.shape, v.dtype) for v in arrays),
        in_specs=[pl.BlockSpec(memory_space=pl.ANY)] * n,
        out_specs=tuple([pl.BlockSpec(memory_space=pl.ANY)] * n),
        scratch_shapes=[pltpu.VMEM(v.shape, v.dtype) for v in arrays]
        + landing
        + [
            pltpu.SemaphoreType.DMA((len(plan), STAGES)),
            pltpu.SemaphoreType.DMA((len(plan), STAGES)),
            pltpu.SemaphoreType.DMA((len(plan),)),
            pltpu.SemaphoreType.DMA((n,)),
        ],
        compiler_params=pltpu.CompilerParams(
            collective_id=0, has_side_effects=True, vmem_limit_bytes=56 * 2**20
        ),
    )(*arrays)


def columns_to_panels(value):
    rows, columns = value.shape
    return jnp.transpose(value.reshape(rows, 8, columns // 8), (1, 0, 2)).astype(jnp.bfloat16)


def panels_to_columns(panels):
    count, rows, width = panels.shape
    return jnp.transpose(panels.astype(jnp.float32), (1, 0, 2)).reshape(rows, count * width)


def sum_gradients(grads):
    (g_in, g_query, g_key, g_value, g_qgain, g_kgain, g_out, g_attn, g_pre, g_gate, g_up, g_down, g_post) = grads
    z_count = lax.axis_size(BLOCKS) // 2
    width = g_in.shape[0]
    gains = [g_in, g_attn, g_pre, g_post, g_qgain, g_kgain]
    sizes = [v.shape[0] for v in gains]
    flat = jnp.concatenate(gains)
    gain_rows = 32
    flat = jnp.pad(flat, (0, 8 * gain_rows * 128 - flat.shape[0])).reshape(8, gain_rows, 128)
    down = g_down.astype(jnp.bfloat16).reshape(8, -1, width)
    out = g_out.astype(jnp.bfloat16).reshape(8, -1, width)
    both = jnp.stack([g_key, g_value])
    head = g_key.shape[1]
    both = jnp.transpose(both.reshape(2, 2, width // 2, 2, head // 2), (0, 1, 3, 2, 4)).reshape(8, width // 2, head // 2)
    arrays = [down, columns_to_panels(g_gate), columns_to_panels(g_up), out, columns_to_panels(g_query), both.astype(jnp.bfloat16), flat]
    plan = []
    for i, v in enumerate(arrays[:-1]):
        rows = v.shape[1] // 2
        plan += [(i, 0, rows, "x"), (i, rows, rows, "y")]
    plan.append((6, 0, gain_rows, "x"))
    down, gate, up, out, query, both, flat = sum_call(arrays, plan, z_count)
    both = jnp.transpose(both.astype(jnp.float32).reshape(2, 2, 2, width // 2, head // 2), (0, 1, 3, 2, 4)).reshape(2, width, head)
    flat = flat.reshape(-1)
    cuts, at = [], 0
    for size in sizes:
        cuts.append(flat[at : at + size])
        at += size
    g_in, g_attn, g_pre, g_post, g_qgain, g_kgain = cuts
    return (
        g_in,
        panels_to_columns(query),
        both[0],
        both[1],
        g_qgain,
        g_kgain,
        out.astype(jnp.float32).reshape(g_out.shape),
        g_attn,
        g_pre,
        panels_to_columns(gate),
        panels_to_columns(up),
        down.astype(jnp.float32).reshape(g_down.shape),
        g_post,
    )


LOG2E = 1.4426950408889634
LN2 = 0.6931471805599453
PIECES = (2, 2, 2, 2, 2, 2, 1)
FIRST = ['y', 'y', 'x', 'v', 'x', 'y', 'x', 'x', 'x', 'y', 'x', 'y', 'y']
SCHEDULES = {
    4: (
        (1, 0), (0, 0), ("S", 0), ("F", 0), (1, 1), ("F", 1), (4, 0), ("M", 0), (4, 1), (3, 0), (0, 1), ("O", 0), (1, 2), (3, 1), ("V", 0), (0, 2),
        (4, 2), (2, 0), (7, 0), (5, 0), ("V", 1), (3, 2), (1, 3), (6, 0), (0, 3), ("V", 2), (2, 1), (5, 1), (0, 4), (1, 4), (4, 3), (4, 4), (7, 1),
        (1, 5), (0, 5), (4, 5), (6, 1), (3, 3), ("P", 0), ("P", 1), ("V", 3), (0, 6), (1, 6), ("P", 2), ("Q", 0), ("Q", 1), (7, 2), (4, 6), (5, 2),
        ("Q", 2), (1, 7), ("Q", 3), (6, 2), (3, 4), ("G", 0), (0, 7), (8, 0), (1, 8), (2, 2), (9, 0), (5, 3), ("T", 0), (8, 1), (4, 7), (7, 3),
        ("K", 0), (4, 8), (1, 9), (0, 8), (5, 4), (10, 0), (6, 3), (7, 4), (9, 1), (12, 0), (3, 5), (8, 2), (6, 4), (5, 5), (7, 5), (2, 3), (10, 1),
        (11, 0), (6, 5), (12, 1), (2, 4), (3, 6), (11, 1), (9, 2), (10, 2), (5, 6), (12, 2), (7, 6), (4, 9), (6, 6), (5, 7), (3, 7), (2, 5), (1, 10),
        (11, 2), (6, 7), (12, 3), (8, 3), (0, 9), (7, 7), (12, 4), (8, 4), (10, 3), (9, 3), (5, 8), (10, 4), (9, 4), (11, 3), (4, 10), (2, 6),
        (11, 4), (7, 8), (3, 8), (6, 8), (8, 5), (5, 9), (12, 5), (10, 5), (7, 9), (6, 9), (11, 5), (8, 6), (9, 5), (0, 10), (12, 6), (2, 7), (11, 6),
        (12, 7), (10, 6), (8, 7), (10, 7), (9, 6), (7, 10), (11, 7), (9, 7), (3, 9), (6, 10), (8, 8), (1, 11), (10, 8), (2, 8), (8, 9), (2, 9),
        (12, 8), (12, 9), (10, 9), (9, 8), (11, 8), (9, 9), (5, 10), (7, 11), (11, 9), (4, 11), (12, 10), (8, 10), (3, 10), (0, 11), (11, 10),
        (7, 12), (10, 10), (2, 10), (4, 12), (9, 10), (6, 11), (8, 11), (10, 11), (5, 11), (12, 11), (11, 11), (8, 12), (3, 11), (2, 11), (12, 12),
        (11, 12), (9, 11), (1, 12), (2, 12), (0, 12), (5, 12), (3, 12), (9, 12), (6, 12), (10, 12),
    )
}


def dot(left, right):
    return jnp.dot(left, right, preferred_element_type=jnp.float32)


def dot_nt(left, right):
    return lax.dot_general(left, right, (((1,), (1,)), ((), ())), preferred_element_type=jnp.float32)


def inverse_rms(value):
    return lax.rsqrt(jnp.mean(value * value, axis=-1, keepdims=True) + EPS)


def rms_back(value, inverse, gain, grad):
    scaled = grad * gain
    normal = value * inverse
    mean = jnp.mean(scaled * normal, axis=-1, keepdims=True)
    terms = grad * normal
    return inverse * (scaled - normal * mean), jnp.sum(terms.reshape(-1, 8, terms.shape[-1]), axis=0)


def turn(value, cosine, sine):
    half = value.shape[-1] // 2
    first, second = value[:, :half], value[:, half:]
    return jnp.concatenate([first * cosine - second * sine, second * cosine + first * sine], axis=-1)


def turn_back(grad, cosine, sine):
    half = grad.shape[-1] // 2
    first, second = grad[:, :half], grad[:, half:]
    return jnp.concatenate([first * cosine + second * sine, second * cosine - first * sine], axis=-1)


def dot_tn(left, right):
    return lax.dot_general(left, right, (((0,), (0,)), ((), ())), preferred_element_type=jnp.float32)


def bf16(value):
    return value.astype(jnp.bfloat16)


def f32(value):
    return value.astype(jnp.float32)


class Names(dict):
    __getattr__ = dict.__getitem__


def layer_kernel(sizes, schedule, names, *refs):
    r = Names(zip(names, refs, strict=True))
    rows, width, hidden, heads, head, z_count = sizes
    scale = head**-0.5
    tile = 128
    tiles = [slice(at, at + tile) for at in range(0, rows, tile)]
    half = head // 2
    me = where_am_i()
    peers = peers_of(me)
    z, y, place = me["z"], me["y"], me["place"]
    last = z_count - 1

    weights = ["x", "w_key", "w_value", "w_query", "w_out", "w_gate", "w_up", "w_down", "dy"]
    joined = heads * head
    wide_k, wide_v = slice(joined, joined + head), slice(joined + head, joined + 2 * head)
    spots = {"w_query": slice(0, joined), "w_key": wide_k, "w_value": wide_v}
    pair = ("w_gate", "w_up")
    loads = {}
    for i, name in enumerate(weights):
        if name in spots:
            spot = r.w_first.at[:, spots[name]]
        elif name in pair:
            spot = r.w_pair.at[pair.index(name)]
        else:
            spot = r[name]
        loads[name] = pltpu.make_async_copy(r[name + "_in"], spot, r.load_sem.at[i])
    early = ("x", "w_key", "w_value")
    for name in early:
        loads[name].start()
    greet(me, peers, z_count)

    def begins(token):
        begin, end = jnp.zeros_like(token), jnp.int32(0)
        for j in range(r.lengths.shape[1]):
            end = end + r.lengths[0, j]
            begin = jnp.where(token >= end, end, begin)
        return begin

    token = place * rows + lax.broadcasted_iota(jnp.int32, (1, rows), 1)
    begin = begins(token)
    entry = f32(lax.broadcasted_iota(jnp.int32, (1, half), 1))
    speed = jnp.exp(-(2.0 * entry / head) * jnp.log(BASE))
    for t in tiles:
        column = place * rows + t.start + lax.broadcasted_iota(jnp.int32, (tile, 1), 0)
        angle = f32(column - begins(column)) * speed
        r.cosine[t, :] = jnp.cos(angle)
        r.sine[t, :] = jnp.sin(angle)
    gain_in = r.norm_in[...].reshape(1, width)
    gain_q = r.query_gain[...].reshape(1, head)
    gain_k = r.key_gain[...].reshape(1, head)
    gain_attn = r.norm_attn[...].reshape(1, width)
    gain_pre = r.norm_pre[...].reshape(1, width)
    gain_post = r.norm_post[...].reshape(1, width)

    def allowed(source):
        key = source * rows + lax.broadcasted_iota(jnp.int32, (rows, rows), 0)
        return (key >= begin) & (key <= token)

    loads["x"].wait()
    loads["w_key"].wait()
    loads["w_value"].wait()
    for name in weights:
        if name not in early:
            loads[name].start()
    for t in tiles:
        x = f32(r.x[t, :])
        r.a[t, :] = bf16(x * inverse_rms(x) * gain_in)
    r.kp[...] = dot(r.a[...], r.w_first[:, wide_k])
    r.kv[place, :, head : 2 * head] = bf16(dot(r.a[...], r.w_first[:, wide_v]))
    for t in tiles:
        kp = r.kp[t, :]
        r.kv[place, t, 0:head] = bf16(turn(kp * inverse_rms(kp) * gain_k, r.cosine[t, :], r.sine[t, :]))

    def send_kv(source, route):
        return pltpu.make_async_remote_copy(
            src_ref=r.kv.at[source],
            dst_ref=r.kv.at[source],
            send_sem=r.kv_send.at[route, source],
            recv_sem=r.kv_recv.at[source],
            device_id=peers["y"] if route else peers["up"],
            device_id_type=MESH,
        )

    def send_half(values):
        half_block = r.kv.at[0, :, head * values : head * (values + 1)]
        return pltpu.make_async_remote_copy(
            src_ref=half_block,
            dst_ref=half_block,
            send_sem=r.half_send.at[values],
            recv_sem=r.half_recv.at[values],
            device_id=peers["up"] if values else peers["y"],
            device_id_type=MESH,
        )

    meet(me, z_count)
    pl.when(z < last)(lambda: send_kv(place, 0).start())
    pl.when(y == 0)(lambda: send_kv(place, 1).start())

    loads["w_query"].wait()
    for h in range(heads):
        wide = slice(h * head, (h + 1) * head)
        r.qp[:, wide] = dot(r.a[...], r.w_first[:, wide])
        for t in tiles:
            qp = r.qp[t, wide]
            q = turn(qp * inverse_rms(qp) * gain_q, r.cosine[t, :], r.sine[t, :])
            q = bf16(q * (scale * LOG2E))
            r.q[h * rows + t.start : h * rows + t.stop, :] = q
            r.qt[:, h * rows + t.start : h * rows + t.stop] = q.T

    columns = [slice(h * rows, (h + 1) * rows) for h in range(heads)]

    def visit(source):
        vt = r.kv[source, :, head : 2 * head].T
        mask = allowed(source)
        for here in columns:
            p = jnp.where(mask, jnp.exp2(dot(r.kv[source, :, 0:head], r.qt[:, here])), 0.0)
            total = jnp.sum(p, axis=0, keepdims=True)
            o = dot(vt, bf16(p))
            r.total[:, here] = r.total[:, here] + total
            r.ot[:, here] = r.ot[:, here] + o

    r.total[...] = jnp.zeros_like(r.total)
    r.ot[...] = jnp.zeros_like(r.ot)

    def take_column(back):
        mine = place - 2 * back

        @pl.when(back <= z)
        def _():
            send_kv(mine, 0).wait_recv()
            pl.when(z < last)(lambda: send_kv(mine, 0).start())
            pl.when(mine > 0)(lambda: send_kv(mine, 1).start())
            pl.when(mine == 0)(lambda: send_half(0).start())

    def attend(step, carry):
        at = step - 1 - y
        back = at // 2 + 1
        other = (at >= 0) & (lax.rem(at + 2, 2) == 1)
        source = jnp.where(at >= 0, place - 2 * back + jnp.where(other, 1 - 2 * y, 0), place - step)

        @pl.when((step == 1) & (y == 1))
        def _():
            send_kv(place - 1, 1).wait_recv()
            pl.when((z == 0) & (z < last))(lambda: send_half(1).start())

        pl.when(at == 0)(lambda: take_column(1))

        @pl.when(other)
        def _():
            take_column(back + 1)
            pl.when(source > 0)(lambda: send_kv(source, 1).wait_recv())

            @pl.when(source == 0)
            def _():
                send_half(1).wait_recv()
                pl.when(z < last)(lambda: send_half(1).start())
                send_half(0).wait_recv()

        visit(source)
        return carry

    lax.fori_loop(0, 1 + y + 2 * z, attend, 0)
    for h, here in enumerate(columns):
        total = r.total[:, here]
        o = r.ot[:, here] * (1.0 / total)
        r.lse[:, here] = jnp.log2(total)
        r.ot[:, here] = o
        r.ob[:, h * head : (h + 1) * head] = bf16(o).T

    loads["w_out"].wait()
    r.ap[...] = dot(r.ob[:, 0:joined], r.w_out[...])
    for t in tiles:
        ap = r.ap[t, :]
        x1 = f32(r.x[t, :]) + ap * inverse_rms(ap) * gain_attn
        r.x1[t, :] = x1
        r.m[t, :] = bf16(x1 * inverse_rms(x1) * gain_pre)
    loads["w_gate"].wait()
    loads["w_up"].wait()
    block = hidden // 8

    def quarters(body):
        def both(pair, carry):
            for quarter in (2 * pair, 2 * pair + 1):
                body(pl.ds(pl.multiple_of(quarter * 2 * block, 128), 2 * block))
            return carry

        lax.fori_loop(0, 2, both, 0)

    def feed(cols):
        gate = dot(r.m[...], r.w_pair[0, :, cols])
        up = dot(r.m[...], r.w_pair[1, :, cols])
        inner = 0.7978845608028654 * (gate + 0.044715 * gate * gate * gate)
        th = jnp.tanh(inner)
        cdf = 0.5 * (1.0 + th)
        act = gate * cdf
        slope = cdf + 0.5 * gate * (1.0 - th * th) * 0.7978845608028654 * (1.0 + 3 * 0.044715 * gate * gate)
        r.hid[:, cols] = bf16(act * up)
        r.side_gate[:, cols] = bf16(slope * up)
        r.side_up[:, cols] = bf16(act)

    quarters(feed)
    loads["w_down"].wait()
    loads["dy"].wait()
    r.wide[...] = dot(r.hid[...], r.w_down[...])
    r.gains[...] = jnp.zeros_like(r.gains)

    def gain(k, terms):
        r.gains[k, :, 0 : terms.shape[1]] = r.gains[k, :, 0 : terms.shape[1]] + terms

    for t in tiles:
        f = r.wide[t, :]
        inverse = inverse_rms(f)
        r.out[t, :] = bf16(r.x1[t, :] + f * inverse * gain_post)
        df, g = rms_back(f, inverse, gain_post, f32(r.dy[t, :]))
        r.df[t, :] = bf16(df)
        gain(3, g)
    def two_blocks(body):
        def both(pair, carry):
            for j in (2 * pair, 2 * pair + 1):
                body(j, pl.ds(pl.multiple_of(j * block, 128), block))
            return carry

        lax.fori_loop(0, 4, both, 0)

    def down_grad(j, cols):
        r.g_down[j] = bf16(dot_tn(r.hid[:, cols], r.df[...]))

    two_blocks(down_grad)

    chunks = []
    sems = (r.red_send, r.red_recv, r.red_local)
    for name, count in r_plan(sizes):
        grad, total = r["g_" + name], r["t_" + name]
        step = grad.shape[1] // count
        for i in range(count):
            number, kind = len(chunks), FIRST[len(chunks)]
            make, first = (LineChunk, {"u": "x", "v": "y"}[kind]) if kind in "uv" else (Chunk, kind)
            landing = tuple(r[f"land{k}_{number}"] for k in range(len(make.landing(step))))
            chunks.append(make(number, grad, total, i * step, step, first, landing, sems, me, peers, z_count))

    def side_grads(part):
        def one(cols):
            dh = dot_nt(r.df[...], r.w_down[cols, :])
            r.side_gate[:, cols] = bf16(dh * f32(r.side_gate[:, cols]))
            r.side_up[:, cols] = bf16(dh * f32(r.side_up[:, cols]))

        quarters(one)

    def feed_grads(part):
        grad, side = ((r.g_gate, r.side_gate), (r.g_up, r.side_up))[part]

        def one(j, cols):
            grad[j] = bf16(dot_tn(r.m[...], side[:, cols]))

        two_blocks(one)

    def middle_back(part):
        r.wide[...] = dot_nt(r.side_gate[...], r.w_pair[0]) + dot_nt(r.side_up[...], r.w_pair[1])
        for t in tiles:
            x1 = r.x1[t, :]
            dx1, g = rms_back(x1, inverse_rms(x1), gain_pre, r.wide[t, :])
            gain(2, g)
            dx1 = dx1 + f32(r.dy[t, :])
            r.x1[t, :] = dx1
            ap = r.ap[t, :]
            dap, g = rms_back(ap, inverse_rms(ap), gain_attn, dx1)
            gain(1, g)
            r.dap[t, :] = bf16(dap)

    def out_back(part):
        for h, here in enumerate(columns):
            wide = slice(h * head, (h + 1) * head)
            g = bf16(dot_tn(r.ob[:, wide], r.dap[...]))
            r.g_out[2 * h] = g[0:half]
            r.g_out[2 * h + 1] = g[half:head]
            do = bf16(dot_nt(r.dap[...], r.w_out[wide, :]))
            r.do[here, :] = do
            turned = do.T
            r.dot[:, here] = turned
            r.delta[:, here] = jnp.sum(f32(turned) * r.ot[:, here], axis=0, keepdims=True)
        r.ot[...] = jnp.zeros_like(r.ot)

    probs, dscores = r.hid.at[:, 0 : heads * rows], r.side_gate.at[:, 0 : heads * rows]

    def visit_back(source, target):
        kt = r.kv[source, :, 0:head].T
        mask = allowed(source)
        for here in columns:
            s = dot(r.kv[source, :, 0:head], r.qt[:, here])
            p = jnp.where(mask, jnp.exp2(s - r.lse[:, here]), 0.0)
            dp = dot(r.kv[source, :, head : 2 * head], r.dot[:, here])
            probs[:, here] = bf16(p)
            dscores[:, here] = bf16(p * (dp - r.delta[:, here]))
        target[:, 0:head] = bf16(dot(dscores[...], r.q[...]))
        target[:, head : 2 * head] = bf16(dot(probs[...], r.do[...]))
        for here in columns:
            r.ot[:, here] = r.ot[:, here] + dot(kt, dscores[:, here])

    def staged(own, row):
        return r.w_pair.at[own, 0:rows, row * 2 * head : (row + 1) * 2 * head]

    def to_partner(row):
        return pltpu.make_async_remote_copy(
            src_ref=staged(0, row),
            dst_ref=r.from_partner.at[row],
            send_sem=r.dkv_send.at[0, row],
            recv_sem=r.dkv_recv.at[0, row],
            device_id=peers["y"],
            device_id_type=MESH,
        )

    def to_below(row):
        return pltpu.make_async_remote_copy(
            src_ref=staged(1, row),
            dst_ref=r.from_above.at[row],
            send_sem=r.dkv_send.at[1, row],
            recv_sem=r.dkv_recv.at[1, row],
            device_id=peers["down"],
            device_id_type=MESH,
        )

    def visit_row(row):
        def one(own, carry):
            column = jnp.where(own == 1, y, 1 - y)

            @pl.when((row < z) | ((row == z) & (column <= y)))
            def _():
                visit_back(2 * row + column, staged(own, row))
                pl.when(own == 0)(lambda: to_partner(row).start())

            return carry

        lax.fori_loop(0, 2, one, 0)

    def pass_down(row):
        @pl.when(row < z)
        def _():
            to_partner(row).wait_recv()
            pl.when(z < last)(lambda: to_below(row).wait_recv())
            for t in tiles:
                value = f32(staged(1, row)[t, :]) + f32(r.from_partner[row, t, :])
                above = jnp.where(z < last, f32(r.from_above[row, t, :]), 0.0)
                staged(1, row)[t, :] = bf16(value + above)
            to_below(row).start()

    def queries_back(h):
        wide = slice(h * head, (h + 1) * head)
        for t in tiles:
            dq = (r.ot[:, h * rows + t.start : h * rows + t.stop] * scale).T
            qp = r.qp[t, wide]
            dqp, g = rms_back(qp, inverse_rms(qp), gain_q, turn_back(dq, r.cosine[t, :], r.sine[t, :]))
            gain(4, g)
            r.ob[t, wide] = bf16(dqp)

    def query_grad(part):
        for h in range(heads):
            g = bf16(dot_tn(r.a[...], r.ob[:, h * head : (h + 1) * head]))
            r.g_query[2 * h] = g[:, 0:half]
            r.g_query[2 * h + 1] = g[:, half:head]

    def own_total(part):
        for row in range(z_count):

            @pl.when(row == z)
            def _():
                pl.when(y == 0)(lambda: to_partner(row).wait_recv())
                pl.when(z < last)(lambda: to_below(row).wait_recv())
                for t in tiles:
                    beside = jnp.where(y == 0, f32(r.from_partner[row, t, :]), 0.0)
                    above = jnp.where(z < last, f32(r.from_above[row, t, :]), 0.0)
                    r.dkv[t, :] = f32(staged(1, row)[t, :]) + beside + above

    def keys_back(part):
        for t in tiles:
            dk = r.dkv[t, 0:head] * LN2
            kp = r.kp[t, :]
            dkp, g = rms_back(kp, inverse_rms(kp), gain_k, turn_back(dk, r.cosine[t, :], r.sine[t, :]))
            gain(5, g)
            r.ob[t, wide_k] = bf16(dkp)
            r.ob[t, wide_v] = bf16(r.dkv[t, head : 2 * head])
        low = width // 2
        g = bf16(dot_tn(r.a[...], r.ob[:, joined : joined + 2 * head]))
        for p in range(8):
            which, upper, side = p // 4, (p // 2) % 2, p % 2
            left = which * head + side * half
            r.g_kv[p] = g[upper * low : (upper + 1) * low, left : left + half]
        r.wide[...] = dot_nt(r.ob[...], r.w_first[...])
        for t in tiles:
            x = f32(r.x[t, :])
            dx, g = rms_back(x, inverse_rms(x), gain_in, r.wide[t, :])
            gain(0, g)
            r.dx[t, :] = bf16(r.x1[t, :] + dx)
        r.g_gain[...] = jnp.zeros_like(r.g_gain)
        at = 0
        for k, size in enumerate((width, width, width, width, head, head)):
            g = jnp.sum(r.gains[k], axis=0, keepdims=True)
            for part in range(size // 128):
                r.g_gain[at // 16, at % 16 : at % 16 + 1, :] = g[:, part * 128 : (part + 1) * 128]
                at += 1

    work = {
        "S": side_grads,
        "F": feed_grads,
        "M": middle_back,
        "O": out_back,
        "V": visit_row,
        "P": pass_down,
        "Q": queries_back,
        "G": query_grad,
        "T": own_total,
        "K": keys_back,
    }
    for what, step in schedule:
        if what in work:
            work[what](step)
        else:
            chunks[what].tick(step)

    pl.when(z < last)(lambda: send_kv(place, 0).wait_send())
    pl.when(y == 0)(lambda: send_kv(place, 1).wait_send())
    pl.when((y == 1) & (z < last))(lambda: send_half(1).wait_send())
    pl.when((y == 0) & (z > 0))(lambda: send_half(0).wait_send())
    for back in range(1, z_count):

        @pl.when(back <= z)
        def _():
            mine = place - 2 * back
            pl.when(z < last)(lambda: send_kv(mine, 0).wait_send())
            pl.when(mine > 0)(lambda: send_kv(mine, 1).wait_send())

    for row in range(z_count):
        pl.when((row < z) | ((row == z) & (y == 1)))(lambda: to_partner(row).wait_send())
        pl.when(row < z)(lambda: to_below(row).wait_send())


def r_plan(sizes):
    return list(zip(("down", "gate", "up", "out", "query", "kv", "gain"), PIECES, strict=True))


def gradient_shapes(sizes):
    rows, width, hidden, heads, head, z_count = sizes
    joined, half = heads * head, head // 2
    return {
        "down": ((8, hidden // 8, width), (8, hidden // 8, width)),
        "gate": ((8, width, hidden // 8), (width, hidden)),
        "up": ((8, width, hidden // 8), (width, hidden)),
        "out": ((8, joined // 8, width), (8, joined // 8, width)),
        "query": ((8, width, joined // 8), (width, joined)),
        "kv": ((8, width // 2, half), (2, 2, width // 2, head)),
        "gain": ((8, 16, 128), (8, 16, 128)),
    }


def layer_scratch(sizes):
    rows, width, hidden, heads, head, z_count = sizes
    joined = heads * head
    low, wide = jnp.bfloat16, jnp.float32
    arrays = {
        "x": ((rows, width), low),
        "w_first": ((width, joined + 2 * head), low),
        "w_out": ((joined, width), low),
        "w_pair": ((2, width, hidden), low),
        "w_down": ((hidden, width), low),
        "dy": ((rows, width), low),
        "a": ((rows, width), low),
        "gains": ((6, 8, width), wide),
        "kp": ((rows, head), wide),
        "kv": ((2 * z_count, rows, 2 * head), low),
        "qp": ((rows, joined), wide),
        "q": ((heads * rows, head), low),
        "qt": ((head, heads * rows), low),
        "cosine": ((rows, head // 2), wide),
        "sine": ((rows, head // 2), wide),
        "wide": ((rows, width), wide),
        "ot": ((head, heads * rows), wide),
        "total": ((1, heads * rows), wide),
        "lse": ((1, heads * rows), wide),
        "delta": ((1, heads * rows), wide),
        "ob": ((rows, joined + 2 * head), low),
        "ap": ((rows, width), wide),
        "x1": ((rows, width), wide),
        "m": ((rows, width), low),
        "hid": ((rows, hidden), low),
        "side_gate": ((rows, hidden), low),
        "side_up": ((rows, hidden), low),
        "df": ((rows, width), low),
        "dap": ((rows, width), low),
        "do": ((heads * rows, head), low),
        "dot": ((head, heads * rows), low),
        "dkv": ((rows, 2 * head), wide),
        "from_partner": ((z_count, rows, 2 * head), low),
        "from_above": ((z_count, rows, 2 * head), low),
    }
    shapes = gradient_shapes(sizes)
    pieces = 0
    for name, count in r_plan(sizes):
        (eight, high, columns), kind = shapes[name][0], wide if name == "gain" else low
        step = high // count
        pieces += count
        arrays["g_" + name] = (shapes[name][0], kind)
        for number in range(pieces - count, pieces):
            for k, shape in enumerate(LineChunk.landing(step) if FIRST[number] in "uv" else Chunk.landing(step)):
                arrays[f"land{k}_{number}"] = (shape + (columns,), kind)
    sems = {
        "load_sem": (9,),
        "kv_send": (2, 2 * z_count),
        "kv_recv": (2 * z_count,),
        "half_send": (2,),
        "half_recv": (2,),
        "dkv_send": (2, z_count),
        "dkv_recv": (2, z_count),
        "red_send": (pieces, STAGES),
        "red_recv": (pieces, STAGES),
        "red_local": (pieces,),
    }
    return arrays, sems


def layer_bytes(sizes):
    total = 0
    for shape, kind in layer_scratch(sizes)[0].values():
        size = jnp.dtype(kind).itemsize
        for n in shape[:-2]:
            size *= n
        total += size * max(shape[-2], 8) * max(shape[-1], 128)
    return total


VMEM_BYTES = 64 * 2**20


def widen_kernel(count, gain_sizes, *refs):
    ins, table_in, both, tokens = refs[: count - 2], refs[count - 2], refs[count - 1], refs[count : count + 2]
    refs = refs[count + 2 :]
    outs, gains_out, tokens_out = refs[:count], refs[count : count + 6], refs[count + 6 : count + 8]
    refs = refs[count + 8 :]
    narrow, broad, gains, (table, came, gone) = refs[: count + 2], refs[count + 2 : 2 * count + 2], refs[2 * count + 2 : 2 * count + 8], refs[2 * count + 8 :]
    ins = (both.at[0], both.at[1]) + ins + tokens + (table_in,)
    outs = outs + tokens_out + gains_out
    held = broad + narrow[count:] + gains
    loads = [pltpu.make_async_copy(ins[i], (narrow + (table,))[i], came.at[i]) for i in range(count + 3)]
    stores = [pltpu.make_async_copy(held[i], outs[i], gone.at[i]) for i in range(count + 8)]
    for item in loads:
        item.start()
    for i in range(count):
        loads[i].wait()

        def body(j, carry):
            here = pl.ds(pl.multiple_of(j * 64, 64), 64)
            broad[i][here, :] = f32(narrow[i][here, :])
            return carry

        lax.fori_loop(0, narrow[i].shape[0] // 64, body, 0)
        stores[i].start()
    for i in (count, count + 1):
        loads[i].wait()
        stores[i].start()
    loads[count + 2].wait()
    at = 0
    for i, gain in enumerate(gains):
        for part in range(gain_sizes[i] // 128):
            gain[part * 128 : (part + 1) * 128] = table[at // 16, at % 16, :]
            at += 1
        stores[count + 2 + i].start()
    for item in stores:
        item.wait()


def widen(both, matrices, table, tokens, gain_sizes):
    count = len(matrices) + 2
    shapes = [both.shape[1:]] * 2 + [v.shape for v in matrices]
    anywhere = pl.BlockSpec(memory_space=pl.ANY)
    return pl.pallas_call(
        functools.partial(widen_kernel, count, gain_sizes),
        out_shape=tuple(jax.ShapeDtypeStruct(shape, jnp.float32) for shape in shapes)
        + tuple(jax.ShapeDtypeStruct((n,), jnp.float32) for n in gain_sizes)
        + tuple(jax.ShapeDtypeStruct(v.shape, v.dtype) for v in tokens),
        in_specs=[anywhere] * (count + 2),
        out_specs=tuple([anywhere] * (count + len(gain_sizes) + 2)),
        scratch_shapes=[pltpu.VMEM(shape, jnp.bfloat16) for shape in shapes + [v.shape for v in tokens]]
        + [pltpu.VMEM(shape, jnp.float32) for shape in shapes]
        + [pltpu.VMEM((n,), jnp.float32) for n in gain_sizes]
        + [pltpu.VMEM(table.shape, table.dtype)]
        + [pltpu.SemaphoreType.DMA((count + 3,)), pltpu.SemaphoreType.DMA((count + 8,))],
        compiler_params=pltpu.CompilerParams(vmem_limit_bytes=VMEM_BYTES),
    )(*matrices, table, both, *tokens)


def whole_layer(sizes, tokens, lengths, cotangent, norm_in, w_query, w_key, w_value, query_gain, key_gain, w_out, norm_attn, norm_pre, w_gate, w_up, w_down, norm_post):
    rows, width, hidden, heads, head, z_count = sizes
    joined = heads * head
    inputs = {
        "lengths": lengths,
        "norm_in": norm_in,
        "query_gain": query_gain,
        "key_gain": key_gain,
        "norm_attn": norm_attn,
        "norm_pre": norm_pre,
        "norm_post": norm_post,
        "x_in": tokens[0],
        "w_key_in": w_key,
        "w_value_in": w_value,
        "w_query_in": w_query,
        "w_out_in": w_out,
        "w_gate_in": w_gate,
        "w_up_in": w_up,
        "w_down_in": w_down,
        "dy_in": cotangent[0],
    }
    spaces = {name: pltpu.SMEM if name == "lengths" else pl.ANY if name.endswith("_in") and name != "norm_in" else pltpu.VMEM for name in inputs}
    shapes = gradient_shapes(sizes)
    outputs = {"out": (rows, width), "dx": (rows, width)}
    outputs.update({"t_" + name: shapes[name][1] for name in shapes})
    arrays, sems = layer_scratch(sizes)
    names = list(inputs) + list(outputs) + list(arrays) + list(sems)
    results = pl.pallas_call(
        functools.partial(layer_kernel, sizes, SCHEDULES[z_count], names),
        out_shape=tuple(
            jax.ShapeDtypeStruct(shape, jnp.float32 if name == "t_gain" else jnp.bfloat16) for name, shape in outputs.items()
        ),
        in_specs=[pl.BlockSpec(memory_space=spaces[name]) for name in inputs],
        out_specs=tuple(
            pl.BlockSpec(memory_space=pl.ANY if name.startswith("t_") else pltpu.VMEM) for name in outputs
        ),
        scratch_shapes=[pltpu.VMEM(*item) for item in arrays.values()]
        + [pltpu.SemaphoreType.DMA(item) for item in sems.values()],
        compiler_params=pltpu.CompilerParams(
            collective_id=1, has_side_effects=True, vmem_limit_bytes=VMEM_BYTES
        ),
    )(*inputs.values())
    r = Names(zip(outputs, results, strict=True))
    matrices = [
        r.t_query,
        r.t_out.reshape(joined, width),
        r.t_gate,
        r.t_up,
        r.t_down.reshape(hidden, width),
    ]
    both = r.t_kv.reshape(2, width, head)
    sums = widen(both, matrices, r.t_gain, (r.out, r.dx), (width, width, width, width, head, head))
    g_key, g_value, g_query, g_out, g_gate, g_up, g_down = sums[:7]
    g_in, g_attn, g_pre, g_post, g_qgain, g_kgain, output, input_grad = sums[7:]
    return (
        output[None],
        input_grad[None],
        g_in,
        g_query,
        g_key,
        g_value,
        g_qgain,
        g_kgain,
        g_out,
        g_attn,
        g_pre,
        g_gate,
        g_up,
        g_down,
        g_post,
    )


def per_device(
    tokens,
    lengths,
    cotangent,
    norm_in,
    w_query,
    w_key,
    w_value,
    query_gain,
    key_gain,
    w_out,
    norm_attn,
    norm_pre,
    w_gate,
    w_up,
    w_down,
    norm_post,
):
    rows = tokens.shape[1]
    head = query_gain.shape[0]
    heads = w_query.shape[1] // head
    sizes = (rows, tokens.shape[2], w_gate.shape[1], heads, head, lax.axis_size(BLOCKS) // 2)
    if sizes[-1] in SCHEDULES and layer_bytes(sizes) <= VMEM_BYTES:
        return whole_layer(
            sizes,
            tokens,
            lengths,
            cotangent,
            norm_in,
            w_query,
            w_key,
            w_value,
            query_gain,
            key_gain,
            w_out,
            norm_attn,
            norm_pre,
            w_gate,
            w_up,
            w_down,
            norm_post,
        )
    scale = head ** (-0.5)
    count = lax.axis_size(BLOCKS)
    place = lax.axis_index(BLOCKS)
    row = lengths[0]
    local_idx = place * rows + jnp.arange(rows, dtype=jnp.int32)
    seg_q, pos_q = segment_of(local_idx, row)
    cosine, sine = rotary_tables(pos_q, head)

    def block_mask(source):
        key_idx = source * rows + jnp.arange(rows, dtype=jnp.int32)
        seg_k, unused = segment_of(key_idx, row)
        return (seg_q[:, None] == seg_k[None, :]) & (local_idx[:, None] >= key_idx[None, :])

    x_in = tokens[0].astype(jnp.float32)
    normal_a = normed(x_in, norm_in).astype(jnp.bfloat16)
    q_proj = jnp.dot(normal_a, w_query, preferred_element_type=jnp.float32).reshape(
        rows, heads, head
    )
    k_proj = jnp.dot(normal_a, w_key, preferred_element_type=jnp.float32)
    v_proj = jnp.dot(normal_a, w_value, preferred_element_type=jnp.float32)
    query = prepare(q_proj, query_gain, cosine[:, None, :], sine[:, None, :]).astype(jnp.bfloat16)
    keys = prepare(k_proj, key_gain, cosine, sine).astype(jnp.bfloat16)
    values = v_proj.astype(jnp.bfloat16)
    q_heads = jnp.transpose(query, (1, 0, 2))

    def absorb(state, pair, source):
        allowed = block_mask(source)
        big, total, accum = state
        raw = jnp.einsum("hqd,kd->hqk", q_heads, pair[0], preferred_element_type=jnp.float32)
        scores = jnp.where(allowed[None], scale * raw, NEG)
        big_new = jnp.maximum(big, jnp.max(scores, axis=-1, keepdims=True))
        expo = jnp.where(allowed[None], jnp.exp(scores - big_new), 0.0)
        fade = jnp.exp(big - big_new)
        total = total * fade + jnp.sum(expo, axis=-1, keepdims=True)
        accum = accum * fade + jnp.einsum(
            "hqk,kd->hqd", expo.astype(jnp.bfloat16), pair[1], preferred_element_type=jnp.float32
        )
        return (big_new, total, accum)

    pair = jnp.stack([keys, values])
    state = (
        jnp.full((heads, rows, 1), NEG, jnp.float32),
        jnp.zeros((heads, rows, 1), jnp.float32),
        jnp.zeros((heads, rows, head), jnp.float32),
    )
    state = absorb(state, pair, place)

    def cycle_forward(step, carry):
        inner, moving = carry
        moving = from_behind(moving, BLOCKS, 1)
        return (absorb(inner, moving, (place - step) % count), moving)

    state, unused_pair = lax.fori_loop(1, count, cycle_forward, (state, pair))
    big, total, accum = state
    attended = accum / total
    lse = big + jnp.log(total)
    joined = jnp.transpose(attended, (1, 0, 2)).reshape(rows, heads * head).astype(jnp.bfloat16)
    a_proj = jnp.dot(joined, w_out, preferred_element_type=jnp.float32)
    x_mid = x_in + normed(a_proj, norm_attn)
    mixed = normed(x_mid, norm_pre).astype(jnp.bfloat16)
    gate = jnp.dot(mixed, w_gate, preferred_element_type=jnp.float32)
    upper = jnp.dot(mixed, w_up, preferred_element_type=jnp.float32)

    def activate(gate_in, upper_in):
        return jax.nn.gelu(gate_in, approximate=True) * upper_in

    hidden = activate(gate, upper).astype(jnp.bfloat16)
    f_proj = jnp.dot(hidden, w_down, preferred_element_type=jnp.float32)
    output = x_mid + normed(f_proj, norm_post)
    grad_y = cotangent[0].astype(jnp.float32)
    d_fproj, g_post = normed_back(f_proj, norm_post, grad_y)
    d_fproj = d_fproj.astype(jnp.bfloat16)
    g_down = dot_tn(hidden, d_fproj)
    d_hidden = dot_nt(d_fproj, w_down)
    d_gate, d_upper = jax.vjp(activate, gate, upper)[1](d_hidden)
    d_gate = d_gate.astype(jnp.bfloat16)
    d_upper = d_upper.astype(jnp.bfloat16)
    g_gate = dot_tn(mixed, d_gate)
    g_up = dot_tn(mixed, d_upper)
    d_mixed = dot_nt(d_gate, w_gate) + dot_nt(d_upper, w_up)
    d_mid, g_pre = normed_back(x_mid, norm_pre, d_mixed)
    d_mid = grad_y + d_mid
    d_aproj, g_attn = normed_back(a_proj, norm_attn, d_mid)
    d_aproj = d_aproj.astype(jnp.bfloat16)
    g_out = dot_tn(joined, d_aproj)
    d_joined = dot_nt(d_aproj, w_out).astype(
        jnp.bfloat16
    )
    do_heads = jnp.transpose(d_joined.reshape(rows, heads, head), (1, 0, 2))
    delta = jnp.sum(do_heads.astype(jnp.float32) * attended, axis=-1, keepdims=True)

    def visit(d_query, moving, grads, source):
        allowed = block_mask(source)
        raw = jnp.einsum("hqd,kd->hqk", q_heads, moving[0], preferred_element_type=jnp.float32)
        probs = jnp.where(allowed[None], jnp.exp(scale * raw - lse), 0.0)
        dv_add = jnp.einsum(
            "hqk,hqd->kd", probs.astype(jnp.bfloat16), do_heads, preferred_element_type=jnp.float32
        )
        d_probs = jnp.einsum("hqd,kd->hqk", do_heads, moving[1], preferred_element_type=jnp.float32)
        d_scores = (scale * probs * (d_probs - delta)).astype(jnp.bfloat16)
        dq_add = jnp.einsum("hqk,kd->hqd", d_scores, moving[0], preferred_element_type=jnp.float32)
        dk_add = jnp.einsum("hqk,hqd->kd", d_scores, q_heads, preferred_element_type=jnp.float32)
        return (d_query + dq_add, grads + jnp.stack([dk_add, dv_add]))

    d_query = jnp.zeros((heads, rows, head), jnp.float32)
    grads = jnp.zeros((2, rows, head), jnp.float32)
    d_query, grads = visit(d_query, pair, grads, place)

    def cycle_backward(step, carry):
        dq_in, moving, grads_in = carry
        moving = from_behind(moving, BLOCKS, 1)
        grads_in = pass_home(grads_in)
        dq_in, grads_in = visit(dq_in, moving, grads_in, (place - step) % count)
        return (dq_in, moving, grads_in)

    d_query, unused_pair, grads = lax.fori_loop(1, count, cycle_backward, (d_query, pair, grads))
    grads = pass_home(grads)

    def query_piece(proj, gain):
        return prepare(proj, gain, cosine[:, None, :], sine[:, None, :])

    def key_piece(proj, gain):
        return prepare(proj, gain, cosine, sine)

    d_qproj, g_qgain = jax.vjp(query_piece, q_proj, query_gain)[1](
        jnp.transpose(d_query, (1, 0, 2))
    )
    d_kproj, g_kgain = jax.vjp(key_piece, k_proj, key_gain)[1](grads[0])
    d_qproj = d_qproj.reshape(rows, heads * head).astype(jnp.bfloat16)
    d_kproj = d_kproj.astype(jnp.bfloat16)
    d_vproj = grads[1].astype(jnp.bfloat16)
    g_query = dot_tn(normal_a, d_qproj)
    g_key = dot_tn(normal_a, d_kproj)
    g_value = dot_tn(normal_a, d_vproj)
    d_normal = dot_nt(d_qproj, w_query)
    d_normal = d_normal + dot_nt(d_kproj, w_key)
    d_normal = d_normal + dot_nt(d_vproj, w_value)
    d_input, g_in = normed_back(x_in, norm_in, d_normal)
    input_grad = (d_mid + d_input).astype(jnp.bfloat16)
    (
        g_in,
        g_query,
        g_key,
        g_value,
        g_qgain,
        g_kgain,
        g_out,
        g_attn,
        g_pre,
        g_gate,
        g_up,
        g_down,
        g_post,
    ) = sum_gradients(
        (
            g_in,
            g_query,
            g_key,
            g_value,
            g_qgain,
            g_kgain,
            g_out,
            g_attn,
            g_pre,
            g_gate,
            g_up,
            g_down,
            g_post,
        )
    )
    return (
        output.astype(jnp.bfloat16)[None],
        input_grad[None],
        g_in,
        g_query,
        g_key,
        g_value,
        g_qgain,
        g_kgain,
        g_out,
        g_attn,
        g_pre,
        g_gate,
        g_up,
        g_down,
        g_post,
    )


def solution(mesh):
    in_specs = (
        P(PARTS, BLOCKS, None),
        P(PARTS, None),
        P(PARTS, BLOCKS, None),
        P(),
        P(),
        P(),
        P(),
        P(),
        P(),
        P(),
        P(),
        P(),
        P(),
        P(),
        P(),
        P(),
    )
    out_specs = (
        P(PARTS, BLOCKS, None),
        P(PARTS, BLOCKS, None),
        P(),
        P(),
        P(),
        P(),
        P(),
        P(),
        P(),
        P(),
        P(),
        P(),
        P(),
        P(),
        P(),
    )
    return jax.shard_map(
        per_device, mesh=mesh, in_specs=in_specs, out_specs=out_specs, check_vma=False
    )
```

```python
import functools

import jax
import jax.numpy as jnp
from jax import lax
from jax.experimental import pallas as pl
from jax.experimental.pallas import tpu as pltpu
from jax.sharding import PartitionSpec as P

BLOCKS, PARTS = "blk", "dp"
EPS = 1e-06
BASE = 1000000.0
NEG = -1e30


def shifted(array, axis, by):
    peers = lax.axis_size(axis)
    return lax.ppermute(array, axis, [(i, (i + by) % peers) for i in range(peers)])


def from_behind(block, axis, distance):
    devices = range(lax.axis_size(axis))
    route = [(i - distance, i) for i in devices if i - distance in devices]
    return lax.ppermute(block, axis, route)


def normed(value, gain):
    return value * lax.rsqrt(jnp.mean(value * value, axis=-1, keepdims=True) + EPS) * gain


def normed_back(value, gain, grad):
    return jax.vjp(normed, value, gain)[1](grad)


def segment_of(index, row):
    ends = jnp.cumsum(row)
    seg = jnp.sum((index[:, None] >= ends[None, :]).astype(jnp.int32), axis=1)
    starts = ends - row
    slots = jnp.arange(row.shape[0], dtype=jnp.int32)
    begin = jnp.sum(jnp.where(slots[None, :] == seg[:, None], starts[None, :], 0), axis=1)
    return (seg, index - begin)


def rotary_tables(places, head):
    half = head // 2
    freq = jnp.exp(-(2.0 * jnp.arange(half, dtype=jnp.float32) / head) * jnp.log(BASE))
    angle = places.astype(jnp.float32)[:, None] * freq[None, :]
    return (jnp.cos(angle), jnp.sin(angle))


def prepare(proj, gain, cosine, sine):
    value = normed(proj, gain)
    half = value.shape[-1] // 2
    first = value[..., :half]
    second = value[..., half:]
    return jnp.concatenate(
        [first * cosine - second * sine, second * cosine + first * sine], axis=-1
    )


def pass_home(grads):
    return shifted(grads.astype(jnp.bfloat16), BLOCKS, 1).astype(grads.dtype)


MESH = pl.DeviceIdType.MESH


def where_am_i():
    place = lax.axis_index(BLOCKS)
    part = lax.axis_index(PARTS)
    return {
        "z": place // 2,
        "y": lax.rem(place, 2),
        "x": part // 2,
        "core": lax.rem(part, 2),
        "place": place,
        "part": part,
    }


def peers_of(me):
    place, part = me["place"], me["part"]
    return {
        "core": {BLOCKS: place, PARTS: part + 1 - 2 * me["core"]},
        "x": {BLOCKS: place, PARTS: part + 2 - 4 * me["x"]},
        "y": {BLOCKS: place + 1 - 2 * me["y"], PARTS: part},
        "up": {BLOCKS: place + 2, PARTS: part},
        "down": {BLOCKS: place - 2, PARTS: part},
    }


def greet(me, peers, z_count):
    barrier = pltpu.get_barrier_semaphore()
    for name in ("core", "x", "y"):
        pl.semaphore_signal(barrier, inc=1, device_id=peers[name], device_id_type=MESH)

    @pl.when(me["z"] < z_count - 1)
    def _():
        pl.semaphore_signal(barrier, inc=1, device_id=peers["up"], device_id_type=MESH)

    @pl.when(me["z"] > 0)
    def _():
        pl.semaphore_signal(barrier, inc=1, device_id=peers["down"], device_id_type=MESH)


def meet(me, z_count):
    ends = (me["z"] == 0).astype(jnp.int32) + (me["z"] == z_count - 1).astype(jnp.int32)
    pl.semaphore_wait(pltpu.get_barrier_semaphore(), 5 - ends)


def add_into(target, start, row, extra, count, rows):
    step = rows if rows < 32 else 16
    for candidate in (160, 128, 80, 64, 48, 32):
        if rows % candidate == 0:
            step = candidate
            break

    def body(index, carry):
        e = index // (rows // step)
        at = pl.multiple_of(lax.rem(index, rows // step) * step, 8)
        here = pl.ds(pl.multiple_of(row + at, 8), step)
        target[start + e, here, :] = target[start + e, here, :] + extra[e, pl.ds(at, step), :]
        return carry

    lax.fori_loop(0, count * (rows // step), body, 0)


STAGES = 10


class Chunk:
    def __init__(self, number, grad, total, row, rows, first, landing, sems, me, peers, z_count):
        self.grad, self.total, self.row, self.rows = grad, total, row, rows
        self.first, self.second = ("x", "y") if first == "x" else ("y", "x")
        self.land0, self.land1, self.land2 = landing
        self.send, self.recv, self.local = sems
        self.number, self.me, self.peers, self.z_count = number, me, peers, z_count
        self.b1, self.b2, self.core = me[self.first], me[self.second], me["core"]
        self.quad = 4 * self.core
        self.pair = self.quad + 2 * self.b1
        self.own = self.pair + self.b2
        self.half = rows // 2

    @staticmethod
    def landing(rows):
        return ((4, rows), (2, rows), (1, 2 * rows))

    def piece(self, start, count, upper=None):
        if upper is None:
            return self.grad.at[pl.ds(start, count), pl.ds(self.row, self.rows), :]
        row = self.row if upper else self.row + self.half
        return self.grad.at[pl.ds(start, count), pl.ds(row, self.half), :]

    def spot(self, count, upper=None):
        row, rows = self.row, self.rows
        if upper is not None:
            row, rows = (row if upper else row + self.half), self.half
        here, columns = pl.ds(row, rows), self.grad.shape[2]
        start = {1: self.own, 2: self.pair, 4: self.quad}[count]
        if len(self.total.shape) == 2:
            return self.total.at[here, pl.ds(pl.multiple_of(start * columns, 128), count * columns)]
        if len(self.total.shape) == 4:
            if count == 4:
                return self.total.at[self.core, :, here, :]
            if count == 2:
                return self.total.at[self.core, self.b1, here, :]
            return self.total.at[self.core, self.b1, here, pl.ds(pl.multiple_of(self.b2 * columns, 128), columns)]
        if count == 1:
            return self.total.at[start, here, :]
        return self.total.at[pl.ds(start, count), here, :]

    def mine(self, upper):
        return self.grad.at[self.own, pl.ds(self.row if upper else self.row + self.half, self.half), :]

    def keep(self, upper):
        return pltpu.make_async_copy(
            self.mine(upper), self.spot(1, upper), self.local.at[self.number]
        )

    def copy(self, stage, peer, source, target):
        return pltpu.make_async_remote_copy(
            src_ref=source,
            dst_ref=target,
            send_sem=self.send.at[self.number, stage],
            recv_sem=self.recv.at[self.number, stage],
            device_id=self.peers[peer],
            device_id_type=MESH,
        )

    def reduce_up(self):
        return self.copy(3, "up", self.piece(self.own, 1, True), self.land2.at[:, pl.ds(self.rows, self.half), :])

    def reduce_down(self):
        return self.copy(4, "down", self.piece(self.own, 1, False), self.land2.at[:, pl.ds(self.rows + self.half, self.half), :])

    def spread_down(self, fresh=False):
        here = self.spot(1, True)
        return self.copy(5, "down", self.mine(True) if fresh else here, here)

    def spread_up(self, fresh=False):
        here = self.spot(1, False)
        return self.copy(6, "up", self.mine(False) if fresh else here, here)

    def step0(self):
        return self.copy(0, "core", self.piece(4 - self.quad, 4), self.land0)

    def step1(self):
        return self.copy(1, self.first, self.piece(self.quad + 2 - 2 * self.b1, 2), self.land1)

    def step2(self):
        return self.copy(2, self.second, self.piece(self.pair + 1 - self.b2, 1), self.land2.at[:, pl.ds(0, self.rows), :])

    def gather(self, stage):
        count, peer = ((1, self.second), (2, self.first), (4, "core"))[stage - 7]
        here = self.spot(count)
        return self.copy(stage, peer, here, here)

    def arrive_upper(self):
        z, last = self.me["z"], self.z_count - 1

        @pl.when(z > 0)
        def _():
            self.reduce_up().wait_recv()
            add_into(self.grad, self.own, self.row, self.land2.at[:, pl.ds(self.rows, self.half), :], 1, self.half)

            @pl.when(z < last)
            def _():
                self.reduce_up().start()

            @pl.when(z == last)
            def _():
                self.spread_down(True).start()
                self.keep(True).start()

    def arrive_lower(self):
        z, last = self.me["z"], self.z_count - 1

        @pl.when(z < last)
        def _():
            self.reduce_down().wait_recv()
            add_into(self.grad, self.own, self.row + self.half, self.land2.at[:, pl.ds(self.rows + self.half, self.half), :], 1, self.half)

            @pl.when(z > 0)
            def _():
                self.reduce_down().start()

            @pl.when(z == 0)
            def _():
                self.spread_up(True).start()
                self.keep(False).start()

    def back_upper(self):
        z, last = self.me["z"], self.z_count - 1

        @pl.when(z < last)
        def _():
            self.spread_down().wait_recv()

            @pl.when(z > 0)
            def _():
                self.spread_down().start()

    def back_lower(self):
        z, last = self.me["z"], self.z_count - 1

        @pl.when(z > 0)
        def _():
            self.spread_up().wait_recv()

            @pl.when(z < last)
            def _():
                self.spread_up().start()

    def tick(self, op):
        z, last = self.me["z"], self.z_count - 1
        if op == 0:
            self.step0().start()
        elif op == 1:
            self.step0().wait_recv()
            add_into(self.grad, self.quad, self.row, self.land0, 4, self.rows)
            self.step1().start()
        elif op == 2:
            self.step1().wait_recv()
            add_into(self.grad, self.pair, self.row, self.land1, 2, self.rows)
            self.step2().start()
        elif op == 3:
            self.step2().wait_recv()
            add_into(self.grad, self.own, self.row, self.land2, 1, self.rows)

            @pl.when(z == 0)
            def _():
                self.reduce_up().start()

            @pl.when(z == last)
            def _():
                self.reduce_down().start()

        elif op == 4:
            pl.when((z > 0) & (2 * z < self.z_count))(self.arrive_upper)
            pl.when((z < last) & (2 * z >= self.z_count))(self.arrive_lower)
        elif op == 5:
            pl.when((z < last) & (2 * z >= self.z_count))(self.arrive_upper)
            pl.when((z > 0) & (2 * z < self.z_count))(self.arrive_lower)
        elif op == 6:
            pl.when(z == last)(self.arrive_upper)
            pl.when(z == 0)(self.arrive_lower)
        elif op == 7:
            pl.when((z < last) & (2 * z >= self.z_count))(self.back_upper)
            pl.when((z > 0) & (2 * z < self.z_count))(self.back_lower)
        elif op == 8:

            @pl.when((z > 0) & (2 * z < self.z_count))
            def _():
                self.back_upper()
                self.gather(7).start()

            @pl.when((z < last) & (2 * z >= self.z_count))
            def _():
                self.back_lower()
                self.gather(7).start()

        elif op == 9:

            @pl.when(z == 0)
            def _():
                self.back_upper()
                self.keep(False).wait()
                self.gather(7).start()

            @pl.when(z == last)
            def _():
                self.back_lower()
                self.keep(True).wait()
                self.gather(7).start()

        elif op == 10:
            self.gather(7).wait_recv()
            self.gather(8).start()
        elif op == 11:
            self.gather(8).wait_recv()
            self.gather(9).start()
        elif op == 12:
            self.gather(9).wait_recv()
            self.drain()

    OPS = 13

    def drain(self):
        z, last = self.me["z"], self.z_count - 1
        self.step0().wait_send()
        self.step1().wait_send()
        self.step2().wait_send()
        for stage in (7, 8, 9):
            self.gather(stage).wait_send()

        @pl.when(z < last)
        def _():
            self.reduce_up().wait_send()
            self.spread_up().wait_send()

        @pl.when(z > 0)
        def _():
            self.reduce_down().wait_send()
            self.spread_down().wait_send()


class LineChunk(Chunk):
    def __init__(self, *args):
        super().__init__(*args[:6], (args[6][0], None, None), *args[7:])
        self.ups, self.downs, self.small = args[6][1:]
        self.entry = self.quad + self.me["z"]
        self.half, self.quarter = self.rows // 2, self.rows // 4
        self.mine_half = pl.multiple_of(self.row + self.b1 * self.half, 16)
        self.mine_quarter = pl.multiple_of(self.mine_half + self.b2 * self.quarter, 16)

    @staticmethod
    def landing(rows):
        return ((4, rows), (3, rows), (3, rows), (1, rows))

    def across(self, stage, name, first, count):
        landing = self.ups if name == "up" else self.downs
        return self.copy(stage, name, self.piece(self.quad + first, count), landing.at[pl.ds(0, count)])

    def back(self, stage, name, first, count):
        here = self.place(self.quad + first, count, self.row, self.rows)
        return self.copy(stage, name, here, here)

    def place(self, start, count, row, rows):
        here, columns = pl.ds(row, rows), self.grad.shape[2]
        if len(self.total.shape) == 2:
            return self.total.at[here, pl.ds(pl.multiple_of(start * columns, 128), count * columns)]
        if count == 1:
            return self.total.at[start, here, :]
        return self.total.at[pl.ds(start, count), here, :]

    def part(self, row, rows):
        return self.grad.at[pl.ds(self.entry, 1), pl.ds(row, rows), :]

    def step1(self):
        other = pl.multiple_of(self.row + (1 - self.b1) * self.half, 16)
        return self.copy(1, self.first, self.part(other, self.half), self.small.at[:, pl.ds(0, self.half), :])

    def step2(self):
        other = pl.multiple_of(self.mine_half + (1 - self.b2) * self.quarter, 16)
        landing = self.small.at[:, pl.ds(self.half, self.quarter), :]
        return self.copy(2, self.second, self.part(other, self.quarter), landing)

    def finished(self):
        return self.grad.at[self.entry, pl.ds(self.mine_quarter, self.quarter), :]

    def keep(self):
        spot = self.place(self.entry, 1, self.mine_quarter, self.quarter)
        return pltpu.make_async_copy(self.finished(), spot, self.local.at[self.number])

    def gather2(self):
        spot = self.place(self.entry, 1, self.mine_quarter, self.quarter)
        return self.copy(7, self.second, self.finished(), spot)

    def gather1(self):
        here = self.place(self.entry, 1, self.mine_half, self.half)
        return self.copy(8, self.first, here, here)

    def gather0(self):
        here = self.place(self.quad, 4, self.row, self.rows)
        return self.copy(9, "core", here, here)

    def at_row(self, k, body):
        pl.when(self.me["z"] == k)(body)

    def from_below(self, k):
        return (k, self.z_count - k)

    def from_above(self, k):
        return (0, k + 1)

    def take_up(self, k):
        first, count = self.from_below(k)
        self.across(3, "up", first, count).wait_recv()
        add_into(self.grad, self.quad + first, self.row, self.ups, count, self.rows)
        if k < self.z_count - 1:
            self.across(3, "up", first + 1, count - 1).start()

    def take_down(self, k):
        first, count = self.from_above(k)
        self.across(4, "down", first, count).wait_recv()
        add_into(self.grad, self.quad + first, self.row, self.downs, count, self.rows)
        if k > 0:
            self.across(4, "down", first, count - 1).start()

    def back_up(self, k):
        self.back(6, "up", 0, k).wait_recv()
        if k < self.z_count - 1:
            self.back(6, "up", 0, k + 1).start()

    def back_down(self, k):
        last = self.z_count - 1
        self.back(5, "down", k + 1, last - k).wait_recv()
        if k > 0:
            self.back(5, "down", k, last - k + 1).start()

    def tick(self, op):
        last, middle = self.z_count - 1, self.z_count // 2
        if op == 0:
            self.step0().start()
        elif op == 1:
            self.step0().wait_recv()
            add_into(self.grad, self.quad, self.row, self.land0, 4, self.rows)
            self.at_row(0, lambda: self.across(3, "up", 1, last).start())
            self.at_row(last, lambda: self.across(4, "down", 0, last).start())
        elif op == 2:
            for k in range(1, last):
                self.at_row(k, functools.partial(self.take_up if k < middle else self.take_down, k))
        elif op == 3:
            for k in range(1, last):

                def arrive(k=k):
                    (self.take_down if k < middle else self.take_up)(k)
                    self.step1().start()

                self.at_row(k, arrive)
        elif op == 4:

            def bottom():
                self.take_down(0)
                self.step1().start()

            def top():
                self.take_up(last)
                self.step1().start()

            self.at_row(0, bottom)
            self.at_row(last, top)
        elif op == 5:
            self.step1().wait_recv()
            add_into(self.grad, self.entry, self.mine_half, self.small, 1, self.half)
            self.step2().start()
        elif op == 6:
            self.step2().wait_recv()
            landing = self.small.at[:, pl.ds(self.half, self.quarter), :]
            add_into(self.grad, self.entry, self.mine_quarter, landing, 1, self.quarter)
            self.keep().start()
            self.gather2().start()
        elif op == 7:
            self.gather2().wait_recv()
            self.keep().wait()
            self.gather1().start()
        elif op == 8:
            self.gather1().wait_recv()
            self.at_row(0, lambda: self.back(6, "up", 0, 1).start())
            self.at_row(last, lambda: self.back(5, "down", last, 1).start())
        elif op == 9:
            for k in range(1, last):
                self.at_row(k, functools.partial(self.back_up if k < middle else self.back_down, k))
        elif op == 10:
            for k in range(1, last):

                def complete(k=k):
                    (self.back_down if k < middle else self.back_up)(k)
                    self.gather0().start()

                self.at_row(k, complete)
        elif op == 11:

            def bottom():
                self.back_down(0)
                self.gather0().start()

            def top():
                self.back_up(last)
                self.gather0().start()

            self.at_row(0, bottom)
            self.at_row(last, top)
        elif op == 12:
            self.gather0().wait_recv()
            self.drain()

    def drain(self):
        last = self.z_count - 1
        for item in (self.step0(), self.step1(), self.step2(), self.gather2(), self.gather1(), self.gather0()):
            item.wait_send()
        for k in range(self.z_count):

            def sent(k=k):
                if k < last:
                    self.across(3, "up", k + 1, last - k).wait_send()
                    self.back(6, "up", 0, k + 1).wait_send()
                if k > 0:
                    self.across(4, "down", 0, k).wait_send()
                    self.back(5, "down", k, last - k + 1).wait_send()

            self.at_row(k, sent)


def sum_kernel(z_count, plan, *refs):
    n = 1 + max(item[0] for item in plan)
    parts = len(plan)
    ins, outs = refs[:n], refs[n : 2 * n]
    rest = refs[2 * n :]
    grads, rest = rest[:n], rest[n:]
    landings = rest[: 3 * parts]
    send, recv, local, load = rest[3 * parts :]
    me = where_am_i()
    peers = peers_of(me)
    loads = [pltpu.make_async_copy(ins[i], grads[i], load.at[i]) for i in range(n)]
    for item in loads:
        item.start()
    greet(me, peers, z_count)
    meet(me, z_count)
    for item in loads:
        item.wait()
    chunks = []
    for number, (i, row, rows, first) in enumerate(plan):
        landing = landings[3 * number : 3 * number + 3]
        chunks.append(
            Chunk(number, grads[i], outs[i], row, rows, first, landing, (send, recv, local), me, peers, z_count)
        )
    for at in range(parts + Chunk.OPS - 1):
        for number in range(parts):
            if 0 <= at - number < Chunk.OPS:
                chunks[number].tick(at - number)


def sum_call(arrays, plan, z_count):
    landing = []
    for i, row, rows, first in plan:
        columns, kind = arrays[i].shape[2], arrays[i].dtype
        landing += [
            pltpu.VMEM((4, rows, columns), kind),
            pltpu.VMEM((2, rows, columns), kind),
            pltpu.VMEM((1, 2 * rows, columns), kind),
        ]
    n = len(arrays)
    return pl.pallas_call(
        functools.partial(sum_kernel, z_count, plan),
        out_shape=tuple(jax.ShapeDtypeStruct(v.shape, v.dtype) for v in arrays),
        in_specs=[pl.BlockSpec(memory_space=pl.ANY)] * n,
        out_specs=tuple([pl.BlockSpec(memory_space=pl.ANY)] * n),
        scratch_shapes=[pltpu.VMEM(v.shape, v.dtype) for v in arrays]
        + landing
        + [
            pltpu.SemaphoreType.DMA((len(plan), STAGES)),
            pltpu.SemaphoreType.DMA((len(plan), STAGES)),
            pltpu.SemaphoreType.DMA((len(plan),)),
            pltpu.SemaphoreType.DMA((n,)),
        ],
        compiler_params=pltpu.CompilerParams(
            collective_id=0, has_side_effects=True, vmem_limit_bytes=56 * 2**20
        ),
    )(*arrays)


def columns_to_panels(value):
    rows, columns = value.shape
    return jnp.transpose(value.reshape(rows, 8, columns // 8), (1, 0, 2)).astype(jnp.bfloat16)


def panels_to_columns(panels):
    count, rows, width = panels.shape
    return jnp.transpose(panels.astype(jnp.float32), (1, 0, 2)).reshape(rows, count * width)


def sum_gradients(grads):
    (g_in, g_query, g_key, g_value, g_qgain, g_kgain, g_out, g_attn, g_pre, g_gate, g_up, g_down, g_post) = grads
    z_count = lax.axis_size(BLOCKS) // 2
    width = g_in.shape[0]
    gains = [g_in, g_attn, g_pre, g_post, g_qgain, g_kgain]
    sizes = [v.shape[0] for v in gains]
    flat = jnp.concatenate(gains)
    gain_rows = 32
    flat = jnp.pad(flat, (0, 8 * gain_rows * 128 - flat.shape[0])).reshape(8, gain_rows, 128)
    down = g_down.astype(jnp.bfloat16).reshape(8, -1, width)
    out = g_out.astype(jnp.bfloat16).reshape(8, -1, width)
    both = jnp.stack([g_key, g_value])
    head = g_key.shape[1]
    both = jnp.transpose(both.reshape(2, 2, width // 2, 2, head // 2), (0, 1, 3, 2, 4)).reshape(8, width // 2, head // 2)
    arrays = [down, columns_to_panels(g_gate), columns_to_panels(g_up), out, columns_to_panels(g_query), both.astype(jnp.bfloat16), flat]
    plan = []
    for i, v in enumerate(arrays[:-1]):
        rows = v.shape[1] // 2
        plan += [(i, 0, rows, "x"), (i, rows, rows, "y")]
    plan.append((6, 0, gain_rows, "x"))
    down, gate, up, out, query, both, flat = sum_call(arrays, plan, z_count)
    both = jnp.transpose(both.astype(jnp.float32).reshape(2, 2, 2, width // 2, head // 2), (0, 1, 3, 2, 4)).reshape(2, width, head)
    flat = flat.reshape(-1)
    cuts, at = [], 0
    for size in sizes:
        cuts.append(flat[at : at + size])
        at += size
    g_in, g_attn, g_pre, g_post, g_qgain, g_kgain = cuts
    return (
        g_in,
        panels_to_columns(query),
        both[0],
        both[1],
        g_qgain,
        g_kgain,
        out.astype(jnp.float32).reshape(g_out.shape),
        g_attn,
        g_pre,
        panels_to_columns(gate),
        panels_to_columns(up),
        down.astype(jnp.float32).reshape(g_down.shape),
        g_post,
    )


LOG2E = 1.4426950408889634
LN2 = 0.6931471805599453
PIECES = (2, 2, 2, 2, 2, 2, 1)
FIRST = ['y', 'y', 'x', 'v', 'x', 'y', 'x', 'x', 'x', 'y', 'x', 'y', 'y']
SCHEDULES = {
    4: (
        (1, 0), (0, 0), ("S", 0), ("F", 0), (1, 1), ("F", 1), (4, 0), ("M", 0), (4, 1), (3, 0), (0, 1), ("O", 0), (1, 2), (3, 1), ("V", 0), (0, 2),
        (4, 2), (2, 0), (7, 0), (5, 0), ("V", 1), (3, 2), (1, 3), (6, 0), (0, 3), ("V", 2), (2, 1), (5, 1), (0, 4), (1, 4), (4, 3), (4, 4), (7, 1),
        (1, 5), (0, 5), (4, 5), (6, 1), (3, 3), ("P", 0), ("P", 1), ("V", 3), (0, 6), (1, 6), ("P", 2), ("Q", 0), ("Q", 1), (7, 2), (4, 6), (5, 2),
        ("Q", 2), (1, 7), ("Q", 3), (6, 2), (3, 4), ("G", 0), (0, 7), (8, 0), (1, 8), (2, 2), (9, 0), (5, 3), ("T", 0), (8, 1), (4, 7), (7, 3),
        ("K", 0), (4, 8), (1, 9), (0, 8), (5, 4), (10, 0), (6, 3), (7, 4), (9, 1), (12, 0), (3, 5), (8, 2), (6, 4), (5, 5), (7, 5), (2, 3), (10, 1),
        (11, 0), (6, 5), (12, 1), (2, 4), (3, 6), (11, 1), (9, 2), (10, 2), (5, 6), (12, 2), (7, 6), (4, 9), (6, 6), (5, 7), (3, 7), (2, 5), (1, 10),
        (11, 2), (6, 7), (12, 3), (8, 3), (0, 9), (7, 7), (12, 4), (8, 4), (10, 3), (9, 3), (5, 8), (10, 4), (9, 4), (11, 3), (4, 10), (2, 6),
        (11, 4), (7, 8), (3, 8), (6, 8), (8, 5), (5, 9), (12, 5), (10, 5), (7, 9), (6, 9), (11, 5), (8, 6), (9, 5), (0, 10), (12, 6), (2, 7), (11, 6),
        (12, 7), (10, 6), (8, 7), (10, 7), (9, 6), (7, 10), (11, 7), (9, 7), (3, 9), (6, 10), (8, 8), (1, 11), (10, 8), (2, 8), (8, 9), (2, 9),
        (12, 8), (12, 9), (10, 9), (9, 8), (11, 8), (9, 9), (5, 10), (7, 11), (11, 9), (4, 11), (12, 10), (8, 10), (3, 10), (0, 11), (11, 10),
        (7, 12), (10, 10), (2, 10), (4, 12), (9, 10), (6, 11), (8, 11), (10, 11), (5, 11), (12, 11), (11, 11), (8, 12), (3, 11), (2, 11), (12, 12),
        (11, 12), (9, 11), (1, 12), (2, 12), (0, 12), (5, 12), (3, 12), (9, 12), (6, 12), (10, 12),
    )
}


def dot(left, right):
    return jnp.dot(left, right, preferred_element_type=jnp.float32)


def dot_nt(left, right):
    return lax.dot_general(left, right, (((1,), (1,)), ((), ())), preferred_element_type=jnp.float32)


def inverse_rms(value):
    return lax.rsqrt(jnp.mean(value * value, axis=-1, keepdims=True) + EPS)


def rms_back(value, inverse, gain, grad):
    scaled = grad * gain
    normal = value * inverse
    mean = jnp.mean(scaled * normal, axis=-1, keepdims=True)
    terms = grad * normal
    return inverse * (scaled - normal * mean), jnp.sum(terms.reshape(-1, 8, terms.shape[-1]), axis=0)


def turn(value, cosine, sine):
    half = value.shape[-1] // 2
    first, second = value[:, :half], value[:, half:]
    return jnp.concatenate([first * cosine - second * sine, second * cosine + first * sine], axis=-1)


def turn_back(grad, cosine, sine):
    half = grad.shape[-1] // 2
    first, second = grad[:, :half], grad[:, half:]
    return jnp.concatenate([first * cosine + second * sine, second * cosine - first * sine], axis=-1)


def dot_tn(left, right):
    return lax.dot_general(left, right, (((0,), (0,)), ((), ())), preferred_element_type=jnp.float32)


def bf16(value):
    return value.astype(jnp.bfloat16)


def f32(value):
    return value.astype(jnp.float32)


class Names(dict):
    __getattr__ = dict.__getitem__


def layer_kernel(sizes, schedule, names, *refs):
    r = Names(zip(names, refs, strict=True))
    rows, width, hidden, heads, head, z_count = sizes
    scale = head**-0.5
    tile = 128
    tiles = [slice(at, at + tile) for at in range(0, rows, tile)]
    half = head // 2
    me = where_am_i()
    peers = peers_of(me)
    z, y, place = me["z"], me["y"], me["place"]
    last = z_count - 1

    weights = ["x", "w_key", "w_value", "w_query", "w_out", "w_gate", "w_up", "w_down", "dy"]
    joined = heads * head
    wide_k, wide_v = slice(joined, joined + head), slice(joined + head, joined + 2 * head)
    spots = {"w_query": slice(0, joined), "w_key": wide_k, "w_value": wide_v}
    pair = ("w_gate", "w_up")
    loads = {}
    for i, name in enumerate(weights):
        if name in spots:
            spot = r.w_first.at[:, spots[name]]
        elif name in pair:
            spot = r.w_pair.at[pair.index(name)]
        else:
            spot = r[name]
        loads[name] = pltpu.make_async_copy(r[name + "_in"], spot, r.load_sem.at[i])
    early = ("x", "w_key", "w_value")
    for name in early:
        loads[name].start()
    greet(me, peers, z_count)

    def begins(token):
        begin, end = jnp.zeros_like(token), jnp.int32(0)
        for j in range(r.lengths.shape[1]):
            end = end + r.lengths[0, j]
            begin = jnp.where(token >= end, end, begin)
        return begin

    token = place * rows + lax.broadcasted_iota(jnp.int32, (1, rows), 1)
    begin = begins(token)
    entry = f32(lax.broadcasted_iota(jnp.int32, (1, half), 1))
    speed = jnp.exp(-(2.0 * entry / head) * jnp.log(BASE))
    for t in tiles:
        column = place * rows + t.start + lax.broadcasted_iota(jnp.int32, (tile, 1), 0)
        angle = f32(column - begins(column)) * speed
        r.cosine[t, :] = jnp.cos(angle)
        r.sine[t, :] = jnp.sin(angle)
    gain_in = r.norm_in[...].reshape(1, width)
    gain_q = r.query_gain[...].reshape(1, head)
    gain_k = r.key_gain[...].reshape(1, head)
    gain_attn = r.norm_attn[...].reshape(1, width)
    gain_pre = r.norm_pre[...].reshape(1, width)
    gain_post = r.norm_post[...].reshape(1, width)

    def allowed(source):
        key = source * rows + lax.broadcasted_iota(jnp.int32, (rows, rows), 0)
        return (key >= begin) & (key <= token)

    loads["x"].wait()
    loads["w_key"].wait()
    loads["w_value"].wait()
    for name in weights:
        if name not in early:
            loads[name].start()
    for t in tiles:
        x = f32(r.x[t, :])
        r.a[t, :] = bf16(x * inverse_rms(x) * gain_in)
    r.kp[...] = dot(r.a[...], r.w_first[:, wide_k])
    r.kv[place, :, head : 2 * head] = bf16(dot(r.a[...], r.w_first[:, wide_v]))
    for t in tiles:
        kp = r.kp[t, :]
        r.kv[place, t, 0:head] = bf16(turn(kp * inverse_rms(kp) * gain_k, r.cosine[t, :], r.sine[t, :]))

    def send_kv(source, route):
        return pltpu.make_async_remote_copy(
            src_ref=r.kv.at[source],
            dst_ref=r.kv.at[source],
            send_sem=r.kv_send.at[route, source],
            recv_sem=r.kv_recv.at[source],
            device_id=peers["y"] if route else peers["up"],
            device_id_type=MESH,
        )

    def send_half(values):
        half_block = r.kv.at[0, :, head * values : head * (values + 1)]
        return pltpu.make_async_remote_copy(
            src_ref=half_block,
            dst_ref=half_block,
            send_sem=r.half_send.at[values],
            recv_sem=r.half_recv.at[values],
            device_id=peers["up"] if values else peers["y"],
            device_id_type=MESH,
        )

    meet(me, z_count)
    pl.when(z < last)(lambda: send_kv(place, 0).start())
    pl.when(y == 0)(lambda: send_kv(place, 1).start())

    loads["w_query"].wait()
    for h in range(heads):
        wide = slice(h * head, (h + 1) * head)
        r.qp[:, wide] = dot(r.a[...], r.w_first[:, wide])
        for t in tiles:
            qp = r.qp[t, wide]
            q = turn(qp * inverse_rms(qp) * gain_q, r.cosine[t, :], r.sine[t, :])
            q = bf16(q * (scale * LOG2E))
            r.q[h * rows + t.start : h * rows + t.stop, :] = q
            r.qt[:, h * rows + t.start : h * rows + t.stop] = q.T

    columns = [slice(h * rows, (h + 1) * rows) for h in range(heads)]

    def visit(source):
        vt = r.kv[source, :, head : 2 * head].T
        mask = allowed(source)
        for here in columns:
            p = jnp.where(mask, jnp.exp2(dot(r.kv[source, :, 0:head], r.qt[:, here])), 0.0)
            total = jnp.sum(p, axis=0, keepdims=True)
            o = dot(vt, bf16(p))
            r.total[:, here] = r.total[:, here] + total
            r.ot[:, here] = r.ot[:, here] + o

    r.total[...] = jnp.zeros_like(r.total)
    r.ot[...] = jnp.zeros_like(r.ot)

    def take_column(back):
        mine = place - 2 * back

        @pl.when(back <= z)
        def _():
            send_kv(mine, 0).wait_recv()
            pl.when(z < last)(lambda: send_kv(mine, 0).start())
            pl.when(mine > 0)(lambda: send_kv(mine, 1).start())
            pl.when(mine == 0)(lambda: send_half(0).start())

    def attend(step, carry):
        at = step - 1 - y
        back = at // 2 + 1
        other = (at >= 0) & (lax.rem(at + 2, 2) == 1)
        source = jnp.where(at >= 0, place - 2 * back + jnp.where(other, 1 - 2 * y, 0), place - step)

        @pl.when((step == 1) & (y == 1))
        def _():
            send_kv(place - 1, 1).wait_recv()
            pl.when((z == 0) & (z < last))(lambda: send_half(1).start())

        pl.when(at == 0)(lambda: take_column(1))

        @pl.when(other)
        def _():
            take_column(back + 1)
            pl.when(source > 0)(lambda: send_kv(source, 1).wait_recv())

            @pl.when(source == 0)
            def _():
                send_half(1).wait_recv()
                pl.when(z < last)(lambda: send_half(1).start())
                send_half(0).wait_recv()

        visit(source)
        return carry

    lax.fori_loop(0, 1 + y + 2 * z, attend, 0)
    for h, here in enumerate(columns):
        total = r.total[:, here]
        o = r.ot[:, here] * (1.0 / total)
        r.lse[:, here] = jnp.log2(total)
        r.ot[:, here] = o
        r.ob[:, h * head : (h + 1) * head] = bf16(o).T

    loads["w_out"].wait()
    r.ap[...] = dot(r.ob[:, 0:joined], r.w_out[...])
    for t in tiles:
        ap = r.ap[t, :]
        x1 = f32(r.x[t, :]) + ap * inverse_rms(ap) * gain_attn
        r.x1[t, :] = x1
        r.m[t, :] = bf16(x1 * inverse_rms(x1) * gain_pre)
    loads["w_gate"].wait()
    loads["w_up"].wait()
    block = hidden // 8

    def quarters(body):
        def both(pair, carry):
            for quarter in (2 * pair, 2 * pair + 1):
                body(pl.ds(pl.multiple_of(quarter * 2 * block, 128), 2 * block))
            return carry

        lax.fori_loop(0, 2, both, 0)

    def feed(cols):
        gate = dot(r.m[...], r.w_pair[0, :, cols])
        up = dot(r.m[...], r.w_pair[1, :, cols])
        inner = 0.7978845608028654 * (gate + 0.044715 * gate * gate * gate)
        th = jnp.tanh(inner)
        cdf = 0.5 * (1.0 + th)
        act = gate * cdf
        slope = cdf + 0.5 * gate * (1.0 - th * th) * 0.7978845608028654 * (1.0 + 3 * 0.044715 * gate * gate)
        r.hid[:, cols] = bf16(act * up)
        r.side_gate[:, cols] = bf16(slope * up)
        r.side_up[:, cols] = bf16(act)

    quarters(feed)
    loads["w_down"].wait()
    loads["dy"].wait()
    r.wide[...] = dot(r.hid[...], r.w_down[...])
    r.gains[...] = jnp.zeros_like(r.gains)

    def gain(k, terms):
        r.gains[k, :, 0 : terms.shape[1]] = r.gains[k, :, 0 : terms.shape[1]] + terms

    for t in tiles:
        f = r.wide[t, :]
        inverse = inverse_rms(f)
        r.out_held[t, :] = bf16(r.x1[t, :] + f * inverse * gain_post)
        df, g = rms_back(f, inverse, gain_post, f32(r.dy[t, :]))
        r.df[t, :] = bf16(df)
        gain(3, g)
    def two_blocks(body):
        def both(pair, carry):
            for j in (2 * pair, 2 * pair + 1):
                body(j, pl.ds(pl.multiple_of(j * block, 128), block))
            return carry

        lax.fori_loop(0, 4, both, 0)

    leaving = [
        pltpu.make_async_copy(r.out_held, r.out, r.load_sem.at[len(weights)]),
        pltpu.make_async_copy(r.dx_held, r.dx, r.load_sem.at[len(weights) + 1]),
    ]
    leaving[0].start()

    def down_grad(j, cols):
        r.g_down[j] = bf16(dot_tn(r.hid[:, cols], r.df[...]))

    two_blocks(down_grad)

    chunks = []
    sems = (r.red_send, r.red_recv, r.red_local)
    for name, count in r_plan(sizes):
        grad, total = r["g_" + name], r["t_" + name]
        step = grad.shape[1] // count
        for i in range(count):
            number, kind = len(chunks), FIRST[len(chunks)]
            make, first = (LineChunk, {"u": "x", "v": "y"}[kind]) if kind in "uv" else (Chunk, kind)
            landing = tuple(r[f"land{k}_{number}"] for k in range(len(make.landing(step))))
            chunks.append(make(number, grad, total, i * step, step, first, landing, sems, me, peers, z_count))

    def side_grads(part):
        def one(cols):
            dh = dot_nt(r.df[...], r.w_down[cols, :])
            r.side_gate[:, cols] = bf16(dh * f32(r.side_gate[:, cols]))
            r.side_up[:, cols] = bf16(dh * f32(r.side_up[:, cols]))

        quarters(one)

    def feed_grads(part):
        grad, side = ((r.g_gate, r.side_gate), (r.g_up, r.side_up))[part]

        def one(j, cols):
            grad[j] = bf16(dot_tn(r.m[...], side[:, cols]))

        two_blocks(one)

    def middle_back(part):
        r.wide[...] = dot_nt(r.side_gate[...], r.w_pair[0]) + dot_nt(r.side_up[...], r.w_pair[1])
        for t in tiles:
            x1 = r.x1[t, :]
            dx1, g = rms_back(x1, inverse_rms(x1), gain_pre, r.wide[t, :])
            gain(2, g)
            dx1 = dx1 + f32(r.dy[t, :])
            r.x1[t, :] = dx1
            ap = r.ap[t, :]
            dap, g = rms_back(ap, inverse_rms(ap), gain_attn, dx1)
            gain(1, g)
            r.dap[t, :] = bf16(dap)

    def out_back(part):
        for h, here in enumerate(columns):
            wide = slice(h * head, (h + 1) * head)
            g = bf16(dot_tn(r.ob[:, wide], r.dap[...]))
            r.g_out[2 * h] = g[0:half]
            r.g_out[2 * h + 1] = g[half:head]
            do = bf16(dot_nt(r.dap[...], r.w_out[wide, :]))
            r.do[here, :] = do
            turned = do.T
            r.dot[:, here] = turned
            r.delta[:, here] = jnp.sum(f32(turned) * r.ot[:, here], axis=0, keepdims=True)
        r.ot[...] = jnp.zeros_like(r.ot)

    probs, dscores = r.hid.at[:, 0 : heads * rows], r.side_gate.at[:, 0 : heads * rows]

    def visit_back(source, target):
        kt = r.kv[source, :, 0:head].T
        mask = allowed(source)
        for here in columns:
            s = dot(r.kv[source, :, 0:head], r.qt[:, here])
            p = jnp.where(mask, jnp.exp2(s - r.lse[:, here]), 0.0)
            dp = dot(r.kv[source, :, head : 2 * head], r.dot[:, here])
            probs[:, here] = bf16(p)
            dscores[:, here] = bf16(p * (dp - r.delta[:, here]))
        target[:, 0:head] = bf16(dot(dscores[...], r.q[...]))
        target[:, head : 2 * head] = bf16(dot(probs[...], r.do[...]))
        for here in columns:
            r.ot[:, here] = r.ot[:, here] + dot(kt, dscores[:, here])

    def staged(own, row):
        return r.w_pair.at[own, 0:rows, row * 2 * head : (row + 1) * 2 * head]

    def to_partner(row):
        return pltpu.make_async_remote_copy(
            src_ref=staged(0, row),
            dst_ref=r.from_partner.at[row],
            send_sem=r.dkv_send.at[0, row],
            recv_sem=r.dkv_recv.at[0, row],
            device_id=peers["y"],
            device_id_type=MESH,
        )

    def to_below(row):
        return pltpu.make_async_remote_copy(
            src_ref=staged(1, row),
            dst_ref=r.from_above.at[row],
            send_sem=r.dkv_send.at[1, row],
            recv_sem=r.dkv_recv.at[1, row],
            device_id=peers["down"],
            device_id_type=MESH,
        )

    def visit_row(row):
        def one(own, carry):
            column = jnp.where(own == 1, y, 1 - y)

            @pl.when((row < z) | ((row == z) & (column <= y)))
            def _():
                visit_back(2 * row + column, staged(own, row))
                pl.when(own == 0)(lambda: to_partner(row).start())

            return carry

        lax.fori_loop(0, 2, one, 0)

    def pass_down(row):
        @pl.when(row < z)
        def _():
            to_partner(row).wait_recv()
            pl.when(z < last)(lambda: to_below(row).wait_recv())
            for t in tiles:
                value = f32(staged(1, row)[t, :]) + f32(r.from_partner[row, t, :])
                above = jnp.where(z < last, f32(r.from_above[row, t, :]), 0.0)
                staged(1, row)[t, :] = bf16(value + above)
            to_below(row).start()

    def queries_back(h):
        wide = slice(h * head, (h + 1) * head)
        for t in tiles:
            dq = (r.ot[:, h * rows + t.start : h * rows + t.stop] * scale).T
            qp = r.qp[t, wide]
            dqp, g = rms_back(qp, inverse_rms(qp), gain_q, turn_back(dq, r.cosine[t, :], r.sine[t, :]))
            gain(4, g)
            r.ob[t, wide] = bf16(dqp)

    def query_grad(part):
        for h in range(heads):
            g = bf16(dot_tn(r.a[...], r.ob[:, h * head : (h + 1) * head]))
            r.g_query[2 * h] = g[:, 0:half]
            r.g_query[2 * h + 1] = g[:, half:head]

    def own_total(part):
        for row in range(z_count):

            @pl.when(row == z)
            def _():
                pl.when(y == 0)(lambda: to_partner(row).wait_recv())
                pl.when(z < last)(lambda: to_below(row).wait_recv())
                for t in tiles:
                    beside = jnp.where(y == 0, f32(r.from_partner[row, t, :]), 0.0)
                    above = jnp.where(z < last, f32(r.from_above[row, t, :]), 0.0)
                    r.dkv[t, :] = f32(staged(1, row)[t, :]) + beside + above

    def keys_back(part):
        for t in tiles:
            dk = r.dkv[t, 0:head] * LN2
            kp = r.kp[t, :]
            dkp, g = rms_back(kp, inverse_rms(kp), gain_k, turn_back(dk, r.cosine[t, :], r.sine[t, :]))
            gain(5, g)
            r.ob[t, wide_k] = bf16(dkp)
            r.ob[t, wide_v] = bf16(r.dkv[t, head : 2 * head])
        low = width // 2
        g = bf16(dot_tn(r.a[...], r.ob[:, joined : joined + 2 * head]))
        for p in range(8):
            which, upper, side = p // 4, (p // 2) % 2, p % 2
            left = which * head + side * half
            r.g_kv[p] = g[upper * low : (upper + 1) * low, left : left + half]
        r.wide[...] = dot_nt(r.ob[...], r.w_first[...])
        for t in tiles:
            x = f32(r.x[t, :])
            dx, g = rms_back(x, inverse_rms(x), gain_in, r.wide[t, :])
            gain(0, g)
            r.dx_held[t, :] = bf16(r.x1[t, :] + dx)
        leaving[1].start()
        r.g_gain[...] = jnp.zeros_like(r.g_gain)
        at = 0
        for k, size in enumerate((width, width, width, width, head, head)):
            g = jnp.sum(r.gains[k], axis=0, keepdims=True)
            for part in range(size // 128):
                r.g_gain[at // 16, at % 16 : at % 16 + 1, :] = g[:, part * 128 : (part + 1) * 128]
                at += 1

    work = {
        "S": side_grads,
        "F": feed_grads,
        "M": middle_back,
        "O": out_back,
        "V": visit_row,
        "P": pass_down,
        "Q": queries_back,
        "G": query_grad,
        "T": own_total,
        "K": keys_back,
    }
    for what, step in schedule:
        if what in work:
            work[what](step)
        else:
            chunks[what].tick(step)

    for item in leaving:
        item.wait()
    pl.when(z < last)(lambda: send_kv(place, 0).wait_send())
    pl.when(y == 0)(lambda: send_kv(place, 1).wait_send())
    pl.when((y == 1) & (z < last))(lambda: send_half(1).wait_send())
    pl.when((y == 0) & (z > 0))(lambda: send_half(0).wait_send())
    for back in range(1, z_count):

        @pl.when(back <= z)
        def _():
            mine = place - 2 * back
            pl.when(z < last)(lambda: send_kv(mine, 0).wait_send())
            pl.when(mine > 0)(lambda: send_kv(mine, 1).wait_send())

    for row in range(z_count):
        pl.when((row < z) | ((row == z) & (y == 1)))(lambda: to_partner(row).wait_send())
        pl.when(row < z)(lambda: to_below(row).wait_send())


def r_plan(sizes):
    return list(zip(("down", "gate", "up", "out", "query", "kv", "gain"), PIECES, strict=True))


def gradient_shapes(sizes):
    rows, width, hidden, heads, head, z_count = sizes
    joined, half = heads * head, head // 2
    return {
        "down": ((8, hidden // 8, width), (8, hidden // 8, width)),
        "gate": ((8, width, hidden // 8), (width, hidden)),
        "up": ((8, width, hidden // 8), (width, hidden)),
        "out": ((8, joined // 8, width), (8, joined // 8, width)),
        "query": ((8, width, joined // 8), (width, joined)),
        "kv": ((8, width // 2, half), (2, 2, width // 2, head)),
        "gain": ((8, 16, 128), (8, 16, 128)),
    }


def layer_scratch(sizes):
    rows, width, hidden, heads, head, z_count = sizes
    joined = heads * head
    low, wide = jnp.bfloat16, jnp.float32
    arrays = {
        "x": ((rows, width), low),
        "w_first": ((width, joined + 2 * head), low),
        "w_out": ((joined, width), low),
        "w_pair": ((2, width, hidden), low),
        "w_down": ((hidden, width), low),
        "dy": ((rows, width), low),
        "a": ((rows, width), low),
        "out_held": ((rows, width), low),
        "dx_held": ((rows, width), low),
        "gains": ((6, 8, width), wide),
        "kp": ((rows, head), wide),
        "kv": ((2 * z_count, rows, 2 * head), low),
        "qp": ((rows, joined), wide),
        "q": ((heads * rows, head), low),
        "qt": ((head, heads * rows), low),
        "cosine": ((rows, head // 2), wide),
        "sine": ((rows, head // 2), wide),
        "wide": ((rows, width), wide),
        "ot": ((head, heads * rows), wide),
        "total": ((1, heads * rows), wide),
        "lse": ((1, heads * rows), wide),
        "delta": ((1, heads * rows), wide),
        "ob": ((rows, joined + 2 * head), low),
        "ap": ((rows, width), wide),
        "x1": ((rows, width), wide),
        "m": ((rows, width), low),
        "hid": ((rows, hidden), low),
        "side_gate": ((rows, hidden), low),
        "side_up": ((rows, hidden), low),
        "df": ((rows, width), low),
        "dap": ((rows, width), low),
        "do": ((heads * rows, head), low),
        "dot": ((head, heads * rows), low),
        "dkv": ((rows, 2 * head), wide),
        "from_partner": ((z_count, rows, 2 * head), low),
        "from_above": ((z_count, rows, 2 * head), low),
    }
    shapes = gradient_shapes(sizes)
    pieces = 0
    for name, count in r_plan(sizes):
        (eight, high, columns), kind = shapes[name][0], wide if name == "gain" else low
        step = high // count
        pieces += count
        arrays["g_" + name] = (shapes[name][0], kind)
        for number in range(pieces - count, pieces):
            for k, shape in enumerate(LineChunk.landing(step) if FIRST[number] in "uv" else Chunk.landing(step)):
                arrays[f"land{k}_{number}"] = (shape + (columns,), kind)
    sems = {
        "load_sem": (11,),
        "kv_send": (2, 2 * z_count),
        "kv_recv": (2 * z_count,),
        "half_send": (2,),
        "half_recv": (2,),
        "dkv_send": (2, z_count),
        "dkv_recv": (2, z_count),
        "red_send": (pieces, STAGES),
        "red_recv": (pieces, STAGES),
        "red_local": (pieces,),
    }
    return arrays, sems


def layer_bytes(sizes):
    total = 0
    for shape, kind in layer_scratch(sizes)[0].values():
        size = jnp.dtype(kind).itemsize
        for n in shape[:-2]:
            size *= n
        total += size * max(shape[-2], 8) * max(shape[-1], 128)
    return total


VMEM_BYTES = 64 * 2**20


def widen_kernel(count, gain_sizes, *refs):
    ins, table_in, both, tokens = refs[: count - 2], refs[count - 2], refs[count - 1], refs[count : count + 2]
    refs = refs[count + 2 :]
    outs, gains_out, tokens_out = refs[:count], refs[count : count + 6], refs[count + 6 : count + 8]
    refs = refs[count + 8 :]
    narrow, broad, gains, (table, came, gone) = refs[: count + 2], refs[count + 2 : 2 * count + 2], refs[2 * count + 2 : 2 * count + 8], refs[2 * count + 8 :]
    ins = (both.at[0], both.at[1]) + ins + tokens + (table_in,)
    outs = outs + tokens_out + gains_out
    held = broad + narrow[count:] + gains
    loads = [pltpu.make_async_copy(ins[i], (narrow + (table,))[i], came.at[i]) for i in range(count + 3)]
    stores = [pltpu.make_async_copy(held[i], outs[i], gone.at[i]) for i in range(count + 8)]
    order = (*range(2, count), 0, 1)
    for i in (*order, *range(count, count + 3)):
        loads[i].start()
    for i in order:
        loads[i].wait()

        def body(j, carry):
            here = pl.ds(pl.multiple_of(j * 64, 64), 64)
            broad[i][here, :] = f32(narrow[i][here, :])
            return carry

        lax.fori_loop(0, narrow[i].shape[0] // 64, body, 0)
        stores[i].start()
    for i in (count, count + 1):
        loads[i].wait()
        stores[i].start()
    loads[count + 2].wait()
    at = 0
    for i, gain in enumerate(gains):
        for part in range(gain_sizes[i] // 128):
            gain[part * 128 : (part + 1) * 128] = table[at // 16, at % 16, :]
            at += 1
        stores[count + 2 + i].start()
    for item in stores:
        item.wait()


def widen(both, matrices, table, tokens, gain_sizes):
    count = len(matrices) + 2
    shapes = [both.shape[1:]] * 2 + [v.shape for v in matrices]
    anywhere = pl.BlockSpec(memory_space=pl.ANY)
    return pl.pallas_call(
        functools.partial(widen_kernel, count, gain_sizes),
        out_shape=tuple(jax.ShapeDtypeStruct(shape, jnp.float32) for shape in shapes)
        + tuple(jax.ShapeDtypeStruct((n,), jnp.float32) for n in gain_sizes)
        + tuple(jax.ShapeDtypeStruct(v.shape, v.dtype) for v in tokens),
        in_specs=[anywhere] * (count + 2),
        out_specs=tuple([anywhere] * (count + len(gain_sizes) + 2)),
        scratch_shapes=[pltpu.VMEM(shape, jnp.bfloat16) for shape in shapes + [v.shape for v in tokens]]
        + [pltpu.VMEM(shape, jnp.float32) for shape in shapes]
        + [pltpu.VMEM((n,), jnp.float32) for n in gain_sizes]
        + [pltpu.VMEM(table.shape, table.dtype)]
        + [pltpu.SemaphoreType.DMA((count + 3,)), pltpu.SemaphoreType.DMA((count + 8,))],
        compiler_params=pltpu.CompilerParams(vmem_limit_bytes=VMEM_BYTES),
    )(*matrices, table, both, *tokens)


def whole_layer(sizes, tokens, lengths, cotangent, norm_in, w_query, w_key, w_value, query_gain, key_gain, w_out, norm_attn, norm_pre, w_gate, w_up, w_down, norm_post):
    rows, width, hidden, heads, head, z_count = sizes
    joined = heads * head
    inputs = {
        "lengths": lengths,
        "norm_in": norm_in,
        "query_gain": query_gain,
        "key_gain": key_gain,
        "norm_attn": norm_attn,
        "norm_pre": norm_pre,
        "norm_post": norm_post,
        "x_in": tokens[0],
        "w_key_in": w_key,
        "w_value_in": w_value,
        "w_query_in": w_query,
        "w_out_in": w_out,
        "w_gate_in": w_gate,
        "w_up_in": w_up,
        "w_down_in": w_down,
        "dy_in": cotangent[0],
    }
    spaces = {name: pltpu.SMEM if name == "lengths" else pl.ANY if name.endswith("_in") and name != "norm_in" else pltpu.VMEM for name in inputs}
    shapes = gradient_shapes(sizes)
    outputs = {"out": (rows, width), "dx": (rows, width)}
    outputs.update({"t_" + name: shapes[name][1] for name in shapes})
    arrays, sems = layer_scratch(sizes)
    names = list(inputs) + list(outputs) + list(arrays) + list(sems)
    results = pl.pallas_call(
        functools.partial(layer_kernel, sizes, SCHEDULES[z_count], names),
        out_shape=tuple(
            jax.ShapeDtypeStruct(shape, jnp.float32 if name == "t_gain" else jnp.bfloat16) for name, shape in outputs.items()
        ),
        in_specs=[pl.BlockSpec(memory_space=spaces[name]) for name in inputs],
        out_specs=tuple(
            pl.BlockSpec(memory_space=pl.ANY) for name in outputs
        ),
        scratch_shapes=[pltpu.VMEM(*item) for item in arrays.values()]
        + [pltpu.SemaphoreType.DMA(item) for item in sems.values()],
        compiler_params=pltpu.CompilerParams(
            collective_id=1, has_side_effects=True, vmem_limit_bytes=VMEM_BYTES
        ),
    )(*inputs.values())
    r = Names(zip(outputs, results, strict=True))
    matrices = [
        r.t_query,
        r.t_out.reshape(joined, width),
        r.t_gate,
        r.t_up,
        r.t_down.reshape(hidden, width),
    ]
    both = r.t_kv.reshape(2, width, head)
    sums = widen(both, matrices, r.t_gain, (r.out, r.dx), (width, width, width, width, head, head))
    g_key, g_value, g_query, g_out, g_gate, g_up, g_down = sums[:7]
    g_in, g_attn, g_pre, g_post, g_qgain, g_kgain, output, input_grad = sums[7:]
    return (
        output[None],
        input_grad[None],
        g_in,
        g_query,
        g_key,
        g_value,
        g_qgain,
        g_kgain,
        g_out,
        g_attn,
        g_pre,
        g_gate,
        g_up,
        g_down,
        g_post,
    )


def per_device(
    tokens,
    lengths,
    cotangent,
    norm_in,
    w_query,
    w_key,
    w_value,
    query_gain,
    key_gain,
    w_out,
    norm_attn,
    norm_pre,
    w_gate,
    w_up,
    w_down,
    norm_post,
):
    rows = tokens.shape[1]
    head = query_gain.shape[0]
    heads = w_query.shape[1] // head
    sizes = (rows, tokens.shape[2], w_gate.shape[1], heads, head, lax.axis_size(BLOCKS) // 2)
    if sizes[-1] in SCHEDULES and layer_bytes(sizes) <= VMEM_BYTES:
        return whole_layer(
            sizes,
            tokens,
            lengths,
            cotangent,
            norm_in,
            w_query,
            w_key,
            w_value,
            query_gain,
            key_gain,
            w_out,
            norm_attn,
            norm_pre,
            w_gate,
            w_up,
            w_down,
            norm_post,
        )
    scale = head ** (-0.5)
    count = lax.axis_size(BLOCKS)
    place = lax.axis_index(BLOCKS)
    row = lengths[0]
    local_idx = place * rows + jnp.arange(rows, dtype=jnp.int32)
    seg_q, pos_q = segment_of(local_idx, row)
    cosine, sine = rotary_tables(pos_q, head)

    def block_mask(source):
        key_idx = source * rows + jnp.arange(rows, dtype=jnp.int32)
        seg_k, unused = segment_of(key_idx, row)
        return (seg_q[:, None] == seg_k[None, :]) & (local_idx[:, None] >= key_idx[None, :])

    x_in = tokens[0].astype(jnp.float32)
    normal_a = normed(x_in, norm_in).astype(jnp.bfloat16)
    q_proj = jnp.dot(normal_a, w_query, preferred_element_type=jnp.float32).reshape(
        rows, heads, head
    )
    k_proj = jnp.dot(normal_a, w_key, preferred_element_type=jnp.float32)
    v_proj = jnp.dot(normal_a, w_value, preferred_element_type=jnp.float32)
    query = prepare(q_proj, query_gain, cosine[:, None, :], sine[:, None, :]).astype(jnp.bfloat16)
    keys = prepare(k_proj, key_gain, cosine, sine).astype(jnp.bfloat16)
    values = v_proj.astype(jnp.bfloat16)
    q_heads = jnp.transpose(query, (1, 0, 2))

    def absorb(state, pair, source):
        allowed = block_mask(source)
        big, total, accum = state
        raw = jnp.einsum("hqd,kd->hqk", q_heads, pair[0], preferred_element_type=jnp.float32)
        scores = jnp.where(allowed[None], scale * raw, NEG)
        big_new = jnp.maximum(big, jnp.max(scores, axis=-1, keepdims=True))
        expo = jnp.where(allowed[None], jnp.exp(scores - big_new), 0.0)
        fade = jnp.exp(big - big_new)
        total = total * fade + jnp.sum(expo, axis=-1, keepdims=True)
        accum = accum * fade + jnp.einsum(
            "hqk,kd->hqd", expo.astype(jnp.bfloat16), pair[1], preferred_element_type=jnp.float32
        )
        return (big_new, total, accum)

    pair = jnp.stack([keys, values])
    state = (
        jnp.full((heads, rows, 1), NEG, jnp.float32),
        jnp.zeros((heads, rows, 1), jnp.float32),
        jnp.zeros((heads, rows, head), jnp.float32),
    )
    state = absorb(state, pair, place)

    def cycle_forward(step, carry):
        inner, moving = carry
        moving = from_behind(moving, BLOCKS, 1)
        return (absorb(inner, moving, (place - step) % count), moving)

    state, unused_pair = lax.fori_loop(1, count, cycle_forward, (state, pair))
    big, total, accum = state
    attended = accum / total
    lse = big + jnp.log(total)
    joined = jnp.transpose(attended, (1, 0, 2)).reshape(rows, heads * head).astype(jnp.bfloat16)
    a_proj = jnp.dot(joined, w_out, preferred_element_type=jnp.float32)
    x_mid = x_in + normed(a_proj, norm_attn)
    mixed = normed(x_mid, norm_pre).astype(jnp.bfloat16)
    gate = jnp.dot(mixed, w_gate, preferred_element_type=jnp.float32)
    upper = jnp.dot(mixed, w_up, preferred_element_type=jnp.float32)

    def activate(gate_in, upper_in):
        return jax.nn.gelu(gate_in, approximate=True) * upper_in

    hidden = activate(gate, upper).astype(jnp.bfloat16)
    f_proj = jnp.dot(hidden, w_down, preferred_element_type=jnp.float32)
    output = x_mid + normed(f_proj, norm_post)
    grad_y = cotangent[0].astype(jnp.float32)
    d_fproj, g_post = normed_back(f_proj, norm_post, grad_y)
    d_fproj = d_fproj.astype(jnp.bfloat16)
    g_down = dot_tn(hidden, d_fproj)
    d_hidden = dot_nt(d_fproj, w_down)
    d_gate, d_upper = jax.vjp(activate, gate, upper)[1](d_hidden)
    d_gate = d_gate.astype(jnp.bfloat16)
    d_upper = d_upper.astype(jnp.bfloat16)
    g_gate = dot_tn(mixed, d_gate)
    g_up = dot_tn(mixed, d_upper)
    d_mixed = dot_nt(d_gate, w_gate) + dot_nt(d_upper, w_up)
    d_mid, g_pre = normed_back(x_mid, norm_pre, d_mixed)
    d_mid = grad_y + d_mid
    d_aproj, g_attn = normed_back(a_proj, norm_attn, d_mid)
    d_aproj = d_aproj.astype(jnp.bfloat16)
    g_out = dot_tn(joined, d_aproj)
    d_joined = dot_nt(d_aproj, w_out).astype(
        jnp.bfloat16
    )
    do_heads = jnp.transpose(d_joined.reshape(rows, heads, head), (1, 0, 2))
    delta = jnp.sum(do_heads.astype(jnp.float32) * attended, axis=-1, keepdims=True)

    def visit(d_query, moving, grads, source):
        allowed = block_mask(source)
        raw = jnp.einsum("hqd,kd->hqk", q_heads, moving[0], preferred_element_type=jnp.float32)
        probs = jnp.where(allowed[None], jnp.exp(scale * raw - lse), 0.0)
        dv_add = jnp.einsum(
            "hqk,hqd->kd", probs.astype(jnp.bfloat16), do_heads, preferred_element_type=jnp.float32
        )
        d_probs = jnp.einsum("hqd,kd->hqk", do_heads, moving[1], preferred_element_type=jnp.float32)
        d_scores = (scale * probs * (d_probs - delta)).astype(jnp.bfloat16)
        dq_add = jnp.einsum("hqk,kd->hqd", d_scores, moving[0], preferred_element_type=jnp.float32)
        dk_add = jnp.einsum("hqk,hqd->kd", d_scores, q_heads, preferred_element_type=jnp.float32)
        return (d_query + dq_add, grads + jnp.stack([dk_add, dv_add]))

    d_query = jnp.zeros((heads, rows, head), jnp.float32)
    grads = jnp.zeros((2, rows, head), jnp.float32)
    d_query, grads = visit(d_query, pair, grads, place)

    def cycle_backward(step, carry):
        dq_in, moving, grads_in = carry
        moving = from_behind(moving, BLOCKS, 1)
        grads_in = pass_home(grads_in)
        dq_in, grads_in = visit(dq_in, moving, grads_in, (place - step) % count)
        return (dq_in, moving, grads_in)

    d_query, unused_pair, grads = lax.fori_loop(1, count, cycle_backward, (d_query, pair, grads))
    grads = pass_home(grads)

    def query_piece(proj, gain):
        return prepare(proj, gain, cosine[:, None, :], sine[:, None, :])

    def key_piece(proj, gain):
        return prepare(proj, gain, cosine, sine)

    d_qproj, g_qgain = jax.vjp(query_piece, q_proj, query_gain)[1](
        jnp.transpose(d_query, (1, 0, 2))
    )
    d_kproj, g_kgain = jax.vjp(key_piece, k_proj, key_gain)[1](grads[0])
    d_qproj = d_qproj.reshape(rows, heads * head).astype(jnp.bfloat16)
    d_kproj = d_kproj.astype(jnp.bfloat16)
    d_vproj = grads[1].astype(jnp.bfloat16)
    g_query = dot_tn(normal_a, d_qproj)
    g_key = dot_tn(normal_a, d_kproj)
    g_value = dot_tn(normal_a, d_vproj)
    d_normal = dot_nt(d_qproj, w_query)
    d_normal = d_normal + dot_nt(d_kproj, w_key)
    d_normal = d_normal + dot_nt(d_vproj, w_value)
    d_input, g_in = normed_back(x_in, norm_in, d_normal)
    input_grad = (d_mid + d_input).astype(jnp.bfloat16)
    (
        g_in,
        g_query,
        g_key,
        g_value,
        g_qgain,
        g_kgain,
        g_out,
        g_attn,
        g_pre,
        g_gate,
        g_up,
        g_down,
        g_post,
    ) = sum_gradients(
        (
            g_in,
            g_query,
            g_key,
            g_value,
            g_qgain,
            g_kgain,
            g_out,
            g_attn,
            g_pre,
            g_gate,
            g_up,
            g_down,
            g_post,
        )
    )
    return (
        output.astype(jnp.bfloat16)[None],
        input_grad[None],
        g_in,
        g_query,
        g_key,
        g_value,
        g_qgain,
        g_kgain,
        g_out,
        g_attn,
        g_pre,
        g_gate,
        g_up,
        g_down,
        g_post,
    )


def solution(mesh):
    in_specs = (
        P(PARTS, BLOCKS, None),
        P(PARTS, None),
        P(PARTS, BLOCKS, None),
        P(),
        P(),
        P(),
        P(),
        P(),
        P(),
        P(),
        P(),
        P(),
        P(),
        P(),
        P(),
        P(),
    )
    out_specs = (
        P(PARTS, BLOCKS, None),
        P(PARTS, BLOCKS, None),
        P(),
        P(),
        P(),
        P(),
        P(),
        P(),
        P(),
        P(),
        P(),
        P(),
        P(),
        P(),
        P(),
    )
    return jax.shard_map(
        per_device, mesh=mesh, in_specs=in_specs, out_specs=out_specs, check_vma=False
    )
```

```python
import functools

import jax
import jax.numpy as jnp
from jax import lax
from jax.experimental import pallas as pl
from jax.experimental.pallas import tpu as pltpu
from jax.sharding import PartitionSpec as P

BLOCKS, PARTS = "blk", "dp"
EPS = 1e-06
BASE = 1000000.0
NEG = -1e30


def shifted(array, axis, by):
    peers = lax.axis_size(axis)
    return lax.ppermute(array, axis, [(i, (i + by) % peers) for i in range(peers)])


def from_behind(block, axis, distance):
    devices = range(lax.axis_size(axis))
    route = [(i - distance, i) for i in devices if i - distance in devices]
    return lax.ppermute(block, axis, route)


def normed(value, gain):
    return value * lax.rsqrt(jnp.mean(value * value, axis=-1, keepdims=True) + EPS) * gain


def normed_back(value, gain, grad):
    return jax.vjp(normed, value, gain)[1](grad)


def segment_of(index, row):
    ends = jnp.cumsum(row)
    seg = jnp.sum((index[:, None] >= ends[None, :]).astype(jnp.int32), axis=1)
    starts = ends - row
    slots = jnp.arange(row.shape[0], dtype=jnp.int32)
    begin = jnp.sum(jnp.where(slots[None, :] == seg[:, None], starts[None, :], 0), axis=1)
    return (seg, index - begin)


def rotary_tables(places, head):
    half = head // 2
    freq = jnp.exp(-(2.0 * jnp.arange(half, dtype=jnp.float32) / head) * jnp.log(BASE))
    angle = places.astype(jnp.float32)[:, None] * freq[None, :]
    return (jnp.cos(angle), jnp.sin(angle))


def prepare(proj, gain, cosine, sine):
    value = normed(proj, gain)
    half = value.shape[-1] // 2
    first = value[..., :half]
    second = value[..., half:]
    return jnp.concatenate(
        [first * cosine - second * sine, second * cosine + first * sine], axis=-1
    )


def pass_home(grads):
    return shifted(grads.astype(jnp.bfloat16), BLOCKS, 1).astype(grads.dtype)


MESH = pl.DeviceIdType.MESH


def where_am_i():
    place = lax.axis_index(BLOCKS)
    part = lax.axis_index(PARTS)
    return {
        "z": place // 2,
        "y": lax.rem(place, 2),
        "x": part // 2,
        "core": lax.rem(part, 2),
        "place": place,
        "part": part,
    }


def peers_of(me):
    place, part = me["place"], me["part"]
    return {
        "core": {BLOCKS: place, PARTS: part + 1 - 2 * me["core"]},
        "x": {BLOCKS: place, PARTS: part + 2 - 4 * me["x"]},
        "y": {BLOCKS: place + 1 - 2 * me["y"], PARTS: part},
        "up": {BLOCKS: place + 2, PARTS: part},
        "down": {BLOCKS: place - 2, PARTS: part},
    }


def greet(me, peers, z_count):
    barrier = pltpu.get_barrier_semaphore()
    for name in ("core", "x", "y"):
        pl.semaphore_signal(barrier, inc=1, device_id=peers[name], device_id_type=MESH)

    @pl.when(me["z"] < z_count - 1)
    def _():
        pl.semaphore_signal(barrier, inc=1, device_id=peers["up"], device_id_type=MESH)

    @pl.when(me["z"] > 0)
    def _():
        pl.semaphore_signal(barrier, inc=1, device_id=peers["down"], device_id_type=MESH)


def meet(me, z_count):
    ends = (me["z"] == 0).astype(jnp.int32) + (me["z"] == z_count - 1).astype(jnp.int32)
    pl.semaphore_wait(pltpu.get_barrier_semaphore(), 5 - ends)


def add_into(target, start, row, extra, count, rows):
    step = rows if rows < 32 else 16
    for candidate in (160, 128, 80, 64, 48, 32):
        if rows % candidate == 0:
            step = candidate
            break

    def body(index, carry):
        e = index // (rows // step)
        at = pl.multiple_of(lax.rem(index, rows // step) * step, 8)
        here = pl.ds(pl.multiple_of(row + at, 8), step)
        target[start + e, here, :] = target[start + e, here, :] + extra[e, pl.ds(at, step), :]
        return carry

    lax.fori_loop(0, count * (rows // step), body, 0)


STAGES = 10


class Chunk:
    def __init__(self, number, grad, total, row, rows, first, landing, sems, me, peers, z_count):
        self.grad, self.total, self.row, self.rows = grad, total, row, rows
        self.first, self.second = ("x", "y") if first == "x" else ("y", "x")
        self.land0, self.land1, self.land2 = landing
        self.send, self.recv, self.local = sems
        self.number, self.me, self.peers, self.z_count = number, me, peers, z_count
        self.b1, self.b2, self.core = me[self.first], me[self.second], me["core"]
        self.quad = 4 * self.core
        self.pair = self.quad + 2 * self.b1
        self.own = self.pair + self.b2
        self.half = rows // 2

    @staticmethod
    def landing(rows):
        return ((4, rows), (2, rows), (1, 2 * rows))

    def piece(self, start, count, upper=None):
        if upper is None:
            return self.grad.at[pl.ds(start, count), pl.ds(self.row, self.rows), :]
        row = self.row if upper else self.row + self.half
        return self.grad.at[pl.ds(start, count), pl.ds(row, self.half), :]

    def spot(self, count, upper=None):
        row, rows = self.row, self.rows
        if upper is not None:
            row, rows = (row if upper else row + self.half), self.half
        here, columns = pl.ds(row, rows), self.grad.shape[2]
        start = {1: self.own, 2: self.pair, 4: self.quad}[count]
        if len(self.total.shape) == 2:
            return self.total.at[here, pl.ds(pl.multiple_of(start * columns, 128), count * columns)]
        if len(self.total.shape) == 4:
            if count == 4:
                return self.total.at[self.core, :, here, :]
            if count == 2:
                return self.total.at[self.core, self.b1, here, :]
            return self.total.at[self.core, self.b1, here, pl.ds(pl.multiple_of(self.b2 * columns, 128), columns)]
        if count == 1:
            return self.total.at[start, here, :]
        return self.total.at[pl.ds(start, count), here, :]

    def mine(self, upper):
        return self.grad.at[self.own, pl.ds(self.row if upper else self.row + self.half, self.half), :]

    def keep(self, upper):
        return pltpu.make_async_copy(
            self.mine(upper), self.spot(1, upper), self.local.at[self.number]
        )

    def copy(self, stage, peer, source, target):
        return pltpu.make_async_remote_copy(
            src_ref=source,
            dst_ref=target,
            send_sem=self.send.at[self.number, stage],
            recv_sem=self.recv.at[self.number, stage],
            device_id=self.peers[peer],
            device_id_type=MESH,
        )

    def reduce_up(self):
        return self.copy(3, "up", self.piece(self.own, 1, True), self.land2.at[:, pl.ds(self.rows, self.half), :])

    def reduce_down(self):
        return self.copy(4, "down", self.piece(self.own, 1, False), self.land2.at[:, pl.ds(self.rows + self.half, self.half), :])

    def spread_down(self, fresh=False):
        here = self.spot(1, True)
        return self.copy(5, "down", self.mine(True) if fresh else here, here)

    def spread_up(self, fresh=False):
        here = self.spot(1, False)
        return self.copy(6, "up", self.mine(False) if fresh else here, here)

    def step0(self):
        return self.copy(0, "core", self.piece(4 - self.quad, 4), self.land0)

    def step1(self):
        return self.copy(1, self.first, self.piece(self.quad + 2 - 2 * self.b1, 2), self.land1)

    def step2(self):
        return self.copy(2, self.second, self.piece(self.pair + 1 - self.b2, 1), self.land2.at[:, pl.ds(0, self.rows), :])

    def gather(self, stage):
        count, peer = ((1, self.second), (2, self.first), (4, "core"))[stage - 7]
        here = self.spot(count)
        return self.copy(stage, peer, here, here)

    def arrive_upper(self):
        z, last = self.me["z"], self.z_count - 1

        @pl.when(z > 0)
        def _():
            self.reduce_up().wait_recv()
            add_into(self.grad, self.own, self.row, self.land2.at[:, pl.ds(self.rows, self.half), :], 1, self.half)

            @pl.when(z < last)
            def _():
                self.reduce_up().start()

            @pl.when(z == last)
            def _():
                self.spread_down(True).start()
                self.keep(True).start()

    def arrive_lower(self):
        z, last = self.me["z"], self.z_count - 1

        @pl.when(z < last)
        def _():
            self.reduce_down().wait_recv()
            add_into(self.grad, self.own, self.row + self.half, self.land2.at[:, pl.ds(self.rows + self.half, self.half), :], 1, self.half)

            @pl.when(z > 0)
            def _():
                self.reduce_down().start()

            @pl.when(z == 0)
            def _():
                self.spread_up(True).start()
                self.keep(False).start()

    def back_upper(self):
        z, last = self.me["z"], self.z_count - 1

        @pl.when(z < last)
        def _():
            self.spread_down().wait_recv()

            @pl.when(z > 0)
            def _():
                self.spread_down().start()

    def back_lower(self):
        z, last = self.me["z"], self.z_count - 1

        @pl.when(z > 0)
        def _():
            self.spread_up().wait_recv()

            @pl.when(z < last)
            def _():
                self.spread_up().start()

    def tick(self, op):
        z, last = self.me["z"], self.z_count - 1
        if op == 0:
            self.step0().start()
        elif op == 1:
            self.step0().wait_recv()
            add_into(self.grad, self.quad, self.row, self.land0, 4, self.rows)
            self.step1().start()
        elif op == 2:
            self.step1().wait_recv()
            add_into(self.grad, self.pair, self.row, self.land1, 2, self.rows)
            self.step2().start()
        elif op == 3:
            self.step2().wait_recv()
            add_into(self.grad, self.own, self.row, self.land2, 1, self.rows)

            @pl.when(z == 0)
            def _():
                self.reduce_up().start()

            @pl.when(z == last)
            def _():
                self.reduce_down().start()

        elif op == 4:
            pl.when((z > 0) & (2 * z < self.z_count))(self.arrive_upper)
            pl.when((z < last) & (2 * z >= self.z_count))(self.arrive_lower)
        elif op == 5:
            pl.when((z < last) & (2 * z >= self.z_count))(self.arrive_upper)
            pl.when((z > 0) & (2 * z < self.z_count))(self.arrive_lower)
        elif op == 6:
            pl.when(z == last)(self.arrive_upper)
            pl.when(z == 0)(self.arrive_lower)
        elif op == 7:
            pl.when((z < last) & (2 * z >= self.z_count))(self.back_upper)
            pl.when((z > 0) & (2 * z < self.z_count))(self.back_lower)
        elif op == 8:

            @pl.when((z > 0) & (2 * z < self.z_count))
            def _():
                self.back_upper()
                self.gather(7).start()

            @pl.when((z < last) & (2 * z >= self.z_count))
            def _():
                self.back_lower()
                self.gather(7).start()

        elif op == 9:

            @pl.when(z == 0)
            def _():
                self.back_upper()
                self.keep(False).wait()
                self.gather(7).start()

            @pl.when(z == last)
            def _():
                self.back_lower()
                self.keep(True).wait()
                self.gather(7).start()

        elif op == 10:
            self.gather(7).wait_recv()
            self.gather(8).start()
        elif op == 11:
            self.gather(8).wait_recv()
            self.gather(9).start()
        elif op == 12:
            self.gather(9).wait_recv()
            self.drain()

    OPS = 13

    def drain(self):
        z, last = self.me["z"], self.z_count - 1
        self.step0().wait_send()
        self.step1().wait_send()
        self.step2().wait_send()
        for stage in (7, 8, 9):
            self.gather(stage).wait_send()

        @pl.when(z < last)
        def _():
            self.reduce_up().wait_send()
            self.spread_up().wait_send()

        @pl.when(z > 0)
        def _():
            self.reduce_down().wait_send()
            self.spread_down().wait_send()


class LineChunk(Chunk):
    def __init__(self, *args):
        super().__init__(*args[:6], (args[6][0], None, None), *args[7:])
        self.ups, self.downs, self.small = args[6][1:]
        self.entry = self.quad + self.me["z"]
        self.half, self.quarter = self.rows // 2, self.rows // 4
        self.mine_half = pl.multiple_of(self.row + self.b1 * self.half, 16)
        self.mine_quarter = pl.multiple_of(self.mine_half + self.b2 * self.quarter, 16)

    @staticmethod
    def landing(rows):
        return ((4, rows), (3, rows), (3, rows), (1, rows))

    def across(self, stage, name, first, count):
        landing = self.ups if name == "up" else self.downs
        return self.copy(stage, name, self.piece(self.quad + first, count), landing.at[pl.ds(0, count)])

    def back(self, stage, name, first, count):
        here = self.place(self.quad + first, count, self.row, self.rows)
        return self.copy(stage, name, here, here)

    def place(self, start, count, row, rows):
        here, columns = pl.ds(row, rows), self.grad.shape[2]
        if len(self.total.shape) == 2:
            return self.total.at[here, pl.ds(pl.multiple_of(start * columns, 128), count * columns)]
        if count == 1:
            return self.total.at[start, here, :]
        return self.total.at[pl.ds(start, count), here, :]

    def part(self, row, rows):
        return self.grad.at[pl.ds(self.entry, 1), pl.ds(row, rows), :]

    def step1(self):
        other = pl.multiple_of(self.row + (1 - self.b1) * self.half, 16)
        return self.copy(1, self.first, self.part(other, self.half), self.small.at[:, pl.ds(0, self.half), :])

    def step2(self):
        other = pl.multiple_of(self.mine_half + (1 - self.b2) * self.quarter, 16)
        landing = self.small.at[:, pl.ds(self.half, self.quarter), :]
        return self.copy(2, self.second, self.part(other, self.quarter), landing)

    def finished(self):
        return self.grad.at[self.entry, pl.ds(self.mine_quarter, self.quarter), :]

    def keep(self):
        spot = self.place(self.entry, 1, self.mine_quarter, self.quarter)
        return pltpu.make_async_copy(self.finished(), spot, self.local.at[self.number])

    def gather2(self):
        spot = self.place(self.entry, 1, self.mine_quarter, self.quarter)
        return self.copy(7, self.second, self.finished(), spot)

    def gather1(self):
        here = self.place(self.entry, 1, self.mine_half, self.half)
        return self.copy(8, self.first, here, here)

    def gather0(self):
        here = self.place(self.quad, 4, self.row, self.rows)
        return self.copy(9, "core", here, here)

    def at_row(self, k, body):
        pl.when(self.me["z"] == k)(body)

    def from_below(self, k):
        return (k, self.z_count - k)

    def from_above(self, k):
        return (0, k + 1)

    def take_up(self, k):
        first, count = self.from_below(k)
        self.across(3, "up", first, count).wait_recv()
        add_into(self.grad, self.quad + first, self.row, self.ups, count, self.rows)
        if k < self.z_count - 1:
            self.across(3, "up", first + 1, count - 1).start()

    def take_down(self, k):
        first, count = self.from_above(k)
        self.across(4, "down", first, count).wait_recv()
        add_into(self.grad, self.quad + first, self.row, self.downs, count, self.rows)
        if k > 0:
            self.across(4, "down", first, count - 1).start()

    def back_up(self, k):
        self.back(6, "up", 0, k).wait_recv()
        if k < self.z_count - 1:
            self.back(6, "up", 0, k + 1).start()

    def back_down(self, k):
        last = self.z_count - 1
        self.back(5, "down", k + 1, last - k).wait_recv()
        if k > 0:
            self.back(5, "down", k, last - k + 1).start()

    def tick(self, op):
        last, middle = self.z_count - 1, self.z_count // 2
        if op == 0:
            self.step0().start()
        elif op == 1:
            self.step0().wait_recv()
            add_into(self.grad, self.quad, self.row, self.land0, 4, self.rows)
            self.at_row(0, lambda: self.across(3, "up", 1, last).start())
            self.at_row(last, lambda: self.across(4, "down", 0, last).start())
        elif op == 2:
            for k in range(1, last):
                self.at_row(k, functools.partial(self.take_up if k < middle else self.take_down, k))
        elif op == 3:
            for k in range(1, last):

                def arrive(k=k):
                    (self.take_down if k < middle else self.take_up)(k)
                    self.step1().start()

                self.at_row(k, arrive)
        elif op == 4:

            def bottom():
                self.take_down(0)
                self.step1().start()

            def top():
                self.take_up(last)
                self.step1().start()

            self.at_row(0, bottom)
            self.at_row(last, top)
        elif op == 5:
            self.step1().wait_recv()
            add_into(self.grad, self.entry, self.mine_half, self.small, 1, self.half)
            self.step2().start()
        elif op == 6:
            self.step2().wait_recv()
            landing = self.small.at[:, pl.ds(self.half, self.quarter), :]
            add_into(self.grad, self.entry, self.mine_quarter, landing, 1, self.quarter)
            self.keep().start()
            self.gather2().start()
        elif op == 7:
            self.gather2().wait_recv()
            self.keep().wait()
            self.gather1().start()
        elif op == 8:
            self.gather1().wait_recv()
            self.at_row(0, lambda: self.back(6, "up", 0, 1).start())
            self.at_row(last, lambda: self.back(5, "down", last, 1).start())
        elif op == 9:
            for k in range(1, last):
                self.at_row(k, functools.partial(self.back_up if k < middle else self.back_down, k))
        elif op == 10:
            for k in range(1, last):

                def complete(k=k):
                    (self.back_down if k < middle else self.back_up)(k)
                    self.gather0().start()

                self.at_row(k, complete)
        elif op == 11:

            def bottom():
                self.back_down(0)
                self.gather0().start()

            def top():
                self.back_up(last)
                self.gather0().start()

            self.at_row(0, bottom)
            self.at_row(last, top)
        elif op == 12:
            self.gather0().wait_recv()
            self.drain()

    def drain(self):
        last = self.z_count - 1
        for item in (self.step0(), self.step1(), self.step2(), self.gather2(), self.gather1(), self.gather0()):
            item.wait_send()
        for k in range(self.z_count):

            def sent(k=k):
                if k < last:
                    self.across(3, "up", k + 1, last - k).wait_send()
                    self.back(6, "up", 0, k + 1).wait_send()
                if k > 0:
                    self.across(4, "down", 0, k).wait_send()
                    self.back(5, "down", k, last - k + 1).wait_send()

            self.at_row(k, sent)


def sum_kernel(z_count, plan, *refs):
    n = 1 + max(item[0] for item in plan)
    parts = len(plan)
    ins, outs = refs[:n], refs[n : 2 * n]
    rest = refs[2 * n :]
    grads, rest = rest[:n], rest[n:]
    landings = rest[: 3 * parts]
    send, recv, local, load = rest[3 * parts :]
    me = where_am_i()
    peers = peers_of(me)
    loads = [pltpu.make_async_copy(ins[i], grads[i], load.at[i]) for i in range(n)]
    for item in loads:
        item.start()
    greet(me, peers, z_count)
    meet(me, z_count)
    for item in loads:
        item.wait()
    chunks = []
    for number, (i, row, rows, first) in enumerate(plan):
        landing = landings[3 * number : 3 * number + 3]
        chunks.append(
            Chunk(number, grads[i], outs[i], row, rows, first, landing, (send, recv, local), me, peers, z_count)
        )
    for at in range(parts + Chunk.OPS - 1):
        for number in range(parts):
            if 0 <= at - number < Chunk.OPS:
                chunks[number].tick(at - number)


def sum_call(arrays, plan, z_count):
    landing = []
    for i, row, rows, first in plan:
        columns, kind = arrays[i].shape[2], arrays[i].dtype
        landing += [
            pltpu.VMEM((4, rows, columns), kind),
            pltpu.VMEM((2, rows, columns), kind),
            pltpu.VMEM((1, 2 * rows, columns), kind),
        ]
    n = len(arrays)
    return pl.pallas_call(
        functools.partial(sum_kernel, z_count, plan),
        out_shape=tuple(jax.ShapeDtypeStruct(v.shape, v.dtype) for v in arrays),
        in_specs=[pl.BlockSpec(memory_space=pl.ANY)] * n,
        out_specs=tuple([pl.BlockSpec(memory_space=pl.ANY)] * n),
        scratch_shapes=[pltpu.VMEM(v.shape, v.dtype) for v in arrays]
        + landing
        + [
            pltpu.SemaphoreType.DMA((len(plan), STAGES)),
            pltpu.SemaphoreType.DMA((len(plan), STAGES)),
            pltpu.SemaphoreType.DMA((len(plan),)),
            pltpu.SemaphoreType.DMA((n,)),
        ],
        compiler_params=pltpu.CompilerParams(
            collective_id=0, has_side_effects=True, vmem_limit_bytes=56 * 2**20
        ),
    )(*arrays)


def columns_to_panels(value):
    rows, columns = value.shape
    return jnp.transpose(value.reshape(rows, 8, columns // 8), (1, 0, 2)).astype(jnp.bfloat16)


def panels_to_columns(panels):
    count, rows, width = panels.shape
    return jnp.transpose(panels.astype(jnp.float32), (1, 0, 2)).reshape(rows, count * width)


def sum_gradients(grads):
    (g_in, g_query, g_key, g_value, g_qgain, g_kgain, g_out, g_attn, g_pre, g_gate, g_up, g_down, g_post) = grads
    z_count = lax.axis_size(BLOCKS) // 2
    width = g_in.shape[0]
    gains = [g_in, g_attn, g_pre, g_post, g_qgain, g_kgain]
    sizes = [v.shape[0] for v in gains]
    flat = jnp.concatenate(gains)
    gain_rows = 32
    flat = jnp.pad(flat, (0, 8 * gain_rows * 128 - flat.shape[0])).reshape(8, gain_rows, 128)
    down = g_down.astype(jnp.bfloat16).reshape(8, -1, width)
    out = g_out.astype(jnp.bfloat16).reshape(8, -1, width)
    both = jnp.stack([g_key, g_value])
    head = g_key.shape[1]
    both = jnp.transpose(both.reshape(2, 2, width // 2, 2, head // 2), (0, 1, 3, 2, 4)).reshape(8, width // 2, head // 2)
    arrays = [down, columns_to_panels(g_gate), columns_to_panels(g_up), out, columns_to_panels(g_query), both.astype(jnp.bfloat16), flat]
    plan = []
    for i, v in enumerate(arrays[:-1]):
        rows = v.shape[1] // 2
        plan += [(i, 0, rows, "x"), (i, rows, rows, "y")]
    plan.append((6, 0, gain_rows, "x"))
    down, gate, up, out, query, both, flat = sum_call(arrays, plan, z_count)
    both = jnp.transpose(both.astype(jnp.float32).reshape(2, 2, 2, width // 2, head // 2), (0, 1, 3, 2, 4)).reshape(2, width, head)
    flat = flat.reshape(-1)
    cuts, at = [], 0
    for size in sizes:
        cuts.append(flat[at : at + size])
        at += size
    g_in, g_attn, g_pre, g_post, g_qgain, g_kgain = cuts
    return (
        g_in,
        panels_to_columns(query),
        both[0],
        both[1],
        g_qgain,
        g_kgain,
        out.astype(jnp.float32).reshape(g_out.shape),
        g_attn,
        g_pre,
        panels_to_columns(gate),
        panels_to_columns(up),
        down.astype(jnp.float32).reshape(g_down.shape),
        g_post,
    )


LOG2E = 1.4426950408889634
LN2 = 0.6931471805599453
PIECES = (2, 2, 2, 2, 2, 2, 1)
FIRST = ['y', 'y', 'x', 'v', 'x', 'y', 'x', 'x', 'x', 'y', 'x', 'y', 'y']
SCHEDULES = {
    4: (
        (1, 0), (0, 0), ("S", 0), ("F", 0), (1, 1), ("F", 1), (4, 0), ("M", 0), (4, 1), (3, 0), (0, 1), ("O", 0), (1, 2), (3, 1), ("V", 0), (0, 2),
        (4, 2), (2, 0), (7, 0), (5, 0), ("V", 1), (3, 2), (1, 3), (6, 0), (0, 3), ("V", 2), (2, 1), (5, 1), (0, 4), (1, 4), (4, 3), (4, 4), (7, 1),
        (1, 5), (0, 5), (4, 5), (6, 1), (3, 3), ("P", 0), ("P", 1), ("V", 3), (0, 6), (1, 6), ("P", 2), ("Q", 0), ("Q", 1), (7, 2), (4, 6), (5, 2),
        ("Q", 2), (1, 7), ("Q", 3), (6, 2), (3, 4), ("G", 0), (0, 7), (8, 0), (1, 8), (2, 2), (9, 0), (5, 3), ("T", 0), (8, 1), (4, 7), (7, 3),
        ("K", 0), (10, 0), (11, 0), (4, 8), (1, 9), (0, 8), (5, 4), (6, 3), (7, 4), (9, 1), ("I", 0), (12, 0), (3, 5), (8, 2), (6, 4), (5, 5), (7, 5), (2, 3), (10, 1),
         (6, 5), (12, 1), (2, 4), (3, 6), (11, 1), (9, 2), (10, 2), (5, 6), (12, 2), (7, 6), (4, 9), (6, 6), (5, 7), (3, 7), (2, 5), (1, 10),
        (11, 2), (6, 7), (12, 3), (8, 3), (0, 9), (7, 7), (12, 4), (8, 4), (10, 3), (9, 3), (5, 8), (10, 4), (9, 4), (11, 3), (4, 10), (2, 6),
        (11, 4), (7, 8), (3, 8), (6, 8), (8, 5), (5, 9), (12, 5), (10, 5), (7, 9), (6, 9), (11, 5), (8, 6), (9, 5), (0, 10), (12, 6), (2, 7), (11, 6),
        (12, 7), (10, 6), (8, 7), (10, 7), (9, 6), (7, 10), (11, 7), (9, 7), (3, 9), (6, 10), (8, 8), (1, 11), (10, 8), (2, 8), (8, 9), (2, 9),
        (12, 8), (12, 9), (10, 9), (9, 8), (11, 8), (9, 9), (5, 10), (7, 11), (11, 9), (4, 11), (12, 10), (8, 10), (3, 10), (0, 11), (11, 10),
        (7, 12), (10, 10), (2, 10), (4, 12), (9, 10), (6, 11), (8, 11), (10, 11), (5, 11), (12, 11), (11, 11), (8, 12), (3, 11), (2, 11), (12, 12),
        (11, 12), (9, 11), (1, 12), (2, 12), (0, 12), (5, 12), (3, 12), (9, 12), (6, 12), (10, 12),
    )
}


def dot(left, right):
    return jnp.dot(left, right, preferred_element_type=jnp.float32)


def dot_nt(left, right):
    return lax.dot_general(left, right, (((1,), (1,)), ((), ())), preferred_element_type=jnp.float32)


def inverse_rms(value):
    return lax.rsqrt(jnp.mean(value * value, axis=-1, keepdims=True) + EPS)


def rms_back(value, inverse, gain, grad):
    scaled = grad * gain
    normal = value * inverse
    mean = jnp.mean(scaled * normal, axis=-1, keepdims=True)
    terms = grad * normal
    return inverse * (scaled - normal * mean), jnp.sum(terms.reshape(-1, 8, terms.shape[-1]), axis=0)


def turn(value, cosine, sine):
    half = value.shape[-1] // 2
    first, second = value[:, :half], value[:, half:]
    return jnp.concatenate([first * cosine - second * sine, second * cosine + first * sine], axis=-1)


def turn_back(grad, cosine, sine):
    half = grad.shape[-1] // 2
    first, second = grad[:, :half], grad[:, half:]
    return jnp.concatenate([first * cosine + second * sine, second * cosine - first * sine], axis=-1)


def dot_tn(left, right):
    return lax.dot_general(left, right, (((0,), (0,)), ((), ())), preferred_element_type=jnp.float32)


def bf16(value):
    return value.astype(jnp.bfloat16)


def f32(value):
    return value.astype(jnp.float32)


class Names(dict):
    __getattr__ = dict.__getitem__


def layer_kernel(sizes, schedule, names, *refs):
    r = Names(zip(names, refs, strict=True))
    rows, width, hidden, heads, head, z_count = sizes
    scale = head**-0.5
    tile = 128
    tiles = [slice(at, at + tile) for at in range(0, rows, tile)]
    half = head // 2
    me = where_am_i()
    peers = peers_of(me)
    z, y, place = me["z"], me["y"], me["place"]
    last = z_count - 1

    weights = ["x", "w_key", "w_value", "w_query", "w_out", "w_gate", "w_up", "w_down", "dy"]
    joined = heads * head
    wide_k, wide_v = slice(joined, joined + head), slice(joined + head, joined + 2 * head)
    spots = {"w_query": slice(0, joined), "w_key": wide_k, "w_value": wide_v}
    pair = ("w_gate", "w_up")
    loads = {}
    for i, name in enumerate(weights):
        if name in spots:
            spot = r.w_first.at[:, spots[name]]
        elif name in pair:
            spot = r.w_pair.at[pair.index(name)]
        else:
            spot = r[name]
        loads[name] = pltpu.make_async_copy(r[name + "_in"], spot, r.load_sem.at[i])
    early = ("x", "w_key", "w_value")
    for name in early:
        loads[name].start()
    greet(me, peers, z_count)

    def begins(token):
        begin, end = jnp.zeros_like(token), jnp.int32(0)
        for j in range(r.lengths.shape[1]):
            end = end + r.lengths[0, j]
            begin = jnp.where(token >= end, end, begin)
        return begin

    token = place * rows + lax.broadcasted_iota(jnp.int32, (1, rows), 1)
    begin = begins(token)
    entry = f32(lax.broadcasted_iota(jnp.int32, (1, half), 1))
    speed = jnp.exp(-(2.0 * entry / head) * jnp.log(BASE))
    for t in tiles:
        column = place * rows + t.start + lax.broadcasted_iota(jnp.int32, (tile, 1), 0)
        angle = f32(column - begins(column)) * speed
        r.cosine[t, :] = jnp.cos(angle)
        r.sine[t, :] = jnp.sin(angle)
    gain_in = r.norm_in[...].reshape(1, width)
    gain_q = r.query_gain[...].reshape(1, head)
    gain_k = r.key_gain[...].reshape(1, head)
    gain_attn = r.norm_attn[...].reshape(1, width)
    gain_pre = r.norm_pre[...].reshape(1, width)
    gain_post = r.norm_post[...].reshape(1, width)

    def allowed(source):
        key = source * rows + lax.broadcasted_iota(jnp.int32, (rows, rows), 0)
        return (key >= begin) & (key <= token)

    loads["x"].wait()
    loads["w_key"].wait()
    loads["w_value"].wait()
    for name in weights:
        if name not in early:
            loads[name].start()
    for t in tiles:
        x = f32(r.x[t, :])
        r.a[t, :] = bf16(x * inverse_rms(x) * gain_in)
    r.kp[...] = dot(r.a[...], r.w_first[:, wide_k])
    r.kv[place, :, head : 2 * head] = bf16(dot(r.a[...], r.w_first[:, wide_v]))
    for t in tiles:
        kp = r.kp[t, :]
        r.kv[place, t, 0:head] = bf16(turn(kp * inverse_rms(kp) * gain_k, r.cosine[t, :], r.sine[t, :]))

    def send_kv(source, route):
        return pltpu.make_async_remote_copy(
            src_ref=r.kv.at[source],
            dst_ref=r.kv.at[source],
            send_sem=r.kv_send.at[route, source],
            recv_sem=r.kv_recv.at[source],
            device_id=peers["y"] if route else peers["up"],
            device_id_type=MESH,
        )

    def send_half(values):
        half_block = r.kv.at[0, :, head * values : head * (values + 1)]
        return pltpu.make_async_remote_copy(
            src_ref=half_block,
            dst_ref=half_block,
            send_sem=r.half_send.at[values],
            recv_sem=r.half_recv.at[values],
            device_id=peers["up"] if values else peers["y"],
            device_id_type=MESH,
        )

    meet(me, z_count)
    pl.when(z < last)(lambda: send_kv(place, 0).start())
    pl.when(y == 0)(lambda: send_kv(place, 1).start())

    loads["w_query"].wait()
    for h in range(heads):
        wide = slice(h * head, (h + 1) * head)
        r.qp[:, wide] = dot(r.a[...], r.w_first[:, wide])
        for t in tiles:
            qp = r.qp[t, wide]
            q = turn(qp * inverse_rms(qp) * gain_q, r.cosine[t, :], r.sine[t, :])
            q = bf16(q * (scale * LOG2E))
            r.q[h * rows + t.start : h * rows + t.stop, :] = q
            r.qt[:, h * rows + t.start : h * rows + t.stop] = q.T

    columns = [slice(h * rows, (h + 1) * rows) for h in range(heads)]

    def visit(source):
        vt = r.kv[source, :, head : 2 * head].T
        mask = allowed(source)
        for here in columns:
            p = jnp.where(mask, jnp.exp2(dot(r.kv[source, :, 0:head], r.qt[:, here])), 0.0)
            total = jnp.sum(p, axis=0, keepdims=True)
            o = dot(vt, bf16(p))
            r.total[:, here] = r.total[:, here] + total
            r.ot[:, here] = r.ot[:, here] + o

    r.total[...] = jnp.zeros_like(r.total)
    r.ot[...] = jnp.zeros_like(r.ot)

    def take_column(back):
        mine = place - 2 * back

        @pl.when(back <= z)
        def _():
            send_kv(mine, 0).wait_recv()
            pl.when(z < last)(lambda: send_kv(mine, 0).start())
            pl.when(mine > 0)(lambda: send_kv(mine, 1).start())
            pl.when(mine == 0)(lambda: send_half(0).start())

    def attend(step, carry):
        at = step - 1 - y
        back = at // 2 + 1
        other = (at >= 0) & (lax.rem(at + 2, 2) == 1)
        source = jnp.where(at >= 0, place - 2 * back + jnp.where(other, 1 - 2 * y, 0), place - step)

        @pl.when((step == 1) & (y == 1))
        def _():
            send_kv(place - 1, 1).wait_recv()
            pl.when((z == 0) & (z < last))(lambda: send_half(1).start())

        pl.when(at == 0)(lambda: take_column(1))

        @pl.when(other)
        def _():
            take_column(back + 1)
            pl.when(source > 0)(lambda: send_kv(source, 1).wait_recv())

            @pl.when(source == 0)
            def _():
                send_half(1).wait_recv()
                pl.when(z < last)(lambda: send_half(1).start())
                send_half(0).wait_recv()

        visit(source)
        return carry

    lax.fori_loop(0, 1 + y + 2 * z, attend, 0)
    for h, here in enumerate(columns):
        total = r.total[:, here]
        o = r.ot[:, here] * (1.0 / total)
        r.lse[:, here] = jnp.log2(total)
        r.ot[:, here] = o
        r.ob[:, h * head : (h + 1) * head] = bf16(o).T

    loads["w_out"].wait()
    r.ap[...] = dot(r.ob[:, 0:joined], r.w_out[...])
    for t in tiles:
        ap = r.ap[t, :]
        x1 = f32(r.x[t, :]) + ap * inverse_rms(ap) * gain_attn
        r.x1[t, :] = x1
        r.m[t, :] = bf16(x1 * inverse_rms(x1) * gain_pre)
    loads["w_gate"].wait()
    loads["w_up"].wait()
    block = hidden // 8

    def quarters(body):
        def both(pair, carry):
            for quarter in (2 * pair, 2 * pair + 1):
                body(pl.ds(pl.multiple_of(quarter * 2 * block, 128), 2 * block))
            return carry

        lax.fori_loop(0, 2, both, 0)

    def feed(cols):
        gate = dot(r.m[...], r.w_pair[0, :, cols])
        up = dot(r.m[...], r.w_pair[1, :, cols])
        inner = 0.7978845608028654 * (gate + 0.044715 * gate * gate * gate)
        th = jnp.tanh(inner)
        cdf = 0.5 * (1.0 + th)
        act = gate * cdf
        slope = cdf + 0.5 * gate * (1.0 - th * th) * 0.7978845608028654 * (1.0 + 3 * 0.044715 * gate * gate)
        r.hid[:, cols] = bf16(act * up)
        r.side_gate[:, cols] = bf16(slope * up)
        r.side_up[:, cols] = bf16(act)

    quarters(feed)
    loads["w_down"].wait()
    loads["dy"].wait()
    r.wide[...] = dot(r.hid[...], r.w_down[...])
    r.gains[...] = jnp.zeros_like(r.gains)

    def gain(k, terms):
        r.gains[k, :, 0 : terms.shape[1]] = r.gains[k, :, 0 : terms.shape[1]] + terms

    for t in tiles:
        f = r.wide[t, :]
        inverse = inverse_rms(f)
        r.out_held[t, :] = bf16(r.x1[t, :] + f * inverse * gain_post)
        df, g = rms_back(f, inverse, gain_post, f32(r.dy[t, :]))
        r.df[t, :] = bf16(df)
        gain(3, g)
    def two_blocks(body):
        def both(pair, carry):
            for j in (2 * pair, 2 * pair + 1):
                body(j, pl.ds(pl.multiple_of(j * block, 128), block))
            return carry

        lax.fori_loop(0, 4, both, 0)

    leaving = [
        pltpu.make_async_copy(r.out_held, r.out, r.load_sem.at[len(weights)]),
        pltpu.make_async_copy(r.dx_held, r.dx, r.load_sem.at[len(weights) + 1]),
    ]
    leaving[0].start()

    def down_grad(j, cols):
        r.g_down[j] = bf16(dot_tn(r.hid[:, cols], r.df[...]))

    two_blocks(down_grad)

    chunks = []
    sems = (r.red_send, r.red_recv, r.red_local)
    for name, count in r_plan(sizes):
        grad, total = r["g_" + name], r["t_" + name]
        step = grad.shape[1] // count
        for i in range(count):
            number, kind = len(chunks), FIRST[len(chunks)]
            make, first = (LineChunk, {"u": "x", "v": "y"}[kind]) if kind in "uv" else (Chunk, kind)
            landing = tuple(r[f"land{k}_{number}"] for k in range(len(make.landing(step))))
            chunks.append(make(number, grad, total, i * step, step, first, landing, sems, me, peers, z_count))

    def side_grads(part):
        def one(cols):
            dh = dot_nt(r.df[...], r.w_down[cols, :])
            r.side_gate[:, cols] = bf16(dh * f32(r.side_gate[:, cols]))
            r.side_up[:, cols] = bf16(dh * f32(r.side_up[:, cols]))

        quarters(one)

    def feed_grads(part):
        grad, side = ((r.g_gate, r.side_gate), (r.g_up, r.side_up))[part]

        def one(j, cols):
            grad[j] = bf16(dot_tn(r.m[...], side[:, cols]))

        two_blocks(one)

    def middle_back(part):
        r.wide[...] = dot_nt(r.side_gate[...], r.w_pair[0]) + dot_nt(r.side_up[...], r.w_pair[1])
        for t in tiles:
            x1 = r.x1[t, :]
            dx1, g = rms_back(x1, inverse_rms(x1), gain_pre, r.wide[t, :])
            gain(2, g)
            dx1 = dx1 + f32(r.dy[t, :])
            r.x1[t, :] = dx1
            ap = r.ap[t, :]
            dap, g = rms_back(ap, inverse_rms(ap), gain_attn, dx1)
            gain(1, g)
            r.dap[t, :] = bf16(dap)

    def out_back(part):
        for h, here in enumerate(columns):
            wide = slice(h * head, (h + 1) * head)
            g = bf16(dot_tn(r.ob[:, wide], r.dap[...]))
            r.g_out[2 * h] = g[0:half]
            r.g_out[2 * h + 1] = g[half:head]
            do = bf16(dot_nt(r.dap[...], r.w_out[wide, :]))
            r.do[here, :] = do
            turned = do.T
            r.dot[:, here] = turned
            r.delta[:, here] = jnp.sum(f32(turned) * r.ot[:, here], axis=0, keepdims=True)
        r.ot[...] = jnp.zeros_like(r.ot)

    probs, dscores = r.hid.at[:, 0 : heads * rows], r.side_gate.at[:, 0 : heads * rows]

    def visit_back(source, target):
        kt = r.kv[source, :, 0:head].T
        mask = allowed(source)
        for here in columns:
            s = dot(r.kv[source, :, 0:head], r.qt[:, here])
            p = jnp.where(mask, jnp.exp2(s - r.lse[:, here]), 0.0)
            dp = dot(r.kv[source, :, head : 2 * head], r.dot[:, here])
            probs[:, here] = bf16(p)
            dscores[:, here] = bf16(p * (dp - r.delta[:, here]))
        target[:, 0:head] = bf16(dot(dscores[...], r.q[...]))
        target[:, head : 2 * head] = bf16(dot(probs[...], r.do[...]))
        for here in columns:
            r.ot[:, here] = r.ot[:, here] + dot(kt, dscores[:, here])

    def staged(own, row):
        return r.w_pair.at[own, 0:rows, row * 2 * head : (row + 1) * 2 * head]

    def to_partner(row):
        return pltpu.make_async_remote_copy(
            src_ref=staged(0, row),
            dst_ref=r.from_partner.at[row],
            send_sem=r.dkv_send.at[0, row],
            recv_sem=r.dkv_recv.at[0, row],
            device_id=peers["y"],
            device_id_type=MESH,
        )

    def to_below(row):
        return pltpu.make_async_remote_copy(
            src_ref=staged(1, row),
            dst_ref=r.from_above.at[row],
            send_sem=r.dkv_send.at[1, row],
            recv_sem=r.dkv_recv.at[1, row],
            device_id=peers["down"],
            device_id_type=MESH,
        )

    def visit_row(row):
        def one(own, carry):
            column = jnp.where(own == 1, y, 1 - y)

            @pl.when((row < z) | ((row == z) & (column <= y)))
            def _():
                visit_back(2 * row + column, staged(own, row))
                pl.when(own == 0)(lambda: to_partner(row).start())

            return carry

        lax.fori_loop(0, 2, one, 0)

    def pass_down(row):
        @pl.when(row < z)
        def _():
            to_partner(row).wait_recv()
            pl.when(z < last)(lambda: to_below(row).wait_recv())
            for t in tiles:
                value = f32(staged(1, row)[t, :]) + f32(r.from_partner[row, t, :])
                above = jnp.where(z < last, f32(r.from_above[row, t, :]), 0.0)
                staged(1, row)[t, :] = bf16(value + above)
            to_below(row).start()

    def queries_back(h):
        wide = slice(h * head, (h + 1) * head)
        for t in tiles:
            dq = (r.ot[:, h * rows + t.start : h * rows + t.stop] * scale).T
            qp = r.qp[t, wide]
            dqp, g = rms_back(qp, inverse_rms(qp), gain_q, turn_back(dq, r.cosine[t, :], r.sine[t, :]))
            gain(4, g)
            r.ob[t, wide] = bf16(dqp)

    def query_grad(part):
        for h in range(heads):
            g = bf16(dot_tn(r.a[...], r.ob[:, h * head : (h + 1) * head]))
            r.g_query[2 * h] = g[:, 0:half]
            r.g_query[2 * h + 1] = g[:, half:head]

    def own_total(part):
        for row in range(z_count):

            @pl.when(row == z)
            def _():
                pl.when(y == 0)(lambda: to_partner(row).wait_recv())
                pl.when(z < last)(lambda: to_below(row).wait_recv())
                for t in tiles:
                    beside = jnp.where(y == 0, f32(r.from_partner[row, t, :]), 0.0)
                    above = jnp.where(z < last, f32(r.from_above[row, t, :]), 0.0)
                    r.dkv[t, :] = f32(staged(1, row)[t, :]) + beside + above

    def keys_back(part):
        for t in tiles:
            dk = r.dkv[t, 0:head] * LN2
            kp = r.kp[t, :]
            dkp, g = rms_back(kp, inverse_rms(kp), gain_k, turn_back(dk, r.cosine[t, :], r.sine[t, :]))
            gain(5, g)
            r.ob[t, wide_k] = bf16(dkp)
            r.ob[t, wide_v] = bf16(r.dkv[t, head : 2 * head])
        low = width // 2
        g = bf16(dot_tn(r.a[...], r.ob[:, joined : joined + 2 * head]))
        for p in range(8):
            which, upper, side = p // 4, (p // 2) % 2, p % 2
            left = which * head + side * half
            r.g_kv[p] = g[upper * low : (upper + 1) * low, left : left + half]

    def input_back(part):
        r.wide[...] = dot_nt(r.ob[...], r.w_first[...])
        for t in tiles:
            x = f32(r.x[t, :])
            dx, g = rms_back(x, inverse_rms(x), gain_in, r.wide[t, :])
            gain(0, g)
            r.dx_held[t, :] = bf16(r.x1[t, :] + dx)
        leaving[1].start()
        r.g_gain[...] = jnp.zeros_like(r.g_gain)
        at = 0
        for k, size in enumerate((width, width, width, width, head, head)):
            g = jnp.sum(r.gains[k], axis=0, keepdims=True)
            for part in range(size // 128):
                r.g_gain[at // 16, at % 16 : at % 16 + 1, :] = g[:, part * 128 : (part + 1) * 128]
                at += 1

    work = {
        "S": side_grads,
        "F": feed_grads,
        "M": middle_back,
        "O": out_back,
        "V": visit_row,
        "P": pass_down,
        "Q": queries_back,
        "G": query_grad,
        "T": own_total,
        "K": keys_back,
        "I": input_back,
    }
    for what, step in schedule:
        if what in work:
            work[what](step)
        else:
            chunks[what].tick(step)

    for item in leaving:
        item.wait()
    pl.when(z < last)(lambda: send_kv(place, 0).wait_send())
    pl.when(y == 0)(lambda: send_kv(place, 1).wait_send())
    pl.when((y == 1) & (z < last))(lambda: send_half(1).wait_send())
    pl.when((y == 0) & (z > 0))(lambda: send_half(0).wait_send())
    for back in range(1, z_count):

        @pl.when(back <= z)
        def _():
            mine = place - 2 * back
            pl.when(z < last)(lambda: send_kv(mine, 0).wait_send())
            pl.when(mine > 0)(lambda: send_kv(mine, 1).wait_send())

    for row in range(z_count):
        pl.when((row < z) | ((row == z) & (y == 1)))(lambda: to_partner(row).wait_send())
        pl.when(row < z)(lambda: to_below(row).wait_send())


def r_plan(sizes):
    return list(zip(("down", "gate", "up", "out", "query", "kv", "gain"), PIECES, strict=True))


def gradient_shapes(sizes):
    rows, width, hidden, heads, head, z_count = sizes
    joined, half = heads * head, head // 2
    return {
        "down": ((8, hidden // 8, width), (8, hidden // 8, width)),
        "gate": ((8, width, hidden // 8), (width, hidden)),
        "up": ((8, width, hidden // 8), (width, hidden)),
        "out": ((8, joined // 8, width), (8, joined // 8, width)),
        "query": ((8, width, joined // 8), (width, joined)),
        "kv": ((8, width // 2, half), (2, 2, width // 2, head)),
        "gain": ((8, 16, 128), (8, 16, 128)),
    }


def layer_scratch(sizes):
    rows, width, hidden, heads, head, z_count = sizes
    joined = heads * head
    low, wide = jnp.bfloat16, jnp.float32
    arrays = {
        "x": ((rows, width), low),
        "w_first": ((width, joined + 2 * head), low),
        "w_out": ((joined, width), low),
        "w_pair": ((2, width, hidden), low),
        "w_down": ((hidden, width), low),
        "dy": ((rows, width), low),
        "a": ((rows, width), low),
        "out_held": ((rows, width), low),
        "dx_held": ((rows, width), low),
        "gains": ((6, 8, width), wide),
        "kp": ((rows, head), wide),
        "kv": ((2 * z_count, rows, 2 * head), low),
        "qp": ((rows, joined), wide),
        "q": ((heads * rows, head), low),
        "qt": ((head, heads * rows), low),
        "cosine": ((rows, head // 2), wide),
        "sine": ((rows, head // 2), wide),
        "wide": ((rows, width), wide),
        "ot": ((head, heads * rows), wide),
        "total": ((1, heads * rows), wide),
        "lse": ((1, heads * rows), wide),
        "delta": ((1, heads * rows), wide),
        "ob": ((rows, joined + 2 * head), low),
        "ap": ((rows, width), wide),
        "x1": ((rows, width), wide),
        "m": ((rows, width), low),
        "hid": ((rows, hidden), low),
        "side_gate": ((rows, hidden), low),
        "side_up": ((rows, hidden), low),
        "df": ((rows, width), low),
        "dap": ((rows, width), low),
        "do": ((heads * rows, head), low),
        "dot": ((head, heads * rows), low),
        "dkv": ((rows, 2 * head), wide),
        "from_partner": ((z_count, rows, 2 * head), low),
        "from_above": ((z_count, rows, 2 * head), low),
    }
    shapes = gradient_shapes(sizes)
    pieces = 0
    for name, count in r_plan(sizes):
        (eight, high, columns), kind = shapes[name][0], wide if name == "gain" else low
        step = high // count
        pieces += count
        arrays["g_" + name] = (shapes[name][0], kind)
        for number in range(pieces - count, pieces):
            for k, shape in enumerate(LineChunk.landing(step) if FIRST[number] in "uv" else Chunk.landing(step)):
                arrays[f"land{k}_{number}"] = (shape + (columns,), kind)
    sems = {
        "load_sem": (11,),
        "kv_send": (2, 2 * z_count),
        "kv_recv": (2 * z_count,),
        "half_send": (2,),
        "half_recv": (2,),
        "dkv_send": (2, z_count),
        "dkv_recv": (2, z_count),
        "red_send": (pieces, STAGES),
        "red_recv": (pieces, STAGES),
        "red_local": (pieces,),
    }
    return arrays, sems


def layer_bytes(sizes):
    total = 0
    for shape, kind in layer_scratch(sizes)[0].values():
        size = jnp.dtype(kind).itemsize
        for n in shape[:-2]:
            size *= n
        total += size * max(shape[-2], 8) * max(shape[-1], 128)
    return total


VMEM_BYTES = 64 * 2**20


def widen_kernel(count, gain_sizes, *refs):
    ins, table_in, both, tokens = refs[: count - 2], refs[count - 2], refs[count - 1], refs[count : count + 2]
    refs = refs[count + 2 :]
    outs, gains_out, tokens_out = refs[:count], refs[count : count + 6], refs[count + 6 : count + 8]
    refs = refs[count + 8 :]
    narrow, broad, gains, (table, came, gone) = refs[: count + 2], refs[count + 2 : 2 * count + 2], refs[2 * count + 2 : 2 * count + 8], refs[2 * count + 8 :]
    ins = (both.at[0], both.at[1]) + ins + tokens + (table_in,)
    outs = outs + tokens_out + gains_out
    held = broad + narrow[count:] + gains
    loads = [pltpu.make_async_copy(ins[i], (narrow + (table,))[i], came.at[i]) for i in range(count + 3)]
    stores = [pltpu.make_async_copy(held[i], outs[i], gone.at[i]) for i in range(count + 8)]
    order = (*range(2, count), 0, 1)
    for i in (*order, *range(count, count + 3)):
        loads[i].start()
    for i in order:
        loads[i].wait()

        def body(j, carry):
            here = pl.ds(pl.multiple_of(j * 64, 64), 64)
            broad[i][here, :] = f32(narrow[i][here, :])
            return carry

        lax.fori_loop(0, narrow[i].shape[0] // 64, body, 0)
        stores[i].start()
    for i in (count, count + 1):
        loads[i].wait()
        stores[i].start()
    loads[count + 2].wait()
    at = 0
    for i, gain in enumerate(gains):
        for part in range(gain_sizes[i] // 128):
            gain[part * 128 : (part + 1) * 128] = table[at // 16, at % 16, :]
            at += 1
        stores[count + 2 + i].start()
    for item in stores:
        item.wait()


def widen(both, matrices, table, tokens, gain_sizes):
    count = len(matrices) + 2
    shapes = [both.shape[1:]] * 2 + [v.shape for v in matrices]
    anywhere = pl.BlockSpec(memory_space=pl.ANY)
    return pl.pallas_call(
        functools.partial(widen_kernel, count, gain_sizes),
        out_shape=tuple(jax.ShapeDtypeStruct(shape, jnp.float32) for shape in shapes)
        + tuple(jax.ShapeDtypeStruct((n,), jnp.float32) for n in gain_sizes)
        + tuple(jax.ShapeDtypeStruct(v.shape, v.dtype) for v in tokens),
        in_specs=[anywhere] * (count + 2),
        out_specs=tuple([anywhere] * (count + len(gain_sizes) + 2)),
        scratch_shapes=[pltpu.VMEM(shape, jnp.bfloat16) for shape in shapes + [v.shape for v in tokens]]
        + [pltpu.VMEM(shape, jnp.float32) for shape in shapes]
        + [pltpu.VMEM((n,), jnp.float32) for n in gain_sizes]
        + [pltpu.VMEM(table.shape, table.dtype)]
        + [pltpu.SemaphoreType.DMA((count + 3,)), pltpu.SemaphoreType.DMA((count + 8,))],
        compiler_params=pltpu.CompilerParams(vmem_limit_bytes=VMEM_BYTES),
    )(*matrices, table, both, *tokens)


def whole_layer(sizes, tokens, lengths, cotangent, norm_in, w_query, w_key, w_value, query_gain, key_gain, w_out, norm_attn, norm_pre, w_gate, w_up, w_down, norm_post):
    rows, width, hidden, heads, head, z_count = sizes
    joined = heads * head
    inputs = {
        "lengths": lengths,
        "norm_in": norm_in,
        "query_gain": query_gain,
        "key_gain": key_gain,
        "norm_attn": norm_attn,
        "norm_pre": norm_pre,
        "norm_post": norm_post,
        "x_in": tokens[0],
        "w_key_in": w_key,
        "w_value_in": w_value,
        "w_query_in": w_query,
        "w_out_in": w_out,
        "w_gate_in": w_gate,
        "w_up_in": w_up,
        "w_down_in": w_down,
        "dy_in": cotangent[0],
    }
    spaces = {name: pltpu.SMEM if name == "lengths" else pl.ANY if name.endswith("_in") and name != "norm_in" else pltpu.VMEM for name in inputs}
    shapes = gradient_shapes(sizes)
    outputs = {"out": (rows, width), "dx": (rows, width)}
    outputs.update({"t_" + name: shapes[name][1] for name in shapes})
    arrays, sems = layer_scratch(sizes)
    names = list(inputs) + list(outputs) + list(arrays) + list(sems)
    results = pl.pallas_call(
        functools.partial(layer_kernel, sizes, SCHEDULES[z_count], names),
        out_shape=tuple(
            jax.ShapeDtypeStruct(shape, jnp.float32 if name == "t_gain" else jnp.bfloat16) for name, shape in outputs.items()
        ),
        in_specs=[pl.BlockSpec(memory_space=spaces[name]) for name in inputs],
        out_specs=tuple(
            pl.BlockSpec(memory_space=pl.ANY) for name in outputs
        ),
        scratch_shapes=[pltpu.VMEM(*item) for item in arrays.values()]
        + [pltpu.SemaphoreType.DMA(item) for item in sems.values()],
        compiler_params=pltpu.CompilerParams(
            collective_id=1, has_side_effects=True, vmem_limit_bytes=VMEM_BYTES
        ),
    )(*inputs.values())
    r = Names(zip(outputs, results, strict=True))
    matrices = [
        r.t_query,
        r.t_out.reshape(joined, width),
        r.t_gate,
        r.t_up,
        r.t_down.reshape(hidden, width),
    ]
    both = r.t_kv.reshape(2, width, head)
    sums = widen(both, matrices, r.t_gain, (r.out, r.dx), (width, width, width, width, head, head))
    g_key, g_value, g_query, g_out, g_gate, g_up, g_down = sums[:7]
    g_in, g_attn, g_pre, g_post, g_qgain, g_kgain, output, input_grad = sums[7:]
    return (
        output[None],
        input_grad[None],
        g_in,
        g_query,
        g_key,
        g_value,
        g_qgain,
        g_kgain,
        g_out,
        g_attn,
        g_pre,
        g_gate,
        g_up,
        g_down,
        g_post,
    )


def per_device(
    tokens,
    lengths,
    cotangent,
    norm_in,
    w_query,
    w_key,
    w_value,
    query_gain,
    key_gain,
    w_out,
    norm_attn,
    norm_pre,
    w_gate,
    w_up,
    w_down,
    norm_post,
):
    rows = tokens.shape[1]
    head = query_gain.shape[0]
    heads = w_query.shape[1] // head
    sizes = (rows, tokens.shape[2], w_gate.shape[1], heads, head, lax.axis_size(BLOCKS) // 2)
    if sizes[-1] in SCHEDULES and layer_bytes(sizes) <= VMEM_BYTES:
        return whole_layer(
            sizes,
            tokens,
            lengths,
            cotangent,
            norm_in,
            w_query,
            w_key,
            w_value,
            query_gain,
            key_gain,
            w_out,
            norm_attn,
            norm_pre,
            w_gate,
            w_up,
            w_down,
            norm_post,
        )
    scale = head ** (-0.5)
    count = lax.axis_size(BLOCKS)
    place = lax.axis_index(BLOCKS)
    row = lengths[0]
    local_idx = place * rows + jnp.arange(rows, dtype=jnp.int32)
    seg_q, pos_q = segment_of(local_idx, row)
    cosine, sine = rotary_tables(pos_q, head)

    def block_mask(source):
        key_idx = source * rows + jnp.arange(rows, dtype=jnp.int32)
        seg_k, unused = segment_of(key_idx, row)
        return (seg_q[:, None] == seg_k[None, :]) & (local_idx[:, None] >= key_idx[None, :])

    x_in = tokens[0].astype(jnp.float32)
    normal_a = normed(x_in, norm_in).astype(jnp.bfloat16)
    q_proj = jnp.dot(normal_a, w_query, preferred_element_type=jnp.float32).reshape(
        rows, heads, head
    )
    k_proj = jnp.dot(normal_a, w_key, preferred_element_type=jnp.float32)
    v_proj = jnp.dot(normal_a, w_value, preferred_element_type=jnp.float32)
    query = prepare(q_proj, query_gain, cosine[:, None, :], sine[:, None, :]).astype(jnp.bfloat16)
    keys = prepare(k_proj, key_gain, cosine, sine).astype(jnp.bfloat16)
    values = v_proj.astype(jnp.bfloat16)
    q_heads = jnp.transpose(query, (1, 0, 2))

    def absorb(state, pair, source):
        allowed = block_mask(source)
        big, total, accum = state
        raw = jnp.einsum("hqd,kd->hqk", q_heads, pair[0], preferred_element_type=jnp.float32)
        scores = jnp.where(allowed[None], scale * raw, NEG)
        big_new = jnp.maximum(big, jnp.max(scores, axis=-1, keepdims=True))
        expo = jnp.where(allowed[None], jnp.exp(scores - big_new), 0.0)
        fade = jnp.exp(big - big_new)
        total = total * fade + jnp.sum(expo, axis=-1, keepdims=True)
        accum = accum * fade + jnp.einsum(
            "hqk,kd->hqd", expo.astype(jnp.bfloat16), pair[1], preferred_element_type=jnp.float32
        )
        return (big_new, total, accum)

    pair = jnp.stack([keys, values])
    state = (
        jnp.full((heads, rows, 1), NEG, jnp.float32),
        jnp.zeros((heads, rows, 1), jnp.float32),
        jnp.zeros((heads, rows, head), jnp.float32),
    )
    state = absorb(state, pair, place)

    def cycle_forward(step, carry):
        inner, moving = carry
        moving = from_behind(moving, BLOCKS, 1)
        return (absorb(inner, moving, (place - step) % count), moving)

    state, unused_pair = lax.fori_loop(1, count, cycle_forward, (state, pair))
    big, total, accum = state
    attended = accum / total
    lse = big + jnp.log(total)
    joined = jnp.transpose(attended, (1, 0, 2)).reshape(rows, heads * head).astype(jnp.bfloat16)
    a_proj = jnp.dot(joined, w_out, preferred_element_type=jnp.float32)
    x_mid = x_in + normed(a_proj, norm_attn)
    mixed = normed(x_mid, norm_pre).astype(jnp.bfloat16)
    gate = jnp.dot(mixed, w_gate, preferred_element_type=jnp.float32)
    upper = jnp.dot(mixed, w_up, preferred_element_type=jnp.float32)

    def activate(gate_in, upper_in):
        return jax.nn.gelu(gate_in, approximate=True) * upper_in

    hidden = activate(gate, upper).astype(jnp.bfloat16)
    f_proj = jnp.dot(hidden, w_down, preferred_element_type=jnp.float32)
    output = x_mid + normed(f_proj, norm_post)
    grad_y = cotangent[0].astype(jnp.float32)
    d_fproj, g_post = normed_back(f_proj, norm_post, grad_y)
    d_fproj = d_fproj.astype(jnp.bfloat16)
    g_down = dot_tn(hidden, d_fproj)
    d_hidden = dot_nt(d_fproj, w_down)
    d_gate, d_upper = jax.vjp(activate, gate, upper)[1](d_hidden)
    d_gate = d_gate.astype(jnp.bfloat16)
    d_upper = d_upper.astype(jnp.bfloat16)
    g_gate = dot_tn(mixed, d_gate)
    g_up = dot_tn(mixed, d_upper)
    d_mixed = dot_nt(d_gate, w_gate) + dot_nt(d_upper, w_up)
    d_mid, g_pre = normed_back(x_mid, norm_pre, d_mixed)
    d_mid = grad_y + d_mid
    d_aproj, g_attn = normed_back(a_proj, norm_attn, d_mid)
    d_aproj = d_aproj.astype(jnp.bfloat16)
    g_out = dot_tn(joined, d_aproj)
    d_joined = dot_nt(d_aproj, w_out).astype(
        jnp.bfloat16
    )
    do_heads = jnp.transpose(d_joined.reshape(rows, heads, head), (1, 0, 2))
    delta = jnp.sum(do_heads.astype(jnp.float32) * attended, axis=-1, keepdims=True)

    def visit(d_query, moving, grads, source):
        allowed = block_mask(source)
        raw = jnp.einsum("hqd,kd->hqk", q_heads, moving[0], preferred_element_type=jnp.float32)
        probs = jnp.where(allowed[None], jnp.exp(scale * raw - lse), 0.0)
        dv_add = jnp.einsum(
            "hqk,hqd->kd", probs.astype(jnp.bfloat16), do_heads, preferred_element_type=jnp.float32
        )
        d_probs = jnp.einsum("hqd,kd->hqk", do_heads, moving[1], preferred_element_type=jnp.float32)
        d_scores = (scale * probs * (d_probs - delta)).astype(jnp.bfloat16)
        dq_add = jnp.einsum("hqk,kd->hqd", d_scores, moving[0], preferred_element_type=jnp.float32)
        dk_add = jnp.einsum("hqk,hqd->kd", d_scores, q_heads, preferred_element_type=jnp.float32)
        return (d_query + dq_add, grads + jnp.stack([dk_add, dv_add]))

    d_query = jnp.zeros((heads, rows, head), jnp.float32)
    grads = jnp.zeros((2, rows, head), jnp.float32)
    d_query, grads = visit(d_query, pair, grads, place)

    def cycle_backward(step, carry):
        dq_in, moving, grads_in = carry
        moving = from_behind(moving, BLOCKS, 1)
        grads_in = pass_home(grads_in)
        dq_in, grads_in = visit(dq_in, moving, grads_in, (place - step) % count)
        return (dq_in, moving, grads_in)

    d_query, unused_pair, grads = lax.fori_loop(1, count, cycle_backward, (d_query, pair, grads))
    grads = pass_home(grads)

    def query_piece(proj, gain):
        return prepare(proj, gain, cosine[:, None, :], sine[:, None, :])

    def key_piece(proj, gain):
        return prepare(proj, gain, cosine, sine)

    d_qproj, g_qgain = jax.vjp(query_piece, q_proj, query_gain)[1](
        jnp.transpose(d_query, (1, 0, 2))
    )
    d_kproj, g_kgain = jax.vjp(key_piece, k_proj, key_gain)[1](grads[0])
    d_qproj = d_qproj.reshape(rows, heads * head).astype(jnp.bfloat16)
    d_kproj = d_kproj.astype(jnp.bfloat16)
    d_vproj = grads[1].astype(jnp.bfloat16)
    g_query = dot_tn(normal_a, d_qproj)
    g_key = dot_tn(normal_a, d_kproj)
    g_value = dot_tn(normal_a, d_vproj)
    d_normal = dot_nt(d_qproj, w_query)
    d_normal = d_normal + dot_nt(d_kproj, w_key)
    d_normal = d_normal + dot_nt(d_vproj, w_value)
    d_input, g_in = normed_back(x_in, norm_in, d_normal)
    input_grad = (d_mid + d_input).astype(jnp.bfloat16)
    (
        g_in,
        g_query,
        g_key,
        g_value,
        g_qgain,
        g_kgain,
        g_out,
        g_attn,
        g_pre,
        g_gate,
        g_up,
        g_down,
        g_post,
    ) = sum_gradients(
        (
            g_in,
            g_query,
            g_key,
            g_value,
            g_qgain,
            g_kgain,
            g_out,
            g_attn,
            g_pre,
            g_gate,
            g_up,
            g_down,
            g_post,
        )
    )
    return (
        output.astype(jnp.bfloat16)[None],
        input_grad[None],
        g_in,
        g_query,
        g_key,
        g_value,
        g_qgain,
        g_kgain,
        g_out,
        g_attn,
        g_pre,
        g_gate,
        g_up,
        g_down,
        g_post,
    )


def solution(mesh):
    in_specs = (
        P(PARTS, BLOCKS, None),
        P(PARTS, None),
        P(PARTS, BLOCKS, None),
        P(),
        P(),
        P(),
        P(),
        P(),
        P(),
        P(),
        P(),
        P(),
        P(),
        P(),
        P(),
        P(),
    )
    out_specs = (
        P(PARTS, BLOCKS, None),
        P(PARTS, BLOCKS, None),
        P(),
        P(),
        P(),
        P(),
        P(),
        P(),
        P(),
        P(),
        P(),
        P(),
        P(),
        P(),
        P(),
    )
    return jax.shard_map(
        per_device, mesh=mesh, in_specs=in_specs, out_specs=out_specs, check_vma=False
    )
```
